32 devices in a mesh: gx: 8 (over z, x), gy: 4 (over y, core).
Axes of the slice: x: 2, y: 2, z: 4, core: 2. Of those that a mesh axis runs over, the one named last changes fastest.
Arguments:
- trial_stress: float32 [16, 1024, 512], P(None, 'gx', 'gy'), may hold values from 1.5 to 3.5
- old_strain: float32 [16, 1024, 512], P(None, 'gx', 'gy'), may hold values from 0 to 0.5
- yield_mask: int32 [16, 1024, 512], P(None, 'gx', 'gy'), may hold values from 0 to 1
- newton_count: int32 [16, 1024, 512], P(None, 'gx', 'gy'), may hold values from 3 to 6
- damage_threshold: float32 [16, 1024, 512], P(None, 'gx', 'gy'), may hold values from 0.1 to 0.5
Outputs:
- plastic_strain: float32 [16, 1024, 512], P(None, 'gx', 'gy')
- damage: float32 [16, 1024, 512], P(None, 'gx', 'gy')
- nodal_force: float32 [2, 16, 1024, 512], P(None, None, 'gx', 'gy')
The draws below stay inside these ranges and needn't reach their ends.
All inputs are finite; a program needn't handle non-finite values.
Results may differ from the reference program's by a relative error of at most 0.00002.
Values sent between devices are 32-bit elements; how exact they have to be, the bound alone decides.
No kernel may reach another device: no remote copies, remote signals or barrier semaphores. Data moves between devices by JAX's collectives and lax.ppermute only.
A program may use at most 64 MiB of HBM per device.

```python
import math
import jax
import jax.numpy as jnp
from jax import lax

CZ = 16
NEWTON_MAX = 6
OUTER = 3
NX = 1024
NY = 512


def draw_yield_mask(key, part):
    key_centre, key_coin = jax.random.split(key)
    centre = jax.random.randint(key_centre, (), 0, NX)
    row_ids = jnp.arange(NX, dtype=jnp.int32)
    distance = jnp.abs(row_ids - centre)
    distance = jnp.minimum(distance, NX - distance)
    inside = (distance * 16 < 3 * NX).astype(jnp.int32)
    coin_flip = jax.random.randint(key_coin, (CZ, NX, NY), 0, 2)
    return (coin_flip * inside[None, :, None]).astype(jnp.int32)


def plant(array, key, least, top_value):
    longest = array.shape.index(max(array.shape))
    spots = []
    for shift in (0, 1):
        where = [jax.random.randint(jax.random.fold_in(key, axis), (), 0, length) for axis, length in enumerate(array.shape)]
        where[longest] = (where[longest] + shift) % array.shape[longest]
        spots.append(tuple(where))
    return array.at[spots[0]].set(least).at[spots[1]].set(top_value)


def levels(rng, extent, cuts, least, largest):
    def one(dim, parts):
        steps = jax.random.uniform(jax.random.fold_in(jax.random.fold_in(rng, 6), dim), (parts,), jnp.float32, least / len(cuts), largest / len(cuts))
        return jnp.repeat(jnp.exp(steps), extent[dim] // parts).reshape((-1,) + (1,) * (len(extent) - dim - 1))

    loudness = one(*cuts[0])
    for cut in cuts[1:]:
        loudness = loudness * one(*cut)
    return loudness


def setup_inputs(seed: int = 0) -> dict:
    keys = jax.random.split(jax.random.key(seed), 6)
    trial_stress = jnp.clip(1.5 + 2.0 * jax.random.uniform(keys[0], (CZ, NX, NY), jnp.float32) ** levels(keys[0], (CZ, NX, NY), ((1, 8), (2, 4)), -0.2, 0.2), 1.5, 3.5)
    old_strain = jnp.clip(0.5 * jax.random.uniform(keys[1], (CZ, NX, NY), jnp.float32) ** levels(keys[1], (CZ, NX, NY), ((1, 8), (2, 4)), -0.2, 0.2), 0.0, 0.5)
    yield_mask = draw_yield_mask(jax.random.fold_in(keys[5], 71), 0)
    newton_count = plant(jax.random.randint(keys[3], (CZ, NX, NY), 3, NEWTON_MAX + 1), jax.random.fold_in(keys[3], 1), 3, NEWTON_MAX).astype(jnp.int32)
    damage_threshold = jnp.clip(0.1 + 0.4 * jax.random.uniform(keys[4], (CZ, NX, NY), jnp.float32) ** levels(keys[4], (CZ, NX, NY), ((1, 8), (2, 4)), -0.2, 0.2), 0.1, 0.5)
    return {"trial_stress": trial_stress, "old_strain": old_strain, "yield_mask": yield_mask, "newton_count": newton_count, "damage_threshold": damage_threshold}


gauss_taps = [math.exp(-((offset - 8) ** 2) / 32.0) for offset in range(17)]


def return_map(stress_in, strain_in, count_in, damage_in):
    increment = jnp.zeros_like(stress_in)
    soften = 1.0 - 0.5 * damage_in
    for sweep_no in range(1, NEWTON_MAX + 1):
        decay_term = jnp.exp(-4.0 * (strain_in + increment))
        residual = stress_in - increment - (1.0 + 0.5 * (1.0 - decay_term)) * soften
        update = increment + 0.4 * residual / (1.0 + 2.0 * decay_term)
        increment = jnp.where(count_in >= sweep_no, update, increment)
    return increment


def smooth_axis(source, axis_index):
    length = source.shape[axis_index]
    widths = [(0, 0)] * source.ndim
    widths[axis_index] = (8, 8)
    padded = jnp.pad(source, widths)
    summed = jnp.zeros_like(source)
    for offset in range(17):
        summed = summed + gauss_taps[offset] * lax.slice_in_dim(padded, offset, offset + length, axis=axis_index)
    return summed


def reference(trial_stress, old_strain, yield_mask, newton_count, damage_threshold):
    counts = yield_mask * newton_count
    weight_z = smooth_axis(jnp.ones((trial_stress.shape[0],), jnp.float32), 0)
    weight_x = smooth_axis(jnp.ones((trial_stress.shape[1],), jnp.float32), 0)
    weight_y = smooth_axis(jnp.ones((trial_stress.shape[2],), jnp.float32), 0)
    normal = weight_z[:, None, None] * weight_x[None, :, None] * weight_y[None, None, :]
    damage = jnp.zeros_like(trial_stress)
    for outer_no in range(OUTER):
        increment = return_map(trial_stress, old_strain, counts, damage)
        plastic_strain = old_strain + increment
        averaged = smooth_axis(smooth_axis(smooth_axis(plastic_strain, 1), 2), 0)
        nonlocal_strain = averaged / normal
        damage = 1.0 - jnp.exp(-jnp.maximum(nonlocal_strain - damage_threshold, 0.0) / 0.3)
    stress = (1.0 - damage) * (trial_stress - increment)
    padded = jnp.pad(stress, ((0, 0), (1, 0), (1, 0)))
    own_cell = padded[:, 1:, 1:]
    upper_cell = padded[:, :-1, 1:]
    left_cell = padded[:, 1:, :-1]
    corner_cell = padded[:, :-1, :-1]
    force_x = 0.5 * (upper_cell + corner_cell - own_cell - left_cell)
    force_y = 0.5 * (left_cell + corner_cell - own_cell - upper_cell)
    return plastic_strain, damage, jnp.stack([force_x, force_y])
```

```python
import functools
import math

import jax
import jax.numpy as jnp
import ml_dtypes
import numpy as np
from jax import lax
from jax.experimental import pallas as pl
from jax.experimental.pallas import tpu as pltpu
from jax.sharding import PartitionSpec as P

OUTER = 3
REACH = 8
LOG2E = math.log2(math.e)
HALF_LN2 = 0.5 * math.log(2.0)
VMEM_BYTES = 24 * 1024 * 1024


def tap(offset):
    return math.exp(-(offset**2) / 32.0) if abs(offset) <= REACH else 0.0


def band(length):
    return np.array([[tap(c - r) for c in range(length)] for r in range(length)])


def depth_matrix(layers):
    weights = band(layers)
    return weights / weights.sum(axis=1, keepdims=True)


def down_block():
    return np.array([[tap(REACH + i - r) for r in range(REACH)] for i in range(REACH)])


def up_block():
    return np.array([[tap(REACH + r - i) for r in range(REACH)] for i in range(REACH)])


def halves(matrix):
    exact = np.asarray(matrix, np.float64)
    high = exact.astype(ml_dtypes.bfloat16)
    low = (exact - high.astype(np.float64)).astype(ml_dtypes.bfloat16)
    return high, low


def left_constant(matrix):
    high, low = halves(matrix)
    return np.block([[high, high], [low, low]])


def right_constant(matrix):
    high, low = halves(matrix)
    return np.block([[high, low], [high, low]])


def split(value):
    high = value.astype(jnp.bfloat16)
    low = (value - high.astype(jnp.float32)).astype(jnp.bfloat16)
    return high, low


def left_product(constant, value):
    rows = constant.shape[0] // 2
    both = jnp.dot(constant, jnp.concatenate(split(value), axis=0), preferred_element_type=jnp.float32)
    return both[:rows] + both[rows:]


def right_product(value, constant):
    cols = constant.shape[1] // 2
    both = jnp.dot(jnp.concatenate(split(value), axis=1), constant, preferred_element_type=jnp.float32)
    return both[:, :cols] + both[:, cols:]


def newton_state(stress, strain, yields, count, soften):
    start = 2.0 * stress - 3.5 * soften
    shift = start + (2.0 * strain - HALF_LN2)
    drop = 0.2 * soften
    state = start
    for sweep_no in range(1, 7):
        update = state * (0.8 - 0.2 * jnp.tanh(shift - state)) - drop
        state = update if sweep_no <= 3 else jnp.where(count >= sweep_no, update, state)
    return jnp.where(yields > 0, state, start)


def plastic(stress, strain, soften, state):
    return (strain + (stress - 1.75 * soften)) - 0.5 * state


def depth_smooth(layers, matrix):
    count = len(layers)
    half = count // 2
    sums = [layers[k] + layers[count - 1 - k] for k in range(half)]
    diffs = [layers[k] - layers[count - 1 - k] for k in range(half)]
    out = [None] * count
    for row in range(half):
        even = odd = None
        for k in range(half):
            near, far = matrix[row, k], matrix[row, count - 1 - k]
            plus, minus = float(0.5 * (near + far)), float(0.5 * (near - far))
            if plus == 0.0 and minus == 0.0:
                continue
            even = sums[k] * plus if even is None else even + sums[k] * plus
            odd = diffs[k] * minus if odd is None else odd + diffs[k] * minus
        out[row] = even + odd
        out[count - 1 - row] = even - odd
    return out


def slot_ids(shape):
    return lax.broadcasted_iota(jnp.int32, shape, 1) // REACH


def sides(axis, even, odd):
    first = lax.axis_index(axis) % 2 == 0
    return jnp.where(first, odd, even), jnp.where(first, even, odd)


def partners(axis, low, high):
    first = lax.axis_index(axis) % 2 == 0
    return jnp.where(first, high, low), jnp.where(first, low, high)


def add_columns(value, layer, low, high):
    cols = value.shape[1]
    slots = slot_ids(value.shape)
    packed = jnp.where(slots == layer, low, high)
    moved = pltpu.roll(packed, (cols - layer * REACH) % cols, 1) if layer else packed
    return value + jnp.where((slots == 0) | (slots == cols // REACH - 1), moved, 0.0)


def retained(smooth, norm, threshold):
    return jnp.exp2(jnp.minimum(threshold - smooth * norm, 0.0) * (LOG2E / 0.3))


def edge_kernel(fresh, *refs):
    if fresh:
        (stress, strain, yields, count, up_ref, down_ref, even_ref, odd_ref, block) = refs
    else:
        (stress, strain, yields, count, threshold, smooth, col_even, col_odd, norm,
         up_ref, down_ref, even_ref, odd_ref, block) = refs
    layers, rows = stress.shape[0], stress.shape[1]
    sent = []
    for first_row, constant in ((0, up_ref), (rows - REACH, down_ref)):
        part = pl.ds(first_row, REACH)
        if not fresh:
            low, high = sides("gy", col_even[part, :], col_odd[part, :])
        for layer in range(layers):
            if fresh:
                soften = jnp.ones_like(stress[layer, part, :])
            else:
                full = add_columns(smooth[layer, part, :], layer, low, high)
                soften = 0.5 + 0.5 * retained(full, norm[part, :], threshold[layer, part, :])
            at = (layer, part, slice(None))
            state = newton_state(stress[at], strain[at], yields[at], count[at], soften)
            block[pl.ds(layer * REACH, REACH), :] = plastic(stress[at], strain[at], soften, state)
        sent.append(left_product(constant[...], block[...]))
    even, odd = partners("gx", *sent)
    even_ref[...] = even
    odd_ref[...] = odd


def main_kernel(depth, fresh, last, *refs):
    if fresh:
        (stress, strain, yields, count, band_ref, toward_low, toward_high, *outs) = refs
    else:
        (stress, strain, yields, count, threshold, smooth, col_even, col_odd, norm,
         band_ref, toward_low, toward_high, *outs) = refs
    if last:
        across, low_cols, high_cols, plastic_out, effective, deep, pack_low, pack_high = outs
    else:
        across, low_cols, high_cols, deep, pack_low, pack_high = outs
    layers, rows, cols = stress.shape

    def sweep(index, carry):
        part = pl.ds(pl.multiple_of(index * REACH, REACH), REACH)
        if not fresh:
            low, high = sides("gy", col_even[part, :], col_odd[part, :])
        values = []
        for layer in range(layers):
            at = (layer, part, slice(None))
            if fresh:
                soften = jnp.ones_like(stress[at])
            else:
                full = add_columns(smooth[at], layer, low, high)
                soften = 0.5 + 0.5 * retained(full, norm[part, :], threshold[at])
            state = newton_state(stress[at], strain[at], yields[at], count[at], soften)
            value = plastic(stress[at], strain[at], soften, state)
            values.append(value)
            if last:
                plastic_out[at] = value
                effective[at] = 1.75 * soften + 0.5 * state
        for layer, value in enumerate(depth_smooth(values, depth)):
            deep[layer, part, :] = value
        return carry

    lax.fori_loop(0, rows // REACH, sweep, 0)

    constant = band_ref[...]
    for layer in range(0, layers, 2):
        pair = jnp.concatenate([deep[layer], deep[layer + 1]], axis=1)
        result = left_product(constant, pair)
        across[layer] = result[:, :cols]
        across[layer + 1] = result[:, cols:]

    def pack(index, carry):
        part = pl.ds(pl.multiple_of(index * REACH, REACH), REACH)
        low, high = pack_edges([across[layer, part, :] for layer in range(layers)])
        pack_low[part, :] = low
        pack_high[part, :] = high
        return carry

    lax.fori_loop(0, rows // REACH, pack, 0)
    low_cols[...] = right_product(pack_low[...], toward_low[...])
    high_cols[...] = right_product(pack_high[...], toward_high[...])


def pack_edges(values):
    cols = values[0].shape[1]
    slots = slot_ids(values[0].shape)
    low = high = jnp.zeros_like(values[0])
    for layer, value in enumerate(values):
        moved = pltpu.roll(value, layer * REACH, 1) if layer else value
        low = jnp.where(slots == layer, moved, low)
        high = jnp.where(slots == (layer - 1) % (cols // REACH), moved, high)
    return low, high


def corner_kernel(row_even, row_odd, low_cols, high_cols, toward_low, toward_high, even_ref, odd_ref):
    rows, cols = low_cols.shape
    layers = row_even.shape[0] // REACH
    low_rows, high_rows = sides("gx", row_even[...], row_odd[...])
    packs = [
        pack_edges([block[layer * REACH : (layer + 1) * REACH] for layer in range(layers)])
        for block in (low_rows, high_rows)
    ]
    low_add = right_product(jnp.concatenate([packs[0][0], packs[1][0]], axis=0), toward_low[...])
    high_add = right_product(jnp.concatenate([packs[0][1], packs[1][1]], axis=0), toward_high[...])
    even, odd = partners("gy", low_cols[...], high_cols[...])
    even_add, odd_add = partners("gy", low_add, high_add)
    for ref, base, add in ((even_ref, even, even_add), (odd_ref, odd, odd_add)):
        ref[...] = base
        ref[pl.ds(0, REACH), :] = base[:REACH] + add[:REACH]
        ref[pl.ds(rows - REACH, REACH), :] = base[rows - REACH :] + add[REACH:]


def column_kernel(across, row_even, row_odd, band_ref, smooth):
    layers, rows, cols = across.shape
    constant = band_ref[...]
    low_rows, high_rows = sides("gx", row_even[...], row_odd[...])
    for layer in range(layers):
        block = slice(layer * REACH, (layer + 1) * REACH)
        value = across[layer]
        value = jnp.concatenate(
            [
                value[:REACH] + low_rows[block],
                value[REACH : rows - REACH],
                value[rows - REACH :] + high_rows[block],
            ],
            axis=0,
        )
        smooth[layer] = right_product(value, constant)


def final_kernel(effective, threshold, smooth, col_even, col_odd, norm, damage, stress):
    layers, rows, cols = effective.shape

    def finish(index, carry):
        part = pl.ds(pl.multiple_of(index * REACH, REACH), REACH)
        low, high = sides("gy", col_even[part, :], col_odd[part, :])
        for layer in range(layers):
            at = (layer, part, slice(None))
            full = add_columns(smooth[at], layer, low, high)
            kept = retained(full, norm[part, :], threshold[at])
            damage[at] = 1.0 - kept
            stress[at] = kept * effective[at]
        return carry

    lax.fori_loop(0, rows // REACH, finish, 0)


def call(kernel, outs, scratch, cost, *operands):
    space = pl.BlockSpec(memory_space=pltpu.VMEM)
    return pl.pallas_call(
        kernel,
        out_shape=[jax.ShapeDtypeStruct(shape, jnp.float32) for shape in outs],
        in_specs=[space] * len(operands),
        out_specs=[space] * len(outs),
        scratch_shapes=[pltpu.VMEM(shape, jnp.float32) for shape in scratch],
        compiler_params=pltpu.CompilerParams(vmem_limit_bytes=VMEM_BYTES),
        cost_estimate=pl.CostEstimate(flops=cost, bytes_accessed=cost // 16, transcendentals=0),
    )(*operands)


def exchange(axis, even, odd):
    count = lax.axis_size(axis)
    results = []
    for start, value in ((0, even), (1, odd)):
        pairs = []
        for low in range(start, count - 1, 2):
            pairs += [(low, low + 1), (low + 1, low)]
        results.append(lax.ppermute(value, axis, pairs))
    return results


def edge_weights(axis, length):
    extent = length * lax.axis_size(axis)
    positions = lax.axis_index(axis) * length + jnp.arange(length, dtype=jnp.int32)
    total = jnp.zeros((length,), jnp.float32)
    for offset in range(-REACH, REACH + 1):
        inside = (positions + offset >= 0) & (positions + offset < extent)
        total = total + jnp.where(inside, tap(offset), 0.0)
    return total


def from_behind(value, axis):
    count = lax.axis_size(axis)
    return lax.ppermute(value, axis, [(source, source + 1) for source in range(count - 1)])


def local(trial_stress, old_strain, yield_mask, newton_count, damage_threshold):
    layers, rows, cols = trial_stress.shape
    slots = cols // REACH
    assert layers == slots and layers % 2 == 0
    depth = depth_matrix(layers)
    to_above = left_constant(np.kron(depth, down_block()))
    to_below = left_constant(np.kron(depth, up_block()))
    row_band = left_constant(band(rows))
    col_band = right_constant(band(cols))
    low_matrix = np.zeros((cols, cols))
    high_matrix = np.zeros((cols, cols))
    for layer in range(layers):
        own = slice(layer * REACH, (layer + 1) * REACH)
        before = (layer - 1) % slots
        other = slice(before * REACH, (before + 1) * REACH)
        low_matrix[own, other] = up_block().T
        high_matrix[other, own] = down_block().T
    toward_low = right_constant(low_matrix)
    toward_high = right_constant(high_matrix)

    norm = 1.0 / (edge_weights("gx", rows)[:, None] * edge_weights("gy", cols)[None, :])
    inputs = (trial_stress, old_strain, yield_mask, newton_count)
    whole = (layers, rows, cols)
    strip = (layers * REACH, cols)
    packed = (rows, layers * REACH)
    work = layers * rows * cols

    state = ()
    for outer_no in range(OUTER):
        fresh, last = outer_no == 0, outer_no == OUTER - 1
        row_even, row_odd = call(
            functools.partial(edge_kernel, fresh),
            [strip, strip], [strip], work * 16,
            *inputs, *state, to_below, to_above,
        )
        row_even, row_odd = exchange("gx", row_even, row_odd)
        across, low_cols, high_cols, *results = call(
            functools.partial(main_kernel, depth, fresh, last),
            [whole, packed, packed] + ([whole, whole] if last else []),
            [whole, packed, packed], work * 400,
            *inputs, *state, row_band, toward_low, toward_high,
        )
        col_even, col_odd = call(
            corner_kernel, [packed, packed], [], work * 16,
            row_even, row_odd, low_cols, high_cols, toward_low, toward_high,
        )
        col_even, col_odd = exchange("gy", col_even, col_odd)
        (smooth,) = call(
            column_kernel, [whole], [], work * 100, across, row_even, row_odd, col_band
        )
        state = (damage_threshold, smooth, col_even, col_odd, norm)
    plastic_strain, effective = results
    damage, stress = call(final_kernel, [whole, whole], [], work * 100, effective, *state)

    upper_row = from_behind(stress[:, rows - 1, :], "gx")
    with_upper = jnp.concatenate([upper_row[:, None, :], stress], axis=1)
    left_column = from_behind(with_upper[:, :, cols - 1], "gy")
    extended = jnp.concatenate([left_column[:, :, None], with_upper], axis=2)
    own_cell = extended[:, 1:, 1:]
    upper_cell = extended[:, :-1, 1:]
    left_cell = extended[:, 1:, :-1]
    corner_cell = extended[:, :-1, :-1]
    force_x = 0.5 * (upper_cell + corner_cell - own_cell - left_cell)
    force_y = 0.5 * (left_cell + corner_cell - own_cell - upper_cell)
    return plastic_strain, damage, jnp.stack([force_x, force_y])


def solution(mesh):
    split_in = P(None, "gx", "gy")
    return jax.shard_map(
        local,
        mesh=mesh,
        in_specs=(split_in,) * 5,
        out_specs=(split_in, split_in, P(None, None, "gx", "gy")),
        check_vma=False,
    )
```

```python
import functools
import math

import jax
import jax.numpy as jnp
import numpy as np
from jax import lax
from jax.experimental import pallas as pl
from jax.experimental.pallas import tpu as pltpu
from jax.sharding import PartitionSpec as P

OUTER = 3
REACH = 8
RATE = math.log2(math.e) / 0.3
HALF_LN2 = 0.5 * math.log(2.0)
VMEM_BYTES = 24 * 1024 * 1024


def tap(offset):
    return math.exp(-(offset**2) / 32.0) if abs(offset) <= REACH else 0.0


def band(rows, cols, shift=0):
    return np.array([[tap(c - r + shift) for c in range(cols)] for r in range(rows)])


def depth_matrix(layers):
    weights = band(layers, layers)
    return weights / weights.sum(axis=1, keepdims=True)


def split(value):
    high = value.astype(jnp.bfloat16)
    low = (value - high.astype(jnp.float32)).astype(jnp.bfloat16)
    return high, low


def left_constant(matrix):
    high, low = split(matrix)
    return jnp.concatenate(
        [jnp.concatenate([high, high], axis=1), jnp.concatenate([low, low], axis=1)], axis=0
    )


def right_constant(matrix):
    both = jnp.concatenate(split(matrix), axis=1)
    return jnp.concatenate([both, both], axis=0)


def left_product(constant, value):
    rows = constant.shape[0] // 2
    halves = jnp.concatenate(split(value), axis=0)
    both = jnp.dot(constant, halves, preferred_element_type=jnp.float32)
    return both[:rows] + both[rows:]


def right_product(value, constant):
    cols = constant.shape[1] // 2
    halves = jnp.concatenate(split(value), axis=1)
    both = jnp.dot(halves, constant, preferred_element_type=jnp.float32)
    return both[:, :cols] + both[:, cols:]


def newton(stress, strain, yields, count, soften):
    start = 2.0 * stress - 3.5 * soften
    shift = start + (2.0 * strain - HALF_LN2)
    drop = 0.2 * soften
    state = start
    for sweep_no in range(1, 7):
        update = state * (0.8 - 0.2 * jnp.tanh(shift - state)) - drop
        state = update if sweep_no <= 3 else jnp.where(count >= sweep_no, update, state)
    moved = (strain + (stress - 1.75 * soften)) - 0.5 * state
    return jnp.where(yields > 0, moved, strain)


def depth_smooth(layers, matrix):
    count = len(layers)
    half = count // 2
    sums = [layers[k] + layers[count - 1 - k] for k in range(half)]
    diffs = [layers[k] - layers[count - 1 - k] for k in range(half)]
    out = [None] * count
    for row in range(half):
        even = odd = None
        for k in range(half):
            near, far = matrix[row, k], matrix[row, count - 1 - k]
            plus, minus = float(0.5 * (near + far)), float(0.5 * (near - far))
            if plus == 0.0 and minus == 0.0:
                continue
            even = sums[k] * plus if even is None else even + sums[k] * plus
            odd = diffs[k] * minus if odd is None else odd + diffs[k] * minus
        out[row] = even + odd
        out[count - 1 - row] = even - odd
    return out


def lane_ids(shape):
    return lax.broadcasted_iota(jnp.int32, shape, len(shape) - 1)


def on_even(axis):
    return lax.axis_index(axis) % 2 == 0


def sides(axis, even, odd):
    return jnp.where(on_even(axis), odd, even), jnp.where(on_even(axis), even, odd)


def send(axis, low, high, even_ref, odd_ref):
    even_ref[...] = jnp.where(on_even(axis), high, low)
    odd_ref[...] = jnp.where(on_even(axis), low, high)


def add_columns(value, layer, low, high):
    cols = value.shape[1]
    slots = lane_ids(value.shape) // REACH
    packed = jnp.where(slots == layer, low, high)
    shift = (cols - layer * REACH) % cols
    moved = packed if isinstance(layer, int) and layer == 0 else pltpu.roll(packed, shift, 1)
    return value + jnp.where((slots == 0) | (slots == cols // REACH - 1), moved, 0.0)


def retained(full, norm, threshold):
    return jnp.exp2(jnp.minimum(threshold - full * norm, 0.0) * RATE)


def first_edge_kernel(stress, strain, yields, count, below, above, even_ref, odd_ref,
                      stress_s, strain_s, yields_s, count_s, block, sems):
    layers, rows, cols = stress.shape
    pairs = ((stress, stress_s), (strain, strain_s), (yields, yields_s), (count, count_s))
    starts = (0, rows - REACH)
    copies = []
    for side, first_row in enumerate(starts):
        for index, (source, target) in enumerate(pairs):
            copies.append(
                pltpu.make_async_copy(
                    source.at[:, pl.ds(first_row, REACH), :], target.at[side], sems.at[side, index]
                )
            )
            copies[-1].start()
    sent = []
    extra = jnp.zeros((even_ref.shape[0] - layers * REACH, cols), jnp.float32)
    for side, matrix in enumerate((below, above)):
        for copy in copies[side * len(pairs) : (side + 1) * len(pairs)]:
            copy.wait()
        for layer in range(layers):
            at = (side, layer)
            block[pl.ds(layer * REACH, REACH), :] = newton(
                stress_s[at], strain_s[at], yields_s[at], count_s[at], jnp.ones((REACH, cols), jnp.float32)
            )
        product = left_product(left_constant(matrix[...]), block[...])
        sent.append(jnp.concatenate([product, extra], axis=0))
    send("gx", *sent, even_ref, odd_ref)


def edge_kernel(group, stress, strain, yields, count, threshold, smooth, col_even, col_odd, norm,
                below, above, even_ref, odd_ref, low_block, high_block, rest):
    layers, rows, cols = stress.shape
    starts = (0, rows - 2 * REACH, rows - REACH)
    received = []
    for first_row in starts:
        part = pl.ds(first_row + REACH, REACH)
        received.append(sides("gy", col_even[part, :], col_odd[part, :]))

    def layer_step(layer):
        for index, first_row in enumerate(starts):
            at = (layer, pl.ds(first_row, REACH), slice(None))
            extended = pl.ds(first_row + REACH, REACH)
            full = add_columns(smooth[layer, extended, :], layer, *received[index])
            soften = 0.5 + 0.5 * retained(full, norm[extended, :], threshold[at])
            value = newton(stress[at], strain[at], yields[at], count[at], soften)
            if index == 0:
                low_block[pl.ds(pl.multiple_of(layer * REACH, REACH), REACH), :] = value
            else:
                row = pl.multiple_of((2 * layer + index - 1) * REACH, REACH)
                high_block[pl.ds(row, REACH), :] = value
            if index == 2:
                kept = (stress[at] + strain[at]) - value
                rest[pl.ds(layer, 1), :] = kept[REACH - 1 :]
                rest[pl.ds(layers + layer, 1), :] = threshold[at][REACH - 1 :]

    def step(index, carry):
        for inner in range(group):
            layer_step(index * group + inner)
        return carry

    lax.fori_loop(0, layers // group, step, 0)
    low = left_product(left_constant(below[...]), low_block[...])
    high = left_product(left_constant(above[...]), high_block[...])
    extra = jnp.zeros((even_ref.shape[0] - low.shape[0], cols), jnp.float32)
    send(
        "gx", jnp.concatenate([low, extra], axis=0), jnp.concatenate([high, rest[...]], axis=0),
        even_ref, odd_ref,
    )


def main_kernel(depth, fresh, *refs):
    if fresh:
        (stress, strain, yields, count, band_ref, low_ref, high_ref, next_ref,
         across, low_cols, high_cols, deep, pack_low, pack_high, pack_next) = refs
    else:
        (stress, strain, yields, count, threshold, smooth, col_even, col_odd, norm, norm_last,
         band_ref, low_ref, high_ref, next_ref,
         across, low_cols, high_cols, plastic,
         deep, pack_low, pack_high, pack_next, pack_threshold, pack_kept) = refs
    layers, rows, cols = stress.shape
    blocks = rows // REACH
    constant = left_constant(band_ref[...])

    def layer_pair(index, carry):
        pair = []
        for inner in range(2):
            layer = 2 * index + inner
            values = []
            for block in range(blocks):
                at = (layer, pl.ds(block * REACH, REACH), slice(None))
                if fresh:
                    soften = jnp.ones((REACH, cols), jnp.float32)
                else:
                    extended = pl.ds((block + 1) * REACH, REACH)
                    low, high = sides("gy", col_even[extended, :], col_odd[extended, :])
                    full = add_columns(smooth[layer, extended, :], layer, low, high)
                    soften = 0.5 + 0.5 * retained(full, norm[extended, :], threshold[at])
                value = newton(stress[at], strain[at], yields[at], count[at], soften)
                values.append(value)
                if not fresh:
                    plastic[at] = value
            pair.append(jnp.concatenate(values, axis=0))
        result = left_product(constant, jnp.concatenate(pair, axis=1))
        deep[2 * index] = result[:, :cols]
        deep[2 * index + 1] = result[:, cols:]
        return carry

    lax.fori_loop(0, layers // 2, layer_pair, 0)

    def row_block(index, carry):
        part = pl.ds(pl.multiple_of(index * REACH, REACH), REACH)
        values = depth_smooth([deep[layer, part, :] for layer in range(layers)], depth)
        for layer, value in enumerate(values):
            across[layer, part, :] = value
        for ref, packed in zip((pack_low, pack_high, pack_next), pack_edges(values)):
            ref[part, :] = packed
        return carry

    lax.fori_loop(0, blocks + 1, row_block, 0)
    low_cols[...] = right_product(pack_low[...], right_constant(low_ref[...]))
    high = right_product(pack_high[...], right_constant(high_ref[...]))
    behind = right_product(pack_next[...], right_constant(next_ref[...]))
    if fresh:
        high_cols[...] = high
        return

    def last_column(index, carry):
        part = pl.ds(pl.multiple_of(index * REACH, REACH), REACH)
        lanes = lane_ids((REACH, cols))
        limit = kept = jnp.zeros((REACH, cols), jnp.float32)
        for layer in range(layers):
            at = (layer, part, slice(None))
            limit = jnp.where(lanes == layer, pltpu.roll(threshold[at], layer + 1, 1), limit)
            rest = (stress[at] + strain[at]) - plastic[at]
            kept = jnp.where(lanes == layers + layer, pltpu.roll(rest, layers + layer + 1, 1), kept)
        extended = pl.ds(pl.multiple_of((index + 1) * REACH, REACH), REACH)
        pack_threshold[extended, :] = limit
        pack_kept[extended, :] = kept
        return carry

    pack_threshold[pl.ds(0, REACH), :] = jnp.zeros((REACH, cols), jnp.float32)
    pack_kept[pl.ds(0, REACH), :] = jnp.zeros((REACH, cols), jnp.float32)
    lax.fori_loop(0, blocks, last_column, 0)
    lanes = lane_ids(pack_kept.shape)
    column = pack_threshold[...] - (high[:, cols:] + behind) * norm_last[...]
    high_cols[:, :cols] = high[:, :cols]
    high_cols[:, cols:] = jnp.where(lanes < layers, column, pack_kept[...])


def pack_edges(values):
    cols = values[0].shape[1]
    count = cols // REACH
    slots = lane_ids(values[0].shape) // REACH
    low = high = ahead = jnp.zeros_like(values[0])
    for layer, value in enumerate(values):
        moved = pltpu.roll(value, layer * REACH, 1) if layer else value
        low = jnp.where(slots == layer, moved, low)
        high = jnp.where(slots == (layer - 1) % count, moved, high)
        ahead = jnp.where(slots == (layer - 2) % count, moved, ahead)
    return low, high, ahead


def corner_kernel(row_even, row_odd, low_cols, high_cols, norm_last, low_ref, high_ref, next_ref,
                  even_ref, odd_ref, own_ref):
    cols = low_ref.shape[0]
    total = low_cols.shape[0]
    layers = (total - REACH) // REACH
    strip = layers * REACH
    from_low, from_high = sides("gx", row_even[...], row_odd[...])
    partial = from_low[strip : strip + layers]
    kept = from_low[strip + layers : strip + 2 * layers]
    limit = from_low[strip + 2 * layers : strip + 3 * layers]
    before = [jnp.broadcast_to(partial[layer : layer + 1], (REACH, cols)) for layer in range(layers)]
    packs = [pack_edges(before)] + [
        pack_edges([block[layer * REACH : (layer + 1) * REACH] for layer in range(layers)])
        for block in (from_low, from_high)
    ]
    low, high, ahead = (jnp.concatenate(group, axis=0) for group in zip(*packs))
    low_add = right_product(low, right_constant(low_ref[...]))
    high_add = right_product(high, right_constant(high_ref[...]))
    behind_add = right_product(ahead, right_constant(next_ref[...]))

    lanes = lane_ids((layers, cols))
    level = lax.broadcasted_iota(jnp.int32, (layers, cols), 0)
    corner_limit = jnp.where(lanes == level, limit[:, cols - 1 :], 0.0)
    corner_kept = jnp.where(lanes == layers + level, kept[:, cols - 1 :], 0.0)
    corner = jnp.sum(corner_limit + corner_kept, axis=0, keepdims=True)

    def place(base, add):
        return jnp.concatenate(
            [base[: 2 * REACH] + add[: 2 * REACH], base[2 * REACH : total - REACH],
             base[total - REACH :] + add[2 * REACH :]],
            axis=0,
        )

    low_all = place(low_cols[...], low_add)
    high_all = place(high_cols[:, :cols], high_add[:, :cols])
    last = norm_last[...]
    behind = high_add[:, cols:] + behind_add
    edges = jnp.concatenate([last[: 2 * REACH], last[total - REACH :]], axis=0)
    lanes = lane_ids(behind.shape)
    drop = jnp.where(lanes < layers, behind * edges, 0.0)
    column = place(high_cols[:, cols:], -drop)
    first = column[:REACH] + corner
    main = column[REACH:]
    quarter = strip // 4
    lanes = lane_ids((quarter, cols))
    folded = main[:quarter]
    for part in range(1, 4):
        moved = pltpu.roll(main[part * quarter : (part + 1) * quarter], part * 2 * layers, 1)
        folded = jnp.where(lanes // (2 * layers) == part, moved, folded)
    extra = jnp.zeros((quarter + REACH, cols), jnp.float32)
    send(
        "gy", jnp.concatenate([low_all[:, :cols], extra], axis=0),
        jnp.concatenate([high_all, folded, first], axis=0), even_ref, odd_ref,
    )
    own_ref[...] = low_all[:, cols:]


def column_kernel(across, row_even, row_odd, band_ref, smooth):
    layers, total, cols = across.shape
    strip = layers * REACH
    constant = right_constant(band_ref[...])

    def step(index, carry):
        for inner in range(2):
            layer = 2 * index + inner
            part = pl.ds(pl.multiple_of(layer * REACH, REACH), REACH)
            low, high = sides("gx", row_even[part, :], row_odd[part, :])
            line = pl.ds(strip + layer, 1)
            before, _ = sides("gx", row_even[line, :], row_odd[line, :])
            value = across[layer]
            value = jnp.concatenate(
                [value[:REACH] + before, value[REACH : 2 * REACH] + low,
                 value[2 * REACH : total - REACH], value[total - REACH :] + high],
                axis=0,
            )
            smooth[layer] = right_product(value, constant)
        return carry

    lax.fori_loop(0, layers // 2, step, 0)


def final_kernel(stress, strain, plastic, threshold, smooth, col_even, col_odd, row_even, row_odd,
                 norm, norm_before, own_cols, plastic_out, damage_out, force_out,
                 columns, damage_s, force_s, copy_sem, sems):
    layers, rows, cols = stress.shape
    total = rows + REACH
    strip = layers * REACH
    whole = pltpu.make_async_copy(plastic, plastic_out, copy_sem)
    whole.start()

    from_low, _ = sides("gy", col_even[...], col_odd[...])
    quarter = rows // 4
    folded = from_low[total : total + quarter]
    pieces = [from_low[total + quarter :], folded]
    for part in range(1, 4):
        pieces.append(pltpu.roll(folded, cols - part * 2 * layers, 1))
    column = jnp.concatenate(pieces, axis=0)
    limit = column - own_cols[...] * norm_before[...]
    kept = jnp.exp2(jnp.minimum(limit, 0.0) * RATE)
    columns[...] = kept * pltpu.roll(column, cols - layers, 1)

    def copies(layer):
        return (
            pltpu.make_async_copy(damage_s.at[layer], damage_out.at[layer], sems.at[0, layer]),
            pltpu.make_async_copy(force_s.at[0, layer], force_out.at[0, layer], sems.at[1, layer]),
            pltpu.make_async_copy(force_s.at[1, layer], force_out.at[1, layer], sems.at[2, layer]),
        )

    def step(layer, carry):
        lanes = lane_ids((REACH, cols))
        top = lax.broadcasted_iota(jnp.int32, (REACH, cols), 0) == 0
        above_sum = above_diff = None
        for block in range(rows // REACH + 1):
            extended = pl.ds(block * REACH, REACH)
            low, high = sides("gy", col_even[extended, :], col_odd[extended, :])
            full = add_columns(smooth[layer, extended, :], layer, low, high)
            if block == 0:
                line = pl.ds(strip + layers + layer, 1)
                rest, _ = sides("gx", row_even[line, :], row_odd[line, :])
                line = pl.ds(strip + 2 * layers + layer, 1)
                limit, _ = sides("gx", row_even[line, :], row_odd[line, :])
            else:
                at = (layer, pl.ds((block - 1) * REACH, REACH), slice(None))
                rest = (stress[at] + strain[at]) - plastic[at]
                limit = threshold[at]
            ratio = retained(full, norm[extended, :], limit)
            value = ratio * rest
            left = jnp.where(
                lanes == 0,
                pltpu.roll(columns[extended, :], (cols - layer) % cols, 1),
                pltpu.roll(value, 1, 1),
            )
            both = pltpu.roll(left + value, 1, 0)
            diff = pltpu.roll(left - value, 1, 0)
            if block:
                damage_s[at] = 1.0 - ratio
                force_s[(0, *at)] = 0.5 * (jnp.where(top, above_sum, both) - (left + value))
                force_s[(1, *at)] = 0.5 * (jnp.where(top, above_diff, diff) + (left - value))
            above_sum, above_diff = both, diff
        for copy in copies(layer):
            copy.start()
        return carry

    lax.fori_loop(0, layers, step, 0)

    def drain(layer, carry):
        for copy in copies(layer):
            copy.wait()
        return carry

    lax.fori_loop(0, layers, drain, 0)
    whole.wait()


def call(kernel, outs, scratch, cost, operands, anywhere=False, outs_anywhere=False):
    inside, outside = pl.BlockSpec(memory_space=pltpu.VMEM), pl.BlockSpec(memory_space=pl.ANY)
    far = 4 if anywhere else 0
    return pl.pallas_call(
        kernel,
        out_shape=[jax.ShapeDtypeStruct(shape, jnp.float32) for shape in outs],
        in_specs=[outside] * far + [inside] * (len(operands) - far),
        out_specs=[outside if outs_anywhere else inside] * len(outs),
        scratch_shapes=[pltpu.VMEM(s, jnp.float32) if isinstance(s, tuple) else s for s in scratch],
        compiler_params=pltpu.CompilerParams(vmem_limit_bytes=VMEM_BYTES),
        cost_estimate=pl.CostEstimate(flops=cost, bytes_accessed=cost // 16, transcendentals=0),
    )(*operands)


def exchange(axis, even, odd):
    count = lax.axis_size(axis)
    results = []
    for start, value in ((0, even), (1, odd)):
        pairs = []
        for low in range(start, count - 1, 2):
            pairs += [(low, low + 1), (low + 1, low)]
        results.append(lax.ppermute(value, axis, pairs))
    return results


def inverse_weights(axis, first, positions, length):
    extent = length * lax.axis_size(axis)
    places = lax.axis_index(axis) * length + first + jnp.arange(positions, dtype=jnp.int32)
    total = jnp.zeros((positions,), jnp.float32)
    for offset in range(-REACH, REACH + 1):
        inside = (places + offset >= 0) & (places + offset < extent)
        total = total + jnp.where(inside, tap(offset), 0.0)
    return 1.0 / jnp.maximum(total, tap(REACH))


def matrices(layers, rows, cols):
    depth = depth_matrix(layers)
    up, down = band(REACH, REACH, REACH), band(REACH, REACH, -REACH)
    below = np.kron(depth, up)
    near = np.concatenate([np.zeros((REACH, REACH)), down], axis=1)
    line = band(1, 2 * REACH, 1 - 2 * REACH)
    above = np.concatenate([np.kron(depth, near), np.kron(depth, line)], axis=0)
    rows_band = np.concatenate([np.zeros((REACH - 1, rows)), band(1, rows, 1), band(rows, rows)])
    slots = cols // REACH
    low, high, ahead = np.zeros((cols, 2 * cols)), np.zeros((cols, 2 * cols)), np.zeros((cols, cols))
    for layer in range(layers):
        own = slice(layer * REACH, (layer + 1) * REACH)
        previous = (layer - 1) % slots
        other = slice(previous * REACH, (previous + 1) * REACH)
        low[own, other] = up.T
        high[other, own] = down.T
        low[own, cols + layer] = [tap(j + 1) for j in range(REACH)]
        high[other, cols + layer] = [tap(REACH - 1 - j) for j in range(REACH)]
        ahead[((layer - 2) % slots) * REACH + REACH - 1, layer] = tap(REACH)
    constants = (below, above, rows_band, band(cols, cols), low, high, ahead)
    return depth, [jnp.asarray(matrix, jnp.float32) for matrix in constants]


def local(trial_stress, old_strain, yield_mask, newton_count, damage_threshold):
    layers, rows, cols = trial_stress.shape
    assert layers * REACH == cols == rows and layers % 2 == 0
    total, strip = rows + REACH, layers * REACH
    depth, (below, above, rows_band, cols_band, low, high, ahead) = matrices(layers, rows, cols)

    across_rows = inverse_weights("gx", -REACH, total, rows)[:, None]
    across_cols = inverse_weights("gy", -1, cols + 1, cols)[None, :]
    norm = across_rows * across_cols[:, 1:]
    norm_last = jnp.broadcast_to(across_rows * across_cols[:, cols:], (total, cols))
    norm_before = jnp.broadcast_to(across_rows * across_cols[:, :1], (total, cols))

    inputs = (trial_stress, old_strain, yield_mask, newton_count)
    whole, wide = (layers, rows, cols), (layers, total, cols)
    sent_rows = (strip + 3 * layers, cols)
    sent_cols = (total + rows // 4 + REACH, cols)
    packed, packed_two = (total, cols), (total, 2 * cols)
    work = layers * rows * cols
    columns = (low, high, ahead)

    for outer_no in range(OUTER):
        if outer_no == 0:
            edge = [pltpu.VMEM((2, layers, REACH, cols), kind) for kind in
                    (jnp.float32, jnp.float32, jnp.int32, jnp.int32)]
            row_even, row_odd = call(
                first_edge_kernel, [sent_rows] * 2,
                edge + [(strip, cols), pltpu.SemaphoreType.DMA((2, 4))], work * 16,
                (*inputs, below, above[:strip].reshape(strip, layers, 2, REACH)[:, :, 1].reshape(strip, strip)),
                anywhere=True,
            )
        else:
            row_even, row_odd = call(
                functools.partial(edge_kernel, 8), [sent_rows] * 2,
                [(strip, cols), (2 * strip, cols), (2 * layers, cols)], work * 16,
                (*inputs, damage_threshold, smooth, col_even, col_odd, norm, below, above),
            )
        row_even, row_odd = exchange("gx", row_even, row_odd)
        if outer_no == 0:
            across, low_cols, high_cols = call(
                functools.partial(main_kernel, depth, True), [wide, packed_two, packed_two],
                [wide, packed, packed, packed], work * 400,
                (*inputs, rows_band, *columns),
            )
        else:
            across, low_cols, high_cols, plastic = call(
                functools.partial(main_kernel, depth, False), [wide, packed_two, packed_two, whole],
                [wide, packed, packed, packed, packed, packed], work * 400,
                (*inputs, damage_threshold, smooth, col_even, col_odd, norm, norm_last,
                 rows_band, *columns),
            )
        col_even, col_odd, own_cols = call(
            corner_kernel, [sent_cols, sent_cols, packed], [], work * 16,
            (row_even, row_odd, low_cols, high_cols, norm_last, *columns),
        )
        col_even, col_odd = exchange("gy", col_even, col_odd)
        (smooth,) = call(
            column_kernel, [wide], [], work * 100, (across, row_even, row_odd, cols_band)
        )
    return tuple(call(
        final_kernel, [whole, whole, (2, *whole)],
        [packed, whole, (2, *whole), pltpu.SemaphoreType.DMA(()), pltpu.SemaphoreType.DMA((3, layers))],
        work * 100,
        (trial_stress, old_strain, plastic, damage_threshold, smooth, col_even, col_odd,
         row_even, row_odd, norm, norm_before, own_cols),
        outs_anywhere=True,
    ))


def solution(mesh):
    split_in = P(None, "gx", "gy")
    return jax.shard_map(
        local,
        mesh=mesh,
        in_specs=(split_in,) * 5,
        out_specs=(split_in, split_in, P(None, None, "gx", "gy")),
        check_vma=False,
    )
```

```python
import functools
import math

import jax
import jax.numpy as jnp
import numpy as np
from jax import lax
from jax.experimental import pallas as pl
from jax.experimental.pallas import tpu as pltpu
from jax.sharding import PartitionSpec as P

OUTER = 3
REACH = 8
RATE = math.log2(math.e) / 0.3
HALF_LN2 = 0.5 * math.log(2.0)
VMEM_BYTES = 24 * 1024 * 1024


def tap(offset):
    return math.exp(-(offset**2) / 32.0) if abs(offset) <= REACH else 0.0


def band(rows, cols, shift=0):
    return np.array([[tap(c - r + shift) for c in range(cols)] for r in range(rows)])


def depth_matrix(layers):
    weights = band(layers, layers)
    return weights / weights.sum(axis=1, keepdims=True)


def split(value):
    high = value.astype(jnp.bfloat16)
    low = (value - high.astype(jnp.float32)).astype(jnp.bfloat16)
    return high, low


def left_constant(matrix):
    high, low = split(matrix)
    return jnp.concatenate(
        [jnp.concatenate([high, high], axis=1), jnp.concatenate([low, low], axis=1)], axis=0
    )


def right_constant(matrix):
    both = jnp.concatenate(split(matrix), axis=1)
    return jnp.concatenate([both, both], axis=0)


def left_product(constant, value):
    rows = constant.shape[0] // 2
    halves = jnp.concatenate(split(value), axis=0)
    both = jnp.dot(constant, halves, preferred_element_type=jnp.float32)
    return both[:rows] + both[rows:]


def right_product(value, constant):
    cols = constant.shape[1] // 2
    halves = jnp.concatenate(split(value), axis=1)
    both = jnp.dot(halves, constant, preferred_element_type=jnp.float32)
    return both[:, :cols] + both[:, cols:]


def newton(stress, strain, yields, count, soften):
    start = 2.0 * stress - 3.5 * soften
    shift = start + (2.0 * strain - HALF_LN2)
    drop = 0.2 * soften
    state = start
    for sweep_no in range(1, 7):
        update = state * (0.8 - 0.2 * jnp.tanh(shift - state)) - drop
        state = update if sweep_no <= 3 else jnp.where(count >= sweep_no, update, state)
    moved = (strain + (stress - 1.75 * soften)) - 0.5 * state
    return jnp.where(yields > 0, moved, strain)


def depth_smooth(layers, matrix):
    count = len(layers)
    half = count // 2
    sums = [layers[k] + layers[count - 1 - k] for k in range(half)]
    diffs = [layers[k] - layers[count - 1 - k] for k in range(half)]
    out = [None] * count
    for row in range(half):
        even = odd = None
        for k in range(half):
            near, far = matrix[row, k], matrix[row, count - 1 - k]
            plus, minus = float(0.5 * (near + far)), float(0.5 * (near - far))
            if plus == 0.0 and minus == 0.0:
                continue
            even = sums[k] * plus if even is None else even + sums[k] * plus
            odd = diffs[k] * minus if odd is None else odd + diffs[k] * minus
        out[row] = even + odd
        out[count - 1 - row] = even - odd
    return out


def lane_ids(shape):
    return lax.broadcasted_iota(jnp.int32, shape, len(shape) - 1)


def on_even(axis):
    return lax.axis_index(axis) % 2 == 0


def sides(axis, even, odd):
    return jnp.where(on_even(axis), odd, even), jnp.where(on_even(axis), even, odd)


def send(axis, low, high, even_ref, odd_ref):
    even_ref[...] = jnp.where(on_even(axis), high, low)
    odd_ref[...] = jnp.where(on_even(axis), low, high)


def add_columns(value, layer, low, high):
    cols = value.shape[1]
    slots = lane_ids(value.shape) >> (REACH.bit_length() - 1)
    packed = jnp.where(slots == layer, low, high)
    shift = (cols - layer * REACH) % cols
    moved = packed if isinstance(layer, int) and layer == 0 else pltpu.roll(packed, shift, 1)
    return value + jnp.where((slots == 0) | (slots == cols // REACH - 1), moved, 0.0)


def retained(full, norm, threshold):
    return jnp.exp2(jnp.minimum(threshold - full * norm, 0.0) * RATE)


def first_edge_kernel(stress, strain, yields, count, below, above,
                      even_ref, odd_ref, norm, norm_last, norm_before, *refs):
    blank_smooth, blank_even, blank_odd, stress_s, strain_s, yields_s, count_s, block, sems = refs
    layers, rows, cols = stress.shape
    pairs = ((stress, stress_s), (strain, strain_s), (yields, yields_s), (count, count_s))
    starts = (0, rows - REACH)
    copies = []
    for side, first_row in enumerate(starts):
        for index, (source, target) in enumerate(pairs):
            copies.append(
                pltpu.make_async_copy(
                    source.at[:, pl.ds(first_row, REACH), :], target.at[side], sems.at[side, index]
                )
            )
            copies[-1].start()
    total = rows + REACH
    ids = lax.broadcasted_iota(jnp.int32, (total, cols), 0)
    down = inverse_weights("gx", ids - REACH, rows)
    lanes = lane_ids((REACH, cols))
    for ref, place in ((norm, lanes), (norm_last, 0 * lanes + (cols - 1)), (norm_before, 0 * lanes - 1)):
        ref[...] = down * inverse_weights("gy", place, cols)[:1]
    sent = []
    extra = jnp.zeros((even_ref.shape[0] - layers * REACH, cols), jnp.float32)
    for side, matrix in enumerate((below, above)):
        for copy in copies[side * len(pairs) : (side + 1) * len(pairs)]:
            copy.wait()
        for layer in range(layers):
            at = (side, layer)
            block[pl.ds(layer * REACH, REACH), :] = newton(
                stress_s[at], strain_s[at], yields_s[at], count_s[at], jnp.ones((REACH, cols), jnp.float32)
            )
        product = left_product(left_constant(matrix[...]), block[...])
        sent.append(jnp.concatenate([product, extra], axis=0))
    send("gx", *sent, even_ref, odd_ref)


def edge_kernel(stress, strain, yields, count, threshold, smooth, col_even, col_odd, norm,
                below, above, even_ref, odd_ref, low_block, high_block, rest):
    layers, rows, cols = stress.shape
    starts = (0, rows - 2 * REACH, rows - REACH)
    received = []
    for first_row in starts:
        part = pl.ds(first_row + REACH, REACH)
        received.append(sides("gy", col_even[part, :], col_odd[part, :]))

    def layer_step(layer):
        for index, first_row in enumerate(starts):
            at = (layer, pl.ds(first_row, REACH), slice(None))
            extended = pl.ds(first_row + REACH, REACH)
            full = add_columns(smooth[layer, extended, :], layer, *received[index])
            soften = 0.5 + 0.5 * retained(full, norm[extended, :], threshold[at])
            value = newton(stress[at], strain[at], yields[at], count[at], soften)
            if index == 0:
                low_block[pl.ds(layer * REACH, REACH), :] = value
            else:
                high_block[pl.ds((2 * layer + index - 1) * REACH, REACH), :] = value
            if index == 2:
                kept = (stress[at] + strain[at]) - value
                rest[pl.ds(layer, 1), :] = kept[REACH - 1 :]
                rest[pl.ds(layers + layer, 1), :] = threshold[at][REACH - 1 :]

    for layer in range(layers):
        layer_step(layer)
    low = left_product(left_constant(below[...]), low_block[...])
    high = left_product(left_constant(above[...]), high_block[...])
    extra = jnp.zeros((even_ref.shape[0] - low.shape[0], cols), jnp.float32)
    send(
        "gx", jnp.concatenate([low, extra], axis=0), jnp.concatenate([high, rest[...]], axis=0),
        even_ref, odd_ref,
    )


def main_kernel(turn, stress, strain, yields, count, threshold, smooth, col_even, col_odd, norm,
                norm_last, band_ref, low_ref, high_ref, next_ref,
                across, low_cols, high_cols, plastic,
                soften, pack_low, pack_high, pack_next, pack_last):
    layers, rows, cols = stress.shape
    step_rows = 2 * REACH
    steps = rows // step_rows

    @pl.when(turn[0] == 0)
    def _():
        soften[...] = jnp.ones_like(soften)

    @pl.when(turn[0] > 0)
    def _():
        def soften_step(index, carry):
            part = pl.ds(pl.multiple_of(index * step_rows, step_rows), step_rows)
            extended = pl.ds(pl.multiple_of(index * step_rows + REACH, REACH), step_rows)
            low, high = sides("gy", col_even[extended, :], col_odd[extended, :])
            for layer in range(layers):
                at = (layer, part, slice(None))
                full = add_columns(smooth[layer, extended, :], layer, low, high)
                soften[at] = 0.5 + 0.5 * retained(full, norm[extended, :], threshold[at])
            return carry

        lax.fori_loop(0, steps, soften_step, 0)

    def newton_step(index, carry):
        part = pl.ds(pl.multiple_of(index * step_rows, step_rows), step_rows)
        for layer in range(layers):
            at = (layer, part, slice(None))
            plastic[at] = newton(stress[at], strain[at], yields[at], count[at], soften[at])
        return carry

    lax.fori_loop(0, steps, newton_step, 0)

    constant = left_constant(band_ref[...])
    for layer in range(0, layers, 2):
        pair = jnp.concatenate([plastic[layer], plastic[layer + 1]], axis=1)
        result = left_product(constant, pair)
        across[layer] = result[:, :cols]
        across[layer + 1] = result[:, cols:]

    def pack(index, carry):
        part = pl.ds(pl.multiple_of(index * REACH, REACH), REACH)
        packs = pack_edges([across[layer, part, :] for layer in range(layers)])
        for ref, packed in zip((pack_low, pack_high, pack_next), packs):
            ref[part, :] = packed
        return carry

    lax.fori_loop(0, rows // REACH + 1, pack, 0)
    low_cols[...] = right_product(pack_low[...], right_constant(low_ref[...]))
    high = right_product(pack_high[...], right_constant(high_ref[...]))
    behind = right_product(pack_next[...], right_constant(next_ref[...]))
    high_cols[:, :cols] = high[:, :cols]

    @pl.when(turn[0] == OUTER - 1)
    def _():
        def last_column(index, carry):
            part = pl.ds(pl.multiple_of(index * step_rows, step_rows), step_rows)
            lanes = lane_ids((step_rows, cols))
            packed = jnp.zeros((step_rows, cols), jnp.float32)
            for layer in range(layers):
                at = (layer, part, slice(None))
                packed = jnp.where(lanes == layer, pltpu.roll(threshold[at], layer + 1, 1), packed)
                rest = (stress[at] + strain[at]) - plastic[at]
                turned = pltpu.roll(rest, layers + layer + 1, 1)
                packed = jnp.where(lanes == layers + layer, turned, packed)
            pack_last[pl.ds(pl.multiple_of(index * step_rows + REACH, REACH), step_rows), :] = packed
            return carry

        pack_last[pl.ds(0, REACH), :] = jnp.zeros((REACH, cols), jnp.float32)
        lax.fori_loop(0, steps, last_column, 0)
        lanes = lane_ids(pack_last.shape)
        drop = (high[:, cols:] + behind) * norm_last[...]
        high_cols[:, cols:] = pack_last[...] - jnp.where(lanes < layers, drop, 0.0)


def pack_edges(values):
    cols = values[0].shape[1]
    count = cols // REACH
    slots = lane_ids(values[0].shape) >> (REACH.bit_length() - 1)
    low = high = ahead = jnp.zeros_like(values[0])
    for layer, value in enumerate(values):
        moved = pltpu.roll(value, layer * REACH, 1) if layer else value
        low = jnp.where(slots == layer, moved, low)
        high = jnp.where(slots == (layer - 1) % count, moved, high)
        ahead = jnp.where(slots == (layer - 2) % count, moved, ahead)
    return low, high, ahead


def corner_kernel(row_even, row_odd, low_cols, high_cols, norm_last, low_ref, high_ref, next_ref,
                  even_ref, odd_ref, own_ref):
    cols = low_ref.shape[0]
    total = low_cols.shape[0]
    layers = (total - REACH) // REACH
    strip = layers * REACH
    from_low, from_high = sides("gx", row_even[...], row_odd[...])
    partial = from_low[strip : strip + layers]
    kept = from_low[strip + layers : strip + 2 * layers]
    limit = from_low[strip + 2 * layers : strip + 3 * layers]
    before = [jnp.broadcast_to(partial[layer : layer + 1], (REACH, cols)) for layer in range(layers)]
    packs = [pack_edges(before)] + [
        pack_edges([block[layer * REACH : (layer + 1) * REACH] for layer in range(layers)])
        for block in (from_low, from_high)
    ]
    low, high, ahead = (jnp.concatenate(group, axis=0) for group in zip(*packs))
    low_add = right_product(low, right_constant(low_ref[...]))
    high_add = right_product(high, right_constant(high_ref[...]))
    behind_add = right_product(ahead, right_constant(next_ref[...]))

    lanes = lane_ids((layers, cols))
    level = lax.broadcasted_iota(jnp.int32, (layers, cols), 0)
    corner_limit = jnp.where(lanes == level, limit[:, cols - 1 :], 0.0)
    corner_kept = jnp.where(lanes == layers + level, kept[:, cols - 1 :], 0.0)
    corner = jnp.sum(corner_limit + corner_kept, axis=0, keepdims=True)

    def place(base, add):
        return jnp.concatenate(
            [base[: 2 * REACH] + add[: 2 * REACH], base[2 * REACH : total - REACH],
             base[total - REACH :] + add[2 * REACH :]],
            axis=0,
        )

    low_all = place(low_cols[...], low_add)
    high_all = place(high_cols[:, :cols], high_add[:, :cols])
    last = norm_last[...]
    behind = high_add[:, cols:] + behind_add
    edges = jnp.concatenate([last[: 2 * REACH], last[total - REACH :]], axis=0)
    lanes = lane_ids(behind.shape)
    drop = jnp.where(lanes < layers, behind * edges, 0.0)
    column = place(high_cols[:, cols:], -drop)
    first = column[:REACH] + corner
    main = column[REACH:]
    quarter = strip // 4
    lanes = lane_ids((quarter, cols))
    folded = main[:quarter]
    for part in range(1, 4):
        moved = pltpu.roll(main[part * quarter : (part + 1) * quarter], part * 2 * layers, 1)
        folded = jnp.where(lanes // (2 * layers) == part, moved, folded)
    extra = jnp.zeros((quarter + REACH, cols), jnp.float32)
    send(
        "gy", jnp.concatenate([low_all[:, :cols], extra], axis=0),
        jnp.concatenate([high_all, folded, first], axis=0), even_ref, odd_ref,
    )
    own_ref[...] = low_all[:, cols:]


def column_kernel(depth, across, row_even, row_odd, band_ref, smooth, deep):
    layers, total, cols = across.shape
    strip = layers * REACH
    edges = (0, REACH, total - REACH)

    def depth_sums(part, values):
        for layer, value in enumerate(depth_smooth(values, depth)):
            deep[layer, part, :] = value

    def step(index, carry):
        for inner in range(2):
            part = pl.ds(pl.multiple_of((2 * index + inner + 2) * REACH, REACH), REACH)
            depth_sums(part, [across[layer, part, :] for layer in range(layers)])
        return carry

    lax.fori_loop(0, (total // REACH - 3) // 2, step, 0)
    for first_row in edges:
        part = pl.ds(first_row, REACH)
        values = []
        for layer in range(layers):
            line = pl.ds(strip + layer, 1) if first_row == 0 else pl.ds(layer * REACH, REACH)
            both = sides("gx", row_even[line, :], row_odd[line, :])
            values.append(across[layer, part, :] + both[first_row > REACH])
        depth_sums(part, values)
    constant = right_constant(band_ref[...])
    for layer in range(layers):
        smooth[layer] = right_product(deep[layer], constant)


def final_kernel(stress, strain, plastic, threshold, smooth, col_even, col_odd, row_even, row_odd,
                 norm, norm_before, own_cols, plastic_out, damage_out, force_out,
                 columns, damage_s, force_s, copy_sem, sems):
    layers, rows, cols = stress.shape
    total = rows + REACH
    strip = layers * REACH
    whole = pltpu.make_async_copy(plastic, plastic_out, copy_sem)
    whole.start()

    from_low, _ = sides("gy", col_even[...], col_odd[...])
    quarter = rows // 4
    folded = from_low[total : total + quarter]
    pieces = [from_low[total + quarter :], folded]
    for part in range(1, 4):
        pieces.append(pltpu.roll(folded, cols - part * 2 * layers, 1))
    column = jnp.concatenate(pieces, axis=0)
    limit = column - own_cols[...] * norm_before[...]
    kept = jnp.exp2(jnp.minimum(limit, 0.0) * RATE)
    columns[...] = kept * pltpu.roll(column, cols - layers, 1)

    def copies(layer):
        return (
            pltpu.make_async_copy(damage_s.at[layer], damage_out.at[layer], sems.at[0, layer]),
            pltpu.make_async_copy(force_s.at[0, layer], force_out.at[0, layer], sems.at[1, layer]),
            pltpu.make_async_copy(force_s.at[1, layer], force_out.at[1, layer], sems.at[2, layer]),
        )

    def layer_step(layer):
        lanes = lane_ids((REACH, cols))
        top = lax.broadcasted_iota(jnp.int32, (REACH, cols), 0) == 0
        above_sum = above_diff = None
        for block in range(rows // REACH + 1):
            extended = pl.ds(block * REACH, REACH)
            low, high = sides("gy", col_even[extended, :], col_odd[extended, :])
            full = add_columns(smooth[layer, extended, :], layer, low, high)
            if block == 0:
                line = pl.ds(strip + layers + layer, 1)
                rest, _ = sides("gx", row_even[line, :], row_odd[line, :])
                line = pl.ds(strip + 2 * layers + layer, 1)
                limit, _ = sides("gx", row_even[line, :], row_odd[line, :])
            else:
                at = (layer, pl.ds((block - 1) * REACH, REACH), slice(None))
                rest = (stress[at] + strain[at]) - plastic[at]
                limit = threshold[at]
            ratio = retained(full, norm[extended, :], limit)
            value = ratio * rest
            left = jnp.where(
                lanes == 0,
                pltpu.roll(columns[extended, :], (cols - layer) % cols, 1),
                pltpu.roll(value, 1, 1),
            )
            both = pltpu.roll(left + value, 1, 0)
            diff = pltpu.roll(left - value, 1, 0)
            if block:
                damage_s[at] = 1.0 - ratio
                force_s[(0, *at)] = 0.5 * (jnp.where(top, above_sum, both) - (left + value))
                force_s[(1, *at)] = 0.5 * (jnp.where(top, above_diff, diff) + (left - value))
            above_sum, above_diff = both, diff

    def step(index, carry):
        for inner in range(2):
            layer_step(2 * index + inner)
        for inner in range(2):
            for copy in copies(2 * index + inner):
                copy.start()
        return carry

    lax.fori_loop(0, layers // 2, step, 0)

    def drain(layer, carry):
        for copy in copies(layer):
            copy.wait()
        return carry

    lax.fori_loop(0, layers, drain, 0)
    whole.wait()


def call(kernel, outs, scratch, cost, operands, spaces=None, outs_space=pltpu.VMEM):
    spaces = spaces or [pltpu.VMEM] * len(operands)
    return pl.pallas_call(
        kernel,
        out_shape=[jax.ShapeDtypeStruct(shape, jnp.float32) for shape in outs],
        in_specs=[pl.BlockSpec(memory_space=space) for space in spaces],
        out_specs=[pl.BlockSpec(memory_space=outs_space)] * len(outs),
        scratch_shapes=[pltpu.VMEM(s, jnp.float32) if isinstance(s, tuple) else s for s in scratch],
        compiler_params=pltpu.CompilerParams(vmem_limit_bytes=VMEM_BYTES),
        cost_estimate=pl.CostEstimate(flops=cost, bytes_accessed=cost // 16, transcendentals=0),
    )(*operands)


def exchange(axis, even, odd):
    count = lax.axis_size(axis)
    results = []
    for start, value in ((1, odd), (0, even)):
        pairs = []
        for low in range(start, count - 1, 2):
            pairs += [(low, low + 1), (low + 1, low)]
        results.append(lax.ppermute(value, axis, pairs))
    return results[::-1]


def inverse_weights(axis, places, length):
    extent = length * lax.axis_size(axis)
    places = places + lax.axis_index(axis) * length
    total = jnp.zeros(places.shape, jnp.float32)
    for offset in range(-REACH, REACH + 1):
        inside = (places + offset >= 0) & (places + offset < extent)
        total = total + jnp.where(inside, tap(offset), 0.0)
    return 1.0 / jnp.maximum(total, tap(REACH))


def matrices(layers, rows, cols):
    depth = depth_matrix(layers)
    up, down = band(REACH, REACH, REACH), band(REACH, REACH, -REACH)
    same = np.eye(layers)
    below = np.kron(same, up)
    near = np.concatenate([np.zeros((REACH, REACH)), down], axis=1)
    line = band(1, 2 * REACH, 1 - 2 * REACH)
    above = np.concatenate([np.kron(same, near), np.kron(same, line)], axis=0)
    rows_band = np.concatenate([np.zeros((REACH - 1, rows)), band(1, rows, 1), band(rows, rows)])
    slots = cols // REACH
    low, high, ahead = np.zeros((cols, 2 * cols)), np.zeros((cols, 2 * cols)), np.zeros((cols, cols))
    for source in range(layers):
        own = slice(source * REACH, (source + 1) * REACH)
        first = (source - 1) % slots * REACH
        other = slice(first, first + REACH)
        for layer in range(layers):
            weight = depth[layer, source]
            first = (layer - 1) % slots * REACH
            low[own, first : first + REACH] = weight * up.T
            high[other, layer * REACH : (layer + 1) * REACH] = weight * down.T
            low[own, cols + layer] = [weight * tap(j + 1) for j in range(REACH)]
            high[other, cols + layer] = [weight * tap(REACH - 1 - j) for j in range(REACH)]
            ahead[((source - 2) % slots) * REACH + REACH - 1, layer] = weight * tap(REACH)
    constants = (below, above, np.kron(same, down), rows_band, band(cols, cols), low, high, ahead)
    return depth, [jnp.asarray(matrix, jnp.float32) for matrix in constants]


def local(trial_stress, old_strain, yield_mask, newton_count, damage_threshold):
    layers, rows, cols = trial_stress.shape
    assert layers * REACH == cols == rows and layers % 2 == 0
    total, strip = rows + REACH, layers * REACH
    depth, constants = matrices(layers, rows, cols)
    below, above, above_first, rows_band, cols_band, *columns = constants

    inputs = (trial_stress, old_strain, yield_mask, newton_count)
    whole, wide = (layers, rows, cols), (layers, total, cols)
    sent_rows = (strip + 3 * layers, cols)
    sent_cols = (total + rows // 4 + REACH, cols)
    packed, packed_two = (total, cols), (total, 2 * cols)
    work = layers * rows * cols

    for outer_no in range(OUTER):
        if outer_no == 0:
            edge = [pltpu.VMEM((2, layers, REACH, cols), kind) for kind in
                    (jnp.float32, jnp.float32, jnp.int32, jnp.int32)]
            row_even, row_odd, norm, norm_last, norm_before, smooth, col_even, col_odd = call(
                first_edge_kernel,
                [sent_rows, sent_rows, packed, packed, packed, wide, sent_cols, sent_cols],
                edge + [(strip, cols), pltpu.SemaphoreType.DMA((2, 4))], work * 16,
                (*inputs, below, above_first), [pltpu.HBM] * 4 + [pltpu.VMEM] * 2,
            )
        else:
            row_even, row_odd = call(
                edge_kernel, [sent_rows] * 2,
                [(strip, cols), (2 * strip, cols), (2 * layers, cols)], work * 16,
                (*inputs, damage_threshold, smooth, col_even, col_odd, norm, below, above),
            )
        row_even, row_odd = exchange("gx", row_even, row_odd)
        turn = jnp.full((1,), outer_no, jnp.int32)
        across, low_cols, high_cols, plastic = call(
            main_kernel, [wide, packed_two, packed_two, whole],
            [whole, packed, packed, packed, packed], work * 400,
            (turn, *inputs, damage_threshold, smooth, col_even, col_odd, norm, norm_last,
             rows_band, *columns),
            [pltpu.SMEM] + [pltpu.VMEM] * 14,
        )
        col_even, col_odd, own_cols = call(
            corner_kernel, [sent_cols, sent_cols, packed], [], work * 16,
            (row_even, row_odd, low_cols, high_cols, norm_last, *columns),
        )
        col_even, col_odd = exchange("gy", col_even, col_odd)
        (smooth,) = call(
            functools.partial(column_kernel, depth), [wide], [wide], work * 100,
            (across, row_even, row_odd, cols_band),
        )
    return tuple(call(
        final_kernel, [whole, whole, (2, *whole)],
        [packed, whole, (2, *whole), pltpu.SemaphoreType.DMA(()), pltpu.SemaphoreType.DMA((3, layers))],
        work * 100,
        (trial_stress, old_strain, plastic, damage_threshold, smooth, col_even, col_odd,
         row_even, row_odd, norm, norm_before, own_cols),
        outs_space=pltpu.HBM,
    ))


def solution(mesh):
    split_in = P(None, "gx", "gy")
    return jax.shard_map(
        local,
        mesh=mesh,
        in_specs=(split_in,) * 5,
        out_specs=(split_in, split_in, P(None, None, "gx", "gy")),
        check_vma=False,
    )
```

```python
import functools
import math

import jax
import jax.numpy as jnp
import numpy as np
from jax import lax
from jax.experimental import pallas as pl
from jax.experimental.pallas import tpu as pltpu
from jax.sharding import PartitionSpec as P

OUTER = 3
REACH = 8
RATE = math.log2(math.e) / 0.3
HALF_LN2 = 0.5 * math.log(2.0)
VMEM_BYTES = 24 * 1024 * 1024


def tap(offset):
    return math.exp(-(offset**2) / 32.0) if abs(offset) <= REACH else 0.0


def band(rows, cols, shift=0):
    return np.array([[tap(c - r + shift) for c in range(cols)] for r in range(rows)])


def depth_matrix(layers):
    weights = band(layers, layers)
    return weights / weights.sum(axis=1, keepdims=True)


def split(value):
    high = value.astype(jnp.bfloat16)
    low = (value - high.astype(jnp.float32)).astype(jnp.bfloat16)
    return high, low


def left_constant(matrix):
    high, low = split(matrix)
    return jnp.concatenate(
        [jnp.concatenate([high, high], axis=1), jnp.concatenate([low, low], axis=1)], axis=0
    )


def right_constant(matrix):
    both = jnp.concatenate(split(matrix), axis=1)
    return jnp.concatenate([both, both], axis=0)


def left_product(constant, value):
    rows = constant.shape[0] // 2
    halves = jnp.concatenate(split(value), axis=0)
    both = jnp.dot(constant, halves, preferred_element_type=jnp.float32)
    return both[:rows] + both[rows:]


def right_product(value, constant):
    cols = constant.shape[1] // 2
    halves = jnp.concatenate(split(value), axis=1)
    both = jnp.dot(halves, constant, preferred_element_type=jnp.float32)
    return both[:, :cols] + both[:, cols:]


def newton(stress, strain, yields, count, soften):
    start = 2.0 * stress - 3.5 * soften
    shift = start + (2.0 * strain - HALF_LN2)
    drop = 0.2 * soften
    state = start
    for sweep_no in range(1, 7):
        update = state * (0.8 - 0.2 * jnp.tanh(shift - state)) - drop
        state = update if sweep_no <= 3 else jnp.where(count >= sweep_no, update, state)
    moved = (strain + (stress - 1.75 * soften)) - 0.5 * state
    return jnp.where(yields > 0, moved, strain)


def depth_smooth(layers, matrix):
    count = len(layers)
    half = count // 2
    sums = [layers[k] + layers[count - 1 - k] for k in range(half)]
    diffs = [layers[k] - layers[count - 1 - k] for k in range(half)]
    out = [None] * count
    for row in range(half):
        even = odd = None
        for k in range(half):
            near, far = matrix[row, k], matrix[row, count - 1 - k]
            plus, minus = float(0.5 * (near + far)), float(0.5 * (near - far))
            if plus == 0.0 and minus == 0.0:
                continue
            even = sums[k] * plus if even is None else even + sums[k] * plus
            odd = diffs[k] * minus if odd is None else odd + diffs[k] * minus
        out[row] = even + odd
        out[count - 1 - row] = even - odd
    return out


def lane_ids(shape):
    return lax.broadcasted_iota(jnp.int32, shape, len(shape) - 1)


def on_even(axis):
    return lax.axis_index(axis) % 2 == 0


def sides(axis, even, odd):
    return jnp.where(on_even(axis), odd, even), jnp.where(on_even(axis), even, odd)


def send(axis, low, high, even_ref, odd_ref):
    even_ref[...] = jnp.where(on_even(axis), high, low)
    odd_ref[...] = jnp.where(on_even(axis), low, high)


def add_columns(value, layer, low, high):
    cols = value.shape[1]
    slots = lane_ids(value.shape) >> (REACH.bit_length() - 1)
    packed = jnp.where(slots == layer, low, high)
    shift = (cols - layer * REACH) % cols
    moved = packed if isinstance(layer, int) and layer == 0 else pltpu.roll(packed, shift, 1)
    return value + jnp.where((slots == 0) | (slots == cols // REACH - 1), moved, 0.0)


def retained(full, norm, threshold):
    return jnp.exp2(jnp.minimum(threshold - full * norm, 0.0) * RATE)


def first_edge_kernel(stress, strain, yields, count,
                      even_ref, odd_ref, norm, norm_last, norm_before, *refs):
    block = refs[-1]
    layers, cols = stress.shape[0], stress.shape[2]
    rows = norm.shape[0] - REACH
    total = rows + REACH
    ids = lax.broadcasted_iota(jnp.int32, (total, cols), 0)
    down = inverse_weights("gx", ids - REACH, rows)
    lanes = lane_ids((REACH, cols))
    for ref, place in ((norm, lanes), (norm_last, 0 * lanes + (cols - 1)), (norm_before, 0 * lanes - 1)):
        ref[...] = down * inverse_weights("gy", place, cols)[:1]
    square = (layers * REACH, layers * REACH)
    line, lane = lax.broadcasted_iota(jnp.int32, square, 0), lane_ids(square)
    steps = (lane & (REACH - 1)) - (line & (REACH - 1))
    band_part = jnp.zeros(square, jnp.float32)
    for step in range(REACH):
        band_part = jnp.where(abs(steps) == step, tap(REACH - step), band_part)
    band_part = jnp.where((line ^ lane) < REACH, band_part, 0.0)
    sent = []
    extra = jnp.zeros((even_ref.shape[0] - layers * REACH, cols), jnp.float32)
    for side, matrix in enumerate(
        (jnp.where(steps <= 0, band_part, 0.0), jnp.where(steps >= 0, band_part, 0.0))
    ):
        for layer in range(layers):
            at = (layer, pl.ds(side * REACH, REACH), slice(None))
            block[pl.ds(layer * REACH, REACH), :] = newton(
                stress[at], strain[at], yields[at], count[at], jnp.ones((REACH, cols), jnp.float32)
            )
        product = left_product(left_constant(matrix), block[...])
        sent.append(jnp.concatenate([product, extra], axis=0))
    send("gx", *sent, even_ref, odd_ref)


def edge_kernel(stress, strain, yields, count, threshold, smooth, col_even, col_odd, norm,
                below, above, even_ref, odd_ref, low_block, high_block, rest):
    layers, rows, cols = stress.shape
    starts = (0, rows - 2 * REACH, rows - REACH)
    received = []
    for first_row in starts:
        part = pl.ds(first_row + REACH, REACH)
        received.append(sides("gy", col_even[part, :], col_odd[part, :]))

    def layer_step(layer):
        for index, first_row in enumerate(starts):
            at = (layer, pl.ds(first_row, REACH), slice(None))
            extended = pl.ds(first_row + REACH, REACH)
            full = add_columns(smooth[layer, extended, :], layer, *received[index])
            soften = 0.5 + 0.5 * retained(full, norm[extended, :], threshold[at])
            value = newton(stress[at], strain[at], yields[at], count[at], soften)
            if index == 0:
                low_block[pl.ds(layer * REACH, REACH), :] = value
            else:
                high_block[pl.ds((2 * layer + index - 1) * REACH, REACH), :] = value
            if index == 2:
                kept = (stress[at] + strain[at]) - value
                rest[pl.ds(layer, 1), :] = kept[REACH - 1 :]
                rest[pl.ds(layers + layer, 1), :] = threshold[at][REACH - 1 :]

    for layer in range(layers):
        layer_step(layer)
    low = left_product(left_constant(below[...]), low_block[...])
    high = left_product(left_constant(above[...]), high_block[...])
    extra = jnp.zeros((even_ref.shape[0] - low.shape[0], cols), jnp.float32)
    send(
        "gx", jnp.concatenate([low, extra], axis=0), jnp.concatenate([high, rest[...]], axis=0),
        even_ref, odd_ref,
    )


def newton_kernel(turn, stress, strain, yields, count, threshold, smooth, col_even, col_odd, norm,
                  waiting, plastic, ready):
    layers, rows, cols = stress.shape
    step_rows = 2 * REACH
    steps = rows // step_rows
    ready[...] = waiting[...]

    @pl.when(turn[0] == 0)
    def _():
        def step(index, carry):
            part = pl.ds(pl.multiple_of(index * step_rows, step_rows), step_rows)
            soften = jnp.ones((step_rows, cols), jnp.float32)
            for layer in range(layers):
                at = (layer, part, slice(None))
                plastic[at] = newton(stress[at], strain[at], yields[at], count[at], soften)
            return carry

        lax.fori_loop(0, steps, step, 0)

    @pl.when(turn[0] > 0)
    def _():
        def step(index, carry):
            part = pl.ds(pl.multiple_of(index * step_rows, step_rows), step_rows)
            extended = pl.ds(pl.multiple_of(index * step_rows + REACH, REACH), step_rows)
            low, high = sides("gy", col_even[extended, :], col_odd[extended, :])
            for layer in range(layers):
                at = (layer, part, slice(None))
                full = add_columns(smooth[layer, extended, :], layer, low, high)
                soften = 0.5 + 0.5 * retained(full, norm[extended, :], threshold[at])
                plastic[at] = newton(stress[at], strain[at], yields[at], count[at], soften)
            return carry

        lax.fori_loop(0, steps, step, 0)


def across_kernel(turn, stress, strain, threshold, plastic, norm_last, band_ref, low_ref, high_ref,
                  next_ref, _, across, low_cols, high_cols, pack_low, pack_high, pack_next, pack_last):
    layers, rows, cols = stress.shape
    total = rows + REACH
    step_rows = 2 * REACH
    constant = left_constant(band_ref[...])
    slots = lane_ids((total, cols)) >> (REACH.bit_length() - 1)
    for layer in range(0, layers, 2):
        pair = jnp.concatenate([plastic[layer], plastic[layer + 1]], axis=1)
        result = left_product(constant, pair)
        for inner in range(2):
            value = result[:, inner * cols : (inner + 1) * cols]
            across[layer + inner] = value
            moved = pltpu.roll(value, (layer + inner) * REACH, 1) if layer + inner else value
            for behind, ref in enumerate((pack_low, pack_high, pack_next)):
                mask = slots == (layer + inner - behind) % (cols // REACH)
                pltpu.store(ref, moved, mask=mask)

    low_cols[...] = right_product(pack_low[...], right_constant(low_ref[...]))
    high = right_product(pack_high[...], right_constant(high_ref[...]))
    behind = right_product(pack_next[...], right_constant(next_ref[...]))
    high_cols[:, :cols] = high[:, :cols]

    @pl.when(turn[0] == OUTER - 1)
    def _():
        def last_column(index, carry):
            part = pl.ds(pl.multiple_of(index * step_rows, step_rows), step_rows)
            lanes = lane_ids((step_rows, cols))
            packed = jnp.zeros((step_rows, cols), jnp.float32)
            for layer in range(layers):
                at = (layer, part, slice(None))
                packed = jnp.where(lanes == layer, pltpu.roll(threshold[at], layer + 1, 1), packed)
                rest = (stress[at] + strain[at]) - plastic[at]
                turned = pltpu.roll(rest, layers + layer + 1, 1)
                packed = jnp.where(lanes == layers + layer, turned, packed)
            pack_last[pl.ds(pl.multiple_of(index * step_rows + REACH, REACH), step_rows), :] = packed
            return carry

        pack_last[pl.ds(0, REACH), :] = jnp.zeros((REACH, cols), jnp.float32)
        lax.fori_loop(0, rows // step_rows, last_column, 0)
        lanes = lane_ids(pack_last.shape)
        drop = (high[:, cols:] + behind) * norm_last[...]
        high_cols[:, cols:] = pack_last[...] - jnp.where(lanes < layers, drop, 0.0)


def pack_edges(values):
    cols = values[0].shape[1]
    count = cols // REACH
    slots = lane_ids(values[0].shape) >> (REACH.bit_length() - 1)
    low = high = ahead = jnp.zeros_like(values[0])
    for layer, value in enumerate(values):
        moved = pltpu.roll(value, layer * REACH, 1) if layer else value
        low = jnp.where(slots == layer, moved, low)
        high = jnp.where(slots == (layer - 1) % count, moved, high)
        ahead = jnp.where(slots == (layer - 2) % count, moved, ahead)
    return low, high, ahead


def corner_kernel(row_even, row_odd, low_cols, high_cols, norm_last, low_ref, high_ref, next_ref,
                  even_ref, odd_ref, own_ref):
    cols = low_ref.shape[0]
    total = low_cols.shape[0]
    layers = (total - REACH) // REACH
    strip = layers * REACH
    from_low, from_high = sides("gx", row_even[...], row_odd[...])
    partial = from_low[strip : strip + layers]
    kept = from_low[strip + layers : strip + 2 * layers]
    limit = from_low[strip + 2 * layers : strip + 3 * layers]
    before = [jnp.broadcast_to(partial[layer : layer + 1], (REACH, cols)) for layer in range(layers)]
    packs = [pack_edges(before)] + [
        pack_edges([block[layer * REACH : (layer + 1) * REACH] for layer in range(layers)])
        for block in (from_low, from_high)
    ]
    low, high, ahead = (jnp.concatenate(group, axis=0) for group in zip(*packs))
    low_add = right_product(low, right_constant(low_ref[...]))
    high_add = right_product(high, right_constant(high_ref[...]))
    behind_add = right_product(ahead, right_constant(next_ref[...]))

    lanes = lane_ids((layers, cols))
    level = lax.broadcasted_iota(jnp.int32, (layers, cols), 0)
    corner_limit = jnp.where(lanes == level, limit[:, cols - 1 :], 0.0)
    corner_kept = jnp.where(lanes == layers + level, kept[:, cols - 1 :], 0.0)
    corner = jnp.sum(corner_limit + corner_kept, axis=0, keepdims=True)

    def place(base, add):
        return jnp.concatenate(
            [base[: 2 * REACH] + add[: 2 * REACH], base[2 * REACH : total - REACH],
             base[total - REACH :] + add[2 * REACH :]],
            axis=0,
        )

    low_all = place(low_cols[...], low_add)
    high_all = place(high_cols[:, :cols], high_add[:, :cols])
    last = norm_last[...]
    behind = high_add[:, cols:] + behind_add
    edges = jnp.concatenate([last[: 2 * REACH], last[total - REACH :]], axis=0)
    lanes = lane_ids(behind.shape)
    drop = jnp.where(lanes < layers, behind * edges, 0.0)
    column = place(high_cols[:, cols:], -drop)
    first = column[:REACH] + corner
    main = column[REACH:]
    quarter = strip // 4
    lanes = lane_ids((quarter, cols))
    folded = main[:quarter]
    for part in range(1, 4):
        moved = pltpu.roll(main[part * quarter : (part + 1) * quarter], part * 2 * layers, 1)
        folded = jnp.where(lanes // (2 * layers) == part, moved, folded)
    extra = jnp.zeros((quarter + REACH, cols), jnp.float32)
    send(
        "gy", jnp.concatenate([low_all[:, :cols], extra], axis=0),
        jnp.concatenate([high_all, folded, first], axis=0), even_ref, odd_ref,
    )
    own_ref[...] = low_all[:, cols:]


def depth_kernel(depth, across, row_even, row_odd, waiting, _, deep, ready):
    layers, total, cols = across.shape
    strip = layers * REACH
    ready[...] = waiting[...]

    def depth_sums(part, values):
        for layer, value in enumerate(depth_smooth(values, depth)):
            deep[layer, part, :] = value

    def step(index, carry):
        for inner in range(2):
            part = pl.ds(pl.multiple_of((2 * index + inner + 2) * REACH, REACH), REACH)
            depth_sums(part, [across[layer, part, :] for layer in range(layers)])
        return carry

    lax.fori_loop(0, (total // REACH - 3) // 2, step, 0)
    for first_row in (0, REACH, total - REACH):
        part = pl.ds(first_row, REACH)
        values = []
        for layer in range(layers):
            line = pl.ds(strip + layer, 1) if first_row == 0 else pl.ds(layer * REACH, REACH)
            both = sides("gx", row_even[line, :], row_odd[line, :])
            values.append(across[layer, part, :] + both[first_row > REACH])
        depth_sums(part, values)


def column_kernel(deep, band_ref, _, smooth):
    constant = right_constant(band_ref[...])
    for layer in range(deep.shape[0]):
        smooth[layer] = right_product(deep[layer], constant)


def final_kernel(stress, strain, plastic, threshold, smooth, col_even, col_odd, row_even, row_odd,
                 norm, norm_before, own_cols, plastic_out, damage_out, force_out,
                 columns, damage_s, force_s, copy_sem, sems):
    layers, rows, cols = stress.shape
    total = rows + REACH
    strip = layers * REACH
    whole = pltpu.make_async_copy(plastic, plastic_out, copy_sem)
    whole.start()

    from_low, _ = sides("gy", col_even[...], col_odd[...])
    quarter = rows // 4
    folded = from_low[total : total + quarter]
    pieces = [from_low[total + quarter :], folded]
    for part in range(1, 4):
        pieces.append(pltpu.roll(folded, cols - part * 2 * layers, 1))
    column = jnp.concatenate(pieces, axis=0)
    limit = column - own_cols[...] * norm_before[...]
    kept = jnp.exp2(jnp.minimum(limit, 0.0) * RATE)
    columns[...] = kept * pltpu.roll(column, cols - layers, 1)

    def copies(layer):
        return (
            pltpu.make_async_copy(damage_s.at[layer], damage_out.at[layer], sems.at[0, layer]),
            pltpu.make_async_copy(force_s.at[0, layer], force_out.at[0, layer], sems.at[1, layer]),
            pltpu.make_async_copy(force_s.at[1, layer], force_out.at[1, layer], sems.at[2, layer]),
        )

    def layer_step(layer):
        lanes = lane_ids((REACH, cols))
        top = lax.broadcasted_iota(jnp.int32, (REACH, cols), 0) == 0
        above_sum = above_diff = None
        for block in range(rows // REACH + 1):
            extended = pl.ds(block * REACH, REACH)
            low, high = sides("gy", col_even[extended, :], col_odd[extended, :])
            full = add_columns(smooth[layer, extended, :], layer, low, high)
            if block == 0:
                line = pl.ds(strip + layers + layer, 1)
                rest, _ = sides("gx", row_even[line, :], row_odd[line, :])
                line = pl.ds(strip + 2 * layers + layer, 1)
                limit, _ = sides("gx", row_even[line, :], row_odd[line, :])
            else:
                at = (layer, pl.ds((block - 1) * REACH, REACH), slice(None))
                rest = (stress[at] + strain[at]) - plastic[at]
                limit = threshold[at]
            ratio = retained(full, norm[extended, :], limit)
            value = ratio * rest
            left = jnp.where(
                lanes == 0,
                pltpu.roll(columns[extended, :], (cols - layer) % cols, 1),
                pltpu.roll(value, 1, 1),
            )
            both = pltpu.roll(left + value, 1, 0)
            diff = pltpu.roll(left - value, 1, 0)
            if block:
                damage_s[at] = 1.0 - ratio
                force_s[(0, *at)] = 0.5 * (jnp.where(top, above_sum, both) - (left + value))
                force_s[(1, *at)] = 0.5 * (jnp.where(top, above_diff, diff) + (left - value))
            above_sum, above_diff = both, diff

    def step(index, carry):
        for inner in range(2):
            layer_step(2 * index + inner)
        for inner in range(2):
            for copy in copies(2 * index + inner):
                copy.start()
        return carry

    lax.fori_loop(0, layers // 2, step, 0)

    def drain(layer, carry):
        for copy in copies(layer):
            copy.wait()
        return carry

    lax.fori_loop(0, layers, drain, 0)
    whole.wait()


def call(kernel, outs, scratch, nanoseconds, operands, spaces=None, outs_space=pltpu.VMEM):
    spaces = spaces or [pltpu.VMEM] * len(operands)
    shapes = [out if isinstance(out, jax.ShapeDtypeStruct) else jax.ShapeDtypeStruct(out, jnp.float32)
              for out in outs]
    return pl.pallas_call(
        kernel,
        out_shape=shapes,
        in_specs=[pl.BlockSpec(memory_space=space) for space in spaces],
        out_specs=[pl.BlockSpec(memory_space=outs_space)] * len(outs),
        scratch_shapes=[pltpu.VMEM(s, jnp.float32) if isinstance(s, tuple) else s for s in scratch],
        compiler_params=pltpu.CompilerParams(vmem_limit_bytes=VMEM_BYTES),
        cost_estimate=pl.CostEstimate(
            flops=nanoseconds * 1_000_000, bytes_accessed=nanoseconds * 1000, transcendentals=0
        ),
    )(*operands)


def exchange(axis, start, value):
    count = lax.axis_size(axis)
    pairs = []
    for low in range(start, count - 1, 2):
        pairs += [(low, low + 1), (low + 1, low)]
    return lax.ppermute(value, axis, pairs)


def inverse_weights(axis, places, length):
    extent = length * lax.axis_size(axis)
    places = places + lax.axis_index(axis) * length
    total = jnp.zeros(places.shape, jnp.float32)
    for offset in range(-REACH, REACH + 1):
        inside = (places + offset >= 0) & (places + offset < extent)
        total = total + jnp.where(inside, tap(offset), 0.0)
    return 1.0 / jnp.maximum(total, tap(REACH))


def matrices(layers, rows, cols):
    depth = depth_matrix(layers)
    up, down = band(REACH, REACH, REACH), band(REACH, REACH, -REACH)
    same = np.eye(layers)
    below = np.kron(same, up)
    near = np.concatenate([np.zeros((REACH, REACH)), down], axis=1)
    line = band(1, 2 * REACH, 1 - 2 * REACH)
    above = np.concatenate([np.kron(same, near), np.kron(same, line)], axis=0)
    rows_band = np.concatenate([np.zeros((REACH - 1, rows)), band(1, rows, 1), band(rows, rows)])
    slots = cols // REACH
    low, high, ahead = np.zeros((cols, 2 * cols)), np.zeros((cols, 2 * cols)), np.zeros((cols, cols))
    for source in range(layers):
        own = slice(source * REACH, (source + 1) * REACH)
        first = (source - 1) % slots * REACH
        other = slice(first, first + REACH)
        for layer in range(layers):
            weight = depth[layer, source]
            first = (layer - 1) % slots * REACH
            low[own, first : first + REACH] = weight * up.T
            high[other, layer * REACH : (layer + 1) * REACH] = weight * down.T
            low[own, cols + layer] = [weight * tap(j + 1) for j in range(REACH)]
            high[other, cols + layer] = [weight * tap(REACH - 1 - j) for j in range(REACH)]
            ahead[((source - 2) % slots) * REACH + REACH - 1, layer] = weight * tap(REACH)
    constants = (below, above, rows_band, band(cols, cols), low, high, ahead)
    return depth, [jnp.asarray(matrix, jnp.float32) for matrix in constants]


def local(trial_stress, old_strain, yield_mask, newton_count, damage_threshold):
    layers, rows, cols = trial_stress.shape
    assert layers * REACH == cols == rows and layers % 2 == 0
    total, strip = rows + REACH, layers * REACH
    depth, constants = matrices(layers, rows, cols)
    below, above, rows_band, cols_band, *columns = constants

    whole, wide = (layers, rows, cols), (layers, total, cols)
    sent_rows = (strip + 3 * layers, cols)
    sent_cols = (total + rows // 4 + REACH, cols)
    packed, packed_two = (total, cols), (total, 2 * cols)

    inputs = (trial_stress, old_strain, yield_mask, newton_count, damage_threshold)
    stress, strain, _, _, threshold = inputs
    edges = [jnp.concatenate([value[:, :REACH], value[:, rows - REACH :]], axis=1) for value in inputs[:4]]
    row_even, row_odd, norm, norm_last, norm_before, smooth, col_even, col_odd = call(
        first_edge_kernel,
        [sent_rows, sent_rows, packed, packed, packed, wide, sent_cols, sent_cols],
        [(strip, cols)], 6000, edges,
    )
    for outer_no in range(OUTER):
        if outer_no:
            row_even, row_odd = call(
                edge_kernel, [sent_rows] * 2,
                [(strip, cols), (2 * strip, cols), (2 * layers, cols)], 800,
                (*inputs, smooth, col_even, col_odd, norm, below, above),
            )
        turn = jnp.full((1,), outer_no, jnp.int32)
        row_even = exchange("gx", 0, row_even)
        plastic, row_odd = call(
            newton_kernel, [whole, sent_rows], [], 3000,
            (turn, *inputs, smooth, col_even, col_odd, norm, row_odd),
            [pltpu.SMEM] + [pltpu.VMEM] * 10,
        )
        row_odd = exchange("gx", 1, row_odd)
        across, low_cols, high_cols = call(
            across_kernel, [wide, packed_two, packed_two],
            [packed, packed, packed, packed], 2000,
            (turn, stress, strain, threshold, plastic, norm_last, rows_band, *columns, row_even),
            [pltpu.SMEM] + [pltpu.VMEM] * 10,
        )
        col_even, col_odd, own_cols = call(
            corner_kernel, [sent_cols, sent_cols, packed], [], 400,
            (row_even, row_odd, low_cols, high_cols, norm_last, *columns),
        )
        col_even = exchange("gy", 0, col_even)
        deep, col_odd = call(
            functools.partial(depth_kernel, depth), [wide, sent_cols], [], 700,
            (across, row_even, row_odd, col_odd, own_cols),
        )
        col_odd = exchange("gy", 1, col_odd)
        (smooth,) = call(column_kernel, [wide], [], 500, (deep, cols_band, col_even))
    return tuple(call(
        final_kernel, [whole, whole, (2, *whole)],
        [packed, whole, (2, *whole), pltpu.SemaphoreType.DMA(()), pltpu.SemaphoreType.DMA((3, layers))],
        3000,
        (stress, strain, plastic, threshold, smooth, col_even, col_odd,
         row_even, row_odd, norm, norm_before, own_cols),
        outs_space=pltpu.HBM,
    ))


def solution(mesh):
    split_in = P(None, "gx", "gy")
    return jax.shard_map(
        local,
        mesh=mesh,
        in_specs=(split_in,) * 5,
        out_specs=(split_in, split_in, P(None, None, "gx", "gy")),
        check_vma=False,
    )
```

```python
import functools
import math

import jax
import jax.numpy as jnp
import numpy as np
from jax import lax
from jax.experimental import pallas as pl
from jax.experimental.pallas import tpu as pltpu
from jax.sharding import PartitionSpec as P

OUTER = 3
REACH = 8
RATE = math.log2(math.e) / 0.3
HALF_LN2 = 0.5 * math.log(2.0)
VMEM_BYTES = 24 * 1024 * 1024
FIRST_VMEM_BYTES = 48 * 1024 * 1024


def tap(offset):
    return math.exp(-(offset**2) / 32.0) if abs(offset) <= REACH else 0.0


def band(rows, cols, shift=0):
    return np.array([[tap(c - r + shift) for c in range(cols)] for r in range(rows)])


def depth_matrix(layers):
    weights = band(layers, layers)
    return weights / weights.sum(axis=1, keepdims=True)


def split(value):
    high = value.astype(jnp.bfloat16)
    low = (value - high.astype(jnp.float32)).astype(jnp.bfloat16)
    return high, low


def left_constant(matrix):
    high, low = split(matrix)
    return jnp.concatenate(
        [jnp.concatenate([high, high], axis=1), jnp.concatenate([low, low], axis=1)], axis=0
    )


def right_constant(matrix):
    both = jnp.concatenate(split(matrix), axis=1)
    return jnp.concatenate([both, both], axis=0)


def left_product(constant, value):
    rows = constant.shape[0] // 2
    halves = jnp.concatenate(split(value), axis=0)
    both = jnp.dot(constant, halves, preferred_element_type=jnp.float32)
    return both[:rows] + both[rows:]


def right_product(value, constant):
    cols = constant.shape[1] // 2
    halves = jnp.concatenate(split(value), axis=1)
    both = jnp.dot(halves, constant, preferred_element_type=jnp.float32)
    return both[:, :cols] + both[:, cols:]


def newton(stress, strain, yields, count, soften):
    start = 2.0 * stress - 3.5 * soften
    shift = start + (2.0 * strain - HALF_LN2)
    drop = 0.2 * soften
    state = start
    for sweep_no in range(1, 7):
        update = state * (0.8 - 0.2 * jnp.tanh(shift - state)) - drop
        state = update if sweep_no <= 3 else jnp.where(count >= sweep_no, update, state)
    moved = (strain + (stress - 1.75 * soften)) - 0.5 * state
    return jnp.where(yields > 0, moved, strain)


def depth_smooth(layers, matrix):
    count = len(layers)
    half = count // 2
    sums = [layers[k] + layers[count - 1 - k] for k in range(half)]
    diffs = [layers[k] - layers[count - 1 - k] for k in range(half)]
    out = [None] * count
    for row in range(half):
        even = odd = None
        for k in range(half):
            near, far = matrix[row, k], matrix[row, count - 1 - k]
            plus, minus = float(0.5 * (near + far)), float(0.5 * (near - far))
            if plus == 0.0 and minus == 0.0:
                continue
            even = sums[k] * plus if even is None else even + sums[k] * plus
            odd = diffs[k] * minus if odd is None else odd + diffs[k] * minus
        out[row] = even + odd
        out[count - 1 - row] = even - odd
    return out


def lane_ids(shape):
    return lax.broadcasted_iota(jnp.int32, shape, len(shape) - 1)


def on_even(axis):
    return lax.axis_index(axis) % 2 == 0


def sides(axis, even, odd):
    return jnp.where(on_even(axis), odd, even), jnp.where(on_even(axis), even, odd)


def send(axis, low, high, even_ref, odd_ref):
    place = lax.axis_index(axis)
    low = jnp.where(place == 0, 0.0, low)
    high = jnp.where(place == lax.axis_size(axis) - 1, 0.0, high)
    even_ref[...] = jnp.where(on_even(axis), high, low)
    odd_ref[...] = jnp.where(on_even(axis), low, high)


def add_columns(value, layer, low, high):
    cols = value.shape[1]
    slots = lane_ids(value.shape) >> (REACH.bit_length() - 1)
    packed = jnp.where(slots == layer, low, high)
    shift = (cols - layer * REACH) % cols
    moved = packed if isinstance(layer, int) and layer == 0 else pltpu.roll(packed, shift, 1)
    return value + jnp.where((slots == 0) | (slots == cols // REACH - 1), moved, 0.0)


def retained(full, norm, threshold):
    return jnp.exp2(jnp.minimum(threshold - full * norm, 0.0) * RATE)


def first_edge_kernel(*refs):
    sources, refs = refs[:5], refs[5:]
    even_ref, odd_ref, norm, norm_last, norm_before, _, _, *refs = refs
    targets, (block, sems) = refs[:5], refs[5:]
    stress, strain, yields, count, _ = targets
    layers, rows, cols = stress.shape
    parts = (pl.ds(0, REACH), pl.ds(rows - REACH, REACH), pl.ds(REACH, rows - 2 * REACH))
    copies = []
    for side, part in enumerate(parts):
        for index, (source, target) in enumerate(zip(sources, targets)):
            copies.append(
                pltpu.make_async_copy(
                    source.at[:, part, :], target.at[:, part, :], sems.at[side, index]
                )
            )
            copies[-1].start()
    total = rows + REACH
    ids = lax.broadcasted_iota(jnp.int32, (total, cols), 0)
    down = inverse_weights("gx", ids - REACH, rows)
    lanes = lane_ids((REACH, cols))
    for ref, place in ((norm, lanes), (norm_last, 0 * lanes + (cols - 1)), (norm_before, 0 * lanes - 1)):
        ref[...] = down * inverse_weights("gy", place, cols)[:1]
    square = (layers * REACH, layers * REACH)
    line, lane = lax.broadcasted_iota(jnp.int32, square, 0), lane_ids(square)
    steps = (lane & (REACH - 1)) - (line & (REACH - 1))
    band_part = jnp.zeros(square, jnp.float32)
    for step in range(REACH):
        band_part = jnp.where(abs(steps) == step, tap(REACH - step), band_part)
    band_part = jnp.where((line ^ lane) < REACH, band_part, 0.0)
    sent = []
    extra = jnp.zeros((even_ref.shape[0] - layers * REACH, cols), jnp.float32)
    for side, matrix in enumerate(
        (jnp.where(steps <= 0, band_part, 0.0), jnp.where(steps >= 0, band_part, 0.0))
    ):
        for copy in copies[side * 5 : side * 5 + 5]:
            copy.wait()
        for layer in range(layers):
            at = (layer, parts[side], slice(None))
            block[pl.ds(layer * REACH, REACH), :] = newton(
                stress[at], strain[at], yields[at], count[at], jnp.ones((REACH, cols), jnp.float32)
            )
        product = left_product(left_constant(matrix), block[...])
        sent.append(jnp.concatenate([product, extra], axis=0))
    send("gx", *sent, even_ref, odd_ref)
    for copy in copies[10:]:
        copy.wait()


def edge_kernel(stress, strain, yields, count, threshold, smooth, _, col_even, col_odd, norm,
                below, above, even_ref, odd_ref, low_block, high_block, rest):
    layers, rows, cols = stress.shape
    starts = (0, rows - 2 * REACH, rows - REACH)
    received = []
    for first_row in starts:
        part = pl.ds(first_row + REACH, REACH)
        received.append(sides("gy", col_even[part, :], col_odd[part, :]))

    def layer_step(layer):
        for index, first_row in enumerate(starts):
            at = (layer, pl.ds(first_row, REACH), slice(None))
            extended = pl.ds(first_row + REACH, REACH)
            full = add_columns(smooth[at], layer, *received[index])
            soften = 0.5 + 0.5 * retained(full, norm[extended, :], threshold[at])
            value = newton(stress[at], strain[at], yields[at], count[at], soften)
            if index == 0:
                low_block[pl.ds(layer * REACH, REACH), :] = value
            else:
                high_block[pl.ds((2 * layer + index - 1) * REACH, REACH), :] = value
            if index == 2:
                kept = (stress[at] + strain[at]) - value
                rest[pl.ds(layer, 1), :] = kept[REACH - 1 :]
                rest[pl.ds(layers + layer, 1), :] = threshold[at][REACH - 1 :]

    for layer in range(layers):
        layer_step(layer)
    low = left_product(left_constant(below[...]), low_block[...])
    high = left_product(left_constant(above[...]), high_block[...])
    extra = jnp.zeros((even_ref.shape[0] - low.shape[0], cols), jnp.float32)
    send(
        "gx", jnp.concatenate([low, extra], axis=0), jnp.concatenate([high, rest[...]], axis=0),
        even_ref, odd_ref,
    )


def main_kernel(turn, stress, strain, yields, count, threshold, smooth, col_even, col_odd, norm,
                norm_last, band_ref, low_ref, high_ref, next_ref,
                across, low_cols, high_cols, plastic, pack_low, pack_high, pack_next, pack_last):
    layers, rows, cols = stress.shape
    total = rows + REACH
    step_rows = 2 * REACH
    steps = rows // step_rows

    @pl.when(turn[0] == 0)
    def _():
        def step(index, carry):
            part = pl.ds(pl.multiple_of(index * step_rows, step_rows), step_rows)
            soften = jnp.ones((step_rows, cols), jnp.float32)
            for layer in range(layers):
                at = (layer, part, slice(None))
                plastic[at] = newton(stress[at], strain[at], yields[at], count[at], soften)
            return carry

        lax.fori_loop(0, steps, step, 0)

    @pl.when(turn[0] > 0)
    def _():
        def step(index, carry):
            part = pl.ds(pl.multiple_of(index * step_rows, step_rows), step_rows)
            extended = pl.ds(pl.multiple_of(index * step_rows + REACH, REACH), step_rows)
            low, high = sides("gy", col_even[extended, :], col_odd[extended, :])
            for layer in range(layers):
                at = (layer, part, slice(None))
                full = add_columns(smooth[at], layer, low, high)
                soften = 0.5 + 0.5 * retained(full, norm[extended, :], threshold[at])
                plastic[at] = newton(stress[at], strain[at], yields[at], count[at], soften)
            return carry

        lax.fori_loop(0, steps, step, 0)

    constant = left_constant(band_ref[...])
    slots = lane_ids((total, cols)) >> (REACH.bit_length() - 1)
    for layer in range(0, layers, 2):
        pair = jnp.concatenate([plastic[layer], plastic[layer + 1]], axis=1)
        result = left_product(constant, pair)
        for inner in range(2):
            value = result[:, inner * cols : (inner + 1) * cols]
            across[layer + inner] = value
            moved = pltpu.roll(value, (layer + inner) * REACH, 1) if layer + inner else value
            for behind, ref in enumerate((pack_low, pack_high, pack_next)):
                mask = slots == (layer + inner - behind) % (cols // REACH)
                pltpu.store(ref, moved, mask=mask)

    low_cols[...] = right_product(pack_low[...], right_constant(low_ref[...]))
    high = right_product(pack_high[...], right_constant(high_ref[...]))
    behind = right_product(pack_next[...], right_constant(next_ref[...]))
    high_cols[:, :cols] = high[:, :cols]

    @pl.when(turn[0] == OUTER - 1)
    def _():
        def last_column(index, carry):
            part = pl.ds(pl.multiple_of(index * step_rows, step_rows), step_rows)
            lanes = lane_ids((step_rows, cols))
            packed = jnp.zeros((step_rows, cols), jnp.float32)
            for layer in range(layers):
                at = (layer, part, slice(None))
                packed = jnp.where(lanes == layer, pltpu.roll(threshold[at], layer + 1, 1), packed)
                rest = (stress[at] + strain[at]) - plastic[at]
                turned = pltpu.roll(rest, layers + layer + 1, 1)
                packed = jnp.where(lanes == layers + layer, turned, packed)
            pack_last[pl.ds(pl.multiple_of(index * step_rows + REACH, REACH), step_rows), :] = packed
            return carry

        pack_last[pl.ds(0, REACH), :] = jnp.zeros((REACH, cols), jnp.float32)
        lax.fori_loop(0, steps, last_column, 0)
        lanes = lane_ids(pack_last.shape)
        drop = (high[:, cols:] + behind) * norm_last[...]
        high_cols[:, cols:] = pack_last[...] - jnp.where(lanes < layers, drop, 0.0)


def pack_edges(values):
    cols = values[0].shape[1]
    count = cols // REACH
    slots = lane_ids(values[0].shape) >> (REACH.bit_length() - 1)
    low = high = ahead = jnp.zeros_like(values[0])
    for layer, value in enumerate(values):
        moved = pltpu.roll(value, layer * REACH, 1) if layer else value
        low = jnp.where(slots == layer, moved, low)
        high = jnp.where(slots == (layer - 1) % count, moved, high)
        ahead = jnp.where(slots == (layer - 2) % count, moved, ahead)
    return low, high, ahead


def corner_kernel(row_even, row_odd, low_cols, high_cols, norm_last, _, low_ref, high_ref, next_ref,
                  even_ref, odd_ref, own_ref):
    cols = low_ref.shape[0]
    total = low_cols.shape[0]
    layers = (total - REACH) // REACH
    strip = layers * REACH
    from_low, from_high = sides("gx", row_even[...], row_odd[...])
    partial = from_low[strip : strip + layers]
    kept = from_low[strip + layers : strip + 2 * layers]
    limit = from_low[strip + 2 * layers : strip + 3 * layers]
    before = [jnp.broadcast_to(partial[layer : layer + 1], (REACH, cols)) for layer in range(layers)]
    packs = [pack_edges(before)] + [
        pack_edges([block[layer * REACH : (layer + 1) * REACH] for layer in range(layers)])
        for block in (from_low, from_high)
    ]
    low, high, ahead = (jnp.concatenate(group, axis=0) for group in zip(*packs))
    low_add = right_product(low, right_constant(low_ref[...]))
    high_add = right_product(high, right_constant(high_ref[...]))
    behind_add = right_product(ahead, right_constant(next_ref[...]))

    lanes = lane_ids((layers, cols))
    level = lax.broadcasted_iota(jnp.int32, (layers, cols), 0)
    corner_limit = jnp.where(lanes == level, limit[:, cols - 1 :], 0.0)
    corner_kept = jnp.where(lanes == layers + level, kept[:, cols - 1 :], 0.0)
    corner = jnp.sum(corner_limit + corner_kept, axis=0, keepdims=True)

    def place(base, add):
        return jnp.concatenate(
            [base[: 2 * REACH] + add[: 2 * REACH], base[2 * REACH : total - REACH],
             base[total - REACH :] + add[2 * REACH :]],
            axis=0,
        )

    low_all = place(low_cols[...], low_add)
    high_all = place(high_cols[:, :cols], high_add[:, :cols])
    last = norm_last[...]
    behind = high_add[:, cols:] + behind_add
    edges = jnp.concatenate([last[: 2 * REACH], last[total - REACH :]], axis=0)
    lanes = lane_ids(behind.shape)
    drop = jnp.where(lanes < layers, behind * edges, 0.0)
    column = place(high_cols[:, cols:], -drop)
    first = column[:REACH] + corner
    main = column[REACH:]
    quarter = strip // 4
    lanes = lane_ids((quarter, cols))
    folded = main[:quarter]
    for part in range(1, 4):
        moved = pltpu.roll(main[part * quarter : (part + 1) * quarter], part * 2 * layers, 1)
        folded = jnp.where(lanes // (2 * layers) == part, moved, folded)
    extra = jnp.zeros((quarter + REACH, cols), jnp.float32)
    send(
        "gy", jnp.concatenate([low_all[:, :cols], extra], axis=0),
        jnp.concatenate([high_all, folded, first], axis=0), even_ref, odd_ref,
    )
    own_ref[...] = low_all[:, cols:]


def column_kernel(depth, across, row_even, row_odd, band_ref, _, smooth, before, deep):
    layers, total, cols = across.shape
    strip = layers * REACH

    def depth_sums(part, values):
        for layer, value in enumerate(depth_smooth(values, depth)):
            deep[layer, part, :] = value

    def step(index, carry):
        for inner in range(2):
            part = pl.ds(pl.multiple_of((2 * index + inner + 2) * REACH, REACH), REACH)
            depth_sums(part, [across[layer, part, :] for layer in range(layers)])
        return carry

    lax.fori_loop(0, (total // REACH - 3) // 2, step, 0)
    for first_row in (0, REACH, total - REACH):
        part = pl.ds(first_row, REACH)
        values = []
        for layer in range(layers):
            line = pl.ds(strip + layer, 1) if first_row == 0 else pl.ds(layer * REACH, REACH)
            both = sides("gx", row_even[line, :], row_odd[line, :])
            values.append(across[layer, part, :] + both[first_row > REACH])
        depth_sums(part, values)
    constant = right_constant(band_ref[...])
    for layer in range(layers):
        result = right_product(deep[layer], constant)
        before[layer] = result[:REACH]
        smooth[layer] = result[REACH:]


def final_kernel(stress, strain, plastic, threshold, smooth, before, col_even, col_odd, row_even, row_odd,
                 norm, norm_before, own_cols, plastic_out, damage_out, force_out,
                 columns, damage_s, force_s, copy_sem, sems):
    layers, rows, cols = stress.shape
    total = rows + REACH
    strip = layers * REACH
    whole = pltpu.make_async_copy(plastic, plastic_out, copy_sem)
    whole.start()

    from_low, _ = sides("gy", col_even[...], col_odd[...])
    quarter = rows // 4
    folded = from_low[total : total + quarter]
    pieces = [from_low[total + quarter :], folded]
    for part in range(1, 4):
        pieces.append(pltpu.roll(folded, cols - part * 2 * layers, 1))
    column = jnp.concatenate(pieces, axis=0)
    limit = column - own_cols[...] * norm_before[...]
    kept = jnp.exp2(jnp.minimum(limit, 0.0) * RATE)
    columns[...] = kept * pltpu.roll(column, cols - layers, 1)

    def copies(layer):
        return (
            pltpu.make_async_copy(damage_s.at[layer], damage_out.at[layer], sems.at[0, layer]),
            pltpu.make_async_copy(force_s.at[0, layer], force_out.at[0, layer], sems.at[1, layer]),
            pltpu.make_async_copy(force_s.at[1, layer], force_out.at[1, layer], sems.at[2, layer]),
        )

    def layer_step(layer):
        lanes = lane_ids((REACH, cols))
        top = lax.broadcasted_iota(jnp.int32, (REACH, cols), 0) == 0
        above_sum = above_diff = None
        for block in range(rows // REACH + 1):
            extended = pl.ds(block * REACH, REACH)
            low, high = sides("gy", col_even[extended, :], col_odd[extended, :])
            if block == 0:
                summed = before[layer]
                line = pl.ds(strip + layers + layer, 1)
                rest, _ = sides("gx", row_even[line, :], row_odd[line, :])
                line = pl.ds(strip + 2 * layers + layer, 1)
                limit, _ = sides("gx", row_even[line, :], row_odd[line, :])
            else:
                at = (layer, pl.ds((block - 1) * REACH, REACH), slice(None))
                rest = (stress[at] + strain[at]) - plastic[at]
                limit = threshold[at]
                summed = smooth[at]
            full = add_columns(summed, layer, low, high)
            ratio = retained(full, norm[extended, :], limit)
            value = ratio * rest
            left = jnp.where(
                lanes == 0,
                pltpu.roll(columns[extended, :], (cols - layer) % cols, 1),
                pltpu.roll(value, 1, 1),
            )
            both = pltpu.roll(left + value, 1, 0)
            diff = pltpu.roll(left - value, 1, 0)
            if block:
                damage_s[at] = 1.0 - ratio
                force_s[(0, *at)] = 0.5 * (jnp.where(top, above_sum, both) - (left + value))
                force_s[(1, *at)] = 0.5 * (jnp.where(top, above_diff, diff) + (left - value))
            above_sum, above_diff = both, diff

    def step(index, carry):
        for inner in range(2):
            layer_step(2 * index + inner)
        for inner in range(2):
            for copy in copies(2 * index + inner):
                copy.start()
        return carry

    lax.fori_loop(0, layers // 2, step, 0)

    def drain(layer, carry):
        for copy in copies(layer):
            copy.wait()
        return carry

    lax.fori_loop(0, layers, drain, 0)
    whole.wait()


def call(kernel, outs, scratch, nanoseconds, operands, spaces=None, outs_space=pltpu.VMEM, limit=VMEM_BYTES):
    spaces = spaces or [pltpu.VMEM] * len(operands)
    shapes = [out if isinstance(out, jax.ShapeDtypeStruct) else jax.ShapeDtypeStruct(out, jnp.float32)
              for out in outs]
    return pl.pallas_call(
        kernel,
        out_shape=shapes,
        in_specs=[pl.BlockSpec(memory_space=space) for space in spaces],
        out_specs=[pl.BlockSpec(memory_space=outs_space)] * len(outs),
        scratch_shapes=[pltpu.VMEM(s, jnp.float32) if isinstance(s, tuple) else s for s in scratch],
        compiler_params=pltpu.CompilerParams(vmem_limit_bytes=limit),
        cost_estimate=pl.CostEstimate(
            flops=nanoseconds * 1_000_000, bytes_accessed=nanoseconds * 1000, transcendentals=0
        ),
    )(*operands)


def exchange(axis, even, odd):
    count = lax.axis_size(axis)
    results = []
    for start, value in ((0, even), (1, odd)):
        partner = list(range(count))
        for low in range(start, count - 1, 2):
            partner[low], partner[low + 1] = low + 1, low
        results.append(lax.ppermute(value, axis, list(enumerate(partner))))
    return results


def inverse_weights(axis, places, length):
    extent = length * lax.axis_size(axis)
    places = places + lax.axis_index(axis) * length
    total = jnp.zeros(places.shape, jnp.float32)
    for offset in range(-REACH, REACH + 1):
        inside = (places + offset >= 0) & (places + offset < extent)
        total = total + jnp.where(inside, tap(offset), 0.0)
    return 1.0 / jnp.maximum(total, tap(REACH))


def matrices(layers, rows, cols):
    depth = depth_matrix(layers)
    up, down = band(REACH, REACH, REACH), band(REACH, REACH, -REACH)
    same = np.eye(layers)
    below = np.kron(same, up)
    near = np.concatenate([np.zeros((REACH, REACH)), down], axis=1)
    line = band(1, 2 * REACH, 1 - 2 * REACH)
    above = np.concatenate([np.kron(same, near), np.kron(same, line)], axis=0)
    rows_band = np.concatenate([np.zeros((REACH - 1, rows)), band(1, rows, 1), band(rows, rows)])
    slots = cols // REACH
    low, high, ahead = np.zeros((cols, 2 * cols)), np.zeros((cols, 2 * cols)), np.zeros((cols, cols))
    for source in range(layers):
        own = slice(source * REACH, (source + 1) * REACH)
        first = (source - 1) % slots * REACH
        other = slice(first, first + REACH)
        for layer in range(layers):
            weight = depth[layer, source]
            first = (layer - 1) % slots * REACH
            low[own, first : first + REACH] = weight * up.T
            high[other, layer * REACH : (layer + 1) * REACH] = weight * down.T
            low[own, cols + layer] = [weight * tap(j + 1) for j in range(REACH)]
            high[other, cols + layer] = [weight * tap(REACH - 1 - j) for j in range(REACH)]
            ahead[((source - 2) % slots) * REACH + REACH - 1, layer] = weight * tap(REACH)
    constants = (below, above, rows_band, band(cols, cols), low, high, ahead)
    return depth, [jnp.asarray(matrix, jnp.float32) for matrix in constants]


def local(trial_stress, old_strain, yield_mask, newton_count, damage_threshold):
    layers, rows, cols = trial_stress.shape
    assert layers * REACH == cols == rows and layers % 2 == 0
    total, strip = rows + REACH, layers * REACH
    depth, constants = matrices(layers, rows, cols)
    below, above, rows_band, cols_band, *columns = constants

    whole, wide = (layers, rows, cols), (layers, total, cols)
    sent_rows = (strip + 3 * layers, cols)
    sent_cols = (total + rows // 4 + REACH, cols)
    packed, packed_two = (total, cols), (total, 2 * cols)

    sources = (trial_stress, old_strain, yield_mask, newton_count, damage_threshold)
    row_even, row_odd, norm, norm_last, norm_before, col_even, col_odd, *inputs = call(
        first_edge_kernel,
        [sent_rows, sent_rows, packed, packed, packed, sent_cols, sent_cols]
        + [jax.ShapeDtypeStruct(whole, source.dtype) for source in sources],
        [(strip, cols), pltpu.SemaphoreType.DMA((3, len(sources)))], 2500,
        sources, [pltpu.HBM] * len(sources), limit=FIRST_VMEM_BYTES,
    )
    stress, strain, _, _, threshold = inputs
    smooth = stress
    for outer_no in range(OUTER):
        if outer_no:
            row_even, row_odd = call(
                edge_kernel, [sent_rows] * 2,
                [(strip, cols), (2 * strip, cols), (2 * layers, cols)], 800,
                (*inputs, smooth, before, col_even, col_odd, norm, below, above),
            )
        row_even, row_odd = exchange("gx", row_even, row_odd)
        turn = jnp.full((1,), outer_no, jnp.int32)
        across, low_cols, high_cols, plastic = call(
            main_kernel, [wide, packed_two, packed_two, whole],
            [packed, packed, packed, packed], 4500,
            (turn, *inputs, smooth, col_even, col_odd, norm, norm_last, rows_band, *columns),
            [pltpu.SMEM] + [pltpu.VMEM] * 14,
        )
        col_even, col_odd, own_cols = call(
            corner_kernel, [sent_cols, sent_cols, packed], [], 400,
            (row_even, row_odd, low_cols, high_cols, norm_last, plastic, *columns),
        )
        col_even, col_odd = exchange("gy", col_even, col_odd)
        smooth, before = call(
            functools.partial(column_kernel, depth), [whole, (layers, REACH, cols)], [wide], 1200,
            (across, row_even, row_odd, cols_band, own_cols),
        )
    return tuple(call(
        final_kernel, [whole, whole, (2, *whole)],
        [packed, whole, (2, *whole), pltpu.SemaphoreType.DMA(()), pltpu.SemaphoreType.DMA((3, layers))],
        3000,
        (stress, strain, plastic, threshold, smooth, before, col_even, col_odd,
         row_even, row_odd, norm, norm_before, own_cols),
        outs_space=pltpu.HBM,
    ))


def solution(mesh):
    split_in = P(None, "gx", "gy")
    return jax.shard_map(
        local,
        mesh=mesh,
        in_specs=(split_in,) * 5,
        out_specs=(split_in, split_in, P(None, None, "gx", "gy")),
        check_vma=False,
    )
```

```python
import functools
import math

import jax
import jax.numpy as jnp
import numpy as np
from jax import lax
from jax.experimental import pallas as pl
from jax.experimental.pallas import tpu as pltpu
from jax.sharding import PartitionSpec as P

OUTER = 3
REACH = 8
RATE = math.log2(math.e) / 0.3
HALF_LN2 = 0.5 * math.log(2.0)
VMEM_BYTES = 24 * 1024 * 1024
FIRST_VMEM_BYTES = 48 * 1024 * 1024


def tap(offset):
    return math.exp(-(offset**2) / 32.0) if abs(offset) <= REACH else 0.0


def band(rows, cols, shift=0):
    return np.array([[tap(c - r + shift) for c in range(cols)] for r in range(rows)])


def depth_matrix(layers):
    weights = band(layers, layers)
    return weights / weights.sum(axis=1, keepdims=True)


def split(value):
    high = value.astype(jnp.bfloat16)
    low = (value - high.astype(jnp.float32)).astype(jnp.bfloat16)
    return high, low


def left_constant(matrix):
    high, low = split(matrix)
    return jnp.concatenate(
        [jnp.concatenate([high, high], axis=1), jnp.concatenate([low, low], axis=1)], axis=0
    )


def right_constant(matrix):
    both = jnp.concatenate(split(matrix), axis=1)
    return jnp.concatenate([both, both], axis=0)


def left_product(constant, value):
    rows = constant.shape[0] // 2
    halves = jnp.concatenate(split(value), axis=0)
    both = jnp.dot(constant, halves, preferred_element_type=jnp.float32)
    return both[:rows] + both[rows:]


def right_product(value, constant):
    cols = constant.shape[1] // 2
    halves = jnp.concatenate(split(value), axis=1)
    both = jnp.dot(halves, constant, preferred_element_type=jnp.float32)
    return both[:, :cols] + both[:, cols:]


def newton(stress, strain, yields, count, soften):
    start = 2.0 * stress - 3.5 * soften
    shift = start + (2.0 * strain - HALF_LN2)
    drop = 0.2 * soften
    state = start
    for sweep_no in range(1, 7):
        update = state * (0.8 - 0.2 * jnp.tanh(shift - state)) - drop
        state = update if sweep_no <= 3 else jnp.where(count >= sweep_no, update, state)
    moved = (strain + (stress - 1.75 * soften)) - 0.5 * state
    return jnp.where(yields > 0, moved, strain)


def depth_smooth(layers, matrix):
    count = len(layers)
    half = count // 2
    sums = [layers[k] + layers[count - 1 - k] for k in range(half)]
    diffs = [layers[k] - layers[count - 1 - k] for k in range(half)]
    out = [None] * count
    for row in range(half):
        even = odd = None
        for k in range(half):
            near, far = matrix[row, k], matrix[row, count - 1 - k]
            plus, minus = float(0.5 * (near + far)), float(0.5 * (near - far))
            if plus == 0.0 and minus == 0.0:
                continue
            even = sums[k] * plus if even is None else even + sums[k] * plus
            odd = diffs[k] * minus if odd is None else odd + diffs[k] * minus
        out[row] = even + odd
        out[count - 1 - row] = even - odd
    return out


def lane_ids(shape):
    return lax.broadcasted_iota(jnp.int32, shape, len(shape) - 1)


def on_even(axis):
    return lax.axis_index(axis) % 2 == 0


def sides(axis, even, odd):
    return jnp.where(on_even(axis), odd, even), jnp.where(on_even(axis), even, odd)


def send(axis, low, high, even_ref, odd_ref):
    place = lax.axis_index(axis)
    low = jnp.where(place == 0, 0.0, low)
    high = jnp.where(place == lax.axis_size(axis) - 1, 0.0, high)
    even_ref[...] = jnp.where(on_even(axis), high, low)
    odd_ref[...] = jnp.where(on_even(axis), low, high)


def add_columns(value, layer, low, high):
    cols = value.shape[1]
    slots = lane_ids(value.shape) >> (REACH.bit_length() - 1)
    packed = jnp.where(slots == layer, low, high)
    shift = (cols - layer * REACH) % cols
    moved = packed if isinstance(layer, int) and layer == 0 else pltpu.roll(packed, shift, 1)
    return value + jnp.where((slots == 0) | (slots == cols // REACH - 1), moved, 0.0)


def retained(full, norm, threshold):
    return jnp.exp2(jnp.minimum(threshold - full * norm, 0.0) * RATE)


def first_edge_kernel(*refs):
    sources, refs = refs[:5], refs[5:]
    even_ref, odd_ref, norm, norm_last, norm_before, _, _, *refs = refs
    targets, (block, sems) = refs[:5], refs[5:]
    stress, strain, yields, count, _ = targets
    layers, rows, cols = stress.shape
    parts = (pl.ds(0, REACH), pl.ds(rows - REACH, REACH), pl.ds(REACH, rows - 2 * REACH))
    copies = []
    for side, part in enumerate(parts):
        for index, (source, target) in enumerate(zip(sources, targets)):
            copies.append(
                pltpu.make_async_copy(
                    source.at[:, part, :], target.at[:, part, :], sems.at[side, index]
                )
            )
            copies[-1].start()
    total = rows + REACH
    ids = lax.broadcasted_iota(jnp.int32, (total, cols), 0)
    down = inverse_weights("gx", ids - REACH, rows)
    lanes = lane_ids((REACH, cols))
    for ref, place in ((norm, lanes), (norm_last, 0 * lanes + (cols - 1)), (norm_before, 0 * lanes - 1)):
        ref[...] = down * inverse_weights("gy", place, cols)[:1]
    square = (layers * REACH, layers * REACH)
    line, lane = lax.broadcasted_iota(jnp.int32, square, 0), lane_ids(square)
    steps = (lane & (REACH - 1)) - (line & (REACH - 1))
    band_part = jnp.zeros(square, jnp.float32)
    for step in range(REACH):
        band_part = jnp.where(abs(steps) == step, tap(REACH - step), band_part)
    band_part = jnp.where((line ^ lane) < REACH, band_part, 0.0)
    sent = []
    extra = jnp.zeros((even_ref.shape[0] - layers * REACH, cols), jnp.float32)
    for side, matrix in enumerate(
        (jnp.where(steps <= 0, band_part, 0.0), jnp.where(steps >= 0, band_part, 0.0))
    ):
        for copy in copies[side * 5 : side * 5 + 5]:
            copy.wait()
        for layer in range(layers):
            at = (layer, parts[side], slice(None))
            block[pl.ds(layer * REACH, REACH), :] = newton(
                stress[at], strain[at], yields[at], count[at], jnp.ones((REACH, cols), jnp.float32)
            )
        product = left_product(left_constant(matrix), block[...])
        sent.append(jnp.concatenate([product, extra], axis=0))
    send("gx", *sent, even_ref, odd_ref)
    for copy in copies[10:]:
        copy.wait()


def edge_kernel(stress, strain, yields, count, threshold, smooth, _, col_even, col_odd, norm,
                below, above, even_ref, odd_ref, low_block, high_block, rest):
    layers, rows, cols = stress.shape
    starts = (0, rows - 2 * REACH, rows - REACH)
    received = []
    for first_row in starts:
        part = pl.ds(first_row + REACH, REACH)
        received.append(sides("gy", col_even[part, :], col_odd[part, :]))

    def layer_step(layer):
        for index, first_row in enumerate(starts):
            at = (layer, pl.ds(first_row, REACH), slice(None))
            extended = pl.ds(first_row + REACH, REACH)
            full = add_columns(smooth[at], layer, *received[index])
            soften = 0.5 + 0.5 * retained(full, norm[extended, :], threshold[at])
            value = newton(stress[at], strain[at], yields[at], count[at], soften)
            if index == 0:
                low_block[pl.ds(layer * REACH, REACH), :] = value
            else:
                high_block[pl.ds((2 * layer + index - 1) * REACH, REACH), :] = value
            if index == 2:
                kept = (stress[at] + strain[at]) - value
                rest[pl.ds(layer, 1), :] = kept[REACH - 1 :]
                rest[pl.ds(layers + layer, 1), :] = threshold[at][REACH - 1 :]

    for layer in range(layers):
        layer_step(layer)
    low = left_product(left_constant(below[...]), low_block[...])
    high = left_product(left_constant(above[...]), high_block[...])
    extra = jnp.zeros((even_ref.shape[0] - low.shape[0], cols), jnp.float32)
    send(
        "gx", jnp.concatenate([low, extra], axis=0), jnp.concatenate([high, rest[...]], axis=0),
        even_ref, odd_ref,
    )


def main_kernel(turn, stress, strain, yields, count, threshold, smooth, col_even, col_odd, norm,
                norm_last, band_ref, low_ref, high_ref, next_ref,
                across, low_cols, high_cols, plastic, pack_low, pack_high, pack_next, pack_last):
    layers, rows, cols = stress.shape
    total = rows + REACH
    step_rows = 4 * REACH
    steps = rows // step_rows

    @pl.when(turn[0] == 0)
    def _():
        def step(index, carry):
            part = pl.ds(pl.multiple_of(index * step_rows, step_rows), step_rows)
            soften = jnp.ones((step_rows, cols), jnp.float32)
            for layer in range(layers):
                at = (layer, part, slice(None))
                plastic[at] = newton(stress[at], strain[at], yields[at], count[at], soften)
            return carry

        lax.fori_loop(0, steps, step, 0)

    @pl.when(turn[0] > 0)
    def _():
        def step(index, carry):
            part = pl.ds(pl.multiple_of(index * step_rows, step_rows), step_rows)
            extended = pl.ds(pl.multiple_of(index * step_rows + REACH, REACH), step_rows)
            low, high = sides("gy", col_even[extended, :], col_odd[extended, :])
            for layer in range(layers):
                at = (layer, part, slice(None))
                full = add_columns(smooth[at], layer, low, high)
                soften = 0.5 + 0.5 * retained(full, norm[extended, :], threshold[at])
                plastic[at] = newton(stress[at], strain[at], yields[at], count[at], soften)
            return carry

        lax.fori_loop(0, steps, step, 0)

    constant = left_constant(band_ref[...])
    slots = lane_ids((total, cols)) >> (REACH.bit_length() - 1)
    for layer in range(0, layers, 2):
        pair = jnp.concatenate([plastic[layer], plastic[layer + 1]], axis=1)
        result = left_product(constant, pair)
        for inner in range(2):
            value = result[:, inner * cols : (inner + 1) * cols]
            across[layer + inner] = value
            moved = pltpu.roll(value, (layer + inner) * REACH, 1) if layer + inner else value
            for behind, ref in enumerate((pack_low, pack_high, pack_next)):
                mask = slots == (layer + inner - behind) % (cols // REACH)
                pltpu.store(ref, moved, mask=mask)

    low_cols[...] = right_product(pack_low[...], right_constant(low_ref[...]))
    high = right_product(pack_high[...], right_constant(high_ref[...]))
    behind = right_product(pack_next[...], right_constant(next_ref[...]))
    high_cols[:, :cols] = high[:, :cols]

    @pl.when(turn[0] == OUTER - 1)
    def _():
        def last_column(index, carry):
            part = pl.ds(pl.multiple_of(index * step_rows, step_rows), step_rows)
            lanes = lane_ids((step_rows, cols))
            packed = jnp.zeros((step_rows, cols), jnp.float32)
            for layer in range(layers):
                at = (layer, part, slice(None))
                packed = jnp.where(lanes == layer, pltpu.roll(threshold[at], layer + 1, 1), packed)
                rest = (stress[at] + strain[at]) - plastic[at]
                turned = pltpu.roll(rest, layers + layer + 1, 1)
                packed = jnp.where(lanes == layers + layer, turned, packed)
            pack_last[pl.ds(pl.multiple_of(index * step_rows + REACH, REACH), step_rows), :] = packed
            return carry

        pack_last[pl.ds(0, REACH), :] = jnp.zeros((REACH, cols), jnp.float32)
        lax.fori_loop(0, steps, last_column, 0)
        lanes = lane_ids(pack_last.shape)
        drop = (high[:, cols:] + behind) * norm_last[...]
        high_cols[:, cols:] = pack_last[...] - jnp.where(lanes < layers, drop, 0.0)


def pack_edges(values):
    cols = values[0].shape[1]
    count = cols // REACH
    slots = lane_ids(values[0].shape) >> (REACH.bit_length() - 1)
    low = high = ahead = jnp.zeros_like(values[0])
    for layer, value in enumerate(values):
        moved = pltpu.roll(value, layer * REACH, 1) if layer else value
        low = jnp.where(slots == layer, moved, low)
        high = jnp.where(slots == (layer - 1) % count, moved, high)
        ahead = jnp.where(slots == (layer - 2) % count, moved, ahead)
    return low, high, ahead


def corner_kernel(row_even, row_odd, low_cols, high_cols, norm_last, _, low_ref, high_ref, next_ref,
                  even_ref, odd_ref, own_ref):
    cols = low_ref.shape[0]
    total = low_cols.shape[0]
    layers = (total - REACH) // REACH
    strip = layers * REACH
    from_low, from_high = sides("gx", row_even[...], row_odd[...])
    partial = from_low[strip : strip + layers]
    kept = from_low[strip + layers : strip + 2 * layers]
    limit = from_low[strip + 2 * layers : strip + 3 * layers]
    before = [jnp.broadcast_to(partial[layer : layer + 1], (REACH, cols)) for layer in range(layers)]
    packs = [pack_edges(before)] + [
        pack_edges([block[layer * REACH : (layer + 1) * REACH] for layer in range(layers)])
        for block in (from_low, from_high)
    ]
    low, high, ahead = (jnp.concatenate(group, axis=0) for group in zip(*packs))
    low_add = right_product(low, right_constant(low_ref[...]))
    high_add = right_product(high, right_constant(high_ref[...]))
    behind_add = right_product(ahead, right_constant(next_ref[...]))

    lanes = lane_ids((layers, cols))
    level = lax.broadcasted_iota(jnp.int32, (layers, cols), 0)
    corner_limit = jnp.where(lanes == level, limit[:, cols - 1 :], 0.0)
    corner_kept = jnp.where(lanes == layers + level, kept[:, cols - 1 :], 0.0)
    corner = jnp.sum(corner_limit + corner_kept, axis=0, keepdims=True)

    def place(base, add):
        return jnp.concatenate(
            [base[: 2 * REACH] + add[: 2 * REACH], base[2 * REACH : total - REACH],
             base[total - REACH :] + add[2 * REACH :]],
            axis=0,
        )

    low_all = place(low_cols[...], low_add)
    high_all = place(high_cols[:, :cols], high_add[:, :cols])
    last = norm_last[...]
    behind = high_add[:, cols:] + behind_add
    edges = jnp.concatenate([last[: 2 * REACH], last[total - REACH :]], axis=0)
    lanes = lane_ids(behind.shape)
    drop = jnp.where(lanes < layers, behind * edges, 0.0)
    column = place(high_cols[:, cols:], -drop)
    first = column[:REACH] + corner
    main = column[REACH:]
    quarter = strip // 4
    lanes = lane_ids((quarter, cols))
    folded = main[:quarter]
    for part in range(1, 4):
        moved = pltpu.roll(main[part * quarter : (part + 1) * quarter], part * 2 * layers, 1)
        folded = jnp.where(lanes // (2 * layers) == part, moved, folded)
    extra = jnp.zeros((quarter + REACH, cols), jnp.float32)
    send(
        "gy", jnp.concatenate([low_all[:, :cols], extra], axis=0),
        jnp.concatenate([high_all, folded, first], axis=0), even_ref, odd_ref,
    )
    own_ref[...] = low_all[:, cols:]


def column_kernel(depth, across, row_even, row_odd, band_ref, _, smooth, before, deep):
    layers, total, cols = across.shape
    strip = layers * REACH

    def depth_sums(part, values):
        for layer, value in enumerate(depth_smooth(values, depth)):
            deep[layer, part, :] = value

    def step(index, carry):
        for inner in range(2):
            part = pl.ds(pl.multiple_of((2 * index + inner + 2) * REACH, REACH), REACH)
            depth_sums(part, [across[layer, part, :] for layer in range(layers)])
        return carry

    lax.fori_loop(0, (total // REACH - 3) // 2, step, 0)
    for first_row in (0, REACH, total - REACH):
        part = pl.ds(first_row, REACH)
        values = []
        for layer in range(layers):
            line = pl.ds(strip + layer, 1) if first_row == 0 else pl.ds(layer * REACH, REACH)
            both = sides("gx", row_even[line, :], row_odd[line, :])
            values.append(across[layer, part, :] + both[first_row > REACH])
        depth_sums(part, values)
    constant = right_constant(band_ref[...])
    for layer in range(layers):
        result = right_product(deep[layer], constant)
        before[layer] = result[:REACH]
        smooth[layer] = result[REACH:]


def final_kernel(stress, strain, plastic, threshold, smooth, before, col_even, col_odd, row_even, row_odd,
                 norm, norm_before, own_cols, plastic_out, damage_out, force_out,
                 columns, damage_s, force_s, copy_sem, sems):
    layers, rows, cols = stress.shape
    total = rows + REACH
    strip = layers * REACH
    whole = pltpu.make_async_copy(plastic, plastic_out, copy_sem)
    whole.start()

    from_low, _ = sides("gy", col_even[...], col_odd[...])
    quarter = rows // 4
    folded = from_low[total : total + quarter]
    pieces = [from_low[total + quarter :], folded]
    for part in range(1, 4):
        pieces.append(pltpu.roll(folded, cols - part * 2 * layers, 1))
    column = jnp.concatenate(pieces, axis=0)
    limit = column - own_cols[...] * norm_before[...]
    kept = jnp.exp2(jnp.minimum(limit, 0.0) * RATE)
    columns[...] = kept * pltpu.roll(column, cols - layers, 1)

    def copies(layer):
        return (
            pltpu.make_async_copy(damage_s.at[layer], damage_out.at[layer], sems.at[0, layer]),
            pltpu.make_async_copy(force_s.at[0, layer], force_out.at[0, layer], sems.at[1, layer]),
            pltpu.make_async_copy(force_s.at[1, layer], force_out.at[1, layer], sems.at[2, layer]),
        )

    def layer_step(layer):
        lanes = lane_ids((REACH, cols))
        top = lax.broadcasted_iota(jnp.int32, (REACH, cols), 0) == 0
        above_sum = above_diff = None
        for block in range(rows // REACH + 1):
            extended = pl.ds(block * REACH, REACH)
            low, high = sides("gy", col_even[extended, :], col_odd[extended, :])
            if block == 0:
                summed = before[layer]
                line = pl.ds(strip + layers + layer, 1)
                rest, _ = sides("gx", row_even[line, :], row_odd[line, :])
                line = pl.ds(strip + 2 * layers + layer, 1)
                limit, _ = sides("gx", row_even[line, :], row_odd[line, :])
            else:
                at = (layer, pl.ds((block - 1) * REACH, REACH), slice(None))
                rest = (stress[at] + strain[at]) - plastic[at]
                limit = threshold[at]
                summed = smooth[at]
            full = add_columns(summed, layer, low, high)
            ratio = retained(full, norm[extended, :], limit)
            value = ratio * rest
            left = jnp.where(
                lanes == 0,
                pltpu.roll(columns[extended, :], (cols - layer) % cols, 1),
                pltpu.roll(value, 1, 1),
            )
            both = pltpu.roll(left + value, 1, 0)
            diff = pltpu.roll(left - value, 1, 0)
            if block:
                damage_s[at] = 1.0 - ratio
                force_s[(0, *at)] = 0.5 * (jnp.where(top, above_sum, both) - (left + value))
                force_s[(1, *at)] = 0.5 * (jnp.where(top, above_diff, diff) + (left - value))
            above_sum, above_diff = both, diff

    def step(index, carry):
        for inner in range(4):
            layer_step(4 * index + inner)
        for inner in range(4):
            for copy in copies(4 * index + inner):
                copy.start()
        return carry

    lax.fori_loop(0, layers // 4, step, 0)

    def drain(layer, carry):
        for copy in copies(layer):
            copy.wait()
        return carry

    lax.fori_loop(0, layers, drain, 0)
    whole.wait()


def call(kernel, outs, scratch, nanoseconds, operands, spaces=None, outs_space=pltpu.VMEM, limit=VMEM_BYTES):
    spaces = spaces or [pltpu.VMEM] * len(operands)
    shapes = [out if isinstance(out, jax.ShapeDtypeStruct) else jax.ShapeDtypeStruct(out, jnp.float32)
              for out in outs]
    return pl.pallas_call(
        kernel,
        out_shape=shapes,
        in_specs=[pl.BlockSpec(memory_space=space) for space in spaces],
        out_specs=[pl.BlockSpec(memory_space=outs_space)] * len(outs),
        scratch_shapes=[pltpu.VMEM(s, jnp.float32) if isinstance(s, tuple) else s for s in scratch],
        compiler_params=pltpu.CompilerParams(vmem_limit_bytes=limit),
        cost_estimate=pl.CostEstimate(
            flops=nanoseconds * 1_000_000, bytes_accessed=nanoseconds * 1000, transcendentals=0
        ),
    )(*operands)


def exchange(axis, even, odd):
    count = lax.axis_size(axis)
    results = []
    for start, value in ((0, even), (1, odd)):
        partner = list(range(count))
        for low in range(start, count + start - 1, 2):
            partner[low], partner[(low + 1) % count] = (low + 1) % count, low
        results.append(lax.ppermute(value, axis, list(enumerate(partner))))
    return results


def inverse_weights(axis, places, length):
    extent = length * lax.axis_size(axis)
    places = places + lax.axis_index(axis) * length
    total = jnp.zeros(places.shape, jnp.float32)
    for offset in range(-REACH, REACH + 1):
        inside = (places + offset >= 0) & (places + offset < extent)
        total = total + jnp.where(inside, tap(offset), 0.0)
    return 1.0 / jnp.maximum(total, tap(REACH))


def matrices(layers, rows, cols):
    depth = depth_matrix(layers)
    up, down = band(REACH, REACH, REACH), band(REACH, REACH, -REACH)
    same = np.eye(layers)
    below = np.kron(same, up)
    near = np.concatenate([np.zeros((REACH, REACH)), down], axis=1)
    line = band(1, 2 * REACH, 1 - 2 * REACH)
    above = np.concatenate([np.kron(same, near), np.kron(same, line)], axis=0)
    rows_band = np.concatenate([np.zeros((REACH - 1, rows)), band(1, rows, 1), band(rows, rows)])
    slots = cols // REACH
    low, high, ahead = np.zeros((cols, 2 * cols)), np.zeros((cols, 2 * cols)), np.zeros((cols, cols))
    for source in range(layers):
        own = slice(source * REACH, (source + 1) * REACH)
        first = (source - 1) % slots * REACH
        other = slice(first, first + REACH)
        for layer in range(layers):
            weight = depth[layer, source]
            first = (layer - 1) % slots * REACH
            low[own, first : first + REACH] = weight * up.T
            high[other, layer * REACH : (layer + 1) * REACH] = weight * down.T
            low[own, cols + layer] = [weight * tap(j + 1) for j in range(REACH)]
            high[other, cols + layer] = [weight * tap(REACH - 1 - j) for j in range(REACH)]
            ahead[((source - 2) % slots) * REACH + REACH - 1, layer] = weight * tap(REACH)
    constants = (below, above, rows_band, band(cols, cols), low, high, ahead)
    return depth, [jnp.asarray(matrix, jnp.float32) for matrix in constants]


def local(trial_stress, old_strain, yield_mask, newton_count, damage_threshold):
    layers, rows, cols = trial_stress.shape
    assert layers * REACH == cols == rows and layers % 2 == 0
    total, strip = rows + REACH, layers * REACH
    depth, constants = matrices(layers, rows, cols)
    below, above, rows_band, cols_band, *columns = constants

    whole, wide = (layers, rows, cols), (layers, total, cols)
    sent_rows = (strip + 3 * layers, cols)
    sent_cols = (total + rows // 4 + REACH, cols)
    packed, packed_two = (total, cols), (total, 2 * cols)

    sources = (trial_stress, old_strain, yield_mask, newton_count, damage_threshold)
    row_even, row_odd, norm, norm_last, norm_before, col_even, col_odd, *inputs = call(
        first_edge_kernel,
        [sent_rows, sent_rows, packed, packed, packed, sent_cols, sent_cols]
        + [jax.ShapeDtypeStruct(whole, source.dtype) for source in sources],
        [(strip, cols), pltpu.SemaphoreType.DMA((3, len(sources)))], 2500,
        sources, [pltpu.HBM] * len(sources), limit=FIRST_VMEM_BYTES,
    )
    stress, strain, _, _, threshold = inputs
    smooth = stress
    for outer_no in range(OUTER):
        if outer_no:
            row_even, row_odd = call(
                edge_kernel, [sent_rows] * 2,
                [(strip, cols), (2 * strip, cols), (2 * layers, cols)], 800,
                (*inputs, smooth, before, col_even, col_odd, norm, below, above),
            )
        row_even, row_odd = exchange("gx", row_even, row_odd)
        turn = jnp.full((1,), outer_no, jnp.int32)
        across, low_cols, high_cols, plastic = call(
            main_kernel, [wide, packed_two, packed_two, whole],
            [packed, packed, packed, packed], 4500,
            (turn, *inputs, smooth, col_even, col_odd, norm, norm_last, rows_band, *columns),
            [pltpu.SMEM] + [pltpu.VMEM] * 14,
        )
        col_even, col_odd, own_cols = call(
            corner_kernel, [sent_cols, sent_cols, packed], [], 400,
            (row_even, row_odd, low_cols, high_cols, norm_last, plastic, *columns),
        )
        col_even, col_odd = exchange("gy", col_even, col_odd)
        smooth, before = call(
            functools.partial(column_kernel, depth), [whole, (layers, REACH, cols)], [wide], 1200,
            (across, row_even, row_odd, cols_band, own_cols),
        )
    return tuple(call(
        final_kernel, [whole, whole, (2, *whole)],
        [packed, whole, (2, *whole), pltpu.SemaphoreType.DMA(()), pltpu.SemaphoreType.DMA((3, layers))],
        3000,
        (stress, strain, plastic, threshold, smooth, before, col_even, col_odd,
         row_even, row_odd, norm, norm_before, own_cols),
        outs_space=pltpu.HBM,
    ))


def solution(mesh):
    split_in = P(None, "gx", "gy")
    return jax.shard_map(
        local,
        mesh=mesh,
        in_specs=(split_in,) * 5,
        out_specs=(split_in, split_in, P(None, None, "gx", "gy")),
        check_vma=False,
    )
```

```python
import functools
import math

import jax
import jax.numpy as jnp
import numpy as np
from jax import lax
from jax.experimental import pallas as pl
from jax.experimental.pallas import tpu as pltpu
from jax.sharding import PartitionSpec as P

OUTER = 3
REACH = 8
RATE = math.log2(math.e) / 0.3
HALF_LN2 = 0.5 * math.log(2.0)
VMEM_BYTES = 24 * 1024 * 1024
FIRST_VMEM_BYTES = 48 * 1024 * 1024


def tap(offset):
    return math.exp(-(offset**2) / 32.0) if abs(offset) <= REACH else 0.0


def band(rows, cols, shift=0):
    return np.array([[tap(c - r + shift) for c in range(cols)] for r in range(rows)])


def depth_matrix(layers):
    weights = band(layers, layers)
    return weights / weights.sum(axis=1, keepdims=True)


def split(value):
    high = value.astype(jnp.bfloat16)
    low = (value - high.astype(jnp.float32)).astype(jnp.bfloat16)
    return high, low


def left_constant(matrix):
    high, low = split(matrix)
    return jnp.concatenate(
        [jnp.concatenate([high, high], axis=1), jnp.concatenate([low, low], axis=1)], axis=0
    )


def right_constant(matrix):
    both = jnp.concatenate(split(matrix), axis=1)
    return jnp.concatenate([both, both], axis=0)


def left_product(constant, value):
    rows = constant.shape[0] // 2
    halves = jnp.concatenate(split(value), axis=0)
    both = jnp.dot(constant, halves, preferred_element_type=jnp.float32)
    return both[:rows] + both[rows:]


def right_product(value, constant):
    cols = constant.shape[1] // 2
    halves = jnp.concatenate(split(value), axis=1)
    both = jnp.dot(halves, constant, preferred_element_type=jnp.float32)
    return both[:, :cols] + both[:, cols:]


def newton(stress, strain, yields, count, soften):
    start = 2.0 * stress - 3.5 * soften
    shift = start + (2.0 * strain - HALF_LN2)
    drop = 0.2 * soften
    state = start
    for sweep_no in range(1, 7):
        update = state * (0.8 - 0.2 * jnp.tanh(shift - state)) - drop
        state = update if sweep_no <= 3 else jnp.where(count >= sweep_no, update, state)
    moved = (strain + (stress - 1.75 * soften)) - 0.5 * state
    return jnp.where(yields > 0, moved, strain)


def depth_smooth(layers, matrix):
    count = len(layers)
    half = count // 2
    sums = [layers[k] + layers[count - 1 - k] for k in range(half)]
    diffs = [layers[k] - layers[count - 1 - k] for k in range(half)]
    out = [None] * count
    for row in range(half):
        even = odd = None
        for k in range(half):
            near, far = matrix[row, k], matrix[row, count - 1 - k]
            plus, minus = float(0.5 * (near + far)), float(0.5 * (near - far))
            if plus == 0.0 and minus == 0.0:
                continue
            even = sums[k] * plus if even is None else even + sums[k] * plus
            odd = diffs[k] * minus if odd is None else odd + diffs[k] * minus
        out[row] = even + odd
        out[count - 1 - row] = even - odd
    return out


def lane_ids(shape):
    return lax.broadcasted_iota(jnp.int32, shape, len(shape) - 1)


def on_even(axis):
    return lax.axis_index(axis) % 2 == 0


def sides(axis, even, odd):
    return jnp.where(on_even(axis), odd, even), jnp.where(on_even(axis), even, odd)


def send(axis, low, high, even_ref, odd_ref):
    place = lax.axis_index(axis)
    low = jnp.where(place == 0, 0.0, low)
    high = jnp.where(place == lax.axis_size(axis) - 1, 0.0, high)
    even_ref[...] = jnp.where(on_even(axis), high, low)
    odd_ref[...] = jnp.where(on_even(axis), low, high)


def layer_slots(shape):
    return lane_ids(shape) >> (REACH.bit_length() - 1)


def ratio(limit):
    return jnp.exp2(jnp.minimum(limit, 0.0) * RATE)


def edge_ratios(edges, received, norms, part, extended):
    both = sides("gy", *(ref[part, :] for ref in received))
    return [
        ratio(edge[extended, :] - value * norm[extended, :])
        for edge, value, norm in zip(edges, both, norms)
    ]


def with_edges(inner, layer, low, high):
    cols = inner.shape[1]
    slots = layer_slots(inner.shape)
    packed = jnp.where(slots == layer, low, high)
    shift = (cols - layer * REACH) % cols
    moved = packed if isinstance(layer, int) and layer == 0 else pltpu.roll(packed, shift, 1)
    return jnp.where((slots == 0) | (slots == cols // REACH - 1), moved, inner)


def first_edge_kernel(*refs):
    sources, refs = refs[:5], refs[5:]
    even_ref, odd_ref, norm, norm_low, norm_high, norm_last, norm_before, _, _, _, *refs = refs
    targets, (block, sems) = refs[:5], refs[5:]
    stress, strain, yields, count, _ = targets
    layers, rows, cols = stress.shape
    parts = (pl.ds(0, REACH), pl.ds(rows - REACH, REACH), pl.ds(REACH, rows - 2 * REACH))
    copies = []
    for side, part in enumerate(parts):
        for index, (source, target) in enumerate(zip(sources, targets)):
            copies.append(
                pltpu.make_async_copy(
                    source.at[:, part, :], target.at[:, part, :], sems.at[side, index]
                )
            )
            copies[-1].start()
    total = rows + REACH
    ids = lax.broadcasted_iota(jnp.int32, (total, cols), 0)
    down = inverse_weights("gx", ids - REACH, rows)
    lanes = lane_ids((REACH, cols))
    within = lanes & (REACH - 1)
    places = (lanes, within, within + (cols - REACH), 0 * lanes + (cols - 1), 0 * lanes - 1)
    for ref, place in zip((norm, norm_low, norm_high, norm_last, norm_before), places):
        ref[...] = down * inverse_weights("gy", place, cols)[:1]
    square = (layers * REACH, layers * REACH)
    line, lane = lax.broadcasted_iota(jnp.int32, square, 0), lane_ids(square)
    steps = (lane & (REACH - 1)) - (line & (REACH - 1))
    band_part = jnp.zeros(square, jnp.float32)
    for step in range(REACH):
        band_part = jnp.where(abs(steps) == step, tap(REACH - step), band_part)
    band_part = jnp.where((line ^ lane) < REACH, band_part, 0.0)
    sent = []
    for side, matrix in enumerate(
        (jnp.where(steps <= 0, band_part, 0.0), jnp.where(steps >= 0, band_part, 0.0))
    ):
        for copy in copies[side * 5 : side * 5 + 5]:
            copy.wait()
        for layer in range(layers):
            at = (layer, parts[side], slice(None))
            block[pl.ds(layer * REACH, REACH), :] = newton(
                stress[at], strain[at], yields[at], count[at], jnp.ones((REACH, cols), jnp.float32)
            )
        sent.append(left_product(left_constant(matrix), block[...]))
    send("gx", *sent, even_ref, odd_ref)
    for copy in copies[10:]:
        copy.wait()


def edge_kernel(stress, strain, yields, count, threshold, kept, _, edge_low, edge_high, norm_low,
                norm_high, col_even, col_odd, below, above,
                even_ref, odd_ref, low_block, high_block, rest):
    layers, rows, cols = stress.shape
    starts = (0, rows - 2 * REACH, rows - REACH)
    packed = [
        edge_ratios(
            (edge_low, edge_high), (col_even, col_odd), (norm_low, norm_high),
            pl.ds(first_row, REACH), pl.ds(first_row + REACH, REACH),
        )
        for first_row in starts
    ]

    def layer_step(layer):
        for index, first_row in enumerate(starts):
            at = (layer, pl.ds(first_row, REACH), slice(None))
            soften = 0.5 + 0.5 * with_edges(kept[at], layer, *packed[index])
            value = newton(stress[at], strain[at], yields[at], count[at], soften)
            if index == 0:
                low_block[pl.ds(layer * REACH, REACH), :] = value
            else:
                high_block[pl.ds((2 * layer + index - 1) * REACH, REACH), :] = value
            if index == 2:
                left = (stress[at] + strain[at]) - value
                rest[pl.ds(layer, 1), :] = left[REACH - 1 :]
                rest[pl.ds(layers + layer, 1), :] = threshold[at][REACH - 1 :]

    for layer in range(layers):
        layer_step(layer)
    low = left_product(left_constant(below[...]), low_block[...])
    high = left_product(left_constant(above[...]), high_block[...])
    extra = jnp.zeros((even_ref.shape[0] - low.shape[0], cols), jnp.float32)
    send(
        "gx", jnp.concatenate([low, extra], axis=0), jnp.concatenate([high, rest[...]], axis=0),
        even_ref, odd_ref,
    )


def main_kernel(turn, stress, strain, yields, count, threshold, kept, edge_low, edge_high, norm_low,
                norm_high, col_even, col_odd, norm_last, band_ref, low_ref, high_ref, next_ref,
                across, low_cols, high_cols, plastic, pack_low, pack_high, pack_next, pack_last):
    layers, rows, cols = stress.shape
    total = rows + REACH
    step_rows = 4 * REACH
    steps = rows // step_rows

    @pl.when(turn[0] == 0)
    def _():
        def step(index, carry):
            part = pl.ds(pl.multiple_of(index * step_rows, step_rows), step_rows)
            soften = jnp.ones((step_rows, cols), jnp.float32)
            for layer in range(layers):
                at = (layer, part, slice(None))
                plastic[at] = newton(stress[at], strain[at], yields[at], count[at], soften)
            return carry

        lax.fori_loop(0, steps, step, 0)

    @pl.when(turn[0] > 0)
    def _():
        def step(index, carry):
            part = pl.ds(pl.multiple_of(index * step_rows, step_rows), step_rows)
            extended = pl.ds(pl.multiple_of(index * step_rows + REACH, REACH), step_rows)
            packed = edge_ratios(
                (edge_low, edge_high), (col_even, col_odd), (norm_low, norm_high), part, extended
            )
            for layer in range(layers):
                at = (layer, part, slice(None))
                soften = 0.5 + 0.5 * with_edges(kept[at], layer, *packed)
                plastic[at] = newton(stress[at], strain[at], yields[at], count[at], soften)
            return carry

        lax.fori_loop(0, steps, step, 0)

    constant = left_constant(band_ref[...])
    slots = layer_slots((total, cols))
    for layer in range(0, layers, 2):
        pair = jnp.concatenate([plastic[layer], plastic[layer + 1]], axis=1)
        result = left_product(constant, pair)
        for inner in range(2):
            value = result[:, inner * cols : (inner + 1) * cols]
            across[layer + inner] = value
            moved = pltpu.roll(value, (layer + inner) * REACH, 1) if layer + inner else value
            for behind, ref in enumerate((pack_low, pack_high, pack_next)):
                mask = slots == (layer + inner - behind) % (cols // REACH)
                pltpu.store(ref, moved, mask=mask)

    low_cols[...] = right_product(pack_low[...], right_constant(low_ref[...]))
    high = right_product(pack_high[...], right_constant(high_ref[...]))
    behind = right_product(pack_next[...], right_constant(next_ref[...]))
    high_cols[:, :cols] = high[:, :cols]

    @pl.when(turn[0] == OUTER - 1)
    def _():
        def last_column(index, carry):
            part = pl.ds(pl.multiple_of(index * step_rows, step_rows), step_rows)
            lanes = lane_ids((step_rows, cols))
            packed = jnp.zeros((step_rows, cols), jnp.float32)
            for layer in range(layers):
                at = (layer, part, slice(None))
                packed = jnp.where(lanes == layer, pltpu.roll(threshold[at], layer + 1, 1), packed)
                rest = (stress[at] + strain[at]) - plastic[at]
                turned = pltpu.roll(rest, layers + layer + 1, 1)
                packed = jnp.where(lanes == layers + layer, turned, packed)
            pack_last[pl.ds(pl.multiple_of(index * step_rows + REACH, REACH), step_rows), :] = packed
            return carry

        pack_last[pl.ds(0, REACH), :] = jnp.zeros((REACH, cols), jnp.float32)
        lax.fori_loop(0, steps, last_column, 0)
        lanes = lane_ids(pack_last.shape)
        drop = (high[:, cols:] + behind) * norm_last[...]
        high_cols[:, cols:] = pack_last[...] - jnp.where(lanes < layers, drop, 0.0)


def pack_edges(values):
    cols = values[0].shape[1]
    count = cols // REACH
    slots = layer_slots(values[0].shape)
    low = high = ahead = jnp.zeros_like(values[0])
    for layer, value in enumerate(values):
        moved = pltpu.roll(value, layer * REACH, 1) if layer else value
        low = jnp.where(slots == layer, moved, low)
        high = jnp.where(slots == (layer - 1) % count, moved, high)
        ahead = jnp.where(slots == (layer - 2) % count, moved, ahead)
    return low, high, ahead


def corner_kernel(row_even, row_odd, rest_even, rest_odd, low_cols, high_cols, norm_last, _, low_ref, high_ref, next_ref,
                  even_ref, odd_ref, own_ref):
    cols = low_ref.shape[0]
    total = low_cols.shape[0]
    layers = (total - REACH) // REACH
    strip = layers * REACH
    from_low, from_high = sides("gx", row_even[...], row_odd[...])
    rest, _ = sides("gx", rest_even[...], rest_odd[...])
    partial, kept, limit = rest[:layers], rest[layers : 2 * layers], rest[2 * layers :]
    before = [jnp.broadcast_to(partial[layer : layer + 1], (REACH, cols)) for layer in range(layers)]
    packs = [pack_edges(before)] + [
        pack_edges([block[layer * REACH : (layer + 1) * REACH] for layer in range(layers)])
        for block in (from_low, from_high)
    ]
    low, high, ahead = (jnp.concatenate(group, axis=0) for group in zip(*packs))
    low_add = right_product(low, right_constant(low_ref[...]))
    high_add = right_product(high, right_constant(high_ref[...]))
    behind_add = right_product(ahead, right_constant(next_ref[...]))

    lanes = lane_ids((layers, cols))
    level = lax.broadcasted_iota(jnp.int32, (layers, cols), 0)
    corner_limit = jnp.where(lanes == level, limit[:, cols - 1 :], 0.0)
    corner_kept = jnp.where(lanes == layers + level, kept[:, cols - 1 :], 0.0)
    corner = jnp.sum(corner_limit + corner_kept, axis=0, keepdims=True)

    def place(base, add):
        return jnp.concatenate(
            [base[: 2 * REACH] + add[: 2 * REACH], base[2 * REACH : total - REACH],
             base[total - REACH :] + add[2 * REACH :]],
            axis=0,
        )

    low_all = place(low_cols[...], low_add)
    high_all = place(high_cols[:, :cols], high_add[:, :cols])
    last = norm_last[...]
    behind = high_add[:, cols:] + behind_add
    edges = jnp.concatenate([last[: 2 * REACH], last[total - REACH :]], axis=0)
    lanes = lane_ids(behind.shape)
    drop = jnp.where(lanes < layers, behind * edges, 0.0)
    column = place(high_cols[:, cols:], -drop)
    first = column[:REACH] + corner
    main = column[REACH:]
    quarter = strip // 4
    lanes = lane_ids((quarter, cols))
    folded = main[:quarter]
    for part in range(1, 4):
        moved = pltpu.roll(main[part * quarter : (part + 1) * quarter], part * 2 * layers, 1)
        folded = jnp.where(lanes // (2 * layers) == part, moved, folded)
    extra = jnp.zeros((quarter + REACH, cols), jnp.float32)
    send(
        "gy", jnp.concatenate([low_all[REACH:, :cols], low_all[:REACH, :cols], extra], axis=0),
        jnp.concatenate([high_all[REACH:], high_all[:REACH], folded, first], axis=0),
        even_ref, odd_ref,
    )
    own_ref[...] = low_all[:, cols:]


def column_kernel(depth, across, row_even, row_odd, rest_even, rest_odd, threshold, norm, band_ref, _,
                  kept, kept_before, edge_low, edge_high, deep):
    layers, total, cols = across.shape

    def depth_sums(part, values):
        for layer, value in enumerate(depth_smooth(values, depth)):
            deep[layer, part, :] = value

    def step(index, carry):
        for inner in range(2):
            part = pl.ds(pl.multiple_of((2 * index + inner + 2) * REACH, REACH), REACH)
            depth_sums(part, [across[layer, part, :] for layer in range(layers)])
        return carry

    lax.fori_loop(0, (total // REACH - 3) // 2, step, 0)
    for first_row in (0, REACH, total - REACH):
        part = pl.ds(first_row, REACH)
        values = []
        for layer in range(layers):
            if first_row:
                line = pl.ds(layer * REACH, REACH)
                both = sides("gx", row_even[line, :], row_odd[line, :])
            else:
                both = sides("gx", rest_even[pl.ds(layer, 1), :], rest_odd[pl.ds(layer, 1), :])
            values.append(across[layer, part, :] + both[first_row > REACH])
        depth_sums(part, values)

    constant = right_constant(band_ref[...])
    slots = layer_slots((total, cols))
    for layer in range(layers):
        nonlocal_strain = right_product(deep[layer], constant) * norm[...]
        line = pl.ds(2 * layers + layer, 1)
        limit, _ = sides("gx", rest_even[line, :], rest_odd[line, :])
        first = limit - nonlocal_strain[:REACH]
        others = threshold[layer] - nonlocal_strain[REACH:]
        kept_before[layer] = ratio(first)
        kept[layer] = ratio(others)
        moved = jnp.concatenate([first, others], axis=0)
        moved = pltpu.roll(moved, layer * REACH, 1) if layer else moved
        pltpu.store(edge_low, moved, mask=slots == layer)
        pltpu.store(edge_high, moved, mask=slots == (layer - 1) % (cols // REACH))


def final_kernel(stress, strain, plastic, inner, inner_before, edge_low, edge_high, norm_low, norm_high,
                 col_even, col_odd, last_even, last_odd, rest_even, rest_odd, norm_before, own_cols,
                 plastic_out, damage_out, force_out, columns, damage_s, force_s, copy_sem, sems):
    layers, rows, cols = stress.shape
    whole = pltpu.make_async_copy(plastic, plastic_out, copy_sem)
    whole.start()

    from_low, _ = sides("gy", last_even[...], last_odd[...])
    folded = from_low[REACH : REACH + rows // 4]
    pieces = [from_low[REACH + rows // 4 :], folded]
    for part in range(1, 4):
        pieces.append(pltpu.roll(folded, cols - part * 2 * layers, 1))
    column = jnp.concatenate(pieces, axis=0)
    kept = ratio(column - own_cols[...] * norm_before[...])
    columns[...] = kept * pltpu.roll(column, cols - layers, 1)

    def copies(layer):
        return (
            pltpu.make_async_copy(damage_s.at[layer], damage_out.at[layer], sems.at[0, layer]),
            pltpu.make_async_copy(force_s.at[0, layer], force_out.at[0, layer], sems.at[1, layer]),
            pltpu.make_async_copy(force_s.at[1, layer], force_out.at[1, layer], sems.at[2, layer]),
        )

    def layer_step(layer):
        lanes = lane_ids((REACH, cols))
        top = lax.broadcasted_iota(jnp.int32, (REACH, cols), 0) == 0
        above_sum = above_diff = None
        for block in range(rows // REACH + 1):
            extended = pl.ds(block * REACH, REACH)
            part = pl.ds((block - 1) * REACH if block else 0, REACH)
            received = (col_even, col_odd) if block else (last_even, last_odd)
            packed = edge_ratios(
                (edge_low, edge_high), received, (norm_low, norm_high), part, extended
            )
            at = (layer, part, slice(None))
            if block:
                rest = (stress[at] + strain[at]) - plastic[at]
            else:
                line = pl.ds(layers + layer, 1)
                rest, _ = sides("gx", rest_even[line, :], rest_odd[line, :])
            kept = with_edges(inner[at] if block else inner_before[layer], layer, *packed)
            value = kept * rest
            left = jnp.where(
                lanes == 0,
                pltpu.roll(columns[extended, :], (cols - layer) % cols, 1),
                pltpu.roll(value, 1, 1),
            )
            both = pltpu.roll(left + value, 1, 0)
            diff = pltpu.roll(left - value, 1, 0)
            if block:
                damage_s[at] = 1.0 - kept
                force_s[(0, *at)] = 0.5 * (jnp.where(top, above_sum, both) - (left + value))
                force_s[(1, *at)] = 0.5 * (jnp.where(top, above_diff, diff) + (left - value))
            above_sum, above_diff = both, diff

    def step(index, carry):
        for near in range(2):
            layer_step(2 * index + near)
        for near in range(2):
            for copy in copies(2 * index + near):
                copy.start()
        return carry

    lax.fori_loop(0, layers // 2, step, 0)

    def drain(layer, carry):
        for copy in copies(layer):
            copy.wait()
        return carry

    lax.fori_loop(0, layers, drain, 0)
    whole.wait()


def call(kernel, outs, scratch, nanoseconds, operands, spaces=None, outs_space=pltpu.VMEM, limit=VMEM_BYTES):
    spaces = spaces or [pltpu.VMEM] * len(operands)
    shapes = [out if isinstance(out, jax.ShapeDtypeStruct) else jax.ShapeDtypeStruct(out, jnp.float32)
              for out in outs]
    return pl.pallas_call(
        kernel,
        out_shape=shapes,
        in_specs=[pl.BlockSpec(memory_space=space) for space in spaces],
        out_specs=[pl.BlockSpec(memory_space=outs_space)] * len(outs),
        scratch_shapes=[pltpu.VMEM(s, jnp.float32) if isinstance(s, tuple) else s for s in scratch],
        compiler_params=pltpu.CompilerParams(vmem_limit_bytes=limit),
        cost_estimate=pl.CostEstimate(
            flops=nanoseconds * 1_000_000, bytes_accessed=nanoseconds * 1000, transcendentals=0
        ),
    )(*operands)


def exchange(axis, other, even, odd):
    names = ("gx", "gy")
    count, across = lax.axis_size(axis), lax.axis_size(other)
    stride = {"gx": lax.axis_size("gy"), "gy": 1}
    results = []
    for start, value in ((0, even), (1, odd)):
        pairs = []
        for place in range(count):
            partner = place + 1 if (place - start) % 2 == 0 else place - 1
            for line in range(across):
                target = (partner, line)
                if not 0 <= partner < count:
                    target = (place, line ^ 1 if line ^ 1 < across else line)
                pairs.append((
                    place * stride[axis] + line * stride[other],
                    target[0] * stride[axis] + target[1] * stride[other],
                ))
        results.append(lax.ppermute(value, names, pairs))
    return results


def inverse_weights(axis, places, length):
    extent = length * lax.axis_size(axis)
    places = places + lax.axis_index(axis) * length
    total = jnp.zeros(places.shape, jnp.float32)
    for offset in range(-REACH, REACH + 1):
        inside = (places + offset >= 0) & (places + offset < extent)
        total = total + jnp.where(inside, tap(offset), 0.0)
    return 1.0 / jnp.maximum(total, tap(REACH))


def matrices(layers, rows, cols):
    depth = depth_matrix(layers)
    up, down = band(REACH, REACH, REACH), band(REACH, REACH, -REACH)
    same = np.eye(layers)
    below = np.kron(same, up)
    near = np.concatenate([np.zeros((REACH, REACH)), down], axis=1)
    line = band(1, 2 * REACH, 1 - 2 * REACH)
    above = np.concatenate([np.kron(same, near), np.kron(same, line)], axis=0)
    rows_band = np.concatenate([np.zeros((REACH - 1, rows)), band(1, rows, 1), band(rows, rows)])
    slots = cols // REACH
    low, high, ahead = np.zeros((cols, 2 * cols)), np.zeros((cols, 2 * cols)), np.zeros((cols, cols))
    for source in range(layers):
        own = slice(source * REACH, (source + 1) * REACH)
        first = (source - 1) % slots * REACH
        other = slice(first, first + REACH)
        for layer in range(layers):
            weight = depth[layer, source]
            first = (layer - 1) % slots * REACH
            low[own, first : first + REACH] = weight * up.T
            high[other, layer * REACH : (layer + 1) * REACH] = weight * down.T
            low[own, cols + layer] = [weight * tap(j + 1) for j in range(REACH)]
            high[other, cols + layer] = [weight * tap(REACH - 1 - j) for j in range(REACH)]
            ahead[((source - 2) % slots) * REACH + REACH - 1, layer] = weight * tap(REACH)
    constants = (below, above, rows_band, band(cols, cols), low, high, ahead)
    return depth, [jnp.asarray(matrix, jnp.float32) for matrix in constants]


def local(trial_stress, old_strain, yield_mask, newton_count, damage_threshold):
    layers, rows, cols = trial_stress.shape
    assert layers * REACH == cols == rows and layers % 2 == 0
    total, strip = rows + REACH, layers * REACH
    depth, constants = matrices(layers, rows, cols)
    below, above, rows_band, cols_band, *columns = constants

    whole, wide, top = (layers, rows, cols), (layers, total, cols), (layers, REACH, cols)
    sent_rows = (strip + 3 * layers, cols)
    sent_cols = (total + rows // 4 + REACH, cols)
    spare = (3 * layers, cols)
    packed, packed_two = (total, cols), (total, 2 * cols)

    sources = (trial_stress, old_strain, yield_mask, newton_count, damage_threshold)
    row_even, row_odd, norm, norm_low, norm_high, norm_last, norm_before, col_even, col_odd, rest, *inputs = call(
        first_edge_kernel,
        [(strip, cols)] * 2 + [packed] * 5 + [(rows, cols)] * 2 + [spare]
        + [jax.ShapeDtypeStruct(whole, source.dtype) for source in sources],
        [(strip, cols), pltpu.SemaphoreType.DMA((3, len(sources)))], 2500,
        sources, [pltpu.HBM] * len(sources), limit=FIRST_VMEM_BYTES,
    )
    stress, strain, _, _, threshold = inputs
    kept, edge_low, edge_high, norms = stress, norm_low, norm_high, (norm_low, norm_high)
    rest_even = rest_odd = rest
    for outer_no in range(OUTER):
        last = outer_no == OUTER - 1
        if outer_no:
            row_even, row_odd = call(
                edge_kernel, [sent_rows] * 2,
                [(strip, cols), (2 * strip, cols), (2 * layers, cols)], 800,
                (*inputs, kept, kept_before, edge_low, edge_high, *norms, col_even, col_odd,
                 below, above),
            )
        if not last:
            row_even, row_odd = row_even[:strip], row_odd[:strip]
        row_even, row_odd = exchange("gx", "gy", row_even, row_odd)
        if last:
            rest_even, rest_odd = row_even[strip:], row_odd[strip:]
            row_even, row_odd = row_even[:strip], row_odd[:strip]
        turn = jnp.full((1,), outer_no, jnp.int32)
        across, low_cols, high_cols, plastic = call(
            main_kernel, [wide, packed_two, packed_two, whole],
            [packed, packed, packed, packed], 4500,
            (turn, *inputs, kept, edge_low, edge_high, *norms, col_even, col_odd, norm_last,
             rows_band, *columns),
            [pltpu.SMEM] + [pltpu.VMEM] * 17,
        )
        col_even, col_odd, own_cols = call(
            corner_kernel, [sent_cols, sent_cols, packed], [], 400,
            (row_even, row_odd, rest_even, rest_odd, low_cols, high_cols, norm_last, plastic, *columns),
        )
        if not last:
            col_even, col_odd = col_even[:rows], col_odd[:rows]
        col_even, col_odd = exchange("gy", "gx", col_even, col_odd)
        if last:
            last_even, last_odd = col_even[rows:], col_odd[rows:]
            col_even, col_odd = col_even[:rows], col_odd[:rows]
        kept, kept_before, edge_low, edge_high = call(
            functools.partial(column_kernel, depth), [whole, top, packed, packed], [wide], 1800,
            (across, row_even, row_odd, rest_even, rest_odd, threshold, norm, cols_band, own_cols),
        )
    return tuple(call(
        final_kernel, [whole, whole, (2, *whole)],
        [packed, whole, (2, *whole), pltpu.SemaphoreType.DMA(()), pltpu.SemaphoreType.DMA((3, layers))],
        3000,
        (stress, strain, plastic, kept, kept_before, edge_low, edge_high, *norms, col_even, col_odd,
         last_even, last_odd, rest_even, rest_odd, norm_before, own_cols),
        outs_space=pltpu.HBM,
    ))


def solution(mesh):
    split_in = P(None, "gx", "gy")
    return jax.shard_map(
        local,
        mesh=mesh,
        in_specs=(split_in,) * 5,
        out_specs=(split_in, split_in, P(None, None, "gx", "gy")),
        check_vma=False,
    )
```

```python
import functools
import math

import jax
import jax.numpy as jnp
import numpy as np
from jax import lax
from jax.experimental import pallas as pl
from jax.experimental.pallas import tpu as pltpu
from jax.sharding import PartitionSpec as P

OUTER = 3
REACH = 8
RATE = math.log2(math.e) / 0.3
HALF_LN2 = 0.5 * math.log(2.0)
VMEM_BYTES = 24 * 1024 * 1024
FIRST_VMEM_BYTES = 48 * 1024 * 1024


def tap(offset):
    return math.exp(-(offset**2) / 32.0) if abs(offset) <= REACH else 0.0


def band(rows, cols, shift=0):
    return np.array([[tap(c - r + shift) for c in range(cols)] for r in range(rows)])


def depth_matrix(layers):
    weights = band(layers, layers)
    return weights / weights.sum(axis=1, keepdims=True)


def split(value):
    high = value.astype(jnp.bfloat16)
    low = (value - high.astype(jnp.float32)).astype(jnp.bfloat16)
    return high, low


def left_constant(matrix):
    high, low = split(matrix)
    return jnp.concatenate(
        [jnp.concatenate([high, high], axis=1), jnp.concatenate([low, low], axis=1)], axis=0
    )


def right_constant(matrix):
    both = jnp.concatenate(split(matrix), axis=1)
    return jnp.concatenate([both, both], axis=0)


def left_product(constant, value):
    rows = constant.shape[0] // 2
    halves = jnp.concatenate(split(value), axis=0)
    both = jnp.dot(constant, halves, preferred_element_type=jnp.float32)
    return both[:rows] + both[rows:]


def right_product(value, constant):
    cols = constant.shape[1] // 2
    halves = jnp.concatenate(split(value), axis=1)
    both = jnp.dot(halves, constant, preferred_element_type=jnp.float32)
    return both[:, :cols] + both[:, cols:]


def newton(stress, strain, yields, count, kept):
    top = (stress + strain) - (0.875 + 0.875 * kept)
    shift = 2.0 * top - HALF_LN2
    state = 2.0 * (top - strain)
    drop = 0.1 + 0.1 * kept
    for sweep_no in range(1, 7):
        update = state * (0.8 - 0.2 * jnp.tanh(shift - state)) - drop
        state = update if sweep_no <= 3 else jnp.where(count >= sweep_no, update, state)
    return jnp.where(yields > 0, top - 0.5 * state, strain)


def depth_smooth(layers, matrix):
    count = len(layers)
    half = count // 2
    sums = [layers[k] + layers[count - 1 - k] for k in range(half)]
    diffs = [layers[k] - layers[count - 1 - k] for k in range(half)]
    out = [None] * count
    for row in range(half):
        even = odd = None
        for k in range(half):
            near, far = matrix[row, k], matrix[row, count - 1 - k]
            plus, minus = float(0.5 * (near + far)), float(0.5 * (near - far))
            if plus == 0.0 and minus == 0.0:
                continue
            even = sums[k] * plus if even is None else even + sums[k] * plus
            odd = diffs[k] * minus if odd is None else odd + diffs[k] * minus
        out[row] = even + odd
        out[count - 1 - row] = even - odd
    return out


def lane_ids(shape):
    return lax.broadcasted_iota(jnp.int32, shape, len(shape) - 1)


def on_even(axis):
    return lax.axis_index(axis) % 2 == 0


def sides(axis, even, odd):
    return jnp.where(on_even(axis), odd, even), jnp.where(on_even(axis), even, odd)


def send(axis, low, high, even_ref, odd_ref):
    place = lax.axis_index(axis)
    low = jnp.where(place == 0, 0.0, low)
    high = jnp.where(place == lax.axis_size(axis) - 1, 0.0, high)
    even_ref[...] = jnp.where(on_even(axis), high, low)
    odd_ref[...] = jnp.where(on_even(axis), low, high)


def layer_slots(shape):
    return lane_ids(shape) >> (REACH.bit_length() - 1)


def ratio(limit):
    return jnp.exp2(jnp.minimum(limit, 0.0) * RATE)


def edge_ratios(edges, received, norms, part, extended):
    both = sides("gy", *(ref[part, :] for ref in received))
    return [
        ratio(edge[extended, :] - value * norm[extended, :])
        for edge, value, norm in zip(edges, both, norms)
    ]


def with_edges(inner, layer, low, high):
    cols = inner.shape[1]
    slots = layer_slots(inner.shape)
    packed = jnp.where(slots == layer, low, high)
    shift = (cols - layer * REACH) % cols
    moved = packed if isinstance(layer, int) and layer == 0 else pltpu.roll(packed, shift, 1)
    return jnp.where((slots == 0) | (slots == cols // REACH - 1), moved, inner)


def first_edge_kernel(*refs):
    sources, refs = refs[:5], refs[5:]
    even_ref, odd_ref, norm, norm_low, norm_high, norm_last, norm_before, _, _, _, *refs = refs
    targets, (block, sems) = refs[:5], refs[5:]
    stress, strain, yields, count, _ = targets
    layers, rows, cols = stress.shape
    parts = (pl.ds(0, REACH), pl.ds(rows - REACH, REACH), pl.ds(REACH, rows - 2 * REACH))
    copies = []
    for side, part in enumerate(parts):
        for index, (source, target) in enumerate(zip(sources, targets)):
            copies.append(
                pltpu.make_async_copy(
                    source.at[:, part, :], target.at[:, part, :], sems.at[side, index]
                )
            )
            copies[-1].start()
    total = rows + REACH
    ids = lax.broadcasted_iota(jnp.int32, (total, cols), 0)
    down = inverse_weights("gx", ids - REACH, rows)
    lanes = lane_ids((REACH, cols))
    within = lanes & (REACH - 1)
    places = (lanes, within, within + (cols - REACH), 0 * lanes + (cols - 1), 0 * lanes - 1)
    for ref, place in zip((norm, norm_low, norm_high, norm_last, norm_before), places):
        ref[...] = down * inverse_weights("gy", place, cols)[:1]
    square = (layers * REACH, layers * REACH)
    line, lane = lax.broadcasted_iota(jnp.int32, square, 0), lane_ids(square)
    steps = (lane & (REACH - 1)) - (line & (REACH - 1))
    band_part = jnp.zeros(square, jnp.float32)
    for step in range(REACH):
        band_part = jnp.where(abs(steps) == step, tap(REACH - step), band_part)
    band_part = jnp.where((line ^ lane) < REACH, band_part, 0.0)
    sent = []
    for side, matrix in enumerate(
        (jnp.where(steps <= 0, band_part, 0.0), jnp.where(steps >= 0, band_part, 0.0))
    ):
        for copy in copies[side * 5 : side * 5 + 5]:
            copy.wait()
        for layer in range(layers):
            at = (layer, parts[side], slice(None))
            block[pl.ds(layer * REACH, REACH), :] = newton(
                stress[at], strain[at], yields[at], count[at], jnp.ones((REACH, cols), jnp.float32)
            )
        product = left_product(left_constant(matrix), block[...])
        sent.append(jnp.concatenate([product, product[:REACH]], axis=0))
    send("gx", *sent, even_ref, odd_ref)
    for copy in copies[10:]:
        copy.wait()


def edge_kernel(stress, strain, yields, count, threshold, kept, _, edge_low, edge_high, norm_low,
                norm_high, col_even, col_odd, below, above,
                even_ref, odd_ref, low_block, high_block, rest):
    layers, rows, cols = stress.shape
    starts = (0, rows - 2 * REACH, rows - REACH)
    packed = [
        edge_ratios(
            (edge_low, edge_high), (col_even, col_odd), (norm_low, norm_high),
            pl.ds(first_row, REACH), pl.ds(first_row + REACH, REACH),
        )
        for first_row in starts
    ]

    def layer_step(layer):
        for index, first_row in enumerate(starts):
            at = (layer, pl.ds(first_row, REACH), slice(None))
            ratios = with_edges(kept[at], layer, *packed[index])
            value = newton(stress[at], strain[at], yields[at], count[at], ratios)
            if index == 0:
                low_block[pl.ds(layer * REACH, REACH), :] = value
            else:
                high_block[pl.ds((2 * layer + index - 1) * REACH, REACH), :] = value
            if index == 2:
                left = (stress[at] + strain[at]) - value
                rest[pl.ds(layer, 1), :] = left[REACH - 1 :]
                rest[pl.ds(layers + layer, 1), :] = threshold[at][REACH - 1 :]

    for layer in range(layers):
        layer_step(layer)
    low = left_product(left_constant(below[...]), low_block[...])
    high = left_product(left_constant(above[...]), high_block[...])
    extra = jnp.zeros((even_ref.shape[0] - low.shape[0], cols), jnp.float32)
    send(
        "gx", jnp.concatenate([low, extra], axis=0), jnp.concatenate([high, rest[...]], axis=0),
        even_ref, odd_ref,
    )


def main_kernel(turn, stress, strain, yields, count, threshold, kept, edge_low, edge_high, norm_low,
                norm_high, col_even, col_odd, norm_last, fixed, band_ref, low_ref, high_ref, next_ref,
                across, low_cols, high_cols, plastic, fixed_out,
                pack_low, pack_high, pack_next, pack_last):
    layers, rows, cols = stress.shape
    total = rows + REACH
    step_rows = 4 * REACH
    lanes = lane_ids((REACH, cols))
    pack_last[pl.ds(0, REACH), :] = jnp.zeros((REACH, cols), jnp.float32)

    def newton_blocks(index, fresh):
        for near in range(step_rows // REACH):
            first = index * step_rows + near * REACH
            part = pl.ds(pl.multiple_of(first, REACH), REACH)
            extended = pl.ds(pl.multiple_of(first + REACH, REACH), REACH)
            if not fresh:
                packed = edge_ratios(
                    (edge_low, edge_high), (col_even, col_odd), (norm_low, norm_high), part, extended
                )
            for layer in range(layers):
                at = (layer, part, slice(None))
                if fresh:
                    ratios = jnp.ones((REACH, cols), jnp.float32)
                else:
                    ratios = with_edges(kept[at], layer, *packed)
                value = newton(stress[at], strain[at], yields[at], count[at], ratios)
                plastic[at] = value
                lane = layers + layer
                if fresh:
                    both = stress[at] + strain[at]
                    pltpu.store(fixed_out.at[extended, :], pltpu.roll(both, lane + 1, 1), mask=lanes == lane)
                    turned = pltpu.roll(threshold[at], layer + 1, 1)
                    pltpu.store(fixed_out.at[extended, :], turned, mask=lanes == layer)
                else:
                    pltpu.store(pack_last.at[extended, :], pltpu.roll(value, lane + 1, 1), mask=lanes == lane)

    @pl.when(turn[0] == 0)
    def _():
        fixed_out[...] = jnp.zeros_like(fixed_out)
        lax.fori_loop(0, rows // step_rows, lambda index, _: newton_blocks(index, True), None)

    @pl.when(turn[0] > 0)
    def _():
        fixed_out[...] = fixed[...]
        lax.fori_loop(0, rows // step_rows, lambda index, _: newton_blocks(index, False), None)

    constant = left_constant(band_ref[...])
    slots = layer_slots((total, cols))
    for layer in range(0, layers, 2):
        pair = jnp.concatenate([plastic[layer], plastic[layer + 1]], axis=1)
        result = left_product(constant, pair)
        for inner in range(2):
            value = result[:, inner * cols : (inner + 1) * cols]
            across[layer + inner] = value
            moved = pltpu.roll(value, (layer + inner) * REACH, 1) if layer + inner else value
            for behind, ref in enumerate((pack_low, pack_high, pack_next)):
                mask = slots == (layer + inner - behind) % (cols // REACH)
                pltpu.store(ref, moved, mask=mask)

    low_cols[...] = right_product(pack_low[...], right_constant(low_ref[...]))
    high = right_product(pack_high[...], right_constant(high_ref[...]))
    behind = right_product(pack_next[...], right_constant(next_ref[...]))
    high_cols[:, :cols] = high[:, :cols]

    drop = (high[:, cols:] + behind) * norm_last[...]
    first_lanes = lane_ids((total, cols)) < layers
    high_cols[:, cols:] = fixed_out[...] - jnp.where(first_lanes, drop, pack_last[...])


def pack_edges(values):
    cols = values[0].shape[1]
    count = cols // REACH
    slots = layer_slots(values[0].shape)
    low = high = ahead = jnp.zeros_like(values[0])
    for layer, value in enumerate(values):
        moved = pltpu.roll(value, layer * REACH, 1) if layer else value
        low = jnp.where(slots == layer, moved, low)
        high = jnp.where(slots == (layer - 1) % count, moved, high)
        ahead = jnp.where(slots == (layer - 2) % count, moved, ahead)
    return low, high, ahead


def corner_kernel(row_even, row_odd, rest_even, rest_odd, low_cols, high_cols, norm_last,
                  _, __, low_ref, high_ref, next_ref, even_ref, odd_ref, own_ref):
    cols = low_ref.shape[0]
    total = low_cols.shape[0]
    layers = (total - REACH) // REACH
    strip = layers * REACH
    from_low, from_high = sides("gx", row_even[...], row_odd[...])
    rest, _ = sides("gx", rest_even[...], rest_odd[...])
    partial, kept, limit = rest[:layers], rest[layers : 2 * layers], rest[2 * layers :]
    before = [jnp.broadcast_to(partial[layer : layer + 1], (REACH, cols)) for layer in range(layers)]
    packs = [pack_edges(before)] + [
        pack_edges([block[layer * REACH : (layer + 1) * REACH] for layer in range(layers)])
        for block in (from_low, from_high)
    ]
    low, high, ahead = (jnp.concatenate(group, axis=0) for group in zip(*packs))
    low_add = right_product(low, right_constant(low_ref[...]))
    high_add = right_product(high, right_constant(high_ref[...]))
    behind_add = right_product(ahead, right_constant(next_ref[...]))

    lanes = lane_ids((layers, cols))
    level = lax.broadcasted_iota(jnp.int32, (layers, cols), 0)
    corner_limit = jnp.where(lanes == level, limit[:, cols - 1 :], 0.0)
    corner_kept = jnp.where(lanes == layers + level, kept[:, cols - 1 :], 0.0)
    corner = jnp.sum(corner_limit + corner_kept, axis=0, keepdims=True)

    def place(base, add):
        return jnp.concatenate(
            [base[: 2 * REACH] + add[: 2 * REACH], base[2 * REACH : total - REACH],
             base[total - REACH :] + add[2 * REACH :]],
            axis=0,
        )

    low_all = place(low_cols[...], low_add)
    high_all = place(high_cols[:, :cols], high_add[:, :cols])
    last = norm_last[...]
    behind = high_add[:, cols:] + behind_add
    edges = jnp.concatenate([last[: 2 * REACH], last[total - REACH :]], axis=0)
    lanes = lane_ids(behind.shape)
    drop = jnp.where(lanes < layers, behind * edges, 0.0)
    column = place(high_cols[:, cols:], -drop)
    first = column[:REACH] + corner
    main = column[REACH:]
    quarter = strip // 4
    lanes = lane_ids((quarter, cols))
    folded = main[:quarter]
    for part in range(1, 4):
        moved = pltpu.roll(main[part * quarter : (part + 1) * quarter], part * 2 * layers, 1)
        folded = jnp.where(lanes // (2 * layers) == part, moved, folded)
    spare = jnp.zeros((REACH, cols), jnp.float32)
    extra = jnp.zeros((quarter + REACH, cols), jnp.float32)
    send(
        "gy", jnp.concatenate([low_all[REACH:, :cols], low_all[:REACH, :cols], extra, spare], axis=0),
        jnp.concatenate([high_all[REACH:], high_all[:REACH], folded, first, spare], axis=0),
        even_ref, odd_ref,
    )
    own_ref[...] = low_all[:, cols:]


def column_kernel(depth, across, row_even, row_odd, rest_even, rest_odd, threshold, norm, band_ref, _,
                  kept, kept_before, edge_low, edge_high, deep):
    layers, total, cols = across.shape

    def depth_sums(part, values):
        for layer, value in enumerate(depth_smooth(values, depth)):
            deep[layer, part, :] = value

    def step(index, carry):
        for inner in range(2):
            part = pl.ds(pl.multiple_of((2 * index + inner + 2) * REACH, REACH), REACH)
            depth_sums(part, [across[layer, part, :] for layer in range(layers)])
        return carry

    lax.fori_loop(0, (total // REACH - 3) // 2, step, 0)
    for first_row in (0, REACH, total - REACH):
        part = pl.ds(first_row, REACH)
        values = []
        for layer in range(layers):
            if first_row:
                line = pl.ds(layer * REACH, REACH)
                both = sides("gx", row_even[line, :], row_odd[line, :])
            else:
                both = sides("gx", rest_even[pl.ds(layer, 1), :], rest_odd[pl.ds(layer, 1), :])
            values.append(across[layer, part, :] + both[first_row > REACH])
        depth_sums(part, values)

    constant = right_constant(band_ref[...])
    slots = layer_slots((total, cols))
    for layer in range(layers):
        nonlocal_strain = right_product(deep[layer], constant) * norm[...]
        line = pl.ds(2 * layers + layer, 1)
        limit, _ = sides("gx", rest_even[line, :], rest_odd[line, :])
        first = limit - nonlocal_strain[:REACH]
        others = threshold[layer] - nonlocal_strain[REACH:]
        kept_before[layer] = ratio(first)
        kept[layer] = ratio(others)
        moved = jnp.concatenate([first, others], axis=0)
        moved = pltpu.roll(moved, layer * REACH, 1) if layer else moved
        pltpu.store(edge_low, moved, mask=slots == layer)
        pltpu.store(edge_high, moved, mask=slots == (layer - 1) % (cols // REACH))


def final_kernel(stress, strain, plastic, inner, inner_before, edge_low, edge_high, norm_low, norm_high,
                 col_even, col_odd, last_even, last_odd, rest_even, rest_odd, norm_before, own_cols,
                 plastic_out, damage_out, force_out, columns, damage_s, force_s, sums, diffs,
                 copy_sem, sems):
    layers, rows, cols = stress.shape
    whole = pltpu.make_async_copy(plastic, plastic_out, copy_sem)
    whole.start()
    from_low, _ = sides("gy", last_even[...], last_odd[...])
    folded = from_low[REACH : REACH + rows // 4]
    pieces = [from_low[REACH + rows // 4 :], folded]
    for part in range(1, 4):
        pieces.append(pltpu.roll(folded, cols - part * 2 * layers, 1))
    column = jnp.concatenate(pieces, axis=0)
    kept = ratio(column - own_cols[...] * norm_before[...])
    columns[...] = (0.5 * kept) * pltpu.roll(column, cols - layers, 1)

    def copies(layer):
        return (
            pltpu.make_async_copy(damage_s.at[layer], damage_out.at[layer], sems.at[0, layer]),
            pltpu.make_async_copy(force_s.at[0, layer], force_out.at[0, layer], sems.at[1, layer]),
            pltpu.make_async_copy(force_s.at[1, layer], force_out.at[1, layer], sems.at[2, layer]),
        )

    def layer_step(layer, near):
        lanes = lane_ids((REACH, cols))
        for block in range(rows // REACH + 1):
            extended = pl.ds(block * REACH, REACH)
            part = pl.ds((block - 1) * REACH if block else 0, REACH)
            received = (col_even, col_odd) if block else (last_even, last_odd)
            packed = edge_ratios(
                (edge_low, edge_high), received, (norm_low, norm_high), part, extended
            )
            at = (layer, part, slice(None))
            if block:
                rest = (stress[at] + strain[at]) - plastic[at]
            else:
                line = pl.ds(layers + layer, 1)
                rest, _ = sides("gx", rest_even[line, :], rest_odd[line, :])
            kept = with_edges(inner[at] if block else inner_before[layer], layer, *packed)
            value = (0.5 * kept) * rest
            left = jnp.where(
                lanes == 0,
                pltpu.roll(columns[extended, :], (cols - layer) % cols, 1),
                pltpu.roll(value, 1, 1),
            )
            both, diff = left + value, left - value
            sums[near, extended, :] = both
            diffs[near, extended, :] = diff
            if block:
                behind = pl.ds(block * REACH - 1, REACH)
                damage_s[at] = 1.0 - kept
                force_s[(0, *at)] = sums[near, behind, :] - both
                force_s[(1, *at)] = diffs[near, behind, :] + diff

    def step(index, carry):
        for near in range(2):
            layer_step(2 * index + near, near)
        for near in range(2):
            for copy in copies(2 * index + near):
                copy.start()
        return carry

    lax.fori_loop(0, layers // 2, step, 0)

    def drain(layer, carry):
        for copy in copies(layer):
            copy.wait()
        return carry

    lax.fori_loop(0, layers, drain, 0)
    whole.wait()


def call(kernel, outs, scratch, nanoseconds, operands, spaces=None, outs_space=pltpu.VMEM, limit=VMEM_BYTES):
    spaces = spaces or [pltpu.VMEM] * len(operands)
    shapes = [out if isinstance(out, jax.ShapeDtypeStruct) else jax.ShapeDtypeStruct(out, jnp.float32)
              for out in outs]
    return pl.pallas_call(
        kernel,
        out_shape=shapes,
        in_specs=[pl.BlockSpec(memory_space=space) for space in spaces],
        out_specs=[pl.BlockSpec(memory_space=outs_space)] * len(outs),
        scratch_shapes=[pltpu.VMEM(s, jnp.float32) if isinstance(s, tuple) else s for s in scratch],
        compiler_params=pltpu.CompilerParams(vmem_limit_bytes=limit),
        cost_estimate=pl.CostEstimate(
            flops=nanoseconds * 1_000_000, bytes_accessed=nanoseconds * 1000, transcendentals=0
        ),
    )(*operands)


def exchange(axis, other, even, odd):
    names = ("gx", "gy")
    count, across = lax.axis_size(axis), lax.axis_size(other)
    stride = {"gx": lax.axis_size("gy"), "gy": 1}
    results = []
    for start, value in ((0, even), (1, odd)):
        pairs = []
        for place in range(count):
            partner = place + 1 if (place - start) % 2 == 0 else place - 1
            for line in range(across):
                target = (partner, line)
                if not 0 <= partner < count:
                    target = (place, line ^ 1 if line ^ 1 < across else line)
                pairs.append((
                    place * stride[axis] + line * stride[other],
                    target[0] * stride[axis] + target[1] * stride[other],
                ))
        results.append(lax.ppermute(value, names, pairs))
    return results


def inverse_weights(axis, places, length):
    extent = length * lax.axis_size(axis)
    places = places + lax.axis_index(axis) * length
    total = jnp.zeros(places.shape, jnp.float32)
    for offset in range(-REACH, REACH + 1):
        inside = (places + offset >= 0) & (places + offset < extent)
        total = total + jnp.where(inside, tap(offset), 0.0)
    return 1.0 / jnp.maximum(total, tap(REACH))


def matrices(layers, rows, cols):
    depth = depth_matrix(layers)
    up, down = band(REACH, REACH, REACH), band(REACH, REACH, -REACH)
    same = np.eye(layers)
    below = np.kron(same, up)
    near = np.concatenate([np.zeros((REACH, REACH)), down], axis=1)
    line = band(1, 2 * REACH, 1 - 2 * REACH)
    above = np.concatenate([np.kron(same, near), np.kron(same, line)], axis=0)
    rows_band = np.concatenate([np.zeros((REACH - 1, rows)), band(1, rows, 1), band(rows, rows)])
    slots = cols // REACH
    low, high, ahead = np.zeros((cols, 2 * cols)), np.zeros((cols, 2 * cols)), np.zeros((cols, cols))
    for source in range(layers):
        own = slice(source * REACH, (source + 1) * REACH)
        first = (source - 1) % slots * REACH
        other = slice(first, first + REACH)
        for layer in range(layers):
            weight = depth[layer, source]
            first = (layer - 1) % slots * REACH
            low[own, first : first + REACH] = weight * up.T
            high[other, layer * REACH : (layer + 1) * REACH] = weight * down.T
            low[own, cols + layer] = [weight * tap(j + 1) for j in range(REACH)]
            high[other, cols + layer] = [weight * tap(REACH - 1 - j) for j in range(REACH)]
            ahead[((source - 2) % slots) * REACH + REACH - 1, layer] = weight * tap(REACH)
    constants = (below, above, rows_band, band(cols, cols), low, high, ahead)
    return depth, [jnp.asarray(matrix, jnp.float32) for matrix in constants]


def local(trial_stress, old_strain, yield_mask, newton_count, damage_threshold):
    layers, rows, cols = trial_stress.shape
    assert layers * REACH == cols == rows and layers % 2 == 0
    total, strip = rows + REACH, layers * REACH
    depth, constants = matrices(layers, rows, cols)
    below, above, rows_band, cols_band, *columns = constants

    whole, wide, top = (layers, rows, cols), (layers, total, cols), (layers, REACH, cols)
    sent_rows = (strip + 3 * layers, cols)
    sent_cols = (total + rows // 4 + 2 * REACH, cols)
    last_cols = total + rows // 4 + REACH
    spare = (3 * layers, cols)
    packed, packed_two = (total, cols), (total, 2 * cols)

    sources = (trial_stress, old_strain, yield_mask, newton_count, damage_threshold)
    row_even, row_odd, norm, norm_low, norm_high, norm_last, norm_before, col_even, col_odd, rest, *inputs = call(
        first_edge_kernel,
        [(strip + REACH, cols)] * 2 + [packed] * 5 + [(rows, cols)] * 2 + [spare]
        + [jax.ShapeDtypeStruct(whole, source.dtype) for source in sources],
        [(strip, cols), pltpu.SemaphoreType.DMA((3, len(sources)))], 2500,
        sources, [pltpu.HBM] * len(sources), limit=FIRST_VMEM_BYTES,
    )
    stress, strain, _, _, threshold = inputs
    kept, edge_low, edge_high, norms = stress, norm_low, norm_high, (norm_low, norm_high)
    rest_even = rest_odd = rest
    fixed = norm_last
    for outer_no in range(OUTER):
        last = outer_no == OUTER - 1
        if outer_no:
            row_even, row_odd = call(
                edge_kernel, [sent_rows] * 2,
                [(strip, cols), (2 * strip, cols), (2 * layers, cols)], 800,
                (*inputs, kept, kept_before, edge_low, edge_high, *norms, col_even, col_odd,
                 below, above),
            )
        if not last:
            row_even, row_odd = row_even[:strip], row_odd[:strip]
        row_even, row_odd = exchange("gx", "gy", row_even, row_odd)
        if last:
            rest_even, rest_odd = row_even[strip:], row_odd[strip:]
            row_even, row_odd = row_even[:strip], row_odd[:strip]
        turn = jnp.full((1,), outer_no, jnp.int32)
        across, low_cols, high_cols, plastic, fixed = call(
            main_kernel, [wide, packed_two, packed_two, whole, packed],
            [packed, packed, packed, packed], 4500,
            (turn, *inputs, kept, edge_low, edge_high, *norms, col_even, col_odd, norm_last,
             fixed, rows_band, *columns),
            [pltpu.SMEM] + [pltpu.VMEM] * 18,
        )
        col_even, col_odd, own_cols = call(
            corner_kernel, [sent_cols, sent_cols, packed], [], 400,
            (row_even, row_odd, rest_even, rest_odd, low_cols, high_cols, norm_last, plastic, fixed, *columns),
        )
        used = last_cols if last else rows
        col_even, col_odd = col_even[:used], col_odd[:used]
        col_even, col_odd = exchange("gy", "gx", col_even, col_odd)
        if last:
            last_even, last_odd = col_even[rows:], col_odd[rows:]
            col_even, col_odd = col_even[:rows], col_odd[:rows]
        kept, kept_before, edge_low, edge_high = call(
            functools.partial(column_kernel, depth), [whole, top, packed, packed], [wide], 1800,
            (across, row_even, row_odd, rest_even, rest_odd, threshold, norm, cols_band, own_cols),
        )
    return tuple(call(
        final_kernel, [whole, whole, (2, *whole)],
        [packed, whole, (2, *whole), (2, *packed), (2, *packed),
         pltpu.SemaphoreType.DMA(()), pltpu.SemaphoreType.DMA((3, layers))],
        3000,
        (stress, strain, plastic, kept, kept_before, edge_low, edge_high, *norms, col_even, col_odd,
         last_even, last_odd, rest_even, rest_odd, norm_before, own_cols),
        outs_space=pltpu.HBM,
    ))


def solution(mesh):
    split_in = P(None, "gx", "gy")
    return jax.shard_map(
        local,
        mesh=mesh,
        in_specs=(split_in,) * 5,
        out_specs=(split_in, split_in, P(None, None, "gx", "gy")),
        check_vma=False,
    )
```

```python
import functools
import math

import jax
import jax.numpy as jnp
import numpy as np
from jax import lax
from jax.experimental import pallas as pl
from jax.experimental.pallas import tpu as pltpu
from jax.sharding import PartitionSpec as P

OUTER = 3
REACH = 8
RATE = math.log2(math.e) / 0.3
HALF_LN2 = 0.5 * math.log(2.0)
VMEM_BYTES = 24 * 1024 * 1024
FIRST_VMEM_BYTES = 48 * 1024 * 1024


def tap(offset):
    return math.exp(-(offset**2) / 32.0) if abs(offset) <= REACH else 0.0


def band(rows, cols, shift=0):
    return np.array([[tap(c - r + shift) for c in range(cols)] for r in range(rows)])


def depth_matrix(layers):
    weights = band(layers, layers)
    return weights / weights.sum(axis=1, keepdims=True)


def split(value):
    high = value.astype(jnp.bfloat16)
    low = (value - high.astype(jnp.float32)).astype(jnp.bfloat16)
    return high, low


def left_constant(matrix):
    high, low = split(matrix)
    return jnp.concatenate(
        [jnp.concatenate([high, high], axis=1), jnp.concatenate([low, low], axis=1)], axis=0
    )


def right_constant(matrix):
    both = jnp.concatenate(split(matrix), axis=1)
    return jnp.concatenate([both, both], axis=0)


def left_product(constant, value):
    rows = constant.shape[0] // 2
    halves = jnp.concatenate(split(value), axis=0)
    both = jnp.dot(constant, halves, preferred_element_type=jnp.float32)
    return both[:rows] + both[rows:]


def right_product(value, constant):
    cols = constant.shape[1] // 2
    halves = jnp.concatenate(split(value), axis=1)
    both = jnp.dot(halves, constant, preferred_element_type=jnp.float32)
    return both[:, :cols] + both[:, cols:]


def first_factor(strain):
    return 0.8 - 0.2 * jnp.tanh(2.0 * strain - HALF_LN2)


def newton(stress, strain, yields, count, kept, factor):
    top = (stress + strain) - (0.875 + 0.875 * kept)
    shift = 2.0 * top - HALF_LN2
    state = 2.0 * (top - strain)
    drop = 0.1 + 0.1 * kept
    for sweep_no in range(1, 7):
        if sweep_no > 1:
            factor = 0.8 - 0.2 * jnp.tanh(shift - state)
        update = state * factor - drop
        state = update if sweep_no <= 3 else jnp.where(count >= sweep_no, update, state)
    return jnp.where(yields > 0, top - 0.5 * state, strain)


def depth_smooth(layers, matrix):
    count = len(layers)
    half = count // 2
    sums = [layers[k] + layers[count - 1 - k] for k in range(half)]
    diffs = [layers[k] - layers[count - 1 - k] for k in range(half)]
    out = [None] * count
    for row in range(half):
        even = odd = None
        for k in range(half):
            near, far = matrix[row, k], matrix[row, count - 1 - k]
            plus, minus = float(0.5 * (near + far)), float(0.5 * (near - far))
            if plus == 0.0 and minus == 0.0:
                continue
            even = sums[k] * plus if even is None else even + sums[k] * plus
            odd = diffs[k] * minus if odd is None else odd + diffs[k] * minus
        out[row] = even + odd
        out[count - 1 - row] = even - odd
    return out


def lane_ids(shape):
    return lax.broadcasted_iota(jnp.int32, shape, len(shape) - 1)


def on_even(axis):
    return lax.axis_index(axis) % 2 == 0


def sides(axis, even, odd):
    return jnp.where(on_even(axis), odd, even), jnp.where(on_even(axis), even, odd)


def send(axis, low, high, even_ref, odd_ref):
    place = lax.axis_index(axis)
    low = jnp.where(place == 0, 0.0, low)
    high = jnp.where(place == lax.axis_size(axis) - 1, 0.0, high)
    even_ref[...] = jnp.where(on_even(axis), high, low)
    odd_ref[...] = jnp.where(on_even(axis), low, high)


def layer_slots(shape):
    return lane_ids(shape) >> (REACH.bit_length() - 1)


def ratio(limit):
    return jnp.exp2(jnp.minimum(limit, 0.0) * RATE)


def edge_ratios(edges, received, norms, part, extended):
    both = sides("gy", *(ref[part, :] for ref in received))
    return [
        ratio(edge[extended, :] - value * norm[extended, :])
        for edge, value, norm in zip(edges, both, norms)
    ]


def with_edges(inner, layer, low, high):
    cols = inner.shape[1]
    slots = layer_slots(inner.shape)
    packed = jnp.where(slots == layer, low, high)
    shift = (cols - layer * REACH) % cols
    moved = packed if isinstance(layer, int) and layer == 0 else pltpu.roll(packed, shift, 1)
    return jnp.where((slots == 0) | (slots == cols // REACH - 1), moved, inner)


def first_edge_kernel(*refs):
    sources, refs = refs[:5], refs[5:]
    even_ref, odd_ref, norm, norm_low, norm_high, norm_last, norm_before, _, _, _, *refs = refs
    targets, (block, sems) = refs[:5], refs[5:]
    stress, strain, yields, count, _ = targets
    layers, rows, cols = stress.shape
    parts = (pl.ds(0, REACH), pl.ds(rows - REACH, REACH), pl.ds(REACH, rows - 2 * REACH))
    copies = []
    for side, part in enumerate(parts):
        for index, (source, target) in enumerate(zip(sources, targets)):
            copies.append(
                pltpu.make_async_copy(
                    source.at[:, part, :], target.at[:, part, :], sems.at[side, index]
                )
            )
            copies[-1].start()
    total = rows + REACH
    ids = lax.broadcasted_iota(jnp.int32, (total, cols), 0)
    down = inverse_weights("gx", ids - REACH, rows)
    lanes = lane_ids((REACH, cols))
    within = lanes & (REACH - 1)
    places = (lanes, within, within + (cols - REACH), 0 * lanes + (cols - 1), 0 * lanes - 1)
    for ref, place in zip((norm, norm_low, norm_high, norm_last, norm_before), places):
        ref[...] = down * inverse_weights("gy", place, cols)[:1]
    square = (layers * REACH, layers * REACH)
    line, lane = lax.broadcasted_iota(jnp.int32, square, 0), lane_ids(square)
    steps = (lane & (REACH - 1)) - (line & (REACH - 1))
    band_part = jnp.zeros(square, jnp.float32)
    for step in range(REACH):
        band_part = jnp.where(abs(steps) == step, tap(REACH - step), band_part)
    band_part = jnp.where((line ^ lane) < REACH, band_part, 0.0)
    sent = []
    for side, matrix in enumerate(
        (jnp.where(steps <= 0, band_part, 0.0), jnp.where(steps >= 0, band_part, 0.0))
    ):
        for copy in copies[side * 5 : side * 5 + 5]:
            copy.wait()
        for layer in range(layers):
            at = (layer, parts[side], slice(None))
            block[pl.ds(layer * REACH, REACH), :] = newton(
                stress[at], strain[at], yields[at], count[at], jnp.ones((REACH, cols), jnp.float32),
                first_factor(strain[at]),
            )
        product = left_product(left_constant(matrix), block[...])
        sent.append(jnp.concatenate([product, product[:REACH]], axis=0))
    send("gx", *sent, even_ref, odd_ref)
    for copy in copies[10:]:
        copy.wait()


def edge_kernel(stress, strain, yields, count, threshold, factor, kept, _, edge_low, edge_high, norm_low,
                norm_high, col_even, col_odd, below, above,
                even_ref, odd_ref, low_block, high_block, rest):
    layers, rows, cols = stress.shape
    starts = (0, rows - 2 * REACH, rows - REACH)
    packed = [
        edge_ratios(
            (edge_low, edge_high), (col_even, col_odd), (norm_low, norm_high),
            pl.ds(first_row, REACH), pl.ds(first_row + REACH, REACH),
        )
        for first_row in starts
    ]

    def layer_step(layer):
        for index, first_row in enumerate(starts):
            at = (layer, pl.ds(first_row, REACH), slice(None))
            ratios = with_edges(kept[at], layer, *packed[index])
            value = newton(stress[at], strain[at], yields[at], count[at], ratios, factor[at])
            if index == 0:
                low_block[pl.ds(layer * REACH, REACH), :] = value
            else:
                high_block[pl.ds((2 * layer + index - 1) * REACH, REACH), :] = value
            if index == 2:
                left = (stress[at] + strain[at]) - value
                rest[pl.ds(layer, 1), :] = left[REACH - 1 :]
                rest[pl.ds(layers + layer, 1), :] = threshold[at][REACH - 1 :]

    for layer in range(layers):
        layer_step(layer)
    low = left_product(left_constant(below[...]), low_block[...])
    high = left_product(left_constant(above[...]), high_block[...])
    extra = jnp.zeros((even_ref.shape[0] - low.shape[0], cols), jnp.float32)
    send(
        "gx", jnp.concatenate([low, extra], axis=0), jnp.concatenate([high, rest[...]], axis=0),
        even_ref, odd_ref,
    )


def main_kernel(turn, stress, strain, yields, count, factor, kept, edge_low, edge_high, norm_low,
                norm_high, col_even, col_odd, norm_last, fixed, band_ref, low_ref, high_ref, next_ref,
                across, low_cols, high_cols, plastic, pack_last, *packs):
    layers, rows, cols = stress.shape
    total = rows + REACH
    step_rows = 4 * REACH
    lanes = lane_ids((REACH, cols))
    pack_last[pl.ds(0, REACH), :] = jnp.zeros((REACH, cols), jnp.float32)

    def newton_blocks(index, fresh):
        for near in range(step_rows // REACH):
            first = index * step_rows + near * REACH
            part = pl.ds(pl.multiple_of(first, REACH), REACH)
            extended = pl.ds(pl.multiple_of(first + REACH, REACH), REACH)
            if not fresh:
                packed = edge_ratios(
                    (edge_low, edge_high), (col_even, col_odd), (norm_low, norm_high), part, extended
                )
            for layer in range(layers):
                at = (layer, part, slice(None))
                if fresh:
                    ratios, lead = jnp.ones((REACH, cols), jnp.float32), first_factor(strain[at])
                else:
                    ratios, lead = with_edges(kept[at], layer, *packed), factor[at]
                value = newton(stress[at], strain[at], yields[at], count[at], ratios, lead)
                plastic[at] = value
                if not fresh:
                    lane = layers + layer
                    pltpu.store(pack_last.at[extended, :], pltpu.roll(value, lane + 1, 1), mask=lanes == lane)

    @pl.when(turn[0] == 0)
    def _():
        lax.fori_loop(0, rows // step_rows, lambda index, _: newton_blocks(index, True), None)

    @pl.when(turn[0] > 0)
    def _():
        lax.fori_loop(0, rows // step_rows, lambda index, _: newton_blocks(index, False), None)

    constant = left_constant(band_ref[...])
    slots = layer_slots((total, cols))
    spread = len(packs)
    for layer in range(0, layers, 2):
        pair = jnp.concatenate([plastic[layer], plastic[layer + 1]], axis=1)
        result = left_product(constant, pair)
        for inner in range(2):
            value = result[:, inner * cols : (inner + 1) * cols]
            across[layer + inner] = value
            moved = pltpu.roll(value, (layer + inner) * REACH, 1) if layer + inner else value
            mask = ((layer + inner - slots) & (layers - 1)) < 3
            pltpu.store(packs[(layer + inner) % spread], moved, mask=mask)

    def gathered(behind):
        source = (slots + behind) & (spread - 1)
        parts = packs[0][...]
        for index in range(1, spread):
            parts = jnp.where(source == index, packs[index][...], parts)
        return parts

    low_cols[...] = right_product(gathered(0), right_constant(low_ref[...]))
    high = right_product(gathered(1), right_constant(high_ref[...]))
    behind = right_product(gathered(2), right_constant(next_ref[...]))
    high_cols[:, :cols] = high[:, :cols]
    drop = (high[:, cols:] + behind) * norm_last[...]
    first_lanes = lane_ids((total, cols)) < layers
    high_cols[:, cols:] = fixed[...] - jnp.where(first_lanes, drop, pack_last[...])


def prepare_kernel(stress, strain, threshold, _, factor, fixed):
    layers, rows, cols = stress.shape
    lanes = lane_ids((REACH, cols))
    fixed[...] = jnp.zeros_like(fixed)

    def step(index, carry):
        for near in range(2):
            first = (2 * index + near) * REACH
            part = pl.ds(pl.multiple_of(first, REACH), REACH)
            extended = pl.ds(pl.multiple_of(first + REACH, REACH), REACH)
            for layer in range(layers):
                at = (layer, part, slice(None))
                factor[at] = first_factor(strain[at])
                for lane, value in ((layer, threshold[at]), (layers + layer, stress[at] + strain[at])):
                    moved = pltpu.roll(value, lane + 1, 1)
                    pltpu.store(fixed.at[extended, :], moved, mask=lanes == lane)
        return carry

    lax.fori_loop(0, rows // (2 * REACH), step, 0)


def pack_edges(values):
    cols = values[0].shape[1]
    count = cols // REACH
    slots = layer_slots(values[0].shape)
    low = high = ahead = jnp.zeros_like(values[0])
    for layer, value in enumerate(values):
        moved = pltpu.roll(value, layer * REACH, 1) if layer else value
        low = jnp.where(slots == layer, moved, low)
        high = jnp.where(slots == (layer - 1) % count, moved, high)
        ahead = jnp.where(slots == (layer - 2) % count, moved, ahead)
    return low, high, ahead


def corner_kernel(row_even, row_odd, rest_even, rest_odd, low_cols, high_cols, norm_last,
                  _, low_ref, high_ref, next_ref, even_ref, odd_ref, own_ref):
    cols = low_ref.shape[0]
    total = low_cols.shape[0]
    layers = (total - REACH) // REACH
    strip = layers * REACH
    from_low, from_high = sides("gx", row_even[...], row_odd[...])
    rest, _ = sides("gx", rest_even[...], rest_odd[...])
    partial, kept, limit = rest[:layers], rest[layers : 2 * layers], rest[2 * layers :]
    before = [jnp.broadcast_to(partial[layer : layer + 1], (REACH, cols)) for layer in range(layers)]
    packs = [pack_edges(before)] + [
        pack_edges([block[layer * REACH : (layer + 1) * REACH] for layer in range(layers)])
        for block in (from_low, from_high)
    ]
    low, high, ahead = (jnp.concatenate(group, axis=0) for group in zip(*packs))
    low_add = right_product(low, right_constant(low_ref[...]))
    high_add = right_product(high, right_constant(high_ref[...]))
    behind_add = right_product(ahead, right_constant(next_ref[...]))

    lanes = lane_ids((layers, cols))
    level = lax.broadcasted_iota(jnp.int32, (layers, cols), 0)
    corner_limit = jnp.where(lanes == level, limit[:, cols - 1 :], 0.0)
    corner_kept = jnp.where(lanes == layers + level, kept[:, cols - 1 :], 0.0)
    corner = jnp.sum(corner_limit + corner_kept, axis=0, keepdims=True)

    def place(base, add):
        return jnp.concatenate(
            [base[: 2 * REACH] + add[: 2 * REACH], base[2 * REACH : total - REACH],
             base[total - REACH :] + add[2 * REACH :]],
            axis=0,
        )

    low_all = place(low_cols[...], low_add)
    high_all = place(high_cols[:, :cols], high_add[:, :cols])
    last = norm_last[...]
    behind = high_add[:, cols:] + behind_add
    edges = jnp.concatenate([last[: 2 * REACH], last[total - REACH :]], axis=0)
    lanes = lane_ids(behind.shape)
    drop = jnp.where(lanes < layers, behind * edges, 0.0)
    column = place(high_cols[:, cols:], -drop)
    first = column[:REACH] + corner
    main = column[REACH:]
    quarter = strip // 4
    lanes = lane_ids((quarter, cols))
    folded = main[:quarter]
    for part in range(1, 4):
        moved = pltpu.roll(main[part * quarter : (part + 1) * quarter], part * 2 * layers, 1)
        folded = jnp.where(lanes // (2 * layers) == part, moved, folded)
    spare = jnp.zeros((REACH, cols), jnp.float32)
    extra = jnp.zeros((quarter + REACH, cols), jnp.float32)
    send(
        "gy", jnp.concatenate([low_all[REACH:, :cols], low_all[:REACH, :cols], extra, spare], axis=0),
        jnp.concatenate([high_all[REACH:], high_all[:REACH], folded, first, spare], axis=0),
        even_ref, odd_ref,
    )
    own_ref[...] = low_all[:, cols:]


def column_kernel(depth, across, row_even, row_odd, rest_even, rest_odd, threshold, norm, band_ref, _,
                  kept, kept_before, edge_low, edge_high, deep):
    layers, total, cols = across.shape

    def depth_sums(part, values):
        for layer, value in enumerate(depth_smooth(values, depth)):
            deep[layer, part, :] = value

    def step(index, carry):
        for inner in range(2):
            part = pl.ds(pl.multiple_of((2 * index + inner + 2) * REACH, REACH), REACH)
            depth_sums(part, [across[layer, part, :] for layer in range(layers)])
        return carry

    lax.fori_loop(0, (total // REACH - 3) // 2, step, 0)
    for first_row in (0, REACH, total - REACH):
        part = pl.ds(first_row, REACH)
        values = []
        for layer in range(layers):
            if first_row:
                line = pl.ds(layer * REACH, REACH)
                both = sides("gx", row_even[line, :], row_odd[line, :])
            else:
                both = sides("gx", rest_even[pl.ds(layer, 1), :], rest_odd[pl.ds(layer, 1), :])
            values.append(across[layer, part, :] + both[first_row > REACH])
        depth_sums(part, values)

    constant = right_constant(band_ref[...])
    slots = layer_slots((total, cols))
    for layer in range(layers):
        nonlocal_strain = right_product(deep[layer], constant) * norm[...]
        line = pl.ds(2 * layers + layer, 1)
        limit, _ = sides("gx", rest_even[line, :], rest_odd[line, :])
        first = limit - nonlocal_strain[:REACH]
        others = threshold[layer] - nonlocal_strain[REACH:]
        kept_before[layer] = ratio(first)
        kept[layer] = ratio(others)
        moved = jnp.concatenate([first, others], axis=0)
        moved = pltpu.roll(moved, layer * REACH, 1) if layer else moved
        pltpu.store(edge_low, moved, mask=slots == layer)
        pltpu.store(edge_high, moved, mask=slots == (layer - 1) % (cols // REACH))


def final_kernel(stress, strain, plastic, inner, inner_before, edge_low, edge_high, norm_low, norm_high,
                 col_even, col_odd, last_even, last_odd, rest_even, rest_odd, norm_before, own_cols,
                 plastic_out, damage_out, force_out, columns, lows, highs, damage_s, force_s, sums, diffs,
                 copy_sem, sems):
    layers, rows, cols = stress.shape
    whole = pltpu.make_async_copy(plastic, plastic_out, copy_sem)
    whole.start()
    from_low, _ = sides("gy", last_even[...], last_odd[...])
    folded = from_low[REACH : REACH + rows // 4]
    pieces = [from_low[REACH + rows // 4 :], folded]
    for part in range(1, 4):
        pieces.append(pltpu.roll(folded, cols - part * 2 * layers, 1))
    column = jnp.concatenate(pieces, axis=0)
    kept = ratio(column - own_cols[...] * norm_before[...])
    columns[...] = (0.5 * kept) * pltpu.roll(column, cols - layers, 1)

    low, high = edge_ratios(
        (edge_low, edge_high), (last_even, last_odd), (norm_low, norm_high),
        pl.ds(0, REACH), pl.ds(0, REACH),
    )
    lows[pl.ds(0, REACH), :], highs[pl.ds(0, REACH), :] = low, high
    low, high = edge_ratios(
        (edge_low, edge_high), (col_even, col_odd), (norm_low, norm_high),
        pl.ds(0, rows), pl.ds(REACH, rows),
    )
    lows[pl.ds(REACH, rows), :], highs[pl.ds(REACH, rows), :] = low, high

    def copies(layer):
        return (
            pltpu.make_async_copy(damage_s.at[layer], damage_out.at[layer], sems.at[0, layer]),
            pltpu.make_async_copy(force_s.at[0, layer], force_out.at[0, layer], sems.at[1, layer]),
            pltpu.make_async_copy(force_s.at[1, layer], force_out.at[1, layer], sems.at[2, layer]),
        )

    def layer_step(layer, near):
        lanes = lane_ids((REACH, cols))
        for block in range(rows // REACH + 1):
            extended = pl.ds(block * REACH, REACH)
            part = pl.ds((block - 1) * REACH if block else 0, REACH)
            packed = lows[extended, :], highs[extended, :]
            at = (layer, part, slice(None))
            if block:
                rest = (stress[at] + strain[at]) - plastic[at]
            else:
                line = pl.ds(layers + layer, 1)
                rest, _ = sides("gx", rest_even[line, :], rest_odd[line, :])
            kept = with_edges(inner[at] if block else inner_before[layer], layer, *packed)
            value = (0.5 * kept) * rest
            left = jnp.where(
                lanes == 0,
                pltpu.roll(columns[extended, :], (cols - layer) % cols, 1),
                pltpu.roll(value, 1, 1),
            )
            both, diff = left + value, left - value
            sums[near, extended, :] = both
            diffs[near, extended, :] = diff
            if block:
                behind = pl.ds(block * REACH - 1, REACH)
                damage_s[at] = 1.0 - kept
                force_s[(0, *at)] = sums[near, behind, :] - both
                force_s[(1, *at)] = diffs[near, behind, :] + diff

    def step(index, carry):
        for near in range(2):
            layer_step(2 * index + near, near)
        for near in range(2):
            for copy in copies(2 * index + near):
                copy.start()
        return carry

    lax.fori_loop(0, layers // 2, step, 0)

    def drain(layer, carry):
        for copy in copies(layer):
            copy.wait()
        return carry

    lax.fori_loop(0, layers, drain, 0)
    whole.wait()


def call(kernel, outs, scratch, nanoseconds, operands, spaces=None, outs_space=pltpu.VMEM, limit=VMEM_BYTES):
    spaces = spaces or [pltpu.VMEM] * len(operands)
    shapes = [out if isinstance(out, jax.ShapeDtypeStruct) else jax.ShapeDtypeStruct(out, jnp.float32)
              for out in outs]
    return pl.pallas_call(
        kernel,
        out_shape=shapes,
        in_specs=[pl.BlockSpec(memory_space=space) for space in spaces],
        out_specs=[pl.BlockSpec(memory_space=outs_space)] * len(outs),
        scratch_shapes=[pltpu.VMEM(s, jnp.float32) if isinstance(s, tuple) else s for s in scratch],
        compiler_params=pltpu.CompilerParams(vmem_limit_bytes=limit),
        cost_estimate=pl.CostEstimate(
            flops=nanoseconds * 1_000_000, bytes_accessed=nanoseconds * 1000, transcendentals=0
        ),
    )(*operands)


def exchange(axis, other, even, odd):
    names = ("gx", "gy")
    count, across = lax.axis_size(axis), lax.axis_size(other)
    stride = {"gx": lax.axis_size("gy"), "gy": 1}
    results = []
    for start, value in ((0, even), (1, odd)):
        pairs = []
        for place in range(count):
            partner = place + 1 if (place - start) % 2 == 0 else place - 1
            for line in range(across):
                target = (partner, line)
                if not 0 <= partner < count:
                    target = (place, line ^ 1 if line ^ 1 < across else line)
                pairs.append((
                    place * stride[axis] + line * stride[other],
                    target[0] * stride[axis] + target[1] * stride[other],
                ))
        results.append(lax.ppermute(value, names, pairs))
    return results


def inverse_weights(axis, places, length):
    extent = length * lax.axis_size(axis)
    places = places + lax.axis_index(axis) * length
    total = jnp.zeros(places.shape, jnp.float32)
    for offset in range(-REACH, REACH + 1):
        inside = (places + offset >= 0) & (places + offset < extent)
        total = total + jnp.where(inside, tap(offset), 0.0)
    return 1.0 / jnp.maximum(total, tap(REACH))


def matrices(layers, rows, cols):
    depth = depth_matrix(layers)
    up, down = band(REACH, REACH, REACH), band(REACH, REACH, -REACH)
    same = np.eye(layers)
    below = np.kron(same, up)
    near = np.concatenate([np.zeros((REACH, REACH)), down], axis=1)
    line = band(1, 2 * REACH, 1 - 2 * REACH)
    above = np.concatenate([np.kron(same, near), np.kron(same, line)], axis=0)
    rows_band = np.concatenate([np.zeros((REACH - 1, rows)), band(1, rows, 1), band(rows, rows)])
    slots = cols // REACH
    low, high, ahead = np.zeros((cols, 2 * cols)), np.zeros((cols, 2 * cols)), np.zeros((cols, cols))
    for source in range(layers):
        own = slice(source * REACH, (source + 1) * REACH)
        first = (source - 1) % slots * REACH
        other = slice(first, first + REACH)
        for layer in range(layers):
            weight = depth[layer, source]
            first = (layer - 1) % slots * REACH
            low[own, first : first + REACH] = weight * up.T
            high[other, layer * REACH : (layer + 1) * REACH] = weight * down.T
            low[own, cols + layer] = [weight * tap(j + 1) for j in range(REACH)]
            high[other, cols + layer] = [weight * tap(REACH - 1 - j) for j in range(REACH)]
            ahead[((source - 2) % slots) * REACH + REACH - 1, layer] = weight * tap(REACH)
    constants = (below, above, rows_band, band(cols, cols), low, high, ahead)
    return depth, [jnp.asarray(matrix, jnp.float32) for matrix in constants]


def local(trial_stress, old_strain, yield_mask, newton_count, damage_threshold):
    layers, rows, cols = trial_stress.shape
    assert layers * REACH == cols == rows and layers & (layers - 1) == 0
    total, strip = rows + REACH, layers * REACH
    depth, constants = matrices(layers, rows, cols)
    below, above, rows_band, cols_band, *columns = constants

    whole, wide, top = (layers, rows, cols), (layers, total, cols), (layers, REACH, cols)
    sent_rows = (strip + 3 * layers, cols)
    sent_cols = (total + rows // 4 + 2 * REACH, cols)
    last_cols = total + rows // 4 + REACH
    spare = (3 * layers, cols)
    packed, packed_two = (total, cols), (total, 2 * cols)

    sources = (trial_stress, old_strain, yield_mask, newton_count, damage_threshold)
    row_even, row_odd, norm, norm_low, norm_high, norm_last, norm_before, col_even, col_odd, rest, *inputs = call(
        first_edge_kernel,
        [(strip + REACH, cols)] * 2 + [packed] * 5 + [(rows, cols)] * 2 + [spare]
        + [jax.ShapeDtypeStruct(whole, source.dtype) for source in sources],
        [(strip, cols), pltpu.SemaphoreType.DMA((3, len(sources)))], 2500,
        sources, [pltpu.HBM] * len(sources), limit=FIRST_VMEM_BYTES,
    )
    stress, strain, _, _, threshold = inputs
    kept, edge_low, edge_high, norms = stress, norm_low, norm_high, (norm_low, norm_high)
    rest_even = rest_odd = rest
    fixed, factor = norm_last, stress
    for outer_no in range(OUTER):
        last = outer_no == OUTER - 1
        if outer_no:
            row_even, row_odd = call(
                edge_kernel, [sent_rows] * 2,
                [(strip, cols), (2 * strip, cols), (2 * layers, cols)], 800,
                (*inputs, factor, kept, kept_before, edge_low, edge_high, *norms, col_even, col_odd,
                 below, above),
            )
        if not last:
            row_even, row_odd = row_even[:strip], row_odd[:strip]
        row_even, row_odd = exchange("gx", "gy", row_even, row_odd)
        if last:
            rest_even, rest_odd = row_even[strip:], row_odd[strip:]
            row_even, row_odd = row_even[:strip], row_odd[:strip]
        turn = jnp.full((1,), outer_no, jnp.int32)
        across, low_cols, high_cols, plastic = call(
            main_kernel, [wide, packed_two, packed_two, whole],
            [packed] * 5, 4500,
            (turn, *inputs[:4], factor, kept, edge_low, edge_high, *norms, col_even, col_odd, norm_last,
             fixed, rows_band, *columns),
            [pltpu.SMEM] + [pltpu.VMEM] * 18,
        )
        col_even, col_odd, own_cols = call(
            corner_kernel, [sent_cols, sent_cols, packed], [], 400,
            (row_even, row_odd, rest_even, rest_odd, low_cols, high_cols, norm_last, plastic, *columns),
        )
        if not outer_no:
            factor, fixed = call(
                prepare_kernel, [whole, packed], [], 1200, (stress, strain, threshold, col_odd),
            )
        used = last_cols if last else rows
        col_even, col_odd = col_even[:used], col_odd[:used]
        col_even, col_odd = exchange("gy", "gx", col_even, col_odd)
        if last:
            last_even, last_odd = col_even[rows:], col_odd[rows:]
            col_even, col_odd = col_even[:rows], col_odd[:rows]
        kept, kept_before, edge_low, edge_high = call(
            functools.partial(column_kernel, depth), [whole, top, packed, packed], [wide], 1800,
            (across, row_even, row_odd, rest_even, rest_odd, threshold, norm, cols_band, own_cols),
        )
    return tuple(call(
        final_kernel, [whole, whole, (2, *whole)],
        [packed] * 3 + [whole, (2, *whole), (2, *packed), (2, *packed),
         pltpu.SemaphoreType.DMA(()), pltpu.SemaphoreType.DMA((3, layers))],
        3000,
        (stress, strain, plastic, kept, kept_before, edge_low, edge_high, *norms, col_even, col_odd,
         last_even, last_odd, rest_even, rest_odd, norm_before, own_cols),
        outs_space=pltpu.HBM,
    ))


def solution(mesh):
    split_in = P(None, "gx", "gy")
    return jax.shard_map(
        local,
        mesh=mesh,
        in_specs=(split_in,) * 5,
        out_specs=(split_in, split_in, P(None, None, "gx", "gy")),
        check_vma=False,
    )
```

```python
import functools
import math

import jax
import jax.numpy as jnp
import numpy as np
from jax import lax
from jax.experimental import pallas as pl
from jax.experimental.pallas import tpu as pltpu
from jax.sharding import PartitionSpec as P

OUTER = 3
REACH = 8
RATE = math.log2(math.e) / 0.3
HALF_LN2 = 0.5 * math.log(2.0)
VMEM_BYTES = 24 * 1024 * 1024
EDGE_VMEM_BYTES = 53 * 1024 * 1024


def tap(offset):
    return math.exp(-(offset**2) / 32.0) if abs(offset) <= REACH else 0.0


def band(rows, cols, shift=0):
    return np.array([[tap(c - r + shift) for c in range(cols)] for r in range(rows)])


def depth_matrix(layers):
    weights = band(layers, layers)
    return weights / weights.sum(axis=1, keepdims=True)


def split(value):
    high = value.astype(jnp.bfloat16)
    low = (value - high.astype(jnp.float32)).astype(jnp.bfloat16)
    return high, low


def left_constant(matrix):
    high, low = split(matrix)
    return jnp.concatenate(
        [jnp.concatenate([high, high], axis=1), jnp.concatenate([low, low], axis=1)], axis=0
    )


def right_constant(matrix):
    both = jnp.concatenate(split(matrix), axis=1)
    return jnp.concatenate([both, both], axis=0)


def left_product(constant, value):
    rows = constant.shape[0] // 2
    halves = jnp.concatenate(split(value), axis=0)
    both = jnp.dot(constant, halves, preferred_element_type=jnp.float32)
    return both[:rows] + both[rows:]


def right_product(value, constant):
    cols = constant.shape[1] // 2
    halves = jnp.concatenate(split(value), axis=1)
    both = jnp.dot(halves, constant, preferred_element_type=jnp.float32)
    return both[:, :cols] + both[:, cols:]


def first_factor(strain):
    return 0.8 - 0.2 * jnp.tanh(2.0 * strain - HALF_LN2)


def newton(stress, strain, yields, count, kept, factor):
    top = (stress + strain) - (0.875 + 0.875 * kept)
    shift = 2.0 * top - HALF_LN2
    state = 2.0 * (top - strain)
    drop = 0.1 + 0.1 * kept
    for sweep_no in range(1, 7):
        if sweep_no > 1:
            factor = 0.8 - 0.2 * jnp.tanh(shift - state)
        update = state * factor - drop
        state = update if sweep_no <= 3 else jnp.where(count >= sweep_no, update, state)
    return jnp.where(yields > 0, top - 0.5 * state, strain)


def depth_smooth(layers, matrix):
    count = len(layers)
    half = count // 2
    sums = [layers[k] + layers[count - 1 - k] for k in range(half)]
    diffs = [layers[k] - layers[count - 1 - k] for k in range(half)]
    out = [None] * count
    for row in range(half):
        even = odd = None
        for k in range(half):
            near, far = matrix[row, k], matrix[row, count - 1 - k]
            plus, minus = float(0.5 * (near + far)), float(0.5 * (near - far))
            if plus == 0.0 and minus == 0.0:
                continue
            even = sums[k] * plus if even is None else even + sums[k] * plus
            odd = diffs[k] * minus if odd is None else odd + diffs[k] * minus
        out[row] = even + odd
        out[count - 1 - row] = even - odd
    return out


def lane_ids(shape):
    return lax.broadcasted_iota(jnp.int32, shape, len(shape) - 1)


def on_even(axis):
    return lax.axis_index(axis) % 2 == 0


def sides(axis, even, odd):
    return jnp.where(on_even(axis), odd, even), jnp.where(on_even(axis), even, odd)


def send(axis, low, high, even_ref, odd_ref):
    place = lax.axis_index(axis)
    low = jnp.where(place == 0, 0.0, low)
    high = jnp.where(place == lax.axis_size(axis) - 1, 0.0, high)
    even_ref[...] = jnp.where(on_even(axis), high, low)
    odd_ref[...] = jnp.where(on_even(axis), low, high)


def layer_slots(shape):
    return lane_ids(shape) >> (REACH.bit_length() - 1)


def ratio(limit):
    return jnp.exp2(jnp.minimum(limit, 0.0) * RATE)


def edge_ratios(edges, received, norms, part, extended):
    both = sides("gy", *(ref[part, :] for ref in received))
    return [
        ratio(edge[extended, :] - value * norm[extended, :])
        for edge, value, norm in zip(edges, both, norms)
    ]


def with_edges(inner, layer, low, high):
    cols = inner.shape[1]
    slots = layer_slots(inner.shape)
    packed = jnp.where(slots == layer, low, high)
    shift = (cols - layer * REACH) % cols
    moved = packed if isinstance(layer, int) and layer == 0 else pltpu.roll(packed, shift, 1)
    return jnp.where((slots == 0) | (slots == cols // REACH - 1), moved, inner)


def first_edge_kernel(*refs):
    sources, refs = refs[:4], refs[4:]
    even_ref, odd_ref, norm, norm_low, norm_high, norm_last, norm_before, _, *refs = refs
    targets, (block, sems) = refs[:4], refs[4:]
    stress, strain, yields, count = targets
    layers, rows, cols = sources[0].shape
    copies = []
    for side, first_row in enumerate((0, rows - REACH)):
        for index, (source, target) in enumerate(zip(sources, targets)):
            copies.append(
                pltpu.make_async_copy(
                    source.at[:, pl.ds(first_row, REACH), :],
                    target.at[:, pl.ds(side * REACH, REACH), :],
                    sems.at[side, index],
                )
            )
            copies[-1].start()
    total = rows + REACH
    ids = lax.broadcasted_iota(jnp.int32, (total, cols), 0)
    down = inverse_weights("gx", ids - REACH, rows)
    lanes = lane_ids((REACH, cols))
    within = lanes & (REACH - 1)
    places = (lanes, within, within + (cols - REACH), 0 * lanes + (cols - 1), 0 * lanes - 1)
    for ref, place in zip((norm, norm_low, norm_high, norm_last, norm_before), places):
        ref[...] = down * inverse_weights("gy", place, cols)[:1]
    square = (layers * REACH, layers * REACH)
    line, lane = lax.broadcasted_iota(jnp.int32, square, 0), lane_ids(square)
    steps = (lane & (REACH - 1)) - (line & (REACH - 1))
    band_part = jnp.zeros(square, jnp.float32)
    for step in range(REACH):
        band_part = jnp.where(abs(steps) == step, tap(REACH - step), band_part)
    band_part = jnp.where((line ^ lane) < REACH, band_part, 0.0)
    sent = []
    for side, matrix in enumerate(
        (jnp.where(steps <= 0, band_part, 0.0), jnp.where(steps >= 0, band_part, 0.0))
    ):
        for copy in copies[side * 4 : side * 4 + 4]:
            copy.wait()
        for layer in range(layers):
            at = (layer, pl.ds(side * REACH, REACH), slice(None))
            block[pl.ds(layer * REACH, REACH), :] = newton(
                stress[at], strain[at], yields[at], count[at], jnp.ones((REACH, cols), jnp.float32),
                first_factor(strain[at]),
            )
        product = left_product(left_constant(matrix), block[...])
        sent.append(jnp.concatenate([product, product[:REACH]], axis=0))
    send("gx", *sent, even_ref, odd_ref)


def edge_kernel(stress, strain, yields, count, threshold, factor, kept, _, edge_low, edge_high, norm_low,
                norm_high, col_even, col_odd, below, above,
                even_ref, odd_ref, low_block, high_block, rest):
    layers, rows, cols = stress.shape
    starts = (0, rows - 2 * REACH, rows - REACH)
    packed = [
        edge_ratios(
            (edge_low, edge_high), (col_even, col_odd), (norm_low, norm_high),
            pl.ds(first_row, REACH), pl.ds(first_row + REACH, REACH),
        )
        for first_row in starts
    ]

    def layer_step(layer):
        for index, first_row in enumerate(starts):
            at = (layer, pl.ds(first_row, REACH), slice(None))
            ratios = with_edges(kept[at], layer, *packed[index])
            value = newton(stress[at], strain[at], yields[at], count[at], ratios, factor[at])
            if index == 0:
                low_block[pl.ds(layer * REACH, REACH), :] = value
            else:
                high_block[pl.ds((2 * layer + index - 1) * REACH, REACH), :] = value
            if index == 2:
                left = (stress[at] + strain[at]) - value
                rest[pl.ds(layer, 1), :] = left[REACH - 1 :]
                rest[pl.ds(layers + layer, 1), :] = threshold[at][REACH - 1 :]

    for layer in range(layers):
        layer_step(layer)
    low = left_product(left_constant(below[...]), low_block[...])
    high = left_product(left_constant(above[...]), high_block[...])
    extra = jnp.zeros((even_ref.shape[0] - low.shape[0], cols), jnp.float32)
    send(
        "gx", jnp.concatenate([low, extra], axis=0), jnp.concatenate([high, rest[...]], axis=0),
        even_ref, odd_ref,
    )


def first_main_kernel(stress, strain, yields, count, band_ref, low_ref, high_ref, next_ref,
                      across, low_cols, high_cols, plastic, *packs):
    layers, rows, cols = stress.shape
    step_rows = 4 * REACH

    def step(index, carry):
        for near in range(step_rows // REACH):
            part = pl.ds(pl.multiple_of(index * step_rows + near * REACH, REACH), REACH)
            for layer in range(layers):
                at = (layer, part, slice(None))
                plastic[at] = newton(
                    stress[at], strain[at], yields[at], count[at],
                    jnp.ones((REACH, cols), jnp.float32), first_factor(strain[at]),
                )
        return carry

    lax.fori_loop(0, rows // step_rows, step, 0)
    smooth_rows(plastic, (band_ref, low_ref, high_ref, next_ref), across, low_cols, high_cols, packs)


def main_kernel(stress, strain, yields, count, factor, kept, edge_low, edge_high, norm_low, norm_high,
                col_even, col_odd, norm_last, fixed, band_ref, low_ref, high_ref, next_ref,
                across, low_cols, high_cols, plastic, pack_last, *packs):
    layers, rows, cols = stress.shape
    total = rows + REACH
    step_rows = 4 * REACH
    lanes = lane_ids((REACH, cols))
    pack_last[pl.ds(0, REACH), :] = jnp.zeros((REACH, cols), jnp.float32)

    def step(index, carry):
        for near in range(step_rows // REACH):
            first = index * step_rows + near * REACH
            part = pl.ds(pl.multiple_of(first, REACH), REACH)
            extended = pl.ds(pl.multiple_of(first + REACH, REACH), REACH)
            packed = edge_ratios(
                (edge_low, edge_high), (col_even, col_odd), (norm_low, norm_high), part, extended
            )
            for layer in range(layers):
                at = (layer, part, slice(None))
                ratios = with_edges(kept[at], layer, *packed)
                value = newton(stress[at], strain[at], yields[at], count[at], ratios, factor[at])
                plastic[at] = value
                lane = layers + layer
                pltpu.store(pack_last.at[extended, :], pltpu.roll(value, lane + 1, 1), mask=lanes == lane)
        return carry

    lax.fori_loop(0, rows // step_rows, step, 0)
    behind = smooth_rows(
        plastic, (band_ref, low_ref, high_ref, next_ref), across, low_cols, high_cols, packs
    )
    drop = behind * norm_last[...]
    first_lanes = lane_ids((total, cols)) < layers
    high_cols[:, cols:] = fixed[...] - jnp.where(first_lanes, drop, pack_last[...])


def smooth_rows(plastic, tables, across, low_cols, high_cols, packs):
    layers, rows, cols = plastic.shape
    total = rows + REACH
    band_ref, low_ref, high_ref, next_ref = tables
    constant = left_constant(band_ref[...])
    slots = layer_slots((total, cols))
    spread = len(packs)
    for layer in range(0, layers, 2):
        pair = jnp.concatenate([plastic[layer], plastic[layer + 1]], axis=1)
        result = left_product(constant, pair)
        for inner in range(2):
            value = result[:, inner * cols : (inner + 1) * cols]
            across[layer + inner] = value
            moved = pltpu.roll(value, (layer + inner) * REACH, 1) if layer + inner else value
            mask = ((layer + inner - slots) & (layers - 1)) < 3
            pltpu.store(packs[(layer + inner) % spread], moved, mask=mask)

    def gathered(behind):
        source = (slots + behind) & (spread - 1)
        parts = packs[0][...]
        for index in range(1, spread):
            parts = jnp.where(source == index, packs[index][...], parts)
        return parts

    low_cols[...] = right_product(gathered(0), right_constant(low_ref[...]))
    high = right_product(gathered(1), right_constant(high_ref[...]))
    behind = right_product(gathered(2), right_constant(next_ref[...]))
    high_cols[:, :cols] = high[:, :cols]
    return high[:, cols:] + behind


def prepare_kernel(stress, strain, threshold, _, factor, fixed):
    layers, rows, cols = stress.shape
    lanes = lane_ids((REACH, cols))
    fixed[...] = jnp.zeros_like(fixed)

    def step(index, carry):
        for near in range(2):
            first = (2 * index + near) * REACH
            part = pl.ds(pl.multiple_of(first, REACH), REACH)
            extended = pl.ds(pl.multiple_of(first + REACH, REACH), REACH)
            for layer in range(layers):
                at = (layer, part, slice(None))
                factor[at] = first_factor(strain[at])
                for lane, value in ((layer, threshold[at]), (layers + layer, stress[at] + strain[at])):
                    moved = pltpu.roll(value, lane + 1, 1)
                    pltpu.store(fixed.at[extended, :], moved, mask=lanes == lane)
        return carry

    lax.fori_loop(0, rows // (2 * REACH), step, 0)


def pack_edges(values):
    cols = values[0].shape[1]
    count = cols // REACH
    slots = layer_slots(values[0].shape)
    low = high = ahead = jnp.zeros_like(values[0])
    for layer, value in enumerate(values):
        moved = pltpu.roll(value, layer * REACH, 1) if layer else value
        low = jnp.where(slots == layer, moved, low)
        high = jnp.where(slots == (layer - 1) % count, moved, high)
        ahead = jnp.where(slots == (layer - 2) % count, moved, ahead)
    return low, high, ahead


def corner_kernel(row_even, row_odd, rest_even, rest_odd, low_cols, high_cols, norm_last,
                  _, low_ref, high_ref, next_ref, even_ref, odd_ref, own_ref):
    cols = low_ref.shape[0]
    total = low_cols.shape[0]
    layers = (total - REACH) // REACH
    strip = layers * REACH
    from_low, from_high = sides("gx", row_even[...], row_odd[...])
    rest, _ = sides("gx", rest_even[...], rest_odd[...])
    partial, kept, limit = rest[:layers], rest[layers : 2 * layers], rest[2 * layers :]
    before = [jnp.broadcast_to(partial[layer : layer + 1], (REACH, cols)) for layer in range(layers)]
    packs = [pack_edges(before)] + [
        pack_edges([block[layer * REACH : (layer + 1) * REACH] for layer in range(layers)])
        for block in (from_low, from_high)
    ]
    low, high, ahead = (jnp.concatenate(group, axis=0) for group in zip(*packs))
    low_add = right_product(low, right_constant(low_ref[...]))
    high_add = right_product(high, right_constant(high_ref[...]))
    behind_add = right_product(ahead, right_constant(next_ref[...]))

    lanes = lane_ids((layers, cols))
    level = lax.broadcasted_iota(jnp.int32, (layers, cols), 0)
    corner_limit = jnp.where(lanes == level, limit[:, cols - 1 :], 0.0)
    corner_kept = jnp.where(lanes == layers + level, kept[:, cols - 1 :], 0.0)
    corner = jnp.sum(corner_limit + corner_kept, axis=0, keepdims=True)

    def place(base, add):
        return jnp.concatenate(
            [base[: 2 * REACH] + add[: 2 * REACH], base[2 * REACH : total - REACH],
             base[total - REACH :] + add[2 * REACH :]],
            axis=0,
        )

    low_all = place(low_cols[...], low_add)
    high_all = place(high_cols[:, :cols], high_add[:, :cols])
    last = norm_last[...]
    behind = high_add[:, cols:] + behind_add
    edges = jnp.concatenate([last[: 2 * REACH], last[total - REACH :]], axis=0)
    lanes = lane_ids(behind.shape)
    drop = jnp.where(lanes < layers, behind * edges, 0.0)
    column = place(high_cols[:, cols:], -drop)
    first = column[:REACH] + corner
    main = column[REACH:]
    quarter = strip // 4
    lanes = lane_ids((quarter, cols))
    folded = main[:quarter]
    for part in range(1, 4):
        moved = pltpu.roll(main[part * quarter : (part + 1) * quarter], part * 2 * layers, 1)
        folded = jnp.where(lanes // (2 * layers) == part, moved, folded)
    spare = jnp.zeros((REACH, cols), jnp.float32)
    extra = jnp.zeros((quarter + REACH, cols), jnp.float32)
    send(
        "gy", jnp.concatenate([low_all[REACH:, :cols], low_all[:REACH, :cols], extra, spare], axis=0),
        jnp.concatenate([high_all[REACH:], high_all[:REACH], folded, first, spare], axis=0),
        even_ref, odd_ref,
    )
    own_ref[...] = low_all[:, cols:]


def column_kernel(depth, across, row_even, row_odd, rest_even, rest_odd, threshold, norm, band_ref, _,
                  kept, kept_before, edge_low, edge_high, deep):
    layers, total, cols = across.shape

    def depth_sums(part, values):
        for layer, value in enumerate(depth_smooth(values, depth)):
            deep[layer, part, :] = value

    def step(index, carry):
        for inner in range(2):
            part = pl.ds(pl.multiple_of((2 * index + inner + 2) * REACH, REACH), REACH)
            depth_sums(part, [across[layer, part, :] for layer in range(layers)])
        return carry

    lax.fori_loop(0, (total // REACH - 3) // 2, step, 0)
    for first_row in (0, REACH, total - REACH):
        part = pl.ds(first_row, REACH)
        values = []
        for layer in range(layers):
            if first_row:
                line = pl.ds(layer * REACH, REACH)
                both = sides("gx", row_even[line, :], row_odd[line, :])
            else:
                both = sides("gx", rest_even[pl.ds(layer, 1), :], rest_odd[pl.ds(layer, 1), :])
            values.append(across[layer, part, :] + both[first_row > REACH])
        depth_sums(part, values)

    constant = right_constant(band_ref[...])
    slots = layer_slots((total, cols))
    for layer in range(layers):
        nonlocal_strain = right_product(deep[layer], constant) * norm[...]
        line = pl.ds(2 * layers + layer, 1)
        limit, _ = sides("gx", rest_even[line, :], rest_odd[line, :])
        first = limit - nonlocal_strain[:REACH]
        others = threshold[layer] - nonlocal_strain[REACH:]
        kept_before[layer] = ratio(first)
        kept[layer] = ratio(others)
        moved = jnp.concatenate([first, others], axis=0)
        moved = pltpu.roll(moved, layer * REACH, 1) if layer else moved
        pltpu.store(edge_low, moved, mask=slots == layer)
        pltpu.store(edge_high, moved, mask=slots == (layer - 1) % (cols // REACH))


def final_kernel(stress, strain, plastic, inner, inner_before, edge_low, edge_high, norm_low, norm_high,
                 col_even, col_odd, last_even, last_odd, rest_even, rest_odd, norm_before, own_cols,
                 plastic_out, damage_out, force_out, columns, lows, highs, damage_s, force_s, sums, diffs,
                 copy_sem, sems):
    layers, rows, cols = stress.shape
    whole = pltpu.make_async_copy(plastic, plastic_out, copy_sem)
    whole.start()
    from_low, _ = sides("gy", last_even[...], last_odd[...])
    folded = from_low[REACH : REACH + rows // 4]
    pieces = [from_low[REACH + rows // 4 :], folded]
    for part in range(1, 4):
        pieces.append(pltpu.roll(folded, cols - part * 2 * layers, 1))
    column = jnp.concatenate(pieces, axis=0)
    kept = ratio(column - own_cols[...] * norm_before[...])
    columns[...] = (0.5 * kept) * pltpu.roll(column, cols - layers, 1)

    low, high = edge_ratios(
        (edge_low, edge_high), (last_even, last_odd), (norm_low, norm_high),
        pl.ds(0, REACH), pl.ds(0, REACH),
    )
    lows[pl.ds(0, REACH), :], highs[pl.ds(0, REACH), :] = low, high
    low, high = edge_ratios(
        (edge_low, edge_high), (col_even, col_odd), (norm_low, norm_high),
        pl.ds(0, rows), pl.ds(REACH, rows),
    )
    lows[pl.ds(REACH, rows), :], highs[pl.ds(REACH, rows), :] = low, high

    def copies(layer):
        return (
            pltpu.make_async_copy(damage_s.at[layer], damage_out.at[layer], sems.at[0, layer]),
            pltpu.make_async_copy(force_s.at[0, layer], force_out.at[0, layer], sems.at[1, layer]),
            pltpu.make_async_copy(force_s.at[1, layer], force_out.at[1, layer], sems.at[2, layer]),
        )

    lanes = lane_ids((REACH, cols))

    def stresses(pair):
        for near in range(2):
            layer = 2 * pair + near
            for block in range(rows // REACH + 1):
                extended = pl.ds(block * REACH, REACH)
                at = (layer, pl.ds((block - 1) * REACH if block else 0, REACH), slice(None))
                if block:
                    rest = (stress[at] + strain[at]) - plastic[at]
                else:
                    line = pl.ds(layers + layer, 1)
                    rest, _ = sides("gx", rest_even[line, :], rest_odd[line, :])
                kept = inner[at] if block else inner_before[layer]
                kept = with_edges(kept, layer, lows[extended, :], highs[extended, :])
                value = (0.5 * kept) * rest
                left = jnp.where(
                    lanes == 0,
                    pltpu.roll(columns[extended, :], (cols - layer) % cols, 1),
                    pltpu.roll(value, 1, 1),
                )
                sums[layer, extended, :] = left + value
                diffs[layer, extended, :] = left - value
                if block:
                    damage_s[at] = 1.0 - kept

    def forces(pair):
        for near in range(2):
            layer = 2 * pair + near
            for block in range(rows // REACH):
                at = (layer, pl.ds(block * REACH, REACH), slice(None))
                here, behind = pl.ds((block + 1) * REACH, REACH), pl.ds((block + 1) * REACH - 1, REACH)
                force_s[(0, *at)] = sums[layer, behind, :] - sums[layer, here, :]
                force_s[(1, *at)] = diffs[layer, behind, :] + diffs[layer, here, :]

    def start(pair):
        for near in range(2):
            for copy in copies(2 * pair + near):
                copy.start()

    def step(pair, carry):
        forces(pair - 1)
        stresses(pair)
        start(pair - 1)
        return carry

    stresses(0)
    lax.fori_loop(1, layers // 2, step, 0)
    forces(layers // 2 - 1)
    start(layers // 2 - 1)

    def drain(layer, carry):
        for copy in copies(layer):
            copy.wait()
        return carry

    lax.fori_loop(0, layers, drain, 0)
    whole.wait()


def call(kernel, outs, scratch, nanoseconds, operands, spaces=None, outs_space=pltpu.VMEM, limit=VMEM_BYTES):
    spaces = spaces or [pltpu.VMEM] * len(operands)
    shapes = [out if isinstance(out, jax.ShapeDtypeStruct) else jax.ShapeDtypeStruct(out, jnp.float32)
              for out in outs]
    return pl.pallas_call(
        kernel,
        out_shape=shapes,
        in_specs=[pl.BlockSpec(memory_space=space) for space in spaces],
        out_specs=[pl.BlockSpec(memory_space=outs_space)] * len(outs),
        scratch_shapes=[pltpu.VMEM(s, jnp.float32) if isinstance(s, tuple) else s for s in scratch],
        compiler_params=pltpu.CompilerParams(vmem_limit_bytes=limit),
        cost_estimate=pl.CostEstimate(
            flops=nanoseconds * 1_000_000, bytes_accessed=nanoseconds * 1000, transcendentals=0
        ),
    )(*operands)


def exchange(axis, other, even, odd):
    names = ("gx", "gy")
    count, across = lax.axis_size(axis), lax.axis_size(other)
    stride = {"gx": lax.axis_size("gy"), "gy": 1}
    results = []
    for start, value in ((0, even), (1, odd)):
        pairs = []
        for place in range(count):
            partner = place + 1 if (place - start) % 2 == 0 else place - 1
            for line in range(across):
                target = (partner, line)
                if not 0 <= partner < count:
                    target = (place, line ^ 1 if line ^ 1 < across else line)
                pairs.append((
                    place * stride[axis] + line * stride[other],
                    target[0] * stride[axis] + target[1] * stride[other],
                ))
        results.append(lax.ppermute(value, names, pairs))
    return results


def inverse_weights(axis, places, length):
    extent = length * lax.axis_size(axis)
    places = places + lax.axis_index(axis) * length
    total = jnp.zeros(places.shape, jnp.float32)
    for offset in range(-REACH, REACH + 1):
        inside = (places + offset >= 0) & (places + offset < extent)
        total = total + jnp.where(inside, tap(offset), 0.0)
    return 1.0 / jnp.maximum(total, tap(REACH))


def matrices(layers, rows, cols):
    depth = depth_matrix(layers)
    up, down = band(REACH, REACH, REACH), band(REACH, REACH, -REACH)
    same = np.eye(layers)
    below = np.kron(same, up)
    near = np.concatenate([np.zeros((REACH, REACH)), down], axis=1)
    line = band(1, 2 * REACH, 1 - 2 * REACH)
    above = np.concatenate([np.kron(same, near), np.kron(same, line)], axis=0)
    rows_band = np.concatenate([np.zeros((REACH - 1, rows)), band(1, rows, 1), band(rows, rows)])
    slots = cols // REACH
    low, high, ahead = np.zeros((cols, 2 * cols)), np.zeros((cols, 2 * cols)), np.zeros((cols, cols))
    for source in range(layers):
        own = slice(source * REACH, (source + 1) * REACH)
        first = (source - 1) % slots * REACH
        other = slice(first, first + REACH)
        for layer in range(layers):
            weight = depth[layer, source]
            first = (layer - 1) % slots * REACH
            low[own, first : first + REACH] = weight * up.T
            high[other, layer * REACH : (layer + 1) * REACH] = weight * down.T
            low[own, cols + layer] = [weight * tap(j + 1) for j in range(REACH)]
            high[other, cols + layer] = [weight * tap(REACH - 1 - j) for j in range(REACH)]
            ahead[((source - 2) % slots) * REACH + REACH - 1, layer] = weight * tap(REACH)
    constants = (below, above, rows_band, band(cols, cols), low, high, ahead)
    return depth, [jnp.asarray(matrix, jnp.float32) for matrix in constants]


def local(trial_stress, old_strain, yield_mask, newton_count, damage_threshold):
    layers, rows, cols = trial_stress.shape
    assert layers * REACH == cols == rows and layers & (layers - 1) == 0
    total, strip = rows + REACH, layers * REACH
    depth, constants = matrices(layers, rows, cols)
    below, above, rows_band, cols_band, *columns = constants

    whole, wide, top = (layers, rows, cols), (layers, total, cols), (layers, REACH, cols)
    sent_rows = (strip + 3 * layers, cols)
    sent_cols = (total + rows // 4 + 2 * REACH, cols)
    last_cols = total + rows // 4 + REACH
    spare = (3 * layers, cols)
    packed, packed_two = (total, cols), (total, 2 * cols)

    inputs = stress, strain, _, _ = (trial_stress, old_strain, yield_mask, newton_count)
    threshold = damage_threshold
    edge = [pltpu.VMEM((layers, 2 * REACH, cols), value.dtype) for value in inputs]
    row_even, row_odd, norm, norm_low, norm_high, norm_last, norm_before, rest = call(
        first_edge_kernel, [(strip + REACH, cols)] * 2 + [packed] * 5 + [spare],
        edge + [(strip, cols), pltpu.SemaphoreType.DMA((2, 4))], 1500,
        inputs, [pltpu.HBM] * 4, limit=EDGE_VMEM_BYTES,
    )
    norms = (norm_low, norm_high)
    rest_even = rest_odd = rest
    for outer_no in range(OUTER):
        last = outer_no == OUTER - 1
        if outer_no:
            row_even, row_odd = call(
                edge_kernel, [sent_rows] * 2,
                [(strip, cols), (2 * strip, cols), (2 * layers, cols)], 800,
                (*inputs, threshold, factor, kept, kept_before, edge_low, edge_high, *norms,
                 col_even, col_odd, below, above),
            )
        if not last:
            row_even, row_odd = row_even[:strip], row_odd[:strip]
        row_even, row_odd = exchange("gx", "gy", row_even, row_odd)
        if last:
            rest_even, rest_odd = row_even[strip:], row_odd[strip:]
            row_even, row_odd = row_even[:strip], row_odd[:strip]
        outs = [wide, packed_two, packed_two, whole]
        if outer_no:
            across, low_cols, high_cols, plastic = call(
                main_kernel, outs, [packed] * 5, 4500,
                (*inputs, factor, kept, edge_low, edge_high, *norms, col_even, col_odd, norm_last,
                 fixed, rows_band, *columns),
            )
        else:
            across, low_cols, high_cols, plastic = call(
                first_main_kernel, outs, [packed] * 4, 4500, (*inputs, rows_band, *columns),
            )
        col_even, col_odd, own_cols = call(
            corner_kernel, [sent_cols, sent_cols, packed], [], 400,
            (row_even, row_odd, rest_even, rest_odd, low_cols, high_cols, norm_last, plastic, *columns),
        )
        if not outer_no:
            factor, fixed = call(
                prepare_kernel, [whole, packed], [], 1200, (stress, strain, threshold, col_odd),
            )
        used = last_cols if last else rows
        col_even, col_odd = col_even[:used], col_odd[:used]
        col_even, col_odd = exchange("gy", "gx", col_even, col_odd)
        if last:
            last_even, last_odd = col_even[rows:], col_odd[rows:]
            col_even, col_odd = col_even[:rows], col_odd[:rows]
        kept, kept_before, edge_low, edge_high = call(
            functools.partial(column_kernel, depth), [whole, top, packed, packed], [wide], 1800,
            (across, row_even, row_odd, rest_even, rest_odd, threshold, norm, cols_band, own_cols),
        )
    return tuple(call(
        final_kernel, [whole, whole, (2, *whole)],
        [packed] * 3 + [whole, (2, *whole), wide, wide,
         pltpu.SemaphoreType.DMA(()), pltpu.SemaphoreType.DMA((3, layers))],
        3000,
        (stress, strain, plastic, kept, kept_before, edge_low, edge_high, *norms, col_even, col_odd,
         last_even, last_odd, rest_even, rest_odd, norm_before, own_cols),
        outs_space=pltpu.HBM,
    ))


def solution(mesh):
    split_in = P(None, "gx", "gy")
    return jax.shard_map(
        local,
        mesh=mesh,
        in_specs=(split_in,) * 5,
        out_specs=(split_in, split_in, P(None, None, "gx", "gy")),
        check_vma=False,
    )
```

```python
import functools
import math

import jax
import jax.numpy as jnp
import numpy as np
from jax import lax
from jax.experimental import pallas as pl
from jax.experimental.pallas import tpu as pltpu
from jax.sharding import PartitionSpec as P

OUTER = 3
REACH = 8
RATE = math.log2(math.e) / 0.3
HALF_LN2 = 0.5 * math.log(2.0)
VMEM_BYTES = 24 * 1024 * 1024
EDGE_VMEM_BYTES = 53 * 1024 * 1024


def tap(offset):
    return math.exp(-(offset**2) / 32.0) if abs(offset) <= REACH else 0.0


def band(rows, cols, shift=0):
    return np.array([[tap(c - r + shift) for c in range(cols)] for r in range(rows)])


def depth_matrix(layers):
    weights = band(layers, layers)
    return weights / weights.sum(axis=1, keepdims=True)


def split(value):
    high = value.astype(jnp.bfloat16)
    low = (value - high.astype(jnp.float32)).astype(jnp.bfloat16)
    return high, low


def left_constant(matrix):
    high, low = split(matrix)
    return jnp.concatenate(
        [jnp.concatenate([high, high], axis=1), jnp.concatenate([low, low], axis=1)], axis=0
    )


def right_constant(matrix):
    both = jnp.concatenate(split(matrix), axis=1)
    return jnp.concatenate([both, both], axis=0)


def left_product(constant, value):
    rows = constant.shape[0] // 2
    halves = jnp.concatenate(split(value), axis=0)
    both = jnp.dot(constant, halves, preferred_element_type=jnp.float32)
    return both[:rows] + both[rows:]


def right_product(value, constant):
    cols = constant.shape[1] // 2
    halves = jnp.concatenate(split(value), axis=1)
    both = jnp.dot(halves, constant, preferred_element_type=jnp.float32)
    return both[:, :cols] + both[:, cols:]


def first_factor(strain):
    return 0.8 - 0.2 * jnp.tanh(2.0 * strain - HALF_LN2)


def newton(stress, strain, yields, count, kept, factor):
    top = (stress + strain) - (0.875 + 0.875 * kept)
    shift = 2.0 * top - HALF_LN2
    state = 2.0 * (top - strain)
    drop = 0.1 + 0.1 * kept
    for sweep_no in range(1, 7):
        if sweep_no > 1:
            factor = 0.8 - 0.2 * jnp.tanh(shift - state)
        update = state * factor - drop
        state = update if sweep_no <= 3 else jnp.where(count >= sweep_no, update, state)
    return jnp.where(yields > 0, top - 0.5 * state, strain)


def depth_smooth(layers, matrix):
    count = len(layers)
    half = count // 2
    sums = [layers[k] + layers[count - 1 - k] for k in range(half)]
    diffs = [layers[k] - layers[count - 1 - k] for k in range(half)]
    out = [None] * count
    for row in range(half):
        even = odd = None
        for k in range(half):
            near, far = matrix[row, k], matrix[row, count - 1 - k]
            plus, minus = float(0.5 * (near + far)), float(0.5 * (near - far))
            if plus == 0.0 and minus == 0.0:
                continue
            even = sums[k] * plus if even is None else even + sums[k] * plus
            odd = diffs[k] * minus if odd is None else odd + diffs[k] * minus
        out[row] = even + odd
        out[count - 1 - row] = even - odd
    return out


def lane_ids(shape):
    return lax.broadcasted_iota(jnp.int32, shape, len(shape) - 1)


def on_even(axis):
    return lax.axis_index(axis) % 2 == 0


def sides(axis, even, odd):
    return jnp.where(on_even(axis), odd, even), jnp.where(on_even(axis), even, odd)


def send(axis, low, high, even_ref, odd_ref):
    place = lax.axis_index(axis)
    low = jnp.where(place == 0, 0.0, low)
    high = jnp.where(place == lax.axis_size(axis) - 1, 0.0, high)
    even_ref[...] = jnp.where(on_even(axis), high, low)
    odd_ref[...] = jnp.where(on_even(axis), low, high)


def layer_slots(shape):
    return lane_ids(shape) >> (REACH.bit_length() - 1)


def ratio(limit):
    return jnp.exp2(jnp.minimum(limit, 0.0) * RATE)


def edge_ratios(edges, received, norms, part, extended):
    both = sides("gy", *(ref[part, :] for ref in received))
    return [
        ratio(edge[extended, :] - value * norm[extended, :])
        for edge, value, norm in zip(edges, both, norms)
    ]


def with_edges(inner, layer, low, high):
    cols = inner.shape[1]
    slots = layer_slots(inner.shape)
    packed = jnp.where(slots == layer, low, high)
    shift = (cols - layer * REACH) % cols
    moved = packed if isinstance(layer, int) and layer == 0 else pltpu.roll(packed, shift, 1)
    return jnp.where((slots == 0) | (slots == cols // REACH - 1), moved, inner)


def first_edge_kernel(*refs):
    sources, refs = refs[:4], refs[4:]
    even_ref, odd_ref, norm, norm_low, norm_high, norm_last, norm_before, _, *refs = refs
    targets, (block, sems) = refs[:4], refs[4:]
    stress, strain, yields, count = targets
    layers, rows, cols = sources[0].shape
    copies = []
    for side, first_row in enumerate((0, rows - REACH)):
        for index, (source, target) in enumerate(zip(sources, targets)):
            copies.append(
                pltpu.make_async_copy(
                    source.at[:, pl.ds(first_row, REACH), :],
                    target.at[:, pl.ds(side * REACH, REACH), :],
                    sems.at[side, index],
                )
            )
            copies[-1].start()
    total = rows + REACH
    ids = lax.broadcasted_iota(jnp.int32, (total, cols), 0)
    down = inverse_weights("gx", ids - REACH, rows)
    lanes = lane_ids((REACH, cols))
    within = lanes & (REACH - 1)
    places = (lanes, within, within + (cols - REACH), 0 * lanes + (cols - 1), 0 * lanes - 1)
    for ref, place in zip((norm, norm_low, norm_high, norm_last, norm_before), places):
        ref[...] = down * inverse_weights("gy", place, cols)[:1]
    square = (layers * REACH, layers * REACH)
    line, lane = lax.broadcasted_iota(jnp.int32, square, 0), lane_ids(square)
    steps = (lane & (REACH - 1)) - (line & (REACH - 1))
    band_part = jnp.zeros(square, jnp.float32)
    for step in range(REACH):
        band_part = jnp.where(abs(steps) == step, tap(REACH - step), band_part)
    band_part = jnp.where((line ^ lane) < REACH, band_part, 0.0)
    sent = []
    for side, matrix in enumerate(
        (jnp.where(steps <= 0, band_part, 0.0), jnp.where(steps >= 0, band_part, 0.0))
    ):
        for copy in copies[side * 4 : side * 4 + 4]:
            copy.wait()
        for layer in range(layers):
            at = (layer, pl.ds(side * REACH, REACH), slice(None))
            block[pl.ds(layer * REACH, REACH), :] = newton(
                stress[at], strain[at], yields[at], count[at], jnp.ones((REACH, cols), jnp.float32),
                first_factor(strain[at]),
            )
        product = left_product(left_constant(matrix), block[...])
        sent.append(jnp.concatenate([product, product[:REACH]], axis=0))
    send("gx", *sent, even_ref, odd_ref)


def edge_kernel(stress, strain, yields, count, threshold, factor, kept, _, edge_low, edge_high, norm_low,
                norm_high, col_even, col_odd, below, above,
                even_ref, odd_ref, low_block, high_block, rest):
    layers, rows, cols = stress.shape

    def packed(part, extended):
        return edge_ratios(
            (edge_low, edge_high), (col_even, col_odd), (norm_low, norm_high), part, extended
        )

    part = pl.ds(rows - 2 * REACH, REACH)
    low, high = packed(part, pl.ds(rows - REACH, REACH))
    for layer in range(layers):
        rest[pl.ds(layer, 1), :] = with_edges(kept[layer, part, :], layer, low, high)[REACH - 1 :]
    at = (slice(None), rows - REACH - 1, slice(None))
    single = newton(stress[at], strain[at], yields[at], count[at], rest[pl.ds(0, layers), :], factor[at])

    for first_row, block in ((0, low_block), (rows - REACH, high_block)):
        low, high = packed(pl.ds(first_row, REACH), pl.ds(first_row + REACH, REACH))
        for layer in range(layers):
            at = (layer, pl.ds(first_row, REACH), slice(None))
            ratios = with_edges(kept[at], layer, low, high)
            value = newton(stress[at], strain[at], yields[at], count[at], ratios, factor[at])
            block[pl.ds(layer * REACH, REACH), :] = value
            if first_row:
                left = (stress[at] + strain[at]) - value
                rest[pl.ds(layer, 1), :] = left[REACH - 1 :]
                rest[pl.ds(layers + layer, 1), :] = threshold[at][REACH - 1 :]

    low = left_product(left_constant(below[...]), low_block[...])
    high = left_product(left_constant(above[...]), high_block[...])
    strip = layers * REACH
    spare = jnp.zeros((REACH, cols), jnp.float32)
    extra = jnp.zeros((even_ref.shape[0] - strip, cols), jnp.float32)
    send(
        "gx", jnp.concatenate([low, extra], axis=0),
        jnp.concatenate([high[:strip], high[strip:] + tap(REACH) * single, rest[...], spare], axis=0),
        even_ref, odd_ref,
    )


def first_main_kernel(stress, strain, yields, count, band_ref, low_ref, high_ref, next_ref,
                      across, low_cols, high_cols, plastic, factor, *packs):
    layers, rows, cols = stress.shape
    step_rows = 4 * REACH

    def step(index, carry):
        for near in range(step_rows // REACH):
            part = pl.ds(pl.multiple_of(index * step_rows + near * REACH, REACH), REACH)
            for layer in range(layers):
                at = (layer, part, slice(None))
                lead = first_factor(strain[at])
                factor[at] = lead
                plastic[at] = newton(
                    stress[at], strain[at], yields[at], count[at],
                    jnp.ones((REACH, cols), jnp.float32), lead,
                )
        return carry

    lax.fori_loop(0, rows // step_rows, step, 0)
    smooth_rows(plastic, (band_ref, low_ref, high_ref, next_ref), across, low_cols, high_cols, packs)


def main_kernel(stress, strain, yields, count, factor, kept, edge_low, edge_high, norm_low, norm_high,
                col_even, col_odd, norm_last, fixed, band_ref, low_ref, high_ref, next_ref,
                across, low_cols, high_cols, plastic, pack_last, *packs):
    layers, rows, cols = stress.shape
    total = rows + REACH
    step_rows = 4 * REACH
    lanes = lane_ids((REACH, cols))
    pack_last[pl.ds(0, REACH), :] = jnp.zeros((REACH, cols), jnp.float32)

    def step(index, carry):
        for near in range(step_rows // REACH):
            first = index * step_rows + near * REACH
            part = pl.ds(pl.multiple_of(first, REACH), REACH)
            extended = pl.ds(pl.multiple_of(first + REACH, REACH), REACH)
            packed = edge_ratios(
                (edge_low, edge_high), (col_even, col_odd), (norm_low, norm_high), part, extended
            )
            for layer in range(layers):
                at = (layer, part, slice(None))
                ratios = with_edges(kept[at], layer, *packed)
                value = newton(stress[at], strain[at], yields[at], count[at], ratios, factor[at])
                plastic[at] = value
                lane = layers + layer
                pltpu.store(pack_last.at[extended, :], pltpu.roll(value, lane + 1, 1), mask=lanes == lane)
        return carry

    lax.fori_loop(0, rows // step_rows, step, 0)
    behind = smooth_rows(
        plastic, (band_ref, low_ref, high_ref, next_ref), across, low_cols, high_cols, packs
    )
    drop = behind * norm_last[...]
    first_lanes = lane_ids((total, cols)) < layers
    high_cols[:, cols:] = fixed[...] - jnp.where(first_lanes, drop, pack_last[...])


def smooth_rows(plastic, tables, across, low_cols, high_cols, packs):
    layers, rows, cols = plastic.shape
    total = rows + REACH
    band_ref, low_ref, high_ref, next_ref = tables
    constant = left_constant(band_ref[...])
    slots = layer_slots((total, cols))
    spread = len(packs)
    for layer in range(0, layers, 2):
        pair = jnp.concatenate([plastic[layer], plastic[layer + 1]], axis=1)
        result = left_product(constant, pair)
        for inner in range(2):
            value = result[:, inner * cols : (inner + 1) * cols]
            across[layer + inner] = value
            moved = pltpu.roll(value, (layer + inner) * REACH, 1) if layer + inner else value
            mask = ((layer + inner - slots) & (layers - 1)) < 3
            pltpu.store(packs[(layer + inner) % spread], moved, mask=mask)

    def gathered(behind):
        source = (slots + behind) & (spread - 1)
        parts = packs[0][...]
        for index in range(1, spread):
            parts = jnp.where(source == index, packs[index][...], parts)
        return parts

    low_cols[...] = right_product(gathered(0), right_constant(low_ref[...]))
    high = right_product(gathered(1), right_constant(high_ref[...]))
    behind = right_product(gathered(2), right_constant(next_ref[...]))
    high_cols[:, :cols] = high[:, :cols]
    return high[:, cols:] + behind


def prepare_kernel(stress, strain, threshold, _, fixed):
    layers, rows, cols = stress.shape
    lanes = lane_ids((REACH, cols))
    fixed[...] = jnp.zeros_like(fixed)

    def step(index, carry):
        for near in range(2):
            first = (2 * index + near) * REACH
            part = pl.ds(pl.multiple_of(first, REACH), REACH)
            extended = pl.ds(pl.multiple_of(first + REACH, REACH), REACH)
            for layer in range(layers):
                at = (layer, part, slice(None))
                for lane, value in ((layer, threshold[at]), (layers + layer, stress[at] + strain[at])):
                    moved = pltpu.roll(value, lane + 1, 1)
                    pltpu.store(fixed.at[extended, :], moved, mask=lanes == lane)
        return carry

    lax.fori_loop(0, rows // (2 * REACH), step, 0)


def pack_edges(values):
    cols = values[0].shape[1]
    count = cols // REACH
    slots = layer_slots(values[0].shape)
    low = high = ahead = jnp.zeros_like(values[0])
    for layer, value in enumerate(values):
        moved = pltpu.roll(value, layer * REACH, 1) if layer else value
        low = jnp.where(slots == layer, moved, low)
        high = jnp.where(slots == (layer - 1) % count, moved, high)
        ahead = jnp.where(slots == (layer - 2) % count, moved, ahead)
    return low, high, ahead


def corner_kernel(row_even, row_odd, rest_even, rest_odd, low_cols, high_cols, norm_last,
                  _, low_ref, high_ref, next_ref, even_ref, odd_ref, own_ref):
    cols = low_ref.shape[0]
    total = low_cols.shape[0]
    layers = (total - REACH) // REACH
    strip = layers * REACH
    from_low, from_high = sides("gx", row_even[...], row_odd[...])
    rest, _ = sides("gx", rest_even[...], rest_odd[...])
    partial, kept, limit = rest[:layers], rest[layers : 2 * layers], rest[2 * layers :]
    before = [jnp.broadcast_to(partial[layer : layer + 1], (REACH, cols)) for layer in range(layers)]
    packs = [pack_edges(before)] + [
        pack_edges([block[layer * REACH : (layer + 1) * REACH] for layer in range(layers)])
        for block in (from_low, from_high)
    ]
    low, high, ahead = (jnp.concatenate(group, axis=0) for group in zip(*packs))
    low_add = right_product(low, right_constant(low_ref[...]))
    high_add = right_product(high, right_constant(high_ref[...]))
    behind_add = right_product(ahead, right_constant(next_ref[...]))

    lanes = lane_ids((layers, cols))
    level = lax.broadcasted_iota(jnp.int32, (layers, cols), 0)
    corner_limit = jnp.where(lanes == level, limit[:, cols - 1 :], 0.0)
    corner_kept = jnp.where(lanes == layers + level, kept[:, cols - 1 :], 0.0)
    corner = jnp.sum(corner_limit + corner_kept, axis=0, keepdims=True)

    def place(base, add):
        return jnp.concatenate(
            [base[: 2 * REACH] + add[: 2 * REACH], base[2 * REACH : total - REACH],
             base[total - REACH :] + add[2 * REACH :]],
            axis=0,
        )

    low_all = place(low_cols[...], low_add)
    high_all = place(high_cols[:, :cols], high_add[:, :cols])
    last = norm_last[...]
    behind = high_add[:, cols:] + behind_add
    edges = jnp.concatenate([last[: 2 * REACH], last[total - REACH :]], axis=0)
    lanes = lane_ids(behind.shape)
    drop = jnp.where(lanes < layers, behind * edges, 0.0)
    column = place(high_cols[:, cols:], -drop)
    first = column[:REACH] + corner
    main = column[REACH:]
    quarter = strip // 4
    lanes = lane_ids((quarter, cols))
    folded = main[:quarter]
    for part in range(1, 4):
        moved = pltpu.roll(main[part * quarter : (part + 1) * quarter], part * 2 * layers, 1)
        folded = jnp.where(lanes // (2 * layers) == part, moved, folded)
    spare = jnp.zeros((REACH, cols), jnp.float32)
    extra = jnp.zeros((quarter + REACH, cols), jnp.float32)
    send(
        "gy", jnp.concatenate([low_all[REACH:, :cols], low_all[:REACH, :cols], extra, spare], axis=0),
        jnp.concatenate([high_all[REACH:], high_all[:REACH], folded, first, spare], axis=0),
        even_ref, odd_ref,
    )
    own_ref[...] = low_all[:, cols:]


def column_kernel(depth, across, row_even, row_odd, rest_even, rest_odd, threshold, norm, band_ref, _,
                  kept, kept_before, edge_low, edge_high, deep):
    layers, total, cols = across.shape

    def depth_sums(part, values):
        for layer, value in enumerate(depth_smooth(values, depth)):
            deep[layer, part, :] = value

    def step(index, carry):
        for inner in range(2):
            part = pl.ds(pl.multiple_of((2 * index + inner + 2) * REACH, REACH), REACH)
            depth_sums(part, [across[layer, part, :] for layer in range(layers)])
        return carry

    lax.fori_loop(0, (total // REACH - 3) // 2, step, 0)
    for first_row in (0, REACH, total - REACH):
        part = pl.ds(first_row, REACH)
        values = []
        for layer in range(layers):
            if first_row:
                line = pl.ds(layer * REACH, REACH)
                both = sides("gx", row_even[line, :], row_odd[line, :])
            else:
                both = sides("gx", rest_even[pl.ds(layer, 1), :], rest_odd[pl.ds(layer, 1), :])
            values.append(across[layer, part, :] + both[first_row > REACH])
        depth_sums(part, values)

    constant = right_constant(band_ref[...])
    slots = layer_slots((total, cols))
    for layer in range(layers):
        nonlocal_strain = right_product(deep[layer], constant) * norm[...]
        line = pl.ds(2 * layers + layer, 1)
        limit, _ = sides("gx", rest_even[line, :], rest_odd[line, :])
        first = limit - nonlocal_strain[:REACH]
        others = threshold[layer] - nonlocal_strain[REACH:]
        kept_before[layer] = ratio(first)
        kept[layer] = ratio(others)
        moved = jnp.concatenate([first, others], axis=0)
        moved = pltpu.roll(moved, layer * REACH, 1) if layer else moved
        pltpu.store(edge_low, moved, mask=slots == layer)
        pltpu.store(edge_high, moved, mask=slots == (layer - 1) % (cols // REACH))


def final_kernel(stress, strain, plastic, inner, inner_before, edge_low, edge_high, norm_low, norm_high,
                 col_even, col_odd, last_even, last_odd, rest_even, rest_odd, norm_before, own_cols,
                 plastic_out, damage_out, force_out, columns, lows, highs, damage_s, force_s, sums, diffs,
                 copy_sem, sems):
    layers, rows, cols = stress.shape
    whole = pltpu.make_async_copy(plastic, plastic_out, copy_sem)
    whole.start()
    from_low, _ = sides("gy", last_even[...], last_odd[...])
    folded = from_low[REACH : REACH + rows // 4]
    pieces = [from_low[REACH + rows // 4 :], folded]
    for part in range(1, 4):
        pieces.append(pltpu.roll(folded, cols - part * 2 * layers, 1))
    column = jnp.concatenate(pieces, axis=0)
    kept = ratio(column - own_cols[...] * norm_before[...])
    columns[...] = (0.5 * kept) * pltpu.roll(column, cols - layers, 1)

    low, high = edge_ratios(
        (edge_low, edge_high), (last_even, last_odd), (norm_low, norm_high),
        pl.ds(0, REACH), pl.ds(0, REACH),
    )
    lows[pl.ds(0, REACH), :], highs[pl.ds(0, REACH), :] = low, high
    low, high = edge_ratios(
        (edge_low, edge_high), (col_even, col_odd), (norm_low, norm_high),
        pl.ds(0, rows), pl.ds(REACH, rows),
    )
    lows[pl.ds(REACH, rows), :], highs[pl.ds(REACH, rows), :] = low, high

    def copies(layer):
        return (
            pltpu.make_async_copy(damage_s.at[layer], damage_out.at[layer], sems.at[0, layer]),
            pltpu.make_async_copy(force_s.at[0, layer], force_out.at[0, layer], sems.at[1, layer]),
            pltpu.make_async_copy(force_s.at[1, layer], force_out.at[1, layer], sems.at[2, layer]),
        )

    lanes = lane_ids((REACH, cols))

    def stresses(pair):
        for near in range(2):
            layer = 2 * pair + near
            for block in range(rows // REACH + 1):
                extended = pl.ds(block * REACH, REACH)
                at = (layer, pl.ds((block - 1) * REACH if block else 0, REACH), slice(None))
                if block:
                    rest = (stress[at] + strain[at]) - plastic[at]
                else:
                    line = pl.ds(layers + layer, 1)
                    rest, _ = sides("gx", rest_even[line, :], rest_odd[line, :])
                kept = inner[at] if block else inner_before[layer]
                kept = with_edges(kept, layer, lows[extended, :], highs[extended, :])
                value = (0.5 * kept) * rest
                left = jnp.where(
                    lanes == 0,
                    pltpu.roll(columns[extended, :], (cols - layer) % cols, 1),
                    pltpu.roll(value, 1, 1),
                )
                sums[layer, extended, :] = left + value
                diffs[layer, extended, :] = left - value
                if block:
                    damage_s[at] = 1.0 - kept

    def forces(pair):
        for near in range(2):
            layer = 2 * pair + near
            for block in range(rows // REACH):
                at = (layer, pl.ds(block * REACH, REACH), slice(None))
                here, behind = pl.ds((block + 1) * REACH, REACH), pl.ds((block + 1) * REACH - 1, REACH)
                force_s[(0, *at)] = sums[layer, behind, :] - sums[layer, here, :]
                force_s[(1, *at)] = diffs[layer, behind, :] + diffs[layer, here, :]

    def start(pair):
        for near in range(2):
            for copy in copies(2 * pair + near):
                copy.start()

    def step(pair, carry):
        forces(pair - 1)
        stresses(pair)
        start(pair - 1)
        return carry

    stresses(0)
    lax.fori_loop(1, layers // 2, step, 0)
    forces(layers // 2 - 1)
    start(layers // 2 - 1)

    def drain(layer, carry):
        for copy in copies(layer):
            copy.wait()
        return carry

    lax.fori_loop(0, layers, drain, 0)
    whole.wait()


def call(kernel, outs, scratch, nanoseconds, operands, spaces=None, outs_space=pltpu.VMEM, limit=VMEM_BYTES):
    spaces = spaces or [pltpu.VMEM] * len(operands)
    shapes = [out if isinstance(out, jax.ShapeDtypeStruct) else jax.ShapeDtypeStruct(out, jnp.float32)
              for out in outs]
    return pl.pallas_call(
        kernel,
        out_shape=shapes,
        in_specs=[pl.BlockSpec(memory_space=space) for space in spaces],
        out_specs=[pl.BlockSpec(memory_space=outs_space)] * len(outs),
        scratch_shapes=[pltpu.VMEM(s, jnp.float32) if isinstance(s, tuple) else s for s in scratch],
        compiler_params=pltpu.CompilerParams(vmem_limit_bytes=limit),
        cost_estimate=pl.CostEstimate(
            flops=nanoseconds * 1_000_000, bytes_accessed=nanoseconds * 1000, transcendentals=0
        ),
    )(*operands)


def exchange(axis, other, even, odd):
    names = ("gx", "gy")
    count, across = lax.axis_size(axis), lax.axis_size(other)
    stride = {"gx": lax.axis_size("gy"), "gy": 1}
    results = []
    for start, value in ((0, even), (1, odd)):
        pairs = []
        for place in range(count):
            partner = place + 1 if (place - start) % 2 == 0 else place - 1
            for line in range(across):
                target = (partner, line)
                if not 0 <= partner < count:
                    target = (place, line ^ 1 if line ^ 1 < across else line)
                pairs.append((
                    place * stride[axis] + line * stride[other],
                    target[0] * stride[axis] + target[1] * stride[other],
                ))
        results.append(lax.ppermute(value, names, pairs))
    return results


def inverse_weights(axis, places, length):
    extent = length * lax.axis_size(axis)
    places = places + lax.axis_index(axis) * length
    total = jnp.zeros(places.shape, jnp.float32)
    for offset in range(-REACH, REACH + 1):
        inside = (places + offset >= 0) & (places + offset < extent)
        total = total + jnp.where(inside, tap(offset), 0.0)
    return 1.0 / jnp.maximum(total, tap(REACH))


def matrices(layers, rows, cols):
    depth = depth_matrix(layers)
    up, down = band(REACH, REACH, REACH), band(REACH, REACH, -REACH)
    same = np.eye(layers)
    below = np.kron(same, up)
    above = np.concatenate([np.kron(same, down), np.kron(same, band(1, REACH, 1 - REACH))], axis=0)
    rows_band = np.concatenate([np.zeros((REACH - 1, rows)), band(1, rows, 1), band(rows, rows)])
    slots = cols // REACH
    low, high, ahead = np.zeros((cols, 2 * cols)), np.zeros((cols, 2 * cols)), np.zeros((cols, cols))
    for source in range(layers):
        own = slice(source * REACH, (source + 1) * REACH)
        first = (source - 1) % slots * REACH
        other = slice(first, first + REACH)
        for layer in range(layers):
            weight = depth[layer, source]
            first = (layer - 1) % slots * REACH
            low[own, first : first + REACH] = weight * up.T
            high[other, layer * REACH : (layer + 1) * REACH] = weight * down.T
            low[own, cols + layer] = [weight * tap(j + 1) for j in range(REACH)]
            high[other, cols + layer] = [weight * tap(REACH - 1 - j) for j in range(REACH)]
            ahead[((source - 2) % slots) * REACH + REACH - 1, layer] = weight * tap(REACH)
    constants = (below, above, rows_band, band(cols, cols), low, high, ahead)
    return depth, [jnp.asarray(matrix, jnp.float32) for matrix in constants]


def local(trial_stress, old_strain, yield_mask, newton_count, damage_threshold):
    layers, rows, cols = trial_stress.shape
    assert layers * REACH == cols == rows and layers & (layers - 1) == 0
    total, strip = rows + REACH, layers * REACH
    depth, constants = matrices(layers, rows, cols)
    below, above, rows_band, cols_band, *columns = constants

    whole, wide, top = (layers, rows, cols), (layers, total, cols), (layers, REACH, cols)
    last_rows = strip + 3 * layers
    sent_rows = (last_rows + REACH, cols)
    sent_cols = (total + rows // 4 + 2 * REACH, cols)
    last_cols = total + rows // 4 + REACH
    spare = (3 * layers, cols)
    packed, packed_two = (total, cols), (total, 2 * cols)

    inputs = stress, strain, _, _ = (trial_stress, old_strain, yield_mask, newton_count)
    threshold = damage_threshold
    edge = [pltpu.VMEM((layers, 2 * REACH, cols), value.dtype) for value in inputs]
    row_even, row_odd, norm, norm_low, norm_high, norm_last, norm_before, rest = call(
        first_edge_kernel, [(strip + REACH, cols)] * 2 + [packed] * 5 + [spare],
        edge + [(strip, cols), pltpu.SemaphoreType.DMA((2, 4))], 1500,
        inputs, [pltpu.HBM] * 4, limit=EDGE_VMEM_BYTES,
    )
    norms = (norm_low, norm_high)
    rest_even = rest_odd = rest
    for outer_no in range(OUTER):
        last = outer_no == OUTER - 1
        if outer_no:
            row_even, row_odd = call(
                edge_kernel, [sent_rows] * 2,
                [(strip, cols), (strip, cols), (2 * layers, cols)], 800,
                (*inputs, threshold, factor, kept, kept_before, edge_low, edge_high, *norms,
                 col_even, col_odd, below, above),
            )
        used = last_rows if last else strip
        row_even, row_odd = row_even[:used], row_odd[:used]
        row_even, row_odd = exchange("gx", "gy", row_even, row_odd)
        if last:
            rest_even, rest_odd = row_even[strip:], row_odd[strip:]
            row_even, row_odd = row_even[:strip], row_odd[:strip]
        outs = [wide, packed_two, packed_two, whole]
        if outer_no:
            across, low_cols, high_cols, plastic = call(
                main_kernel, outs, [packed] * 5, 4500,
                (*inputs, factor, kept, edge_low, edge_high, *norms, col_even, col_odd, norm_last,
                 fixed, rows_band, *columns),
            )
        else:
            across, low_cols, high_cols, plastic, factor = call(
                first_main_kernel, outs + [whole], [packed] * 4, 4500, (*inputs, rows_band, *columns),
            )
        col_even, col_odd, own_cols = call(
            corner_kernel, [sent_cols, sent_cols, packed], [], 400,
            (row_even, row_odd, rest_even, rest_odd, low_cols, high_cols, norm_last, plastic, *columns),
        )
        if not outer_no:
            (fixed,) = call(prepare_kernel, [packed], [], 800, (stress, strain, threshold, col_odd))
        used = last_cols if last else rows
        col_even, col_odd = col_even[:used], col_odd[:used]
        col_even, col_odd = exchange("gy", "gx", col_even, col_odd)
        if last:
            last_even, last_odd = col_even[rows:], col_odd[rows:]
            col_even, col_odd = col_even[:rows], col_odd[:rows]
        kept, kept_before, edge_low, edge_high = call(
            functools.partial(column_kernel, depth), [whole, top, packed, packed], [wide], 1800,
            (across, row_even, row_odd, rest_even, rest_odd, threshold, norm, cols_band, own_cols),
        )
    return tuple(call(
        final_kernel, [whole, whole, (2, *whole)],
        [packed] * 3 + [whole, (2, *whole), wide, wide,
         pltpu.SemaphoreType.DMA(()), pltpu.SemaphoreType.DMA((3, layers))],
        3000,
        (stress, strain, plastic, kept, kept_before, edge_low, edge_high, *norms, col_even, col_odd,
         last_even, last_odd, rest_even, rest_odd, norm_before, own_cols),
        outs_space=pltpu.HBM,
    ))


def solution(mesh):
    split_in = P(None, "gx", "gy")
    return jax.shard_map(
        local,
        mesh=mesh,
        in_specs=(split_in,) * 5,
        out_specs=(split_in, split_in, P(None, None, "gx", "gy")),
        check_vma=False,
    )
```

```python
import functools
import math

import jax
import jax.numpy as jnp
import numpy as np
from jax import lax
from jax.experimental import pallas as pl
from jax.experimental.pallas import tpu as pltpu
from jax.sharding import PartitionSpec as P

OUTER = 3
REACH = 8
RATE = math.log2(math.e) / 0.3
HALF_LN2 = 0.5 * math.log(2.0)
VMEM_BYTES = 24 * 1024 * 1024
EDGE_VMEM_BYTES = 53 * 1024 * 1024


def tap(offset):
    return math.exp(-(offset**2) / 32.0) if abs(offset) <= REACH else 0.0


def band(rows, cols, shift=0):
    return np.array([[tap(c - r + shift) for c in range(cols)] for r in range(rows)])


def depth_matrix(layers):
    weights = band(layers, layers)
    return weights / weights.sum(axis=1, keepdims=True)


def split(value):
    high = value.astype(jnp.bfloat16)
    low = (value - high.astype(jnp.float32)).astype(jnp.bfloat16)
    return high, low


def left_constant(matrix):
    high, low = split(matrix)
    return jnp.concatenate(
        [jnp.concatenate([high, high], axis=1), jnp.concatenate([low, low], axis=1)], axis=0
    )


def right_constant(matrix):
    both = jnp.concatenate(split(matrix), axis=1)
    return jnp.concatenate([both, both], axis=0)


def left_product(constant, value):
    rows = constant.shape[0] // 2
    halves = jnp.concatenate(split(value), axis=0)
    both = jnp.dot(constant, halves, preferred_element_type=jnp.float32)
    return both[:rows] + both[rows:]


def right_product(value, constant):
    cols = constant.shape[1] // 2
    halves = jnp.concatenate(split(value), axis=1)
    both = jnp.dot(halves, constant, preferred_element_type=jnp.float32)
    return both[:, :cols] + both[:, cols:]


def first_factor(strain):
    return 0.8 - 0.2 * jnp.tanh(2.0 * strain - HALF_LN2)


def newton(stress, strain, yields, count, kept, factor):
    top = (stress + strain) - (0.875 + 0.875 * kept)
    shift = 2.0 * top - HALF_LN2
    state = 2.0 * (top - strain)
    drop = 0.1 + 0.1 * kept
    for sweep_no in range(1, 7):
        if sweep_no > 1:
            factor = 0.8 - 0.2 * jnp.tanh(shift - state)
        update = state * factor - drop
        state = update if sweep_no <= 3 else jnp.where(count >= sweep_no, update, state)
    return jnp.where(yields > 0, top - 0.5 * state, strain)


def depth_smooth(layers, matrix):
    count = len(layers)
    half = count // 2
    sums = [layers[k] + layers[count - 1 - k] for k in range(half)]
    diffs = [layers[k] - layers[count - 1 - k] for k in range(half)]
    out = [None] * count
    for row in range(half):
        even = odd = None
        for k in range(half):
            near, far = matrix[row, k], matrix[row, count - 1 - k]
            plus, minus = float(0.5 * (near + far)), float(0.5 * (near - far))
            if plus == 0.0 and minus == 0.0:
                continue
            even = sums[k] * plus if even is None else even + sums[k] * plus
            odd = diffs[k] * minus if odd is None else odd + diffs[k] * minus
        out[row] = even + odd
        out[count - 1 - row] = even - odd
    return out


def lane_ids(shape):
    return lax.broadcasted_iota(jnp.int32, shape, len(shape) - 1)


def on_even(axis):
    return lax.axis_index(axis) % 2 == 0


def sides(axis, even, odd):
    return jnp.where(on_even(axis), odd, even), jnp.where(on_even(axis), even, odd)


def send(axis, low, high, even_ref, odd_ref):
    place = lax.axis_index(axis)
    low = jnp.where(place == 0, 0.0, low)
    high = jnp.where(place == lax.axis_size(axis) - 1, 0.0, high)
    even_ref[...] = jnp.where(on_even(axis), high, low)
    odd_ref[...] = jnp.where(on_even(axis), low, high)


def layer_slots(shape):
    return lane_ids(shape) >> (REACH.bit_length() - 1)


def ratio(limit):
    return jnp.exp2(jnp.minimum(limit, 0.0) * RATE)


def edge_ratios(edges, received, norms, part, extended):
    both = sides("gy", *(ref[part, :] for ref in received))
    return [
        ratio(edge[extended, :] - value * norm[extended, :])
        for edge, value, norm in zip(edges, both, norms)
    ]


def with_edges(inner, layer, low, high):
    cols = inner.shape[1]
    slots = layer_slots(inner.shape)
    packed = jnp.where(slots == layer, low, high)
    shift = (cols - layer * REACH) % cols
    moved = packed if isinstance(layer, int) and layer == 0 else pltpu.roll(packed, shift, 1)
    return jnp.where((slots == 0) | (slots == cols // REACH - 1), moved, inner)


def first_edge_kernel(*refs):
    sources, refs = refs[:4], refs[4:]
    even_ref, odd_ref, norm, norm_low, norm_high, norm_last, norm_before, _, *refs = refs
    targets, (block, sems) = refs[:4], refs[4:]
    stress, strain, yields, count = targets
    layers, rows, cols = sources[0].shape
    copies = []
    for side, first_row in enumerate((0, rows - REACH)):
        for index, (source, target) in enumerate(zip(sources, targets)):
            copies.append(
                pltpu.make_async_copy(
                    source.at[:, pl.ds(first_row, REACH), :],
                    target.at[:, pl.ds(side * REACH, REACH), :],
                    sems.at[side, index],
                )
            )
            copies[-1].start()
    total = rows + REACH
    ids = lax.broadcasted_iota(jnp.int32, (total, cols), 0)
    down = inverse_weights("gx", ids - REACH, rows)
    lanes = lane_ids((REACH, cols))
    within = lanes & (REACH - 1)
    places = (lanes, within, within + (cols - REACH), 0 * lanes + (cols - 1), 0 * lanes - 1)
    for ref, place in zip((norm, norm_low, norm_high, norm_last, norm_before), places):
        ref[...] = down * inverse_weights("gy", place, cols)[:1]
    square = (layers * REACH, layers * REACH)
    line, lane = lax.broadcasted_iota(jnp.int32, square, 0), lane_ids(square)
    steps = (lane & (REACH - 1)) - (line & (REACH - 1))
    band_part = jnp.zeros(square, jnp.float32)
    for step in range(REACH):
        band_part = jnp.where(abs(steps) == step, tap(REACH - step), band_part)
    band_part = jnp.where((line ^ lane) < REACH, band_part, 0.0)
    sent = []
    for side, matrix in enumerate(
        (jnp.where(steps <= 0, band_part, 0.0), jnp.where(steps >= 0, band_part, 0.0))
    ):
        for copy in copies[side * 4 : side * 4 + 4]:
            copy.wait()
        for layer in range(layers):
            at = (layer, pl.ds(side * REACH, REACH), slice(None))
            block[pl.ds(layer * REACH, REACH), :] = newton(
                stress[at], strain[at], yields[at], count[at], jnp.ones((REACH, cols), jnp.float32),
                first_factor(strain[at]),
            )
        product = left_product(left_constant(matrix), block[...])
        sent.append(jnp.concatenate([product, product[:REACH]], axis=0))
    send("gx", *sent, even_ref, odd_ref)


def edge_kernel(stress, strain, yields, count, threshold, factor, kept, _, edge_low, edge_high, norm_low,
                norm_high, col_even, col_odd, below, above,
                even_ref, odd_ref, low_block, high_block, rest):
    layers, rows, cols = stress.shape

    def packed(part, extended):
        return edge_ratios(
            (edge_low, edge_high), (col_even, col_odd), (norm_low, norm_high), part, extended
        )

    part = pl.ds(rows - 2 * REACH, REACH)
    low, high = packed(part, pl.ds(rows - REACH, REACH))
    for layer in range(layers):
        rest[pl.ds(layer, 1), :] = with_edges(kept[layer, part, :], layer, low, high)[REACH - 1 :]
    at = (slice(None), rows - REACH - 1, slice(None))
    single = newton(stress[at], strain[at], yields[at], count[at], rest[pl.ds(0, layers), :], factor[at])

    for first_row, block in ((0, low_block), (rows - REACH, high_block)):
        low, high = packed(pl.ds(first_row, REACH), pl.ds(first_row + REACH, REACH))
        for layer in range(layers):
            at = (layer, pl.ds(first_row, REACH), slice(None))
            ratios = with_edges(kept[at], layer, low, high)
            value = newton(stress[at], strain[at], yields[at], count[at], ratios, factor[at])
            block[pl.ds(layer * REACH, REACH), :] = value
            if first_row:
                left = (stress[at] + strain[at]) - value
                rest[pl.ds(layer, 1), :] = left[REACH - 1 :]
                rest[pl.ds(layers + layer, 1), :] = threshold[at][REACH - 1 :]

    low = left_product(left_constant(below[...]), low_block[...])
    high = left_product(left_constant(above[...]), high_block[...])
    strip = layers * REACH
    extra = jnp.zeros((even_ref.shape[0] - strip, cols), jnp.float32)
    send(
        "gx", jnp.concatenate([low, extra], axis=0),
        jnp.concatenate([high[:strip], high[strip:] + tap(REACH) * single, rest[...]], axis=0),
        even_ref, odd_ref,
    )


def first_main_kernel(stress, strain, yields, count, band_ref, low_ref, high_ref, next_ref,
                      across, low_cols, high_cols, plastic, factor, *packs):
    layers, rows, cols = stress.shape
    step_rows = 4 * REACH

    def step(index, carry):
        for near in range(step_rows // REACH):
            part = pl.ds(pl.multiple_of(index * step_rows + near * REACH, REACH), REACH)
            for layer in range(layers):
                at = (layer, part, slice(None))
                lead = first_factor(strain[at])
                factor[at] = lead
                plastic[at] = newton(
                    stress[at], strain[at], yields[at], count[at],
                    jnp.ones((REACH, cols), jnp.float32), lead,
                )
        return carry

    lax.fori_loop(0, rows // step_rows, step, 0)
    smooth_rows(plastic, (band_ref, low_ref, high_ref, next_ref), across, low_cols, high_cols, packs)


def main_kernel(stress, strain, yields, count, factor, kept, edge_low, edge_high, norm_low, norm_high,
                col_even, col_odd, norm_last, fixed, band_ref, low_ref, high_ref, next_ref,
                across, low_cols, high_cols, plastic, pack_last, *packs):
    layers, rows, cols = stress.shape
    total = rows + REACH
    step_rows = 4 * REACH
    lanes = lane_ids((REACH, cols))
    pack_last[pl.ds(0, REACH), :] = jnp.zeros((REACH, cols), jnp.float32)

    def step(index, carry):
        for near in range(step_rows // REACH):
            first = index * step_rows + near * REACH
            part = pl.ds(pl.multiple_of(first, REACH), REACH)
            extended = pl.ds(pl.multiple_of(first + REACH, REACH), REACH)
            packed = edge_ratios(
                (edge_low, edge_high), (col_even, col_odd), (norm_low, norm_high), part, extended
            )
            for layer in range(layers):
                at = (layer, part, slice(None))
                ratios = with_edges(kept[at], layer, *packed)
                value = newton(stress[at], strain[at], yields[at], count[at], ratios, factor[at])
                plastic[at] = value
                lane = layers + layer
                pltpu.store(pack_last.at[extended, :], pltpu.roll(value, lane + 1, 1), mask=lanes == lane)
        return carry

    lax.fori_loop(0, rows // step_rows, step, 0)
    behind = smooth_rows(
        plastic, (band_ref, low_ref, high_ref, next_ref), across, low_cols, high_cols, packs
    )
    drop = behind * norm_last[...]
    first_lanes = lane_ids((total, cols)) < layers
    high_cols[:, cols:] = fixed[...] - jnp.where(first_lanes, drop, pack_last[...])


def smooth_rows(plastic, tables, across, low_cols, high_cols, packs):
    layers, rows, cols = plastic.shape
    total = rows + REACH
    band_ref, low_ref, high_ref, next_ref = tables
    constant = left_constant(band_ref[...])
    slots = layer_slots((total, cols))
    spread = len(packs)
    for layer in range(0, layers, 2):
        pair = jnp.concatenate([plastic[layer], plastic[layer + 1]], axis=1)
        result = left_product(constant, pair)
        for inner in range(2):
            value = result[:, inner * cols : (inner + 1) * cols]
            across[layer + inner] = value
            moved = pltpu.roll(value, (layer + inner) * REACH, 1) if layer + inner else value
            mask = ((layer + inner - slots) & (layers - 1)) < 3
            pltpu.store(packs[(layer + inner) % spread], moved, mask=mask)

    def gathered(behind):
        source = (slots + behind) & (spread - 1)
        parts = packs[0][...]
        for index in range(1, spread):
            parts = jnp.where(source == index, packs[index][...], parts)
        return parts

    low_cols[...] = right_product(gathered(0), right_constant(low_ref[...]))
    high = right_product(gathered(1), right_constant(high_ref[...]))
    behind = right_product(gathered(2), right_constant(next_ref[...]))
    high_cols[:, :cols] = high[:, :cols]
    return high[:, cols:] + behind


def prepare_kernel(stress, strain, threshold, _, fixed):
    layers, rows, cols = stress.shape
    lanes = lane_ids((REACH, cols))
    fixed[...] = jnp.zeros_like(fixed)

    def step(index, carry):
        for near in range(2):
            first = (2 * index + near) * REACH
            part = pl.ds(pl.multiple_of(first, REACH), REACH)
            extended = pl.ds(pl.multiple_of(first + REACH, REACH), REACH)
            for layer in range(layers):
                at = (layer, part, slice(None))
                for lane, value in ((layer, threshold[at]), (layers + layer, stress[at] + strain[at])):
                    moved = pltpu.roll(value, lane + 1, 1)
                    pltpu.store(fixed.at[extended, :], moved, mask=lanes == lane)
        return carry

    lax.fori_loop(0, rows // (2 * REACH), step, 0)


def pack_edges(values):
    cols = values[0].shape[1]
    count = cols // REACH
    slots = layer_slots(values[0].shape)
    low = high = ahead = jnp.zeros_like(values[0])
    for layer, value in enumerate(values):
        moved = pltpu.roll(value, layer * REACH, 1) if layer else value
        low = jnp.where(slots == layer, moved, low)
        high = jnp.where(slots == (layer - 1) % count, moved, high)
        ahead = jnp.where(slots == (layer - 2) % count, moved, ahead)
    return low, high, ahead


def corner_kernel(row_even, row_odd, rest_even, rest_odd, low_cols, high_cols, norm_last,
                  _, low_ref, high_ref, next_ref, even_ref, odd_ref, own_ref):
    cols = low_ref.shape[0]
    total = low_cols.shape[0]
    layers = (total - REACH) // REACH
    strip = layers * REACH
    from_low, from_high = sides("gx", row_even[...], row_odd[...])
    rest, _ = sides("gx", rest_even[...], rest_odd[...])
    partial, kept, limit = rest[:layers], rest[layers : 2 * layers], rest[2 * layers :]
    before = [jnp.broadcast_to(partial[layer : layer + 1], (REACH, cols)) for layer in range(layers)]
    packs = [pack_edges(before)] + [
        pack_edges([block[layer * REACH : (layer + 1) * REACH] for layer in range(layers)])
        for block in (from_low, from_high)
    ]
    low, high, ahead = (jnp.concatenate(group, axis=0) for group in zip(*packs))
    low_add = right_product(low, right_constant(low_ref[...]))
    high_add = right_product(high, right_constant(high_ref[...]))
    behind_add = right_product(ahead, right_constant(next_ref[...]))

    lanes = lane_ids((layers, cols))
    level = lax.broadcasted_iota(jnp.int32, (layers, cols), 0)
    corner_limit = jnp.where(lanes == level, limit[:, cols - 1 :], 0.0)
    corner_kept = jnp.where(lanes == layers + level, kept[:, cols - 1 :], 0.0)
    corner = jnp.sum(corner_limit + corner_kept, axis=0, keepdims=True)

    def place(base, add):
        return jnp.concatenate(
            [base[: 2 * REACH] + add[: 2 * REACH], base[2 * REACH : total - REACH],
             base[total - REACH :] + add[2 * REACH :]],
            axis=0,
        )

    low_all = place(low_cols[...], low_add)
    high_all = place(high_cols[:, :cols], high_add[:, :cols])
    last = norm_last[...]
    behind = high_add[:, cols:] + behind_add
    edges = jnp.concatenate([last[: 2 * REACH], last[total - REACH :]], axis=0)
    lanes = lane_ids(behind.shape)
    drop = jnp.where(lanes < layers, behind * edges, 0.0)
    column = place(high_cols[:, cols:], -drop)
    first = column[:REACH] + corner
    main = column[REACH:]
    quarter = strip // 4
    lanes = lane_ids((quarter, cols))
    folded = main[:quarter]
    for part in range(1, 4):
        moved = pltpu.roll(main[part * quarter : (part + 1) * quarter], part * 2 * layers, 1)
        folded = jnp.where(lanes // (2 * layers) == part, moved, folded)
    spare = jnp.zeros((REACH, cols), jnp.float32)
    extra = jnp.zeros((quarter + REACH, cols), jnp.float32)
    send(
        "gy", jnp.concatenate([low_all[REACH:, :cols], low_all[:REACH, :cols], extra, spare], axis=0),
        jnp.concatenate([high_all[REACH:], high_all[:REACH], folded, first, spare], axis=0),
        even_ref, odd_ref,
    )
    own_ref[...] = low_all[:, cols:]


def column_kernel(depth, across, row_even, row_odd, rest_even, rest_odd, threshold, norm, band_ref, _,
                  kept, kept_before, edge_low, edge_high, deep):
    layers, total, cols = across.shape

    def depth_sums(part, values):
        for layer, value in enumerate(depth_smooth(values, depth)):
            deep[layer, part, :] = value

    def step(index, carry):
        for inner in range(2):
            part = pl.ds(pl.multiple_of((2 * index + inner + 2) * REACH, REACH), REACH)
            depth_sums(part, [across[layer, part, :] for layer in range(layers)])
        return carry

    lax.fori_loop(0, (total // REACH - 3) // 2, step, 0)
    for first_row in (0, REACH, total - REACH):
        part = pl.ds(first_row, REACH)
        values = []
        for layer in range(layers):
            if first_row:
                line = pl.ds(layer * REACH, REACH)
                both = sides("gx", row_even[line, :], row_odd[line, :])
            else:
                both = sides("gx", rest_even[pl.ds(layer, 1), :], rest_odd[pl.ds(layer, 1), :])
            values.append(across[layer, part, :] + both[first_row > REACH])
        depth_sums(part, values)

    constant = right_constant(band_ref[...])
    slots = layer_slots((total, cols))
    for layer in range(layers):
        nonlocal_strain = right_product(deep[layer], constant) * norm[...]
        line = pl.ds(2 * layers + layer, 1)
        limit, _ = sides("gx", rest_even[line, :], rest_odd[line, :])
        first = limit - nonlocal_strain[:REACH]
        others = threshold[layer] - nonlocal_strain[REACH:]
        kept_before[layer] = ratio(first)
        kept[layer] = ratio(others)
        moved = jnp.concatenate([first, others], axis=0)
        moved = pltpu.roll(moved, layer * REACH, 1) if layer else moved
        pltpu.store(edge_low, moved, mask=slots == layer)
        pltpu.store(edge_high, moved, mask=slots == (layer - 1) % (cols // REACH))


def final_kernel(stress, strain, plastic, inner, inner_before, edge_low, edge_high, norm_low, norm_high,
                 col_even, col_odd, last_even, last_odd, rest_even, rest_odd, norm_before, own_cols,
                 plastic_out, damage_out, force_out, columns, lows, highs, damage_s, force_s, sums, diffs,
                 copy_sem, sems):
    layers, rows, cols = stress.shape
    whole = pltpu.make_async_copy(plastic, plastic_out, copy_sem)
    whole.start()
    from_low, _ = sides("gy", last_even[...], last_odd[...])
    folded = from_low[REACH : REACH + rows // 4]
    pieces = [from_low[REACH + rows // 4 :], folded]
    for part in range(1, 4):
        pieces.append(pltpu.roll(folded, cols - part * 2 * layers, 1))
    column = jnp.concatenate(pieces, axis=0)
    kept = ratio(column - own_cols[...] * norm_before[...])
    columns[...] = (0.5 * kept) * pltpu.roll(column, cols - layers, 1)

    low, high = edge_ratios(
        (edge_low, edge_high), (last_even, last_odd), (norm_low, norm_high),
        pl.ds(0, REACH), pl.ds(0, REACH),
    )
    lows[pl.ds(0, REACH), :], highs[pl.ds(0, REACH), :] = low, high
    low, high = edge_ratios(
        (edge_low, edge_high), (col_even, col_odd), (norm_low, norm_high),
        pl.ds(0, rows), pl.ds(REACH, rows),
    )
    lows[pl.ds(REACH, rows), :], highs[pl.ds(REACH, rows), :] = low, high

    def copies(layer):
        return (
            pltpu.make_async_copy(damage_s.at[layer], damage_out.at[layer], sems.at[0, layer]),
            pltpu.make_async_copy(force_s.at[0, layer], force_out.at[0, layer], sems.at[1, layer]),
            pltpu.make_async_copy(force_s.at[1, layer], force_out.at[1, layer], sems.at[2, layer]),
        )

    lanes = lane_ids((REACH, cols))

    def stresses(pair):
        for near in range(2):
            layer = 2 * pair + near
            for block in range(rows // REACH + 1):
                extended = pl.ds(block * REACH, REACH)
                at = (layer, pl.ds((block - 1) * REACH if block else 0, REACH), slice(None))
                if block:
                    rest = (stress[at] + strain[at]) - plastic[at]
                else:
                    line = pl.ds(layers + layer, 1)
                    rest, _ = sides("gx", rest_even[line, :], rest_odd[line, :])
                kept = inner[at] if block else inner_before[layer]
                kept = with_edges(kept, layer, lows[extended, :], highs[extended, :])
                value = (0.5 * kept) * rest
                left = jnp.where(
                    lanes == 0,
                    pltpu.roll(columns[extended, :], (cols - layer) % cols, 1),
                    pltpu.roll(value, 1, 1),
                )
                sums[layer, extended, :] = left + value
                diffs[layer, extended, :] = left - value
                if block:
                    damage_s[at] = 1.0 - kept

    def forces(pair):
        for near in range(2):
            layer = 2 * pair + near
            for block in range(rows // REACH):
                at = (layer, pl.ds(block * REACH, REACH), slice(None))
                here, behind = pl.ds((block + 1) * REACH, REACH), pl.ds((block + 1) * REACH - 1, REACH)
                force_s[(0, *at)] = sums[layer, behind, :] - sums[layer, here, :]
                force_s[(1, *at)] = diffs[layer, behind, :] + diffs[layer, here, :]

    def start(pair):
        for near in range(2):
            for copy in copies(2 * pair + near):
                copy.start()

    def step(pair, carry):
        forces(pair - 1)
        stresses(pair)
        start(pair - 1)
        return carry

    stresses(0)
    lax.fori_loop(1, layers // 2, step, 0)
    forces(layers // 2 - 1)
    start(layers // 2 - 1)

    def drain(layer, carry):
        for copy in copies(layer):
            copy.wait()
        return carry

    lax.fori_loop(0, layers, drain, 0)
    whole.wait()


def call(kernel, outs, scratch, nanoseconds, operands, spaces=None, outs_space=pltpu.VMEM, limit=VMEM_BYTES):
    spaces = spaces or [pltpu.VMEM] * len(operands)
    shapes = [out if isinstance(out, jax.ShapeDtypeStruct) else jax.ShapeDtypeStruct(out, jnp.float32)
              for out in outs]
    return pl.pallas_call(
        kernel,
        out_shape=shapes,
        in_specs=[pl.BlockSpec(memory_space=space) for space in spaces],
        out_specs=[pl.BlockSpec(memory_space=outs_space)] * len(outs),
        scratch_shapes=[pltpu.VMEM(s, jnp.float32) if isinstance(s, tuple) else s for s in scratch],
        compiler_params=pltpu.CompilerParams(vmem_limit_bytes=limit),
        cost_estimate=pl.CostEstimate(
            flops=nanoseconds * 1_000_000, bytes_accessed=nanoseconds * 1000, transcendentals=0
        ),
    )(*operands)


def exchange(axis, other, even, odd):
    names = ("gx", "gy")
    count, across = lax.axis_size(axis), lax.axis_size(other)
    stride = {"gx": lax.axis_size("gy"), "gy": 1}
    results = []
    for start, value in ((0, even), (1, odd)):
        pairs = []
        for place in range(count):
            partner = place + 1 if (place - start) % 2 == 0 else place - 1
            for line in range(across):
                target = (partner, line)
                if not 0 <= partner < count:
                    target = (place, line ^ 1 if line ^ 1 < across else line)
                pairs.append((
                    place * stride[axis] + line * stride[other],
                    target[0] * stride[axis] + target[1] * stride[other],
                ))
        results.append(lax.ppermute(value, names, pairs))
    return results


def inverse_weights(axis, places, length):
    extent = length * lax.axis_size(axis)
    places = places + lax.axis_index(axis) * length
    total = jnp.zeros(places.shape, jnp.float32)
    for offset in range(-REACH, REACH + 1):
        inside = (places + offset >= 0) & (places + offset < extent)
        total = total + jnp.where(inside, tap(offset), 0.0)
    return 1.0 / jnp.maximum(total, tap(REACH))


def matrices(layers, rows, cols):
    depth = depth_matrix(layers)
    up, down = band(REACH, REACH, REACH), band(REACH, REACH, -REACH)
    same = np.eye(layers)
    below = np.kron(same, up)
    above = np.concatenate([np.kron(same, down), np.kron(same, band(1, REACH, 1 - REACH))], axis=0)
    rows_band = np.concatenate([np.zeros((REACH - 1, rows)), band(1, rows, 1), band(rows, rows)])
    slots = cols // REACH
    low, high, ahead = np.zeros((cols, 2 * cols)), np.zeros((cols, 2 * cols)), np.zeros((cols, cols))
    for source in range(layers):
        own = slice(source * REACH, (source + 1) * REACH)
        first = (source - 1) % slots * REACH
        other = slice(first, first + REACH)
        for layer in range(layers):
            weight = depth[layer, source]
            first = (layer - 1) % slots * REACH
            low[own, first : first + REACH] = weight * up.T
            high[other, layer * REACH : (layer + 1) * REACH] = weight * down.T
            low[own, cols + layer] = [weight * tap(j + 1) for j in range(REACH)]
            high[other, cols + layer] = [weight * tap(REACH - 1 - j) for j in range(REACH)]
            ahead[((source - 2) % slots) * REACH + REACH - 1, layer] = weight * tap(REACH)
    constants = (below, above, rows_band, band(cols, cols), low, high, ahead)
    return depth, [jnp.asarray(matrix, jnp.float32) for matrix in constants]


def local(trial_stress, old_strain, yield_mask, newton_count, damage_threshold):
    layers, rows, cols = trial_stress.shape
    assert layers * REACH == cols == rows and layers & (layers - 1) == 0
    total, strip = rows + REACH, layers * REACH
    depth, constants = matrices(layers, rows, cols)
    below, above, rows_band, cols_band, *columns = constants

    whole, wide, top = (layers, rows, cols), (layers, total, cols), (layers, REACH, cols)
    sent_rows = (strip + 3 * layers, cols)
    sent_cols = (total + rows // 4 + 2 * REACH, cols)
    last_cols = total + rows // 4 + REACH
    spare = (3 * layers, cols)
    packed, packed_two = (total, cols), (total, 2 * cols)

    inputs = stress, strain, _, _ = (trial_stress, old_strain, yield_mask, newton_count)
    threshold = damage_threshold
    edge = [pltpu.VMEM((layers, 2 * REACH, cols), value.dtype) for value in inputs]
    row_even, row_odd, norm, norm_low, norm_high, norm_last, norm_before, rest = call(
        first_edge_kernel, [(strip + REACH, cols)] * 2 + [packed] * 5 + [spare],
        edge + [(strip, cols), pltpu.SemaphoreType.DMA((2, 4))], 1500,
        inputs, [pltpu.HBM] * 4, limit=EDGE_VMEM_BYTES,
    )
    norms = (norm_low, norm_high)
    rest_even = rest_odd = rest
    for outer_no in range(OUTER):
        last = outer_no == OUTER - 1
        if outer_no:
            row_even, row_odd = call(
                edge_kernel, [sent_rows] * 2,
                [(strip, cols), (strip, cols), (2 * layers, cols)], 800,
                (*inputs, threshold, factor, kept, kept_before, edge_low, edge_high, *norms,
                 col_even, col_odd, below, above),
            )
        if not last:
            row_even, row_odd = row_even[:strip], row_odd[:strip]
        row_even, row_odd = exchange("gx", "gy", row_even, row_odd)
        if last:
            rest_even, rest_odd = row_even[strip:], row_odd[strip:]
            row_even, row_odd = row_even[:strip], row_odd[:strip]
        outs = [wide, packed_two, packed_two, whole]
        if outer_no:
            across, low_cols, high_cols, plastic = call(
                main_kernel, outs, [packed] * 5, 4500,
                (*inputs, factor, kept, edge_low, edge_high, *norms, col_even, col_odd, norm_last,
                 fixed, rows_band, *columns),
            )
        else:
            across, low_cols, high_cols, plastic, factor = call(
                first_main_kernel, outs + [whole], [packed] * 4, 4500, (*inputs, rows_band, *columns),
            )
        col_even, col_odd, own_cols = call(
            corner_kernel, [sent_cols, sent_cols, packed], [], 400,
            (row_even, row_odd, rest_even, rest_odd, low_cols, high_cols, norm_last, plastic, *columns),
        )
        if not outer_no:
            (fixed,) = call(prepare_kernel, [packed], [], 800, (stress, strain, threshold, col_odd))
        used = last_cols if last else rows
        col_even, col_odd = col_even[:used], col_odd[:used]
        col_even, col_odd = exchange("gy", "gx", col_even, col_odd)
        if last:
            last_even, last_odd = col_even[rows:], col_odd[rows:]
            col_even, col_odd = col_even[:rows], col_odd[:rows]
        kept, kept_before, edge_low, edge_high = call(
            functools.partial(column_kernel, depth), [whole, top, packed, packed], [wide], 1800,
            (across, row_even, row_odd, rest_even, rest_odd, threshold, norm, cols_band, own_cols),
        )
    return tuple(call(
        final_kernel, [whole, whole, (2, *whole)],
        [packed] * 3 + [whole, (2, *whole), wide, wide,
         pltpu.SemaphoreType.DMA(()), pltpu.SemaphoreType.DMA((3, layers))],
        3000,
        (stress, strain, plastic, kept, kept_before, edge_low, edge_high, *norms, col_even, col_odd,
         last_even, last_odd, rest_even, rest_odd, norm_before, own_cols),
        outs_space=pltpu.HBM,
    ))


def solution(mesh):
    split_in = P(None, "gx", "gy")
    return jax.shard_map(
        local,
        mesh=mesh,
        in_specs=(split_in,) * 5,
        out_specs=(split_in, split_in, P(None, None, "gx", "gy")),
        check_vma=False,
    )
```

```python
import functools
import math

import jax
import jax.numpy as jnp
import numpy as np
from jax import lax
from jax.experimental import pallas as pl
from jax.experimental.pallas import tpu as pltpu
from jax.sharding import PartitionSpec as P

OUTER = 3
REACH = 8
RATE = math.log2(math.e) / 0.3
HALF_LN2 = 0.5 * math.log(2.0)
VMEM_BYTES = 24 * 1024 * 1024
EDGE_VMEM_BYTES = 53 * 1024 * 1024


def tap(offset):
    return math.exp(-(offset**2) / 32.0) if abs(offset) <= REACH else 0.0


def band(rows, cols, shift=0):
    return np.array([[tap(c - r + shift) for c in range(cols)] for r in range(rows)])


def depth_matrix(layers):
    weights = band(layers, layers)
    return weights / weights.sum(axis=1, keepdims=True)


def split(value):
    high = value.astype(jnp.bfloat16)
    low = (value - high.astype(jnp.float32)).astype(jnp.bfloat16)
    return high, low


def left_constant(matrix):
    high, low = split(matrix)
    return jnp.concatenate(
        [jnp.concatenate([high, high], axis=1), jnp.concatenate([low, low], axis=1)], axis=0
    )


def right_constant(matrix):
    both = jnp.concatenate(split(matrix), axis=1)
    return jnp.concatenate([both, both], axis=0)


def left_product(constant, value):
    rows = constant.shape[0] // 2
    halves = jnp.concatenate(split(value), axis=0)
    both = jnp.dot(constant, halves, preferred_element_type=jnp.float32)
    return both[:rows] + both[rows:]


def right_product(value, constant):
    cols = constant.shape[1] // 2
    halves = jnp.concatenate(split(value), axis=1)
    both = jnp.dot(halves, constant, preferred_element_type=jnp.float32)
    return both[:, :cols] + both[:, cols:]


def first_factor(strain):
    return 0.8 - 0.2 * jnp.tanh(2.0 * strain - HALF_LN2)


def newton(stress, strain, yields, count, kept, factor):
    top = (stress + strain) - (0.875 + 0.875 * kept)
    shift = 2.0 * top - HALF_LN2
    state = 2.0 * (top - strain)
    drop = 0.1 + 0.1 * kept
    for sweep_no in range(1, 7):
        if sweep_no > 1:
            factor = 0.8 - 0.2 * jnp.tanh(shift - state)
        update = state * factor - drop
        state = update if sweep_no <= 3 else jnp.where(count >= sweep_no, update, state)
    return jnp.where(yields > 0, top - 0.5 * state, strain)


def depth_smooth(layers, matrix):
    count = len(layers)
    half = count // 2
    sums = [layers[k] + layers[count - 1 - k] for k in range(half)]
    diffs = [layers[k] - layers[count - 1 - k] for k in range(half)]
    out = [None] * count
    for row in range(half):
        even = odd = None
        for k in range(half):
            near, far = matrix[row, k], matrix[row, count - 1 - k]
            plus, minus = float(0.5 * (near + far)), float(0.5 * (near - far))
            if plus == 0.0 and minus == 0.0:
                continue
            even = sums[k] * plus if even is None else even + sums[k] * plus
            odd = diffs[k] * minus if odd is None else odd + diffs[k] * minus
        out[row] = even + odd
        out[count - 1 - row] = even - odd
    return out


def lane_ids(shape):
    return lax.broadcasted_iota(jnp.int32, shape, len(shape) - 1)


def on_even(axis):
    return lax.axis_index(axis) % 2 == 0


def sides(axis, even, odd):
    return jnp.where(on_even(axis), odd, even), jnp.where(on_even(axis), even, odd)


def send(axis, low, high, even_ref, odd_ref):
    place = lax.axis_index(axis)
    low = jnp.where(place == 0, 0.0, low)
    high = jnp.where(place == lax.axis_size(axis) - 1, 0.0, high)
    even_ref[...] = jnp.where(on_even(axis), high, low)
    odd_ref[...] = jnp.where(on_even(axis), low, high)


def layer_slots(shape):
    return lane_ids(shape) >> (REACH.bit_length() - 1)


def ratio(limit):
    return jnp.exp2(jnp.minimum(limit, 0.0) * RATE)


def edge_ratios(edges, received, norms, part, extended):
    both = sides("gy", *(ref[part, :] for ref in received))
    return [
        ratio(edge[extended, :] - value * norm[extended, :])
        for edge, value, norm in zip(edges, both, norms)
    ]


def with_edges(inner, layer, low, high):
    cols = inner.shape[1]
    slots = layer_slots(inner.shape)
    packed = jnp.where(slots == layer, low, high)
    shift = (cols - layer * REACH) % cols
    moved = packed if isinstance(layer, int) and layer == 0 else pltpu.roll(packed, shift, 1)
    return jnp.where((slots == 0) | (slots == cols // REACH - 1), moved, inner)


def first_edge_kernel(*refs):
    sources, refs = refs[:4], refs[4:]
    even_ref, odd_ref, norm, norm_low, norm_high, norm_last, norm_before, _, *refs = refs
    targets, (block, sems) = refs[:4], refs[4:]
    stress, strain, yields, count = targets
    layers, rows, cols = sources[0].shape
    copies = []
    for side, first_row in enumerate((0, rows - REACH)):
        for index, (source, target) in enumerate(zip(sources, targets)):
            copies.append(
                pltpu.make_async_copy(
                    source.at[:, pl.ds(first_row, REACH), :],
                    target.at[:, pl.ds(side * REACH, REACH), :],
                    sems.at[side, index],
                )
            )
            copies[-1].start()
    total = rows + REACH
    ids = lax.broadcasted_iota(jnp.int32, (total, cols), 0)
    down = inverse_weights("gx", ids - REACH, rows)
    lanes = lane_ids((REACH, cols))
    within = lanes & (REACH - 1)
    places = (lanes, within, within + (cols - REACH), 0 * lanes + (cols - 1), 0 * lanes - 1)
    for ref, place in zip((norm, norm_low, norm_high, norm_last, norm_before), places):
        ref[...] = down * inverse_weights("gy", place, cols)[:1]
    square = (layers * REACH, layers * REACH)
    line, lane = lax.broadcasted_iota(jnp.int32, square, 0), lane_ids(square)
    steps = (lane & (REACH - 1)) - (line & (REACH - 1))
    band_part = jnp.zeros(square, jnp.float32)
    for step in range(REACH):
        band_part = jnp.where(abs(steps) == step, tap(REACH - step), band_part)
    band_part = jnp.where((line ^ lane) < REACH, band_part, 0.0)
    sent = []
    for side, matrix in enumerate(
        (jnp.where(steps <= 0, band_part, 0.0), jnp.where(steps >= 0, band_part, 0.0))
    ):
        for copy in copies[side * 4 : side * 4 + 4]:
            copy.wait()
        for layer in range(layers):
            at = (layer, pl.ds(side * REACH, REACH), slice(None))
            block[pl.ds(layer * REACH, REACH), :] = newton(
                stress[at], strain[at], yields[at], count[at], jnp.ones((REACH, cols), jnp.float32),
                first_factor(strain[at]),
            )
        product = left_product(left_constant(matrix), block[...])
        sent.append(jnp.concatenate([product, product[:REACH]], axis=0))
    send("gx", *sent, even_ref, odd_ref)


def edge_kernel(stress, strain, yields, count, threshold, factor, kept, _, edge_low, edge_high, norm_low,
                norm_high, col_even, col_odd, below, above,
                even_ref, odd_ref, low_block, high_block, rest):
    layers, rows, cols = stress.shape

    def packed(part, extended):
        return edge_ratios(
            (edge_low, edge_high), (col_even, col_odd), (norm_low, norm_high), part, extended
        )

    part = pl.ds(rows - 2 * REACH, REACH)
    low, high = packed(part, pl.ds(rows - REACH, REACH))
    for layer in range(layers):
        rest[pl.ds(layer, 1), :] = with_edges(kept[layer, part, :], layer, low, high)[REACH - 1 :]
    at = (slice(None), rows - REACH - 1, slice(None))
    single = newton(stress[at], strain[at], yields[at], count[at], rest[pl.ds(0, layers), :], factor[at])

    for first_row, block in ((0, low_block), (rows - REACH, high_block)):
        low, high = packed(pl.ds(first_row, REACH), pl.ds(first_row + REACH, REACH))
        for layer in range(layers):
            at = (layer, pl.ds(first_row, REACH), slice(None))
            ratios = with_edges(kept[at], layer, low, high)
            value = newton(stress[at], strain[at], yields[at], count[at], ratios, factor[at])
            block[pl.ds(layer * REACH, REACH), :] = value
            if first_row:
                left = (stress[at] + strain[at]) - value
                rest[pl.ds(layer, 1), :] = left[REACH - 1 :]
                rest[pl.ds(layers + layer, 1), :] = threshold[at][REACH - 1 :]

    low = left_product(left_constant(below[...]), low_block[...])
    high = left_product(left_constant(above[...]), high_block[...])
    strip = layers * REACH
    extra = jnp.zeros((even_ref.shape[0] - strip, cols), jnp.float32)
    send(
        "gx", jnp.concatenate([low, extra], axis=0),
        jnp.concatenate([high[:strip], high[strip:] + tap(REACH) * single, rest[...]], axis=0),
        even_ref, odd_ref,
    )


def first_main_kernel(stress, strain, yields, count, band_ref, low_ref, high_ref, next_ref,
                      across, low_cols, high_cols, plastic, factor, *packs):
    layers, rows, cols = stress.shape
    step_rows = 4 * REACH

    def step(index, carry):
        for near in range(step_rows // REACH):
            part = pl.ds(pl.multiple_of(index * step_rows + near * REACH, REACH), REACH)
            for layer in range(layers):
                at = (layer, part, slice(None))
                lead = first_factor(strain[at])
                factor[at] = lead
                plastic[at] = newton(
                    stress[at], strain[at], yields[at], count[at],
                    jnp.ones((REACH, cols), jnp.float32), lead,
                )
        return carry

    lax.fori_loop(0, rows // step_rows, step, 0)
    smooth_rows(plastic, (band_ref, low_ref, high_ref, next_ref), across, low_cols, high_cols, packs)


def main_kernel(stress, strain, yields, count, factor, kept, edge_low, edge_high, norm_low, norm_high,
                col_even, col_odd, norm_last, fixed, band_ref, low_ref, high_ref, next_ref,
                across, low_cols, high_cols, plastic, pack_last, *packs):
    layers, rows, cols = stress.shape
    total = rows + REACH
    step_rows = 4 * REACH
    lanes = lane_ids((REACH, cols))
    pack_last[pl.ds(0, REACH), :] = jnp.zeros((REACH, cols), jnp.float32)

    def step(index, carry):
        for near in range(step_rows // REACH):
            first = index * step_rows + near * REACH
            part = pl.ds(pl.multiple_of(first, REACH), REACH)
            extended = pl.ds(pl.multiple_of(first + REACH, REACH), REACH)
            packed = edge_ratios(
                (edge_low, edge_high), (col_even, col_odd), (norm_low, norm_high), part, extended
            )
            for layer in range(layers):
                at = (layer, part, slice(None))
                ratios = with_edges(kept[at], layer, *packed)
                value = newton(stress[at], strain[at], yields[at], count[at], ratios, factor[at])
                plastic[at] = value
                lane = layers + layer
                pltpu.store(pack_last.at[extended, :], pltpu.roll(value, lane + 1, 1), mask=lanes == lane)
        return carry

    lax.fori_loop(0, rows // step_rows, step, 0)
    behind = smooth_rows(
        plastic, (band_ref, low_ref, high_ref, next_ref), across, low_cols, high_cols, packs
    )
    drop = behind * norm_last[...]
    first_lanes = lane_ids((total, cols)) < layers
    high_cols[:, cols:] = fixed[...] - jnp.where(first_lanes, drop, pack_last[...])


def smooth_rows(plastic, tables, across, low_cols, high_cols, packs):
    layers, rows, cols = plastic.shape
    total = rows + REACH
    band_ref, low_ref, high_ref, next_ref = tables
    constant = left_constant(band_ref[...])
    slots = layer_slots((total, cols))
    spread = len(packs)
    for layer in range(0, layers, 2):
        pair = jnp.concatenate([plastic[layer], plastic[layer + 1]], axis=1)
        result = left_product(constant, pair)
        for inner in range(2):
            value = result[:, inner * cols : (inner + 1) * cols]
            across[layer + inner] = value
            moved = pltpu.roll(value, (layer + inner) * REACH, 1) if layer + inner else value
            mask = ((layer + inner - slots) & (layers - 1)) < 3
            pltpu.store(packs[(layer + inner) % spread], moved, mask=mask)

    def gathered(behind):
        source = (slots + behind) & (spread - 1)
        parts = packs[0][...]
        for index in range(1, spread):
            parts = jnp.where(source == index, packs[index][...], parts)
        return parts

    low_cols[...] = right_product(gathered(0), right_constant(low_ref[...]))
    high = right_product(gathered(1), right_constant(high_ref[...]))
    behind = right_product(gathered(2), right_constant(next_ref[...]))
    high_cols[:, :cols] = high[:, :cols]
    return high[:, cols:] + behind


def prepare_kernel(stress, strain, threshold, _, fixed):
    layers, rows, cols = stress.shape
    lanes = lane_ids((REACH, cols))
    fixed[...] = jnp.zeros_like(fixed)

    def step(index, carry):
        for near in range(2):
            first = (2 * index + near) * REACH
            part = pl.ds(pl.multiple_of(first, REACH), REACH)
            extended = pl.ds(pl.multiple_of(first + REACH, REACH), REACH)
            for layer in range(layers):
                at = (layer, part, slice(None))
                for lane, value in ((layer, threshold[at]), (layers + layer, stress[at] + strain[at])):
                    moved = pltpu.roll(value, lane + 1, 1)
                    pltpu.store(fixed.at[extended, :], moved, mask=lanes == lane)
        return carry

    lax.fori_loop(0, rows // (2 * REACH), step, 0)


def pack_edges(values):
    cols = values[0].shape[1]
    count = cols // REACH
    slots = layer_slots(values[0].shape)
    low = high = ahead = jnp.zeros_like(values[0])
    for layer, value in enumerate(values):
        moved = pltpu.roll(value, layer * REACH, 1) if layer else value
        low = jnp.where(slots == layer, moved, low)
        high = jnp.where(slots == (layer - 1) % count, moved, high)
        ahead = jnp.where(slots == (layer - 2) % count, moved, ahead)
    return low, high, ahead


def corner_kernel(row_even, row_odd, rest_even, rest_odd, low_cols, high_cols, norm_last,
                  _, low_ref, high_ref, next_ref, even_ref, odd_ref, own_ref):
    cols = low_ref.shape[0]
    total = low_cols.shape[0]
    layers = (total - REACH) // REACH
    strip = layers * REACH
    from_low, from_high = sides("gx", row_even[...], row_odd[...])
    rest, _ = sides("gx", rest_even[...], rest_odd[...])
    partial, kept, limit = rest[:layers], rest[layers : 2 * layers], rest[2 * layers :]
    before = [jnp.broadcast_to(partial[layer : layer + 1], (REACH, cols)) for layer in range(layers)]
    packs = [pack_edges(before)] + [
        pack_edges([block[layer * REACH : (layer + 1) * REACH] for layer in range(layers)])
        for block in (from_low, from_high)
    ]
    low, high, ahead = (jnp.concatenate(group, axis=0) for group in zip(*packs))
    low_add = right_product(low, right_constant(low_ref[...]))
    high_add = right_product(high, right_constant(high_ref[...]))
    behind_add = right_product(ahead, right_constant(next_ref[...]))

    lanes = lane_ids((layers, cols))
    level = lax.broadcasted_iota(jnp.int32, (layers, cols), 0)
    corner_limit = jnp.where(lanes == level, limit[:, cols - 1 :], 0.0)
    corner_kept = jnp.where(lanes == layers + level, kept[:, cols - 1 :], 0.0)
    corner = jnp.sum(corner_limit + corner_kept, axis=0, keepdims=True)

    def place(base, add):
        return jnp.concatenate(
            [base[: 2 * REACH] + add[: 2 * REACH], base[2 * REACH : total - REACH],
             base[total - REACH :] + add[2 * REACH :]],
            axis=0,
        )

    low_all = place(low_cols[...], low_add)
    high_all = place(high_cols[:, :cols], high_add[:, :cols])
    last = norm_last[...]
    behind = high_add[:, cols:] + behind_add
    edges = jnp.concatenate([last[: 2 * REACH], last[total - REACH :]], axis=0)
    lanes = lane_ids(behind.shape)
    drop = jnp.where(lanes < layers, behind * edges, 0.0)
    column = place(high_cols[:, cols:], -drop)
    first = column[:REACH] + corner
    main = column[REACH:]
    quarter = strip // 4
    lanes = lane_ids((quarter, cols))
    folded = main[:quarter]
    for part in range(1, 4):
        moved = pltpu.roll(main[part * quarter : (part + 1) * quarter], part * 2 * layers, 1)
        folded = jnp.where(lanes // (2 * layers) == part, moved, folded)
    spare = jnp.zeros((REACH, cols), jnp.float32)
    extra = jnp.zeros((quarter + REACH, cols), jnp.float32)
    send(
        "gy", jnp.concatenate([low_all[REACH:, :cols], low_all[:REACH, :cols], extra, spare], axis=0),
        jnp.concatenate([high_all[REACH:], high_all[:REACH], folded, first, spare], axis=0),
        even_ref, odd_ref,
    )
    own_ref[...] = low_all[:, cols:]


def column_kernel(depth, across, row_even, row_odd, rest_even, rest_odd, threshold, norm, band_ref, _,
                  plastic, kept, kept_before, edge_low, edge_high, plastic_out, deep, copy_sem):
    layers, total, cols = across.shape
    whole = pltpu.make_async_copy(plastic, plastic_out, copy_sem)
    whole.start()

    def depth_sums(part, values):
        for layer, value in enumerate(depth_smooth(values, depth)):
            deep[layer, part, :] = value

    def step(index, carry):
        for inner in range(2):
            part = pl.ds(pl.multiple_of((2 * index + inner + 2) * REACH, REACH), REACH)
            depth_sums(part, [across[layer, part, :] for layer in range(layers)])
        return carry

    lax.fori_loop(0, (total // REACH - 3) // 2, step, 0)
    for first_row in (0, REACH, total - REACH):
        part = pl.ds(first_row, REACH)
        values = []
        for layer in range(layers):
            if first_row:
                line = pl.ds(layer * REACH, REACH)
                both = sides("gx", row_even[line, :], row_odd[line, :])
            else:
                both = sides("gx", rest_even[pl.ds(layer, 1), :], rest_odd[pl.ds(layer, 1), :])
            values.append(across[layer, part, :] + both[first_row > REACH])
        depth_sums(part, values)

    constant = right_constant(band_ref[...])
    slots = layer_slots((total, cols))
    for layer in range(layers):
        nonlocal_strain = right_product(deep[layer], constant) * norm[...]
        line = pl.ds(2 * layers + layer, 1)
        limit, _ = sides("gx", rest_even[line, :], rest_odd[line, :])
        first = limit - nonlocal_strain[:REACH]
        others = threshold[layer] - nonlocal_strain[REACH:]
        kept_before[layer] = ratio(first)
        kept[layer] = ratio(others)
        moved = jnp.concatenate([first, others], axis=0)
        moved = pltpu.roll(moved, layer * REACH, 1) if layer else moved
        pltpu.store(edge_low, moved, mask=slots == layer)
        pltpu.store(edge_high, moved, mask=slots == (layer - 1) % (cols // REACH))
    whole.wait()


def final_kernel(stress, strain, plastic, inner, inner_before, edge_low, edge_high, norm_low, norm_high,
                 col_even, col_odd, last_even, last_odd, rest_even, rest_odd, norm_before, own_cols,
                 damage_out, force_out, columns, lows, highs, damage_s, force_s, sums, diffs, sems):
    layers, rows, cols = stress.shape
    from_low, _ = sides("gy", last_even[...], last_odd[...])
    folded = from_low[REACH : REACH + rows // 4]
    pieces = [from_low[REACH + rows // 4 :], folded]
    for part in range(1, 4):
        pieces.append(pltpu.roll(folded, cols - part * 2 * layers, 1))
    column = jnp.concatenate(pieces, axis=0)
    kept = ratio(column - own_cols[...] * norm_before[...])
    columns[...] = (0.5 * kept) * pltpu.roll(column, cols - layers, 1)

    low, high = edge_ratios(
        (edge_low, edge_high), (last_even, last_odd), (norm_low, norm_high),
        pl.ds(0, REACH), pl.ds(0, REACH),
    )
    lows[pl.ds(0, REACH), :], highs[pl.ds(0, REACH), :] = low, high
    low, high = edge_ratios(
        (edge_low, edge_high), (col_even, col_odd), (norm_low, norm_high),
        pl.ds(0, rows), pl.ds(REACH, rows),
    )
    lows[pl.ds(REACH, rows), :], highs[pl.ds(REACH, rows), :] = low, high

    def copies(layer):
        return (
            pltpu.make_async_copy(damage_s.at[layer], damage_out.at[layer], sems.at[0, layer]),
            pltpu.make_async_copy(force_s.at[0, layer], force_out.at[0, layer], sems.at[1, layer]),
            pltpu.make_async_copy(force_s.at[1, layer], force_out.at[1, layer], sems.at[2, layer]),
        )

    lanes = lane_ids((REACH, cols))

    def stresses(pair):
        for near in range(2):
            layer = 2 * pair + near
            for block in range(rows // REACH + 1):
                extended = pl.ds(block * REACH, REACH)
                at = (layer, pl.ds((block - 1) * REACH if block else 0, REACH), slice(None))
                if block:
                    rest = (stress[at] + strain[at]) - plastic[at]
                else:
                    line = pl.ds(layers + layer, 1)
                    rest, _ = sides("gx", rest_even[line, :], rest_odd[line, :])
                kept = inner[at] if block else inner_before[layer]
                kept = with_edges(kept, layer, lows[extended, :], highs[extended, :])
                value = (0.5 * kept) * rest
                left = jnp.where(
                    lanes == 0,
                    pltpu.roll(columns[extended, :], (cols - layer) % cols, 1),
                    pltpu.roll(value, 1, 1),
                )
                sums[layer, extended, :] = left + value
                diffs[layer, extended, :] = left - value
                if block:
                    damage_s[at] = 1.0 - kept

    def forces(pair):
        for near in range(2):
            layer = 2 * pair + near
            for block in range(rows // REACH):
                at = (layer, pl.ds(block * REACH, REACH), slice(None))
                here, behind = pl.ds((block + 1) * REACH, REACH), pl.ds((block + 1) * REACH - 1, REACH)
                force_s[(0, *at)] = sums[layer, behind, :] - sums[layer, here, :]
                force_s[(1, *at)] = diffs[layer, behind, :] + diffs[layer, here, :]

    def start(pair):
        for near in range(2):
            for copy in copies(2 * pair + near):
                copy.start()

    def step(pair, carry):
        forces(pair - 1)
        stresses(pair)
        start(pair - 1)
        return carry

    stresses(0)
    lax.fori_loop(1, layers // 2, step, 0)
    forces(layers // 2 - 1)
    start(layers // 2 - 1)

    def drain(layer, carry):
        for copy in copies(layer):
            copy.wait()
        return carry

    lax.fori_loop(0, layers, drain, 0)


def call(kernel, outs, scratch, nanoseconds, operands, spaces=None, outs_space=None, limit=VMEM_BYTES):
    spaces = spaces or [pltpu.VMEM] * len(operands)
    outs_space = outs_space or [pltpu.VMEM] * len(outs)
    shapes = [out if isinstance(out, jax.ShapeDtypeStruct) else jax.ShapeDtypeStruct(out, jnp.float32)
              for out in outs]
    return pl.pallas_call(
        kernel,
        out_shape=shapes,
        in_specs=[pl.BlockSpec(memory_space=space) for space in spaces],
        out_specs=[pl.BlockSpec(memory_space=space) for space in outs_space],
        scratch_shapes=[pltpu.VMEM(s, jnp.float32) if isinstance(s, tuple) else s for s in scratch],
        compiler_params=pltpu.CompilerParams(vmem_limit_bytes=limit),
        cost_estimate=pl.CostEstimate(
            flops=nanoseconds * 1_000_000, bytes_accessed=nanoseconds * 1000, transcendentals=0
        ),
    )(*operands)


def exchange(axis, other, even, odd):
    names = ("gx", "gy")
    count, across = lax.axis_size(axis), lax.axis_size(other)
    stride = {"gx": lax.axis_size("gy"), "gy": 1}
    results = []
    for start, value in ((0, even), (1, odd)):
        pairs = []
        for place in range(count):
            partner = place + 1 if (place - start) % 2 == 0 else place - 1
            for line in range(across):
                target = (partner, line)
                if not 0 <= partner < count:
                    target = (place, line ^ 1 if line ^ 1 < across else line)
                pairs.append((
                    place * stride[axis] + line * stride[other],
                    target[0] * stride[axis] + target[1] * stride[other],
                ))
        results.append(lax.ppermute(value, names, pairs))
    return results


def inverse_weights(axis, places, length):
    extent = length * lax.axis_size(axis)
    places = places + lax.axis_index(axis) * length
    total = jnp.zeros(places.shape, jnp.float32)
    for offset in range(-REACH, REACH + 1):
        inside = (places + offset >= 0) & (places + offset < extent)
        total = total + jnp.where(inside, tap(offset), 0.0)
    return 1.0 / jnp.maximum(total, tap(REACH))


def matrices(layers, rows, cols):
    depth = depth_matrix(layers)
    up, down = band(REACH, REACH, REACH), band(REACH, REACH, -REACH)
    same = np.eye(layers)
    below = np.kron(same, up)
    above = np.concatenate([np.kron(same, down), np.kron(same, band(1, REACH, 1 - REACH))], axis=0)
    rows_band = np.concatenate([np.zeros((REACH - 1, rows)), band(1, rows, 1), band(rows, rows)])
    slots = cols // REACH
    low, high, ahead = np.zeros((cols, 2 * cols)), np.zeros((cols, 2 * cols)), np.zeros((cols, cols))
    for source in range(layers):
        own = slice(source * REACH, (source + 1) * REACH)
        first = (source - 1) % slots * REACH
        other = slice(first, first + REACH)
        for layer in range(layers):
            weight = depth[layer, source]
            first = (layer - 1) % slots * REACH
            low[own, first : first + REACH] = weight * up.T
            high[other, layer * REACH : (layer + 1) * REACH] = weight * down.T
            low[own, cols + layer] = [weight * tap(j + 1) for j in range(REACH)]
            high[other, cols + layer] = [weight * tap(REACH - 1 - j) for j in range(REACH)]
            ahead[((source - 2) % slots) * REACH + REACH - 1, layer] = weight * tap(REACH)
    constants = (below, above, rows_band, band(cols, cols), low, high, ahead)
    return depth, [jnp.asarray(matrix, jnp.float32) for matrix in constants]


def local(trial_stress, old_strain, yield_mask, newton_count, damage_threshold):
    layers, rows, cols = trial_stress.shape
    assert layers * REACH == cols == rows and layers & (layers - 1) == 0
    total, strip = rows + REACH, layers * REACH
    depth, constants = matrices(layers, rows, cols)
    below, above, rows_band, cols_band, *columns = constants

    whole, wide, top = (layers, rows, cols), (layers, total, cols), (layers, REACH, cols)
    sent_rows = (strip + 3 * layers, cols)
    sent_cols = (total + rows // 4 + 2 * REACH, cols)
    last_cols = total + rows // 4 + REACH
    spare = (3 * layers, cols)
    packed, packed_two = (total, cols), (total, 2 * cols)

    inputs = stress, strain, _, _ = (trial_stress, old_strain, yield_mask, newton_count)
    threshold = damage_threshold
    edge = [pltpu.VMEM((layers, 2 * REACH, cols), value.dtype) for value in inputs]
    row_even, row_odd, norm, norm_low, norm_high, norm_last, norm_before, rest = call(
        first_edge_kernel, [(strip + REACH, cols)] * 2 + [packed] * 5 + [spare],
        edge + [(strip, cols), pltpu.SemaphoreType.DMA((2, 4))], 1500,
        inputs, [pltpu.HBM] * 4, limit=EDGE_VMEM_BYTES,
    )
    norms = (norm_low, norm_high)
    rest_even = rest_odd = rest
    for outer_no in range(OUTER):
        last = outer_no == OUTER - 1
        if outer_no:
            row_even, row_odd = call(
                edge_kernel, [sent_rows] * 2,
                [(strip, cols), (strip, cols), (2 * layers, cols)], 800,
                (*inputs, threshold, factor, kept, kept_before, edge_low, edge_high, *norms,
                 col_even, col_odd, below, above),
            )
        if not last:
            row_even, row_odd = row_even[:strip], row_odd[:strip]
        row_even, row_odd = exchange("gx", "gy", row_even, row_odd)
        if last:
            rest_even, rest_odd = row_even[strip:], row_odd[strip:]
            row_even, row_odd = row_even[:strip], row_odd[:strip]
        outs = [wide, packed_two, packed_two, whole]
        if outer_no:
            across, low_cols, high_cols, plastic = call(
                main_kernel, outs, [packed] * 5, 4500,
                (*inputs, factor, kept, edge_low, edge_high, *norms, col_even, col_odd, norm_last,
                 fixed, rows_band, *columns),
            )
        else:
            across, low_cols, high_cols, plastic, factor = call(
                first_main_kernel, outs + [whole], [packed] * 4, 4500, (*inputs, rows_band, *columns),
            )
        col_even, col_odd, own_cols = call(
            corner_kernel, [sent_cols, sent_cols, packed], [], 400,
            (row_even, row_odd, rest_even, rest_odd, low_cols, high_cols, norm_last, plastic, *columns),
        )
        if not outer_no:
            (fixed,) = call(prepare_kernel, [packed], [], 800, (stress, strain, threshold, col_odd))
        used = last_cols if last else rows
        col_even, col_odd = col_even[:used], col_odd[:used]
        col_even, col_odd = exchange("gy", "gx", col_even, col_odd)
        if last:
            last_even, last_odd = col_even[rows:], col_odd[rows:]
            col_even, col_odd = col_even[:rows], col_odd[:rows]
        kept, kept_before, edge_low, edge_high, plastic_out = call(
            functools.partial(column_kernel, depth), [whole, top, packed, packed, whole],
            [wide, pltpu.SemaphoreType.DMA(())], 1800,
            (across, row_even, row_odd, rest_even, rest_odd, threshold, norm, cols_band, own_cols,
             plastic),
            outs_space=[pltpu.VMEM] * 4 + [pltpu.HBM],
        )
    damage, force = call(
        final_kernel, [whole, (2, *whole)],
        [packed] * 3 + [whole, (2, *whole), wide, wide, pltpu.SemaphoreType.DMA((3, layers))],
        3000,
        (stress, strain, plastic, kept, kept_before, edge_low, edge_high, *norms, col_even, col_odd,
         last_even, last_odd, rest_even, rest_odd, norm_before, own_cols),
        outs_space=[pltpu.HBM] * 2,
    )
    return plastic_out, damage, force


def solution(mesh):
    split_in = P(None, "gx", "gy")
    return jax.shard_map(
        local,
        mesh=mesh,
        in_specs=(split_in,) * 5,
        out_specs=(split_in, split_in, P(None, None, "gx", "gy")),
        check_vma=False,
    )
```

```python
import functools
import math

import jax
import jax.numpy as jnp
import numpy as np
from jax import lax
from jax.experimental import pallas as pl
from jax.experimental.pallas import tpu as pltpu
from jax.sharding import PartitionSpec as P

OUTER = 3
REACH = 8
RATE = math.log2(math.e) / 0.3
HALF_LN2 = 0.5 * math.log(2.0)
VMEM_BYTES = 24 * 1024 * 1024
EDGE_VMEM_BYTES = 53 * 1024 * 1024


def tap(offset):
    return math.exp(-(offset**2) / 32.0) if abs(offset) <= REACH else 0.0


def band(rows, cols, shift=0):
    return np.array([[tap(c - r + shift) for c in range(cols)] for r in range(rows)])


def depth_matrix(layers):
    weights = band(layers, layers)
    return weights / weights.sum(axis=1, keepdims=True)


def split(value):
    high = value.astype(jnp.bfloat16)
    low = (value - high.astype(jnp.float32)).astype(jnp.bfloat16)
    return high, low


def left_constant(matrix):
    high, low = split(matrix)
    return jnp.concatenate(
        [jnp.concatenate([high, high], axis=1), jnp.concatenate([low, low], axis=1)], axis=0
    )


def right_constant(matrix):
    both = jnp.concatenate(split(matrix), axis=1)
    return jnp.concatenate([both, both], axis=0)


def left_product(constant, value):
    rows = constant.shape[0] // 2
    halves = jnp.concatenate(split(value), axis=0)
    both = jnp.dot(constant, halves, preferred_element_type=jnp.float32)
    return both[:rows] + both[rows:]


def right_product(value, constant):
    cols = constant.shape[1] // 2
    halves = jnp.concatenate(split(value), axis=1)
    both = jnp.dot(halves, constant, preferred_element_type=jnp.float32)
    return both[:, :cols] + both[:, cols:]


def first_factor(strain):
    return 0.8 - 0.2 * jnp.tanh(2.0 * strain - HALF_LN2)


def newton(stress, strain, yields, count, kept, factor):
    top = (stress + strain) - (0.875 + 0.875 * kept)
    shift = 2.0 * top - HALF_LN2
    state = 2.0 * (top - strain)
    drop = 0.1 + 0.1 * kept
    for sweep_no in range(1, 7):
        if sweep_no > 1:
            factor = 0.8 - 0.2 * jnp.tanh(shift - state)
        update = state * factor - drop
        state = update if sweep_no <= 3 else jnp.where(count >= sweep_no, update, state)
    return jnp.where(yields > 0, top - 0.5 * state, strain)


def depth_smooth(layers, matrix):
    count = len(layers)
    half = count // 2
    sums = [layers[k] + layers[count - 1 - k] for k in range(half)]
    diffs = [layers[k] - layers[count - 1 - k] for k in range(half)]
    out = [None] * count
    for row in range(half):
        even = odd = None
        for k in range(half):
            near, far = matrix[row, k], matrix[row, count - 1 - k]
            plus, minus = float(0.5 * (near + far)), float(0.5 * (near - far))
            if plus == 0.0 and minus == 0.0:
                continue
            even = sums[k] * plus if even is None else even + sums[k] * plus
            odd = diffs[k] * minus if odd is None else odd + diffs[k] * minus
        out[row] = even + odd
        out[count - 1 - row] = even - odd
    return out


def lane_ids(shape):
    return lax.broadcasted_iota(jnp.int32, shape, len(shape) - 1)


def on_even(axis):
    return lax.axis_index(axis) % 2 == 0


def sides(axis, even, odd):
    return jnp.where(on_even(axis), odd, even), jnp.where(on_even(axis), even, odd)


def send(axis, low, high, even_ref, odd_ref):
    place = lax.axis_index(axis)
    low = jnp.where(place == 0, 0.0, low)
    high = jnp.where(place == lax.axis_size(axis) - 1, 0.0, high)
    even_ref[...] = jnp.where(on_even(axis), high, low)
    odd_ref[...] = jnp.where(on_even(axis), low, high)


def layer_slots(shape):
    return lane_ids(shape) >> (REACH.bit_length() - 1)


def ratio(limit):
    return jnp.exp2(jnp.minimum(limit, 0.0) * RATE)


def edge_ratios(edges, received, norms, part, extended):
    both = sides("gy", *(ref[part, :] for ref in received))
    return [
        ratio(edge[extended, :] - value * norm[extended, :])
        for edge, value, norm in zip(edges, both, norms)
    ]


def with_edges(inner, layer, low, high):
    cols = inner.shape[1]
    slots = layer_slots(inner.shape)
    packed = jnp.where(slots == layer, low, high)
    shift = (cols - layer * REACH) % cols
    moved = packed if isinstance(layer, int) and layer == 0 else pltpu.roll(packed, shift, 1)
    return jnp.where((slots == 0) | (slots == cols // REACH - 1), moved, inner)


def first_edge_kernel(*refs):
    sources, refs = refs[:4], refs[4:]
    even_ref, odd_ref, norm, norm_low, norm_high, norm_last, norm_before, _, *refs = refs
    targets, (block, sems) = refs[:4], refs[4:]
    stress, strain, yields, count = targets
    layers, rows, cols = sources[0].shape
    copies = []
    for side, first_row in enumerate((0, rows - REACH)):
        for index, (source, target) in enumerate(zip(sources, targets)):
            copies.append(
                pltpu.make_async_copy(
                    source.at[:, pl.ds(first_row, REACH), :],
                    target.at[:, pl.ds(side * REACH, REACH), :],
                    sems.at[side, index],
                )
            )
            copies[-1].start()
    total = rows + REACH
    ids = lax.broadcasted_iota(jnp.int32, (total, cols), 0)
    down = inverse_weights("gx", ids - REACH, rows)
    lanes = lane_ids((REACH, cols))
    within = lanes & (REACH - 1)
    places = (lanes, within, within + (cols - REACH), 0 * lanes + (cols - 1), 0 * lanes - 1)
    for ref, place in zip((norm, norm_low, norm_high, norm_last, norm_before), places):
        ref[...] = down * inverse_weights("gy", place, cols)[:1]
    square = (layers * REACH, layers * REACH)
    line, lane = lax.broadcasted_iota(jnp.int32, square, 0), lane_ids(square)
    steps = (lane & (REACH - 1)) - (line & (REACH - 1))
    band_part = jnp.zeros(square, jnp.float32)
    for step in range(REACH):
        band_part = jnp.where(abs(steps) == step, tap(REACH - step), band_part)
    band_part = jnp.where((line ^ lane) < REACH, band_part, 0.0)
    sent = []
    for side, matrix in enumerate(
        (jnp.where(steps <= 0, band_part, 0.0), jnp.where(steps >= 0, band_part, 0.0))
    ):
        for copy in copies[side * 4 : side * 4 + 4]:
            copy.wait()
        for layer in range(layers):
            at = (layer, pl.ds(side * REACH, REACH), slice(None))
            block[pl.ds(layer * REACH, REACH), :] = newton(
                stress[at], strain[at], yields[at], count[at], jnp.ones((REACH, cols), jnp.float32),
                first_factor(strain[at]),
            )
        product = left_product(left_constant(matrix), block[...])
        sent.append(jnp.concatenate([product, product[:REACH]], axis=0))
    send("gx", *sent, even_ref, odd_ref)


def edge_kernel(stress, strain, yields, count, threshold, factor, kept, _, edge_low, edge_high, norm_low,
                norm_high, col_even, col_odd, below, above,
                even_ref, odd_ref, low_block, high_block, rest):
    layers, rows, cols = stress.shape

    def packed(part, extended):
        return edge_ratios(
            (edge_low, edge_high), (col_even, col_odd), (norm_low, norm_high), part, extended
        )

    part = pl.ds(rows - 2 * REACH, REACH)
    low, high = packed(part, pl.ds(rows - REACH, REACH))
    for layer in range(layers):
        rest[pl.ds(layer, 1), :] = with_edges(kept[layer, part, :], layer, low, high)[REACH - 1 :]
    at = (slice(None), rows - REACH - 1, slice(None))
    single = newton(stress[at], strain[at], yields[at], count[at], rest[pl.ds(0, layers), :], factor[at])

    for first_row, block in ((0, low_block), (rows - REACH, high_block)):
        low, high = packed(pl.ds(first_row, REACH), pl.ds(first_row + REACH, REACH))
        for layer in range(layers):
            at = (layer, pl.ds(first_row, REACH), slice(None))
            ratios = with_edges(kept[at], layer, low, high)
            value = newton(stress[at], strain[at], yields[at], count[at], ratios, factor[at])
            block[pl.ds(layer * REACH, REACH), :] = value
            if first_row:
                left = (stress[at] + strain[at]) - value
                rest[pl.ds(layer, 1), :] = left[REACH - 1 :]
                rest[pl.ds(layers + layer, 1), :] = threshold[at][REACH - 1 :]

    low = left_product(left_constant(below[...]), low_block[...])
    high = left_product(left_constant(above[...]), high_block[...])
    strip = layers * REACH
    extra = jnp.zeros((even_ref.shape[0] - strip, cols), jnp.float32)
    send(
        "gx", jnp.concatenate([low, extra], axis=0),
        jnp.concatenate([high[:strip], high[strip:] + tap(REACH) * single, rest[...]], axis=0),
        even_ref, odd_ref,
    )


def first_main_kernel(stress, strain, yields, count, band_ref, low_ref, high_ref, next_ref,
                      across, low_cols, high_cols, plastic, factor, *packs):
    layers, rows, cols = stress.shape
    step_rows = 4 * REACH

    def step(index, carry):
        for near in range(step_rows // REACH):
            part = pl.ds(pl.multiple_of(index * step_rows + near * REACH, REACH), REACH)
            for layer in range(layers):
                at = (layer, part, slice(None))
                lead = first_factor(strain[at])
                factor[at] = lead
                plastic[at] = newton(
                    stress[at], strain[at], yields[at], count[at],
                    jnp.ones((REACH, cols), jnp.float32), lead,
                )
        return carry

    lax.fori_loop(0, rows // step_rows, step, 0)
    smooth_rows(plastic, (band_ref, low_ref, high_ref, next_ref), across, low_cols, high_cols, packs)


def main_kernel(stress, strain, yields, count, factor, kept, edge_low, edge_high, norm_low, norm_high,
                col_even, col_odd, norm_last, fixed, band_ref, low_ref, high_ref, next_ref,
                across, low_cols, high_cols, plastic, pack_last, *packs):
    layers, rows, cols = stress.shape
    total = rows + REACH
    step_rows = 4 * REACH
    lanes = lane_ids((REACH, cols))
    pack_last[pl.ds(0, REACH), :] = jnp.zeros((REACH, cols), jnp.float32)

    def step(index, carry):
        for near in range(step_rows // REACH):
            first = index * step_rows + near * REACH
            part = pl.ds(pl.multiple_of(first, REACH), REACH)
            extended = pl.ds(pl.multiple_of(first + REACH, REACH), REACH)
            packed = edge_ratios(
                (edge_low, edge_high), (col_even, col_odd), (norm_low, norm_high), part, extended
            )
            for layer in range(layers):
                at = (layer, part, slice(None))
                ratios = with_edges(kept[at], layer, *packed)
                value = newton(stress[at], strain[at], yields[at], count[at], ratios, factor[at])
                plastic[at] = value
                lane = layers + layer
                pltpu.store(pack_last.at[extended, :], pltpu.roll(value, lane + 1, 1), mask=lanes == lane)
        return carry

    lax.fori_loop(0, rows // step_rows, step, 0)
    behind = smooth_rows(
        plastic, (band_ref, low_ref, high_ref, next_ref), across, low_cols, high_cols, packs
    )
    drop = behind * norm_last[...]
    first_lanes = lane_ids((total, cols)) < layers
    high_cols[:, cols:] = fixed[...] - jnp.where(first_lanes, drop, pack_last[...])


def smooth_rows(plastic, tables, across, low_cols, high_cols, packs):
    layers, rows, cols = plastic.shape
    total = rows + REACH
    band_ref, low_ref, high_ref, next_ref = tables
    constant = left_constant(band_ref[...])
    slots = layer_slots((total, cols))
    spread = len(packs)
    for layer in range(0, layers, 2):
        pair = jnp.concatenate([plastic[layer], plastic[layer + 1]], axis=1)
        result = left_product(constant, pair)
        for inner in range(2):
            value = result[:, inner * cols : (inner + 1) * cols]
            across[layer + inner] = value
            moved = pltpu.roll(value, (layer + inner) * REACH, 1) if layer + inner else value
            mask = ((layer + inner - slots) & (layers - 1)) < 3
            pltpu.store(packs[(layer + inner) % spread], moved, mask=mask)

    def gathered(behind):
        source = (slots + behind) & (spread - 1)
        parts = packs[0][...]
        for index in range(1, spread):
            parts = jnp.where(source == index, packs[index][...], parts)
        return parts

    low_cols[...] = right_product(gathered(0), right_constant(low_ref[...]))
    high = right_product(gathered(1), right_constant(high_ref[...]))
    behind = right_product(gathered(2), right_constant(next_ref[...]))
    high_cols[:, :cols] = high[:, :cols]
    return high[:, cols:] + behind


def prepare_kernel(stress, strain, threshold, _, fixed):
    layers, rows, cols = stress.shape
    lanes = lane_ids((REACH, cols))
    fixed[...] = jnp.zeros_like(fixed)

    def step(index, carry):
        for near in range(2):
            first = (2 * index + near) * REACH
            part = pl.ds(pl.multiple_of(first, REACH), REACH)
            extended = pl.ds(pl.multiple_of(first + REACH, REACH), REACH)
            for layer in range(layers):
                at = (layer, part, slice(None))
                for lane, value in ((layer, threshold[at]), (layers + layer, stress[at] + strain[at])):
                    moved = pltpu.roll(value, lane + 1, 1)
                    pltpu.store(fixed.at[extended, :], moved, mask=lanes == lane)
        return carry

    lax.fori_loop(0, rows // (2 * REACH), step, 0)


def pack_edges(values):
    cols = values[0].shape[1]
    count = cols // REACH
    slots = layer_slots(values[0].shape)
    low = high = ahead = jnp.zeros_like(values[0])
    for layer, value in enumerate(values):
        moved = pltpu.roll(value, layer * REACH, 1) if layer else value
        low = jnp.where(slots == layer, moved, low)
        high = jnp.where(slots == (layer - 1) % count, moved, high)
        ahead = jnp.where(slots == (layer - 2) % count, moved, ahead)
    return low, high, ahead


def corner_kernel(row_even, row_odd, rest_even, rest_odd, low_cols, high_cols, norm_last,
                  _, low_ref, high_ref, next_ref, even_ref, odd_ref, own_ref):
    cols = low_ref.shape[0]
    total = low_cols.shape[0]
    layers = (total - REACH) // REACH
    strip = layers * REACH
    from_low, from_high = sides("gx", row_even[...], row_odd[...])
    rest, _ = sides("gx", rest_even[...], rest_odd[...])
    partial, kept, limit = rest[:layers], rest[layers : 2 * layers], rest[2 * layers :]
    before = [jnp.broadcast_to(partial[layer : layer + 1], (REACH, cols)) for layer in range(layers)]
    packs = [pack_edges(before)] + [
        pack_edges([block[layer * REACH : (layer + 1) * REACH] for layer in range(layers)])
        for block in (from_low, from_high)
    ]
    low, high, ahead = (jnp.concatenate(group, axis=0) for group in zip(*packs))
    low_add = right_product(low, right_constant(low_ref[...]))
    high_add = right_product(high, right_constant(high_ref[...]))
    behind_add = right_product(ahead, right_constant(next_ref[...]))

    lanes = lane_ids((layers, cols))
    level = lax.broadcasted_iota(jnp.int32, (layers, cols), 0)
    corner_limit = jnp.where(lanes == level, limit[:, cols - 1 :], 0.0)
    corner_kept = jnp.where(lanes == layers + level, kept[:, cols - 1 :], 0.0)
    corner = jnp.sum(corner_limit + corner_kept, axis=0, keepdims=True)

    def place(base, add):
        return jnp.concatenate(
            [base[: 2 * REACH] + add[: 2 * REACH], base[2 * REACH : total - REACH],
             base[total - REACH :] + add[2 * REACH :]],
            axis=0,
        )

    low_all = place(low_cols[...], low_add)
    high_all = place(high_cols[:, :cols], high_add[:, :cols])
    last = norm_last[...]
    behind = high_add[:, cols:] + behind_add
    edges = jnp.concatenate([last[: 2 * REACH], last[total - REACH :]], axis=0)
    lanes = lane_ids(behind.shape)
    drop = jnp.where(lanes < layers, behind * edges, 0.0)
    column = place(high_cols[:, cols:], -drop)
    first = column[:REACH] + corner
    main = column[REACH:]
    quarter = strip // 4
    lanes = lane_ids((quarter, cols))
    folded = main[:quarter]
    for part in range(1, 4):
        moved = pltpu.roll(main[part * quarter : (part + 1) * quarter], part * 2 * layers, 1)
        folded = jnp.where(lanes // (2 * layers) == part, moved, folded)
    spare = jnp.zeros((REACH, cols), jnp.float32)
    extra = jnp.zeros((quarter + REACH, cols), jnp.float32)
    send(
        "gy", jnp.concatenate([low_all[REACH:, :cols], low_all[:REACH, :cols], extra, spare], axis=0),
        jnp.concatenate([high_all[REACH:], high_all[:REACH], folded, first, spare], axis=0),
        even_ref, odd_ref,
    )
    own_ref[...] = low_all[:, cols:]


def column_kernel(depth, across, row_even, row_odd, rest_even, rest_odd, threshold, norm, band_ref, _,
                  kept, kept_before, edge_low, edge_high, deep):
    layers, total, cols = across.shape

    def depth_sums(part, values):
        for layer, value in enumerate(depth_smooth(values, depth)):
            deep[layer, part, :] = value

    def step(index, carry):
        for inner in range(2):
            part = pl.ds(pl.multiple_of((2 * index + inner + 2) * REACH, REACH), REACH)
            depth_sums(part, [across[layer, part, :] for layer in range(layers)])
        return carry

    lax.fori_loop(0, (total // REACH - 3) // 2, step, 0)
    for first_row in (0, REACH, total - REACH):
        part = pl.ds(first_row, REACH)
        values = []
        for layer in range(layers):
            if first_row:
                line = pl.ds(layer * REACH, REACH)
                both = sides("gx", row_even[line, :], row_odd[line, :])
            else:
                both = sides("gx", rest_even[pl.ds(layer, 1), :], rest_odd[pl.ds(layer, 1), :])
            values.append(across[layer, part, :] + both[first_row > REACH])
        depth_sums(part, values)

    constant = right_constant(band_ref[...])
    slots = layer_slots((total, cols))
    for layer in range(layers):
        nonlocal_strain = right_product(deep[layer], constant) * norm[...]
        line = pl.ds(2 * layers + layer, 1)
        limit, _ = sides("gx", rest_even[line, :], rest_odd[line, :])
        first = limit - nonlocal_strain[:REACH]
        others = threshold[layer] - nonlocal_strain[REACH:]
        kept_before[layer] = ratio(first)
        kept[layer] = ratio(others)
        moved = jnp.concatenate([first, others], axis=0)
        moved = pltpu.roll(moved, layer * REACH, 1) if layer else moved
        pltpu.store(edge_low, moved, mask=slots == layer)
        pltpu.store(edge_high, moved, mask=slots == (layer - 1) % (cols // REACH))


def final_kernel(stress, strain, plastic, inner, inner_before, edge_low, edge_high, norm_low, norm_high,
                 col_even, col_odd, last_even, last_odd, rest_even, rest_odd, norm_before, own_cols,
                 plastic_out, damage_out, force_out, columns, lows, highs, damage_s, force_s, half, sums, diffs,
                 copy_sem, sems):
    layers, rows, cols = stress.shape
    whole = pltpu.make_async_copy(plastic, plastic_out, copy_sem)
    whole.start()
    from_low, _ = sides("gy", last_even[...], last_odd[...])
    folded = from_low[REACH : REACH + rows // 4]
    pieces = [from_low[REACH + rows // 4 :], folded]
    for part in range(1, 4):
        pieces.append(pltpu.roll(folded, cols - part * 2 * layers, 1))
    column = jnp.concatenate(pieces, axis=0)
    kept = ratio(column - own_cols[...] * norm_before[...])
    columns[...] = (0.5 * kept) * pltpu.roll(column, cols - layers, 1)

    low, high = edge_ratios(
        (edge_low, edge_high), (last_even, last_odd), (norm_low, norm_high),
        pl.ds(0, REACH), pl.ds(0, REACH),
    )
    lows[pl.ds(0, REACH), :], highs[pl.ds(0, REACH), :] = low, high
    low, high = edge_ratios(
        (edge_low, edge_high), (col_even, col_odd), (norm_low, norm_high),
        pl.ds(0, rows), pl.ds(REACH, rows),
    )
    lows[pl.ds(REACH, rows), :], highs[pl.ds(REACH, rows), :] = low, high

    def copies(layer):
        return (
            pltpu.make_async_copy(damage_s.at[layer], damage_out.at[layer], sems.at[0, layer]),
            pltpu.make_async_copy(force_s.at[0, layer], force_out.at[0, layer], sems.at[1, layer]),
            pltpu.make_async_copy(force_s.at[1, layer], force_out.at[1, layer], sems.at[2, layer]),
        )

    lanes = lane_ids((REACH, cols))

    def layers_of(pair):
        for near in range(2):
            for block in range(rows // REACH + 1):
                yield 2 * pair + near, block, pl.ds(block * REACH, REACH)

    def damages(pair):
        for layer, block, extended in layers_of(pair):
            at = (layer, pl.ds((block - 1) * REACH if block else 0, REACH), slice(None))
            if block:
                rest = (stress[at] + strain[at]) - plastic[at]
            else:
                line = pl.ds(layers + layer, 1)
                rest, _ = sides("gx", rest_even[line, :], rest_odd[line, :])
            kept = inner[at] if block else inner_before[layer]
            kept = with_edges(kept, layer, lows[extended, :], highs[extended, :])
            half[layer, extended, :] = (0.5 * kept) * rest
            if block:
                damage_s[at] = 1.0 - kept

    def neighbours(pair):
        for layer, block, extended in layers_of(pair):
            value = half[layer, extended, :]
            left = jnp.where(
                lanes == 0,
                pltpu.roll(columns[extended, :], (cols - layer) % cols, 1),
                pltpu.roll(value, 1, 1),
            )
            sums[layer, extended, :] = left + value
            diffs[layer, extended, :] = left - value

    def forces(pair):
        for near in range(2):
            layer = 2 * pair + near
            for block in range(rows // REACH):
                at = (layer, pl.ds(block * REACH, REACH), slice(None))
                here, behind = pl.ds((block + 1) * REACH, REACH), pl.ds((block + 1) * REACH - 1, REACH)
                force_s[(0, *at)] = sums[layer, behind, :] - sums[layer, here, :]
                force_s[(1, *at)] = diffs[layer, behind, :] + diffs[layer, here, :]

    def start(pair):
        for near in range(2):
            for copy in copies(2 * pair + near):
                copy.start()

    def step(pair, carry):
        forces(pair - 2)
        neighbours(pair - 1)
        damages(pair)
        start(pair - 2)
        return carry

    pairs = layers // 2
    damages(0)
    neighbours(0)
    damages(1)
    lax.fori_loop(2, pairs, step, 0)
    forces(pairs - 2)
    neighbours(pairs - 1)
    start(pairs - 2)
    forces(pairs - 1)
    start(pairs - 1)

    def drain(layer, carry):
        for copy in copies(layer):
            copy.wait()
        return carry

    lax.fori_loop(0, layers, drain, 0)
    whole.wait()


def call(kernel, outs, scratch, nanoseconds, operands, spaces=None, outs_space=pltpu.VMEM, limit=VMEM_BYTES):
    spaces = spaces or [pltpu.VMEM] * len(operands)
    shapes = [out if isinstance(out, jax.ShapeDtypeStruct) else jax.ShapeDtypeStruct(out, jnp.float32)
              for out in outs]
    return pl.pallas_call(
        kernel,
        out_shape=shapes,
        in_specs=[pl.BlockSpec(memory_space=space) for space in spaces],
        out_specs=[pl.BlockSpec(memory_space=outs_space)] * len(outs),
        scratch_shapes=[pltpu.VMEM(s, jnp.float32) if isinstance(s, tuple) else s for s in scratch],
        compiler_params=pltpu.CompilerParams(vmem_limit_bytes=limit),
        cost_estimate=pl.CostEstimate(
            flops=nanoseconds * 1_000_000, bytes_accessed=nanoseconds * 1000, transcendentals=0
        ),
    )(*operands)


def exchange(axis, other, even, odd):
    names = ("gx", "gy")
    count, across = lax.axis_size(axis), lax.axis_size(other)
    stride = {"gx": lax.axis_size("gy"), "gy": 1}
    results = []
    for start, value in ((0, even), (1, odd)):
        pairs = []
        for place in range(count):
            partner = place + 1 if (place - start) % 2 == 0 else place - 1
            for line in range(across):
                target = (partner, line)
                if not 0 <= partner < count:
                    target = (place, line ^ 1 if line ^ 1 < across else line)
                pairs.append((
                    place * stride[axis] + line * stride[other],
                    target[0] * stride[axis] + target[1] * stride[other],
                ))
        results.append(lax.ppermute(value, names, pairs))
    return results


def inverse_weights(axis, places, length):
    extent = length * lax.axis_size(axis)
    places = places + lax.axis_index(axis) * length
    total = jnp.zeros(places.shape, jnp.float32)
    for offset in range(-REACH, REACH + 1):
        inside = (places + offset >= 0) & (places + offset < extent)
        total = total + jnp.where(inside, tap(offset), 0.0)
    return 1.0 / jnp.maximum(total, tap(REACH))


def matrices(layers, rows, cols):
    depth = depth_matrix(layers)
    up, down = band(REACH, REACH, REACH), band(REACH, REACH, -REACH)
    same = np.eye(layers)
    below = np.kron(same, up)
    above = np.concatenate([np.kron(same, down), np.kron(same, band(1, REACH, 1 - REACH))], axis=0)
    rows_band = np.concatenate([np.zeros((REACH - 1, rows)), band(1, rows, 1), band(rows, rows)])
    slots = cols // REACH
    low, high, ahead = np.zeros((cols, 2 * cols)), np.zeros((cols, 2 * cols)), np.zeros((cols, cols))
    for source in range(layers):
        own = slice(source * REACH, (source + 1) * REACH)
        first = (source - 1) % slots * REACH
        other = slice(first, first + REACH)
        for layer in range(layers):
            weight = depth[layer, source]
            first = (layer - 1) % slots * REACH
            low[own, first : first + REACH] = weight * up.T
            high[other, layer * REACH : (layer + 1) * REACH] = weight * down.T
            low[own, cols + layer] = [weight * tap(j + 1) for j in range(REACH)]
            high[other, cols + layer] = [weight * tap(REACH - 1 - j) for j in range(REACH)]
            ahead[((source - 2) % slots) * REACH + REACH - 1, layer] = weight * tap(REACH)
    constants = (below, above, rows_band, band(cols, cols), low, high, ahead)
    return depth, [jnp.asarray(matrix, jnp.float32) for matrix in constants]


def local(trial_stress, old_strain, yield_mask, newton_count, damage_threshold):
    layers, rows, cols = trial_stress.shape
    assert layers * REACH == cols == rows and layers & (layers - 1) == 0
    total, strip = rows + REACH, layers * REACH
    depth, constants = matrices(layers, rows, cols)
    below, above, rows_band, cols_band, *columns = constants

    whole, wide, top = (layers, rows, cols), (layers, total, cols), (layers, REACH, cols)
    sent_rows = (strip + 3 * layers, cols)
    sent_cols = (total + rows // 4 + 2 * REACH, cols)
    last_cols = total + rows // 4 + REACH
    spare = (3 * layers, cols)
    packed, packed_two = (total, cols), (total, 2 * cols)

    inputs = stress, strain, _, _ = (trial_stress, old_strain, yield_mask, newton_count)
    threshold = damage_threshold
    edge = [pltpu.VMEM((layers, 2 * REACH, cols), value.dtype) for value in inputs]
    row_even, row_odd, norm, norm_low, norm_high, norm_last, norm_before, rest = call(
        first_edge_kernel, [(strip + REACH, cols)] * 2 + [packed] * 5 + [spare],
        edge + [(strip, cols), pltpu.SemaphoreType.DMA((2, 4))], 1500,
        inputs, [pltpu.HBM] * 4, limit=EDGE_VMEM_BYTES,
    )
    norms = (norm_low, norm_high)
    rest_even = rest_odd = rest
    for outer_no in range(OUTER):
        last = outer_no == OUTER - 1
        if outer_no:
            row_even, row_odd = call(
                edge_kernel, [sent_rows] * 2,
                [(strip, cols), (strip, cols), (2 * layers, cols)], 800,
                (*inputs, threshold, factor, kept, kept_before, edge_low, edge_high, *norms,
                 col_even, col_odd, below, above),
            )
        if not last:
            row_even, row_odd = row_even[:strip], row_odd[:strip]
        row_even, row_odd = exchange("gx", "gy", row_even, row_odd)
        if last:
            rest_even, rest_odd = row_even[strip:], row_odd[strip:]
            row_even, row_odd = row_even[:strip], row_odd[:strip]
        outs = [wide, packed_two, packed_two, whole]
        if outer_no:
            across, low_cols, high_cols, plastic = call(
                main_kernel, outs, [packed] * 5, 4500,
                (*inputs, factor, kept, edge_low, edge_high, *norms, col_even, col_odd, norm_last,
                 fixed, rows_band, *columns),
            )
        else:
            across, low_cols, high_cols, plastic, factor = call(
                first_main_kernel, outs + [whole], [packed] * 4, 4500, (*inputs, rows_band, *columns),
            )
        col_even, col_odd, own_cols = call(
            corner_kernel, [sent_cols, sent_cols, packed], [], 400,
            (row_even, row_odd, rest_even, rest_odd, low_cols, high_cols, norm_last, plastic, *columns),
        )
        if not outer_no:
            (fixed,) = call(prepare_kernel, [packed], [], 800, (stress, strain, threshold, col_odd))
        used = last_cols if last else rows
        col_even, col_odd = col_even[:used], col_odd[:used]
        col_even, col_odd = exchange("gy", "gx", col_even, col_odd)
        if last:
            last_even, last_odd = col_even[rows:], col_odd[rows:]
            col_even, col_odd = col_even[:rows], col_odd[:rows]
        kept, kept_before, edge_low, edge_high = call(
            functools.partial(column_kernel, depth), [whole, top, packed, packed], [wide], 1800,
            (across, row_even, row_odd, rest_even, rest_odd, threshold, norm, cols_band, own_cols),
        )
    return tuple(call(
        final_kernel, [whole, whole, (2, *whole)],
        [packed] * 3 + [whole, (2, *whole), wide, wide, wide,
         pltpu.SemaphoreType.DMA(()), pltpu.SemaphoreType.DMA((3, layers))],
        3000,
        (stress, strain, plastic, kept, kept_before, edge_low, edge_high, *norms, col_even, col_odd,
         last_even, last_odd, rest_even, rest_odd, norm_before, own_cols),
        outs_space=pltpu.HBM,
    ))


def solution(mesh):
    split_in = P(None, "gx", "gy")
    return jax.shard_map(
        local,
        mesh=mesh,
        in_specs=(split_in,) * 5,
        out_specs=(split_in, split_in, P(None, None, "gx", "gy")),
        check_vma=False,
    )
```

```python
import functools
import math

import jax
import jax.numpy as jnp
import numpy as np
from jax import lax
from jax.experimental import pallas as pl
from jax.experimental.pallas import tpu as pltpu
from jax.sharding import PartitionSpec as P

OUTER = 3
REACH = 8
RATE = math.log2(math.e) / 0.3
HALF_LN2 = 0.5 * math.log(2.0)
VMEM_BYTES = 24 * 1024 * 1024
EDGE_VMEM_BYTES = 53 * 1024 * 1024


def tap(offset):
    return math.exp(-(offset**2) / 32.0) if abs(offset) <= REACH else 0.0


def band(rows, cols, shift=0):
    return np.array([[tap(c - r + shift) for c in range(cols)] for r in range(rows)])


def depth_matrix(layers):
    weights = band(layers, layers)
    return weights / weights.sum(axis=1, keepdims=True)


def split(value):
    high = value.astype(jnp.bfloat16)
    low = (value - high.astype(jnp.float32)).astype(jnp.bfloat16)
    return high, low


def left_constant(matrix):
    high, low = split(matrix)
    return jnp.concatenate(
        [jnp.concatenate([high, high], axis=1), jnp.concatenate([low, low], axis=1)], axis=0
    )


def right_constant(matrix):
    both = jnp.concatenate(split(matrix), axis=1)
    return jnp.concatenate([both, both], axis=0)


def left_product(constant, value):
    rows = constant.shape[0] // 2
    halves = jnp.concatenate(split(value), axis=0)
    both = jnp.dot(constant, halves, preferred_element_type=jnp.float32)
    return both[:rows] + both[rows:]


def right_product(value, constant):
    cols = constant.shape[1] // 2
    halves = jnp.concatenate(split(value), axis=1)
    both = jnp.dot(halves, constant, preferred_element_type=jnp.float32)
    return both[:, :cols] + both[:, cols:]


def first_factor(strain):
    return 0.8 - 0.2 * jnp.tanh(2.0 * strain - HALF_LN2)


def newton(stress, strain, yields, count, kept, factor):
    top = (stress + strain) - (0.875 + 0.875 * kept)
    shift = 2.0 * top - HALF_LN2
    state = 2.0 * (top - strain)
    drop = 0.1 + 0.1 * kept
    for sweep_no in range(1, 7):
        if sweep_no > 1:
            factor = 0.8 - 0.2 * jnp.tanh(shift - state)
        update = state * factor - drop
        state = update if sweep_no <= 3 else jnp.where(count >= sweep_no, update, state)
    return jnp.where(yields > 0, top - 0.5 * state, strain)


def depth_smooth(layers, matrix):
    count = len(layers)
    half = count // 2
    sums = [layers[k] + layers[count - 1 - k] for k in range(half)]
    diffs = [layers[k] - layers[count - 1 - k] for k in range(half)]
    out = [None] * count
    for row in range(half):
        even = odd = None
        for k in range(half):
            near, far = matrix[row, k], matrix[row, count - 1 - k]
            plus, minus = float(0.5 * (near + far)), float(0.5 * (near - far))
            if plus == 0.0 and minus == 0.0:
                continue
            even = sums[k] * plus if even is None else even + sums[k] * plus
            odd = diffs[k] * minus if odd is None else odd + diffs[k] * minus
        out[row] = even + odd
        out[count - 1 - row] = even - odd
    return out


def lane_ids(shape):
    return lax.broadcasted_iota(jnp.int32, shape, len(shape) - 1)


def on_even(axis):
    return lax.axis_index(axis) % 2 == 0


def sides(axis, even, odd):
    return jnp.where(on_even(axis), odd, even), jnp.where(on_even(axis), even, odd)


def send(axis, low, high, even_ref, odd_ref):
    place = lax.axis_index(axis)
    low = jnp.where(place == 0, 0.0, low)
    high = jnp.where(place == lax.axis_size(axis) - 1, 0.0, high)
    even_ref[...] = jnp.where(on_even(axis), high, low)
    odd_ref[...] = jnp.where(on_even(axis), low, high)


def layer_slots(shape):
    return lane_ids(shape) >> (REACH.bit_length() - 1)


def ratio(limit):
    return jnp.exp2(jnp.minimum(limit, 0.0) * RATE)


def edge_ratios(edges, received, norms, part, extended):
    both = sides("gy", *(ref[part, :] for ref in received))
    return [
        ratio(edge[extended, :] - value * norm[extended, :])
        for edge, value, norm in zip(edges, both, norms)
    ]


def with_edges(inner, layer, low, high):
    cols = inner.shape[1]
    slots = layer_slots(inner.shape)
    packed = jnp.where(slots == layer, low, high)
    shift = (cols - layer * REACH) % cols
    moved = packed if isinstance(layer, int) and layer == 0 else pltpu.roll(packed, shift, 1)
    return jnp.where((slots == 0) | (slots == cols // REACH - 1), moved, inner)


def first_edge_kernel(*refs):
    sources, refs = refs[:4], refs[4:]
    even_ref, odd_ref, norm, norm_low, norm_high, norm_last, norm_before, _, *refs = refs
    targets, (block, sems) = refs[:4], refs[4:]
    stress, strain, yields, count = targets
    layers, rows, cols = sources[0].shape
    copies = []
    for side, first_row in enumerate((0, rows - REACH)):
        for index, (source, target) in enumerate(zip(sources, targets)):
            copies.append(
                pltpu.make_async_copy(
                    source.at[:, pl.ds(first_row, REACH), :],
                    target.at[:, pl.ds(side * REACH, REACH), :],
                    sems.at[side, index],
                )
            )
            copies[-1].start()
    total = rows + REACH
    ids = lax.broadcasted_iota(jnp.int32, (total, cols), 0)
    down = inverse_weights("gx", ids - REACH, rows)
    lanes = lane_ids((REACH, cols))
    within = lanes & (REACH - 1)
    places = (lanes, within, within + (cols - REACH), 0 * lanes + (cols - 1), 0 * lanes - 1)
    for ref, place in zip((norm, norm_low, norm_high, norm_last, norm_before), places):
        ref[...] = down * inverse_weights("gy", place, cols)[:1]
    square = (layers * REACH, layers * REACH)
    line, lane = lax.broadcasted_iota(jnp.int32, square, 0), lane_ids(square)
    steps = (lane & (REACH - 1)) - (line & (REACH - 1))
    band_part = jnp.zeros(square, jnp.float32)
    for step in range(REACH):
        band_part = jnp.where(abs(steps) == step, tap(REACH - step), band_part)
    band_part = jnp.where((line ^ lane) < REACH, band_part, 0.0)
    sent = []
    for side, matrix in enumerate(
        (jnp.where(steps <= 0, band_part, 0.0), jnp.where(steps >= 0, band_part, 0.0))
    ):
        for copy in copies[side * 4 : side * 4 + 4]:
            copy.wait()
        for layer in range(layers):
            at = (layer, pl.ds(side * REACH, REACH), slice(None))
            block[pl.ds(layer * REACH, REACH), :] = newton(
                stress[at], strain[at], yields[at], count[at], jnp.ones((REACH, cols), jnp.float32),
                first_factor(strain[at]),
            )
        sent.append(left_product(left_constant(matrix), block[...]))
    send("gx", *sent, even_ref, odd_ref)


def edge_kernel(stress, strain, yields, count, threshold, factor, kept, _, edge_low, edge_high, norm_low,
                norm_high, col_even, col_odd, below, above,
                even_ref, odd_ref, low_block, high_block, rest):
    layers, rows, cols = stress.shape

    def packed(part, extended):
        return edge_ratios(
            (edge_low, edge_high), (col_even, col_odd), (norm_low, norm_high), part, extended
        )

    part = pl.ds(rows - 2 * REACH, REACH)
    low, high = packed(part, pl.ds(rows - REACH, REACH))
    for layer in range(layers):
        rest[pl.ds(layer, 1), :] = with_edges(kept[layer, part, :], layer, low, high)[REACH - 1 :]
    at = (slice(None), rows - REACH - 1, slice(None))
    single = newton(stress[at], strain[at], yields[at], count[at], rest[pl.ds(0, layers), :], factor[at])

    for first_row, block in ((0, low_block), (rows - REACH, high_block)):
        low, high = packed(pl.ds(first_row, REACH), pl.ds(first_row + REACH, REACH))
        for layer in range(layers):
            at = (layer, pl.ds(first_row, REACH), slice(None))
            ratios = with_edges(kept[at], layer, low, high)
            value = newton(stress[at], strain[at], yields[at], count[at], ratios, factor[at])
            block[pl.ds(layer * REACH, REACH), :] = value
            if first_row:
                left = (stress[at] + strain[at]) - value
                rest[pl.ds(layer, 1), :] = left[REACH - 1 :]
                rest[pl.ds(layers + layer, 1), :] = threshold[at][REACH - 1 :]

    low = left_product(left_constant(below[...]), low_block[...])
    high = left_product(left_constant(above[...]), high_block[...])
    strip = layers * REACH
    extra = jnp.zeros((even_ref.shape[0] - strip, cols), jnp.float32)
    send(
        "gx", jnp.concatenate([low, extra], axis=0),
        jnp.concatenate([high[:strip], high[strip:] + tap(REACH) * single, rest[...]], axis=0),
        even_ref, odd_ref,
    )


def first_main_kernel(stress, strain, yields, count, band_ref, low_ref, high_ref, next_ref,
                      across, low_cols, high_cols, plastic, factor, *packs):
    layers, rows, cols = stress.shape
    step_rows = 4 * REACH

    def step(index, carry):
        for near in range(step_rows // REACH):
            part = pl.ds(pl.multiple_of(index * step_rows + near * REACH, REACH), REACH)
            for layer in range(layers):
                at = (layer, part, slice(None))
                lead = first_factor(strain[at])
                factor[at] = lead
                plastic[at] = newton(
                    stress[at], strain[at], yields[at], count[at],
                    jnp.ones((REACH, cols), jnp.float32), lead,
                )
        return carry

    lax.fori_loop(0, rows // step_rows, step, 0)
    smooth_rows(plastic, (band_ref, low_ref, high_ref, next_ref), across, low_cols, high_cols, packs)


def main_kernel(stress, strain, yields, count, factor, kept, edge_low, edge_high, norm_low, norm_high,
                col_even, col_odd, norm_last, fixed, band_ref, low_ref, high_ref, next_ref,
                across, low_cols, high_cols, plastic, pack_last, *packs):
    layers, rows, cols = stress.shape
    total = rows + REACH
    step_rows = 4 * REACH
    lanes = lane_ids((REACH, cols))
    pack_last[pl.ds(0, REACH), :] = jnp.zeros((REACH, cols), jnp.float32)

    def step(index, carry):
        for near in range(step_rows // REACH):
            first = index * step_rows + near * REACH
            part = pl.ds(pl.multiple_of(first, REACH), REACH)
            extended = pl.ds(pl.multiple_of(first + REACH, REACH), REACH)
            packed = edge_ratios(
                (edge_low, edge_high), (col_even, col_odd), (norm_low, norm_high), part, extended
            )
            for layer in range(layers):
                at = (layer, part, slice(None))
                ratios = with_edges(kept[at], layer, *packed)
                value = newton(stress[at], strain[at], yields[at], count[at], ratios, factor[at])
                plastic[at] = value
                lane = layers + layer
                pltpu.store(pack_last.at[extended, :], pltpu.roll(value, lane + 1, 1), mask=lanes == lane)
        return carry

    lax.fori_loop(0, rows // step_rows, step, 0)
    behind = smooth_rows(
        plastic, (band_ref, low_ref, high_ref, next_ref), across, low_cols, high_cols, packs
    )
    drop = behind * norm_last[...]
    first_lanes = lane_ids((total, cols)) < layers
    high_cols[:, cols:] = fixed[...] - jnp.where(first_lanes, drop, pack_last[...])


def smooth_rows(plastic, tables, across, low_cols, high_cols, packs):
    layers, rows, cols = plastic.shape
    total = rows + REACH
    band_ref, low_ref, high_ref, next_ref = tables
    constant = left_constant(band_ref[...])
    slots = layer_slots((total, cols))
    spread = len(packs)
    for layer in range(0, layers, 2):
        pair = jnp.concatenate([plastic[layer], plastic[layer + 1]], axis=1)
        result = left_product(constant, pair)
        for inner in range(2):
            value = result[:, inner * cols : (inner + 1) * cols]
            across[layer + inner] = value
            moved = pltpu.roll(value, (layer + inner) * REACH, 1) if layer + inner else value
            mask = ((layer + inner - slots) & (layers - 1)) < 3
            pltpu.store(packs[(layer + inner) % spread], moved, mask=mask)

    def gathered(behind):
        source = (slots + behind) & (spread - 1)
        parts = packs[0][...]
        for index in range(1, spread):
            parts = jnp.where(source == index, packs[index][...], parts)
        return parts

    low_cols[...] = right_product(gathered(0), right_constant(low_ref[...]))
    high = right_product(gathered(1), right_constant(high_ref[...]))
    behind = right_product(gathered(2), right_constant(next_ref[...]))
    high_cols[:, :cols] = high[:, :cols]
    return high[:, cols:] + behind


def prepare_kernel(stress, strain, threshold, _, fixed):
    layers, rows, cols = stress.shape
    lanes = lane_ids((REACH, cols))
    fixed[...] = jnp.zeros_like(fixed)

    def step(index, carry):
        for near in range(2):
            first = (2 * index + near) * REACH
            part = pl.ds(pl.multiple_of(first, REACH), REACH)
            extended = pl.ds(pl.multiple_of(first + REACH, REACH), REACH)
            for layer in range(layers):
                at = (layer, part, slice(None))
                for lane, value in ((layer, threshold[at]), (layers + layer, stress[at] + strain[at])):
                    moved = pltpu.roll(value, lane + 1, 1)
                    pltpu.store(fixed.at[extended, :], moved, mask=lanes == lane)
        return carry

    lax.fori_loop(0, rows // (2 * REACH), step, 0)


def pack_edges(values):
    cols = values[0].shape[1]
    count = cols // REACH
    slots = layer_slots(values[0].shape)
    low = high = ahead = jnp.zeros_like(values[0])
    for layer, value in enumerate(values):
        moved = pltpu.roll(value, layer * REACH, 1) if layer else value
        low = jnp.where(slots == layer, moved, low)
        high = jnp.where(slots == (layer - 1) % count, moved, high)
        ahead = jnp.where(slots == (layer - 2) % count, moved, ahead)
    return low, high, ahead


def corner_kernel(row_even, row_odd, rest_even, rest_odd, low_cols, high_cols, norm_last,
                  _, low_ref, high_ref, next_ref, even_ref, odd_ref, own_ref):
    cols = low_ref.shape[0]
    total = low_cols.shape[0]
    layers = (total - REACH) // REACH
    strip = layers * REACH
    from_low, from_high = sides("gx", row_even[...], row_odd[...])
    rest, _ = sides("gx", rest_even[...], rest_odd[...])
    partial, kept, limit = rest[:layers], rest[layers : 2 * layers], rest[2 * layers :]
    before = [jnp.broadcast_to(partial[layer : layer + 1], (REACH, cols)) for layer in range(layers)]
    packs = [pack_edges(before)] + [
        pack_edges([block[layer * REACH : (layer + 1) * REACH] for layer in range(layers)])
        for block in (from_low, from_high)
    ]
    low, high, ahead = (jnp.concatenate(group, axis=0) for group in zip(*packs))
    low_add = right_product(low, right_constant(low_ref[...]))
    high_add = right_product(high, right_constant(high_ref[...]))
    behind_add = right_product(ahead, right_constant(next_ref[...]))

    lanes = lane_ids((layers, cols))
    level = lax.broadcasted_iota(jnp.int32, (layers, cols), 0)
    corner_limit = jnp.where(lanes == level, limit[:, cols - 1 :], 0.0)
    corner_kept = jnp.where(lanes == layers + level, kept[:, cols - 1 :], 0.0)
    corner = jnp.sum(corner_limit + corner_kept, axis=0, keepdims=True)

    def place(base, add):
        return jnp.concatenate(
            [base[: 2 * REACH] + add[: 2 * REACH], base[2 * REACH : total - REACH],
             base[total - REACH :] + add[2 * REACH :]],
            axis=0,
        )

    low_all = place(low_cols[...], low_add)
    high_all = place(high_cols[:, :cols], high_add[:, :cols])
    last = norm_last[...]
    behind = high_add[:, cols:] + behind_add
    edges = jnp.concatenate([last[: 2 * REACH], last[total - REACH :]], axis=0)
    lanes = lane_ids(behind.shape)
    drop = jnp.where(lanes < layers, behind * edges, 0.0)
    column = place(high_cols[:, cols:], -drop)
    first = column[:REACH] + corner
    main = column[REACH:]
    quarter = strip // 4
    lanes = lane_ids((quarter, cols))
    folded = main[:quarter]
    for part in range(1, 4):
        moved = pltpu.roll(main[part * quarter : (part + 1) * quarter], part * 2 * layers, 1)
        folded = jnp.where(lanes // (2 * layers) == part, moved, folded)
    spare = jnp.zeros((REACH, cols), jnp.float32)
    extra = jnp.zeros((quarter + REACH, cols), jnp.float32)
    send(
        "gy", jnp.concatenate([low_all[REACH:, :cols], low_all[:REACH, :cols], extra, spare], axis=0),
        jnp.concatenate([high_all[REACH:], high_all[:REACH], folded, first, spare], axis=0),
        even_ref, odd_ref,
    )
    own_ref[...] = low_all[:, cols:]


def column_kernel(depth, across, row_even, row_odd, rest_even, rest_odd, threshold, norm, band_ref, _,
                  kept, kept_before, edge_low, edge_high, deep):
    layers, total, cols = across.shape

    def depth_sums(part, values):
        for layer, value in enumerate(depth_smooth(values, depth)):
            deep[layer, part, :] = value

    def step(index, carry):
        for inner in range(2):
            part = pl.ds(pl.multiple_of((2 * index + inner + 2) * REACH, REACH), REACH)
            depth_sums(part, [across[layer, part, :] for layer in range(layers)])
        return carry

    lax.fori_loop(0, (total // REACH - 3) // 2, step, 0)
    for first_row in (0, REACH, total - REACH):
        part = pl.ds(first_row, REACH)
        values = []
        for layer in range(layers):
            if first_row:
                line = pl.ds(layer * REACH, REACH)
                both = sides("gx", row_even[line, :], row_odd[line, :])
            else:
                both = sides("gx", rest_even[pl.ds(layer, 1), :], rest_odd[pl.ds(layer, 1), :])
            values.append(across[layer, part, :] + both[first_row > REACH])
        depth_sums(part, values)

    constant = right_constant(band_ref[...])
    slots = layer_slots((total, cols))
    for layer in range(layers):
        nonlocal_strain = right_product(deep[layer], constant) * norm[...]
        line = pl.ds(2 * layers + layer, 1)
        limit, _ = sides("gx", rest_even[line, :], rest_odd[line, :])
        first = limit - nonlocal_strain[:REACH]
        others = threshold[layer] - nonlocal_strain[REACH:]
        kept_before[layer] = ratio(first)
        kept[layer] = ratio(others)
        moved = jnp.concatenate([first, others], axis=0)
        moved = pltpu.roll(moved, layer * REACH, 1) if layer else moved
        pltpu.store(edge_low, moved, mask=slots == layer)
        pltpu.store(edge_high, moved, mask=slots == (layer - 1) % (cols // REACH))


def final_kernel(stress, strain, plastic, inner, inner_before, edge_low, edge_high, norm_low, norm_high,
                 col_even, col_odd, last_even, last_odd, rest_even, rest_odd, norm_before, own_cols,
                 plastic_out, damage_out, force_out, columns, lows, highs, damage_s, force_s, half, sums, diffs,
                 copy_sem, sems):
    layers, rows, cols = stress.shape
    whole = pltpu.make_async_copy(plastic, plastic_out, copy_sem)
    whole.start()
    from_low, _ = sides("gy", last_even[...], last_odd[...])
    folded = from_low[REACH : REACH + rows // 4]
    pieces = [from_low[REACH + rows // 4 :], folded]
    for part in range(1, 4):
        pieces.append(pltpu.roll(folded, cols - part * 2 * layers, 1))
    column = jnp.concatenate(pieces, axis=0)
    kept = ratio(column - own_cols[...] * norm_before[...])
    columns[...] = (0.5 * kept) * pltpu.roll(column, cols - layers, 1)

    low, high = edge_ratios(
        (edge_low, edge_high), (last_even, last_odd), (norm_low, norm_high),
        pl.ds(0, REACH), pl.ds(0, REACH),
    )
    lows[pl.ds(0, REACH), :], highs[pl.ds(0, REACH), :] = low, high
    low, high = edge_ratios(
        (edge_low, edge_high), (col_even, col_odd), (norm_low, norm_high),
        pl.ds(0, rows), pl.ds(REACH, rows),
    )
    lows[pl.ds(REACH, rows), :], highs[pl.ds(REACH, rows), :] = low, high

    def copies(layer):
        return (
            pltpu.make_async_copy(damage_s.at[layer], damage_out.at[layer], sems.at[0, layer]),
            pltpu.make_async_copy(force_s.at[0, layer], force_out.at[0, layer], sems.at[1, layer]),
            pltpu.make_async_copy(force_s.at[1, layer], force_out.at[1, layer], sems.at[2, layer]),
        )

    lanes = lane_ids((REACH, cols))

    def layers_of(pair):
        for near in range(2):
            for block in range(rows // REACH + 1):
                yield 2 * pair + near, block, pl.ds(block * REACH, REACH)

    def damages(pair):
        for layer, block, extended in layers_of(pair):
            at = (layer, pl.ds((block - 1) * REACH if block else 0, REACH), slice(None))
            if block:
                rest = (stress[at] + strain[at]) - plastic[at]
            else:
                line = pl.ds(layers + layer, 1)
                rest, _ = sides("gx", rest_even[line, :], rest_odd[line, :])
            kept = inner[at] if block else inner_before[layer]
            kept = with_edges(kept, layer, lows[extended, :], highs[extended, :])
            half[layer, extended, :] = (0.5 * kept) * rest
            if block:
                damage_s[at] = 1.0 - kept

    def neighbours(pair):
        for layer, block, extended in layers_of(pair):
            value = half[layer, extended, :]
            left = jnp.where(
                lanes == 0,
                pltpu.roll(columns[extended, :], (cols - layer) % cols, 1),
                pltpu.roll(value, 1, 1),
            )
            sums[layer, extended, :] = left + value
            diffs[layer, extended, :] = left - value

    def forces(pair):
        for near in range(2):
            layer = 2 * pair + near
            for block in range(rows // REACH):
                at = (layer, pl.ds(block * REACH, REACH), slice(None))
                here, behind = pl.ds((block + 1) * REACH, REACH), pl.ds((block + 1) * REACH - 1, REACH)
                force_s[(0, *at)] = sums[layer, behind, :] - sums[layer, here, :]
                force_s[(1, *at)] = diffs[layer, behind, :] + diffs[layer, here, :]

    def start(pair):
        for near in range(2):
            for copy in copies(2 * pair + near):
                copy.start()

    def step(pair, carry):
        forces(pair - 2)
        neighbours(pair - 1)
        damages(pair)
        start(pair - 2)
        return carry

    pairs = layers // 2
    damages(0)
    neighbours(0)
    damages(1)
    lax.fori_loop(2, pairs, step, 0)
    forces(pairs - 2)
    neighbours(pairs - 1)
    start(pairs - 2)
    forces(pairs - 1)
    start(pairs - 1)

    def drain(layer, carry):
        for copy in copies(layer):
            copy.wait()
        return carry

    lax.fori_loop(0, layers, drain, 0)
    whole.wait()


def call(kernel, outs, scratch, nanoseconds, operands, spaces=None, outs_space=pltpu.VMEM, limit=VMEM_BYTES):
    spaces = spaces or [pltpu.VMEM] * len(operands)
    shapes = [out if isinstance(out, jax.ShapeDtypeStruct) else jax.ShapeDtypeStruct(out, jnp.float32)
              for out in outs]
    return pl.pallas_call(
        kernel,
        out_shape=shapes,
        in_specs=[pl.BlockSpec(memory_space=space) for space in spaces],
        out_specs=[pl.BlockSpec(memory_space=outs_space)] * len(outs),
        scratch_shapes=[pltpu.VMEM(s, jnp.float32) if isinstance(s, tuple) else s for s in scratch],
        compiler_params=pltpu.CompilerParams(vmem_limit_bytes=limit),
        cost_estimate=pl.CostEstimate(
            flops=nanoseconds * 1_000_000, bytes_accessed=nanoseconds * 1000, transcendentals=0
        ),
    )(*operands)


def exchange(axis, other, even, odd):
    names = ("gx", "gy")
    count, across = lax.axis_size(axis), lax.axis_size(other)
    stride = {"gx": lax.axis_size("gy"), "gy": 1}
    results = []
    for start, value in ((0, even), (1, odd)):
        pairs = []
        for place in range(count):
            partner = place + 1 if (place - start) % 2 == 0 else place - 1
            for line in range(across):
                target = (partner, line)
                if not 0 <= partner < count:
                    target = (place, line ^ 1 if line ^ 1 < across else line)
                pairs.append((
                    place * stride[axis] + line * stride[other],
                    target[0] * stride[axis] + target[1] * stride[other],
                ))
        results.append(lax.ppermute(value, names, pairs))
    return results


def inverse_weights(axis, places, length):
    extent = length * lax.axis_size(axis)
    places = places + lax.axis_index(axis) * length
    total = jnp.zeros(places.shape, jnp.float32)
    for offset in range(-REACH, REACH + 1):
        inside = (places + offset >= 0) & (places + offset < extent)
        total = total + jnp.where(inside, tap(offset), 0.0)
    return 1.0 / jnp.maximum(total, tap(REACH))


def matrices(layers, rows, cols):
    depth = depth_matrix(layers)
    up, down = band(REACH, REACH, REACH), band(REACH, REACH, -REACH)
    same = np.eye(layers)
    below = np.kron(same, up)
    above = np.concatenate([np.kron(same, down), np.kron(same, band(1, REACH, 1 - REACH))], axis=0)
    rows_band = np.concatenate([np.zeros((REACH - 1, rows)), band(1, rows, 1), band(rows, rows)])
    slots = cols // REACH
    low, high, ahead = np.zeros((cols, 2 * cols)), np.zeros((cols, 2 * cols)), np.zeros((cols, cols))
    for source in range(layers):
        own = slice(source * REACH, (source + 1) * REACH)
        first = (source - 1) % slots * REACH
        other = slice(first, first + REACH)
        for layer in range(layers):
            weight = depth[layer, source]
            first = (layer - 1) % slots * REACH
            low[own, first : first + REACH] = weight * up.T
            high[other, layer * REACH : (layer + 1) * REACH] = weight * down.T
            low[own, cols + layer] = [weight * tap(j + 1) for j in range(REACH)]
            high[other, cols + layer] = [weight * tap(REACH - 1 - j) for j in range(REACH)]
            ahead[((source - 2) % slots) * REACH + REACH - 1, layer] = weight * tap(REACH)
    constants = (below, above, rows_band, band(cols, cols), low, high, ahead)
    return depth, [jnp.asarray(matrix, jnp.float32) for matrix in constants]


def local(trial_stress, old_strain, yield_mask, newton_count, damage_threshold):
    layers, rows, cols = trial_stress.shape
    assert layers * REACH == cols == rows and layers & (layers - 1) == 0
    total, strip = rows + REACH, layers * REACH
    depth, constants = matrices(layers, rows, cols)
    below, above, rows_band, cols_band, *columns = constants

    whole, wide, top = (layers, rows, cols), (layers, total, cols), (layers, REACH, cols)
    sent_rows = (strip + 3 * layers, cols)
    sent_cols = (total + rows // 4 + 2 * REACH, cols)
    last_cols = total + rows // 4 + REACH
    spare = (3 * layers, cols)
    packed, packed_two = (total, cols), (total, 2 * cols)

    inputs = stress, strain, _, _ = (trial_stress, old_strain, yield_mask, newton_count)
    threshold = damage_threshold
    edge = [pltpu.VMEM((layers, 2 * REACH, cols), value.dtype) for value in inputs]
    row_even, row_odd, norm, norm_low, norm_high, norm_last, norm_before, rest = call(
        first_edge_kernel, [(strip, cols)] * 2 + [packed] * 5 + [spare],
        edge + [(strip, cols), pltpu.SemaphoreType.DMA((2, 4))], 1500,
        inputs, [pltpu.HBM] * 4, limit=EDGE_VMEM_BYTES,
    )
    norms = (norm_low, norm_high)
    rest_even = rest_odd = rest
    for outer_no in range(OUTER):
        last = outer_no == OUTER - 1
        if outer_no:
            row_even, row_odd = call(
                edge_kernel, [sent_rows] * 2,
                [(strip, cols), (strip, cols), (2 * layers, cols)], 800,
                (*inputs, threshold, factor, kept, kept_before, edge_low, edge_high, *norms,
                 col_even, col_odd, below, above),
            )
        if not last:
            row_even, row_odd = row_even[:strip], row_odd[:strip]
        row_even, row_odd = exchange("gx", "gy", row_even, row_odd)
        if last:
            rest_even, rest_odd = row_even[strip:], row_odd[strip:]
            row_even, row_odd = row_even[:strip], row_odd[:strip]
        outs = [wide, packed_two, packed_two, whole]
        if outer_no:
            across, low_cols, high_cols, plastic = call(
                main_kernel, outs, [packed] * 5, 4500,
                (*inputs, factor, kept, edge_low, edge_high, *norms, col_even, col_odd, norm_last,
                 fixed, rows_band, *columns),
            )
        else:
            across, low_cols, high_cols, plastic, factor = call(
                first_main_kernel, outs + [whole], [packed] * 4, 4500, (*inputs, rows_band, *columns),
            )
        col_even, col_odd, own_cols = call(
            corner_kernel, [sent_cols, sent_cols, packed], [], 400,
            (row_even, row_odd, rest_even, rest_odd, low_cols, high_cols, norm_last, plastic, *columns),
        )
        if not outer_no:
            (fixed,) = call(prepare_kernel, [packed], [], 800, (stress, strain, threshold, col_odd))
        used = last_cols if last else rows
        col_even, col_odd = col_even[:used], col_odd[:used]
        col_even, col_odd = exchange("gy", "gx", col_even, col_odd)
        if last:
            last_even, last_odd = col_even[rows:], col_odd[rows:]
            col_even, col_odd = col_even[:rows], col_odd[:rows]
        kept, kept_before, edge_low, edge_high = call(
            functools.partial(column_kernel, depth), [whole, top, packed, packed], [wide], 1800,
            (across, row_even, row_odd, rest_even, rest_odd, threshold, norm, cols_band, own_cols),
        )
    return tuple(call(
        final_kernel, [whole, whole, (2, *whole)],
        [packed] * 3 + [whole, (2, *whole), wide, wide, wide,
         pltpu.SemaphoreType.DMA(()), pltpu.SemaphoreType.DMA((3, layers))],
        3000,
        (stress, strain, plastic, kept, kept_before, edge_low, edge_high, *norms, col_even, col_odd,
         last_even, last_odd, rest_even, rest_odd, norm_before, own_cols),
        outs_space=pltpu.HBM,
    ))


def solution(mesh):
    split_in = P(None, "gx", "gy")
    return jax.shard_map(
        local,
        mesh=mesh,
        in_specs=(split_in,) * 5,
        out_specs=(split_in, split_in, P(None, None, "gx", "gy")),
        check_vma=False,
    )
```

```python
import functools
import math

import jax
import jax.numpy as jnp
import numpy as np
from jax import lax
from jax.experimental import pallas as pl
from jax.experimental.pallas import tpu as pltpu
from jax.sharding import PartitionSpec as P

OUTER = 3
REACH = 8
RATE = math.log2(math.e) / 0.3
HALF_LN2 = 0.5 * math.log(2.0)
VMEM_BYTES = 24 * 1024 * 1024
EDGE_VMEM_BYTES = 53 * 1024 * 1024


def tap(offset):
    return math.exp(-(offset**2) / 32.0) if abs(offset) <= REACH else 0.0


def band(rows, cols, shift=0):
    return np.array([[tap(c - r + shift) for c in range(cols)] for r in range(rows)])


def depth_matrix(layers):
    weights = band(layers, layers)
    return weights / weights.sum(axis=1, keepdims=True)


def split(value):
    high = value.astype(jnp.bfloat16)
    low = (value - high.astype(jnp.float32)).astype(jnp.bfloat16)
    return high, low


def left_constant(matrix):
    high, low = split(matrix)
    return jnp.concatenate(
        [jnp.concatenate([high, high], axis=1), jnp.concatenate([low, low], axis=1)], axis=0
    )


def right_constant(matrix):
    both = jnp.concatenate(split(matrix), axis=1)
    return jnp.concatenate([both, both], axis=0)


def left_product(constant, value):
    rows = constant.shape[0] // 2
    halves = jnp.concatenate(split(value), axis=0)
    both = jnp.dot(constant, halves, preferred_element_type=jnp.float32)
    return both[:rows] + both[rows:]


def right_product(value, constant):
    cols = constant.shape[1] // 2
    halves = jnp.concatenate(split(value), axis=1)
    both = jnp.dot(halves, constant, preferred_element_type=jnp.float32)
    return both[:, :cols] + both[:, cols:]


def first_factor(strain):
    return 0.8 - 0.2 * jnp.tanh(2.0 * strain - HALF_LN2)


def newton(stress, strain, yields, count, kept, factor):
    top = (stress + strain) - (0.875 + 0.875 * kept)
    shift = 2.0 * top - HALF_LN2
    state = 2.0 * (top - strain)
    drop = 0.1 + 0.1 * kept
    for sweep_no in range(1, 7):
        if sweep_no > 1:
            factor = 0.8 - 0.2 * jnp.tanh(shift - state)
        update = state * factor - drop
        state = update if sweep_no <= 3 else jnp.where(count >= sweep_no, update, state)
    return jnp.where(yields > 0, top - 0.5 * state, strain)


def depth_smooth(layers, matrix):
    count = len(layers)
    half = count // 2
    sums = [layers[k] + layers[count - 1 - k] for k in range(half)]
    diffs = [layers[k] - layers[count - 1 - k] for k in range(half)]
    out = [None] * count
    for row in range(half):
        even = odd = None
        for k in range(half):
            near, far = matrix[row, k], matrix[row, count - 1 - k]
            plus, minus = float(0.5 * (near + far)), float(0.5 * (near - far))
            if plus == 0.0 and minus == 0.0:
                continue
            even = sums[k] * plus if even is None else even + sums[k] * plus
            odd = diffs[k] * minus if odd is None else odd + diffs[k] * minus
        out[row] = even + odd
        out[count - 1 - row] = even - odd
    return out


def lane_ids(shape):
    return lax.broadcasted_iota(jnp.int32, shape, len(shape) - 1)


def on_even(axis):
    return lax.axis_index(axis) % 2 == 0


def sides(axis, even, odd):
    return jnp.where(on_even(axis), odd, even), jnp.where(on_even(axis), even, odd)


def send(axis, low, high, even_ref, odd_ref):
    place = lax.axis_index(axis)
    low = jnp.where(place == 0, 0.0, low)
    high = jnp.where(place == lax.axis_size(axis) - 1, 0.0, high)
    even_ref[...] = jnp.where(on_even(axis), high, low)
    odd_ref[...] = jnp.where(on_even(axis), low, high)


def layer_slots(shape):
    return lane_ids(shape) >> (REACH.bit_length() - 1)


def ratio(limit):
    return jnp.exp2(jnp.minimum(limit, 0.0) * RATE)


def edge_ratios(edges, received, norms, part, extended):
    both = sides("gy", *(ref[part, :] for ref in received))
    return [
        ratio(edge[extended, :] - value * norm[extended, :])
        for edge, value, norm in zip(edges, both, norms)
    ]


def with_edges(inner, layer, low, high):
    cols = inner.shape[1]
    slots = layer_slots(inner.shape)
    packed = jnp.where(slots == layer, low, high)
    shift = (cols - layer * REACH) % cols
    moved = packed if isinstance(layer, int) and layer == 0 else pltpu.roll(packed, shift, 1)
    return jnp.where((slots == 0) | (slots == cols // REACH - 1), moved, inner)


def first_edge_kernel(*refs):
    sources, refs = refs[:4], refs[4:]
    even_ref, odd_ref, norm, norm_low, norm_high, norm_last, norm_before, _, *refs = refs
    targets, (block, sems) = refs[:4], refs[4:]
    stress, strain, yields, count = targets
    layers, rows, cols = sources[0].shape
    copies = []
    for side, first_row in enumerate((0, rows - REACH)):
        for index, (source, target) in enumerate(zip(sources, targets)):
            copies.append(
                pltpu.make_async_copy(
                    source.at[:, pl.ds(first_row, REACH), :],
                    target.at[:, pl.ds(side * REACH, REACH), :],
                    sems.at[side, index],
                )
            )
            copies[-1].start()
    total = rows + REACH
    ids = lax.broadcasted_iota(jnp.int32, (total, cols), 0)
    down = inverse_weights("gx", ids - REACH, rows)
    lanes = lane_ids((REACH, cols))
    within = lanes & (REACH - 1)
    places = (lanes, within, within + (cols - REACH), 0 * lanes + (cols - 1), 0 * lanes - 1)
    for ref, place in zip((norm, norm_low, norm_high, norm_last, norm_before), places):
        ref[...] = down * inverse_weights("gy", place, cols)[:1]
    square = (layers * REACH, layers * REACH)
    line, lane = lax.broadcasted_iota(jnp.int32, square, 0), lane_ids(square)
    steps = (lane & (REACH - 1)) - (line & (REACH - 1))
    band_part = jnp.zeros(square, jnp.float32)
    for step in range(REACH):
        band_part = jnp.where(abs(steps) == step, tap(REACH - step), band_part)
    band_part = jnp.where((line ^ lane) < REACH, band_part, 0.0)
    sent = []
    for side, matrix in enumerate(
        (jnp.where(steps <= 0, band_part, 0.0), jnp.where(steps >= 0, band_part, 0.0))
    ):
        for copy in copies[side * 4 : side * 4 + 4]:
            copy.wait()
        for layer in range(layers):
            at = (layer, pl.ds(side * REACH, REACH), slice(None))
            block[pl.ds(layer * REACH, REACH), :] = newton(
                stress[at], strain[at], yields[at], count[at], jnp.ones((REACH, cols), jnp.float32),
                first_factor(strain[at]),
            )
        product = left_product(left_constant(matrix), block[...])
        sent.append(jnp.concatenate([product, product[:REACH]], axis=0))
    send("gx", *sent, even_ref, odd_ref)


def edge_kernel(stress, strain, yields, count, threshold, factor, kept, _, edge_low, edge_high, norm_low,
                norm_high, col_even, col_odd, below, above,
                even_ref, odd_ref, low_block, high_block, rest):
    layers, rows, cols = stress.shape

    def packed(part, extended):
        return edge_ratios(
            (edge_low, edge_high), (col_even, col_odd), (norm_low, norm_high), part, extended
        )

    part = pl.ds(rows - 2 * REACH, REACH)
    low, high = packed(part, pl.ds(rows - REACH, REACH))
    for layer in range(layers):
        rest[pl.ds(layer, 1), :] = with_edges(kept[layer, part, :], layer, low, high)[REACH - 1 :]
    at = (slice(None), rows - REACH - 1, slice(None))
    single = newton(stress[at], strain[at], yields[at], count[at], rest[pl.ds(0, layers), :], factor[at])

    for first_row, block in ((0, low_block), (rows - REACH, high_block)):
        low, high = packed(pl.ds(first_row, REACH), pl.ds(first_row + REACH, REACH))
        for layer in range(layers):
            at = (layer, pl.ds(first_row, REACH), slice(None))
            ratios = with_edges(kept[at], layer, low, high)
            value = newton(stress[at], strain[at], yields[at], count[at], ratios, factor[at])
            block[pl.ds(layer * REACH, REACH), :] = value
            if first_row:
                left = (stress[at] + strain[at]) - value
                rest[pl.ds(layer, 1), :] = left[REACH - 1 :]
                rest[pl.ds(layers + layer, 1), :] = threshold[at][REACH - 1 :]

    low = left_product(left_constant(below[...]), low_block[...])
    high = left_product(left_constant(above[...]), high_block[...])
    strip = layers * REACH
    extra = jnp.zeros((even_ref.shape[0] - strip, cols), jnp.float32)
    send(
        "gx", jnp.concatenate([low, extra], axis=0),
        jnp.concatenate([high[:strip], high[strip:] + tap(REACH) * single, rest[...]], axis=0),
        even_ref, odd_ref,
    )


def first_main_kernel(stress, strain, yields, count, band_ref, low_ref, high_ref, next_ref,
                      across, low_cols, high_cols, plastic, factor, *packs):
    layers, rows, cols = stress.shape
    step_rows = 4 * REACH

    def step(index, carry):
        for near in range(step_rows // REACH):
            part = pl.ds(pl.multiple_of(index * step_rows + near * REACH, REACH), REACH)
            for layer in range(layers):
                at = (layer, part, slice(None))
                lead = first_factor(strain[at])
                factor[at] = lead
                plastic[at] = newton(
                    stress[at], strain[at], yields[at], count[at],
                    jnp.ones((REACH, cols), jnp.float32), lead,
                )
        return carry

    lax.fori_loop(0, rows // step_rows, step, 0)
    smooth_rows(plastic, (band_ref, low_ref, high_ref, next_ref), across, low_cols, high_cols, packs)


def main_kernel(stress, strain, yields, count, factor, kept, edge_low, edge_high, norm_low, norm_high,
                col_even, col_odd, norm_last, fixed, band_ref, low_ref, high_ref, next_ref,
                across, low_cols, high_cols, plastic, pack_last, *packs):
    layers, rows, cols = stress.shape
    total = rows + REACH
    step_rows = 4 * REACH
    lanes = lane_ids((REACH, cols))
    pack_last[pl.ds(0, REACH), :] = jnp.zeros((REACH, cols), jnp.float32)

    def step(index, carry):
        for near in range(step_rows // REACH):
            first = index * step_rows + near * REACH
            part = pl.ds(pl.multiple_of(first, REACH), REACH)
            extended = pl.ds(pl.multiple_of(first + REACH, REACH), REACH)
            packed = edge_ratios(
                (edge_low, edge_high), (col_even, col_odd), (norm_low, norm_high), part, extended
            )
            for layer in range(layers):
                at = (layer, part, slice(None))
                ratios = with_edges(kept[at], layer, *packed)
                value = newton(stress[at], strain[at], yields[at], count[at], ratios, factor[at])
                plastic[at] = value
                lane = layers + layer
                pltpu.store(pack_last.at[extended, :], pltpu.roll(value, lane + 1, 1), mask=lanes == lane)
        return carry

    lax.fori_loop(0, rows // step_rows, step, 0)
    behind = smooth_rows(
        plastic, (band_ref, low_ref, high_ref, next_ref), across, low_cols, high_cols, packs
    )
    drop = behind * norm_last[...]
    first_lanes = lane_ids((total, cols)) < layers
    high_cols[:, cols:] = fixed[...] - jnp.where(first_lanes, drop, pack_last[...])


def smooth_rows(plastic, tables, across, low_cols, high_cols, packs):
    layers, rows, cols = plastic.shape
    total = rows + REACH
    band_ref, low_ref, high_ref, next_ref = tables
    constant = left_constant(band_ref[...])
    slots = layer_slots((total, cols))
    spread = len(packs)
    for layer in range(0, layers, 2):
        pair = jnp.concatenate([plastic[layer], plastic[layer + 1]], axis=1)
        result = left_product(constant, pair)
        for inner in range(2):
            value = result[:, inner * cols : (inner + 1) * cols]
            across[layer + inner] = value
            moved = pltpu.roll(value, (layer + inner) * REACH, 1) if layer + inner else value
            mask = ((layer + inner - slots) & (layers - 1)) < 3
            pltpu.store(packs[(layer + inner) % spread], moved, mask=mask)

    def gathered(behind):
        source = (slots + behind) & (spread - 1)
        parts = packs[0][...]
        for index in range(1, spread):
            parts = jnp.where(source == index, packs[index][...], parts)
        return parts

    low_cols[...] = right_product(gathered(0), right_constant(low_ref[...]))
    high = right_product(gathered(1), right_constant(high_ref[...]))
    behind = right_product(gathered(2), right_constant(next_ref[...]))
    high_cols[:, :cols] = high[:, :cols]
    return high[:, cols:] + behind


def prepare_kernel(stress, strain, threshold, _, fixed):
    layers, rows, cols = stress.shape
    lanes = lane_ids((REACH, cols))
    fixed[...] = jnp.zeros_like(fixed)

    def step(index, carry):
        for near in range(2):
            first = (2 * index + near) * REACH
            part = pl.ds(pl.multiple_of(first, REACH), REACH)
            extended = pl.ds(pl.multiple_of(first + REACH, REACH), REACH)
            for layer in range(layers):
                at = (layer, part, slice(None))
                for lane, value in ((layer, threshold[at]), (layers + layer, stress[at] + strain[at])):
                    moved = pltpu.roll(value, lane + 1, 1)
                    pltpu.store(fixed.at[extended, :], moved, mask=lanes == lane)
        return carry

    lax.fori_loop(0, rows // (2 * REACH), step, 0)


def pack_edges(values):
    cols = values[0].shape[1]
    count = cols // REACH
    slots = layer_slots(values[0].shape)
    low = high = ahead = jnp.zeros_like(values[0])
    for layer, value in enumerate(values):
        moved = pltpu.roll(value, layer * REACH, 1) if layer else value
        low = jnp.where(slots == layer, moved, low)
        high = jnp.where(slots == (layer - 1) % count, moved, high)
        ahead = jnp.where(slots == (layer - 2) % count, moved, ahead)
    return low, high, ahead


def corner_kernel(row_even, row_odd, rest_even, rest_odd, low_cols, high_cols, norm_last,
                  _, low_ref, high_ref, next_ref, even_ref, odd_ref, own_ref):
    cols = low_ref.shape[0]
    total = low_cols.shape[0]
    layers = (total - REACH) // REACH
    strip = layers * REACH
    from_low, from_high = sides("gx", row_even[...], row_odd[...])
    rest, _ = sides("gx", rest_even[...], rest_odd[...])
    partial, kept, limit = rest[:layers], rest[layers : 2 * layers], rest[2 * layers :]
    before = [jnp.broadcast_to(partial[layer : layer + 1], (REACH, cols)) for layer in range(layers)]
    packs = [pack_edges(before)] + [
        pack_edges([block[layer * REACH : (layer + 1) * REACH] for layer in range(layers)])
        for block in (from_low, from_high)
    ]
    low, high, ahead = (jnp.concatenate(group, axis=0) for group in zip(*packs))
    low_add = right_product(low, right_constant(low_ref[...]))
    high_add = right_product(high, right_constant(high_ref[...]))
    behind_add = right_product(ahead, right_constant(next_ref[...]))

    lanes = lane_ids((layers, cols))
    level = lax.broadcasted_iota(jnp.int32, (layers, cols), 0)
    corner_limit = jnp.where(lanes == level, limit[:, cols - 1 :], 0.0)
    corner_kept = jnp.where(lanes == layers + level, kept[:, cols - 1 :], 0.0)
    corner = jnp.sum(corner_limit + corner_kept, axis=0, keepdims=True)

    def place(base, add):
        return jnp.concatenate(
            [base[: 2 * REACH] + add[: 2 * REACH], base[2 * REACH : total - REACH],
             base[total - REACH :] + add[2 * REACH :]],
            axis=0,
        )

    low_all = place(low_cols[...], low_add)
    high_all = place(high_cols[:, :cols], high_add[:, :cols])
    last = norm_last[...]
    behind = high_add[:, cols:] + behind_add
    edges = jnp.concatenate([last[: 2 * REACH], last[total - REACH :]], axis=0)
    lanes = lane_ids(behind.shape)
    drop = jnp.where(lanes < layers, behind * edges, 0.0)
    column = place(high_cols[:, cols:], -drop)
    first = column[:REACH] + corner
    main = column[REACH:]
    quarter = strip // 4
    lanes = lane_ids((quarter, cols))
    folded = main[:quarter]
    for part in range(1, 4):
        moved = pltpu.roll(main[part * quarter : (part + 1) * quarter], part * 2 * layers, 1)
        folded = jnp.where(lanes // (2 * layers) == part, moved, folded)
    spare = jnp.zeros((REACH, cols), jnp.float32)
    extra = jnp.zeros((quarter + REACH, cols), jnp.float32)
    send(
        "gy", jnp.concatenate([low_all[REACH:, :cols], low_all[:REACH, :cols], extra, spare], axis=0),
        jnp.concatenate([high_all[REACH:], high_all[:REACH], folded, first, spare], axis=0),
        even_ref, odd_ref,
    )
    own_ref[...] = low_all[:, cols:]


def column_kernel(depth, across, row_even, row_odd, rest_even, rest_odd, threshold, norm, band_ref, _,
                  plastic, kept, kept_before, edge_low, edge_high, plastic_out, deep, copy_sem):
    layers, total, cols = across.shape
    whole = pltpu.make_async_copy(plastic, plastic_out, copy_sem)
    whole.start()

    def depth_sums(part, values):
        for layer, value in enumerate(depth_smooth(values, depth)):
            deep[layer, part, :] = value

    def step(index, carry):
        for inner in range(2):
            part = pl.ds(pl.multiple_of((2 * index + inner + 2) * REACH, REACH), REACH)
            depth_sums(part, [across[layer, part, :] for layer in range(layers)])
        return carry

    lax.fori_loop(0, (total // REACH - 3) // 2, step, 0)
    for first_row in (0, REACH, total - REACH):
        part = pl.ds(first_row, REACH)
        values = []
        for layer in range(layers):
            if first_row:
                line = pl.ds(layer * REACH, REACH)
                both = sides("gx", row_even[line, :], row_odd[line, :])
            else:
                both = sides("gx", rest_even[pl.ds(layer, 1), :], rest_odd[pl.ds(layer, 1), :])
            values.append(across[layer, part, :] + both[first_row > REACH])
        depth_sums(part, values)

    constant = right_constant(band_ref[...])
    slots = layer_slots((total, cols))
    for layer in range(layers):
        nonlocal_strain = right_product(deep[layer], constant) * norm[...]
        line = pl.ds(2 * layers + layer, 1)
        limit, _ = sides("gx", rest_even[line, :], rest_odd[line, :])
        first = limit - nonlocal_strain[:REACH]
        others = threshold[layer] - nonlocal_strain[REACH:]
        kept_before[layer] = ratio(first)
        kept[layer] = ratio(others)
        moved = jnp.concatenate([first, others], axis=0)
        moved = pltpu.roll(moved, layer * REACH, 1) if layer else moved
        pltpu.store(edge_low, moved, mask=slots == layer)
        pltpu.store(edge_high, moved, mask=slots == (layer - 1) % (cols // REACH))
    whole.wait()


def final_kernel(stress, strain, plastic, inner, inner_before, edge_low, edge_high, norm_low, norm_high,
                 col_even, col_odd, last_even, last_odd, rest_even, rest_odd, norm_before, own_cols,
                 damage_out, force_out, columns, lows, highs, damage_s, force_s, half, sums, diffs,
                 sems):
    layers, rows, cols = stress.shape
    from_low, _ = sides("gy", last_even[...], last_odd[...])
    folded = from_low[REACH : REACH + rows // 4]
    pieces = [from_low[REACH + rows // 4 :], folded]
    for part in range(1, 4):
        pieces.append(pltpu.roll(folded, cols - part * 2 * layers, 1))
    column = jnp.concatenate(pieces, axis=0)
    kept = ratio(column - own_cols[...] * norm_before[...])
    columns[...] = (0.5 * kept) * pltpu.roll(column, cols - layers, 1)

    low, high = edge_ratios(
        (edge_low, edge_high), (last_even, last_odd), (norm_low, norm_high),
        pl.ds(0, REACH), pl.ds(0, REACH),
    )
    lows[pl.ds(0, REACH), :], highs[pl.ds(0, REACH), :] = low, high
    low, high = edge_ratios(
        (edge_low, edge_high), (col_even, col_odd), (norm_low, norm_high),
        pl.ds(0, rows), pl.ds(REACH, rows),
    )
    lows[pl.ds(REACH, rows), :], highs[pl.ds(REACH, rows), :] = low, high

    def copies(layer):
        return (
            pltpu.make_async_copy(damage_s.at[layer], damage_out.at[layer], sems.at[0, layer]),
            pltpu.make_async_copy(force_s.at[0, layer], force_out.at[0, layer], sems.at[1, layer]),
            pltpu.make_async_copy(force_s.at[1, layer], force_out.at[1, layer], sems.at[2, layer]),
        )

    lanes = lane_ids((REACH, cols))

    def layers_of(pair):
        for near in range(2):
            for block in range(rows // REACH + 1):
                yield 2 * pair + near, block, pl.ds(block * REACH, REACH)

    def damages(pair):
        for layer, block, extended in layers_of(pair):
            at = (layer, pl.ds((block - 1) * REACH if block else 0, REACH), slice(None))
            if block:
                rest = (stress[at] + strain[at]) - plastic[at]
            else:
                line = pl.ds(layers + layer, 1)
                rest, _ = sides("gx", rest_even[line, :], rest_odd[line, :])
            kept = inner[at] if block else inner_before[layer]
            kept = with_edges(kept, layer, lows[extended, :], highs[extended, :])
            half[layer, extended, :] = (0.5 * kept) * rest
            if block:
                damage_s[at] = 1.0 - kept

    def neighbours(pair):
        for layer, block, extended in layers_of(pair):
            value = half[layer, extended, :]
            left = jnp.where(
                lanes == 0,
                pltpu.roll(columns[extended, :], (cols - layer) % cols, 1),
                pltpu.roll(value, 1, 1),
            )
            sums[layer, extended, :] = left + value
            diffs[layer, extended, :] = left - value

    def forces(pair):
        for near in range(2):
            layer = 2 * pair + near
            for block in range(rows // REACH):
                at = (layer, pl.ds(block * REACH, REACH), slice(None))
                here, behind = pl.ds((block + 1) * REACH, REACH), pl.ds((block + 1) * REACH - 1, REACH)
                force_s[(0, *at)] = sums[layer, behind, :] - sums[layer, here, :]
                force_s[(1, *at)] = diffs[layer, behind, :] + diffs[layer, here, :]

    def start(pair):
        for near in range(2):
            for copy in copies(2 * pair + near):
                copy.start()

    def step(pair, carry):
        forces(pair - 2)
        neighbours(pair - 1)
        damages(pair)
        start(pair - 2)
        return carry

    pairs = layers // 2
    damages(0)
    neighbours(0)
    damages(1)
    lax.fori_loop(2, pairs, step, 0)
    forces(pairs - 2)
    neighbours(pairs - 1)
    start(pairs - 2)
    forces(pairs - 1)
    start(pairs - 1)

    def drain(layer, carry):
        for copy in copies(layer):
            copy.wait()
        return carry

    lax.fori_loop(0, layers, drain, 0)


def call(kernel, outs, scratch, nanoseconds, operands, spaces=None, outs_space=None, limit=VMEM_BYTES):
    spaces = spaces or [pltpu.VMEM] * len(operands)
    outs_space = outs_space or [pltpu.VMEM] * len(outs)
    shapes = [out if isinstance(out, jax.ShapeDtypeStruct) else jax.ShapeDtypeStruct(out, jnp.float32)
              for out in outs]
    return pl.pallas_call(
        kernel,
        out_shape=shapes,
        in_specs=[pl.BlockSpec(memory_space=space) for space in spaces],
        out_specs=[pl.BlockSpec(memory_space=space) for space in outs_space],
        scratch_shapes=[pltpu.VMEM(s, jnp.float32) if isinstance(s, tuple) else s for s in scratch],
        compiler_params=pltpu.CompilerParams(vmem_limit_bytes=limit),
        cost_estimate=pl.CostEstimate(
            flops=nanoseconds * 1_000_000, bytes_accessed=nanoseconds * 1000, transcendentals=0
        ),
    )(*operands)


def exchange(axis, other, even, odd):
    names = ("gx", "gy")
    count, across = lax.axis_size(axis), lax.axis_size(other)
    stride = {"gx": lax.axis_size("gy"), "gy": 1}
    results = []
    for start, value in ((0, even), (1, odd)):
        pairs = []
        for place in range(count):
            partner = place + 1 if (place - start) % 2 == 0 else place - 1
            for line in range(across):
                target = (partner, line)
                if not 0 <= partner < count:
                    target = (place, line ^ 1 if line ^ 1 < across else line)
                pairs.append((
                    place * stride[axis] + line * stride[other],
                    target[0] * stride[axis] + target[1] * stride[other],
                ))
        results.append(lax.ppermute(value, names, pairs))
    return results


def inverse_weights(axis, places, length):
    extent = length * lax.axis_size(axis)
    places = places + lax.axis_index(axis) * length
    total = jnp.zeros(places.shape, jnp.float32)
    for offset in range(-REACH, REACH + 1):
        inside = (places + offset >= 0) & (places + offset < extent)
        total = total + jnp.where(inside, tap(offset), 0.0)
    return 1.0 / jnp.maximum(total, tap(REACH))


def matrices(layers, rows, cols):
    depth = depth_matrix(layers)
    up, down = band(REACH, REACH, REACH), band(REACH, REACH, -REACH)
    same = np.eye(layers)
    below = np.kron(same, up)
    above = np.concatenate([np.kron(same, down), np.kron(same, band(1, REACH, 1 - REACH))], axis=0)
    rows_band = np.concatenate([np.zeros((REACH - 1, rows)), band(1, rows, 1), band(rows, rows)])
    slots = cols // REACH
    low, high, ahead = np.zeros((cols, 2 * cols)), np.zeros((cols, 2 * cols)), np.zeros((cols, cols))
    for source in range(layers):
        own = slice(source * REACH, (source + 1) * REACH)
        first = (source - 1) % slots * REACH
        other = slice(first, first + REACH)
        for layer in range(layers):
            weight = depth[layer, source]
            first = (layer - 1) % slots * REACH
            low[own, first : first + REACH] = weight * up.T
            high[other, layer * REACH : (layer + 1) * REACH] = weight * down.T
            low[own, cols + layer] = [weight * tap(j + 1) for j in range(REACH)]
            high[other, cols + layer] = [weight * tap(REACH - 1 - j) for j in range(REACH)]
            ahead[((source - 2) % slots) * REACH + REACH - 1, layer] = weight * tap(REACH)
    constants = (below, above, rows_band, band(cols, cols), low, high, ahead)
    return depth, [jnp.asarray(matrix, jnp.float32) for matrix in constants]


def local(trial_stress, old_strain, yield_mask, newton_count, damage_threshold):
    layers, rows, cols = trial_stress.shape
    assert layers * REACH == cols == rows and layers & (layers - 1) == 0
    total, strip = rows + REACH, layers * REACH
    depth, constants = matrices(layers, rows, cols)
    below, above, rows_band, cols_band, *columns = constants

    whole, wide, top = (layers, rows, cols), (layers, total, cols), (layers, REACH, cols)
    sent_rows = (strip + 3 * layers, cols)
    sent_cols = (total + rows // 4 + 2 * REACH, cols)
    last_cols = total + rows // 4 + REACH
    spare = (3 * layers, cols)
    packed, packed_two = (total, cols), (total, 2 * cols)

    inputs = stress, strain, _, _ = (trial_stress, old_strain, yield_mask, newton_count)
    threshold = damage_threshold
    edge = [pltpu.VMEM((layers, 2 * REACH, cols), value.dtype) for value in inputs]
    row_even, row_odd, norm, norm_low, norm_high, norm_last, norm_before, rest = call(
        first_edge_kernel, [(strip + REACH, cols)] * 2 + [packed] * 5 + [spare],
        edge + [(strip, cols), pltpu.SemaphoreType.DMA((2, 4))], 1500,
        inputs, [pltpu.HBM] * 4, limit=EDGE_VMEM_BYTES,
    )
    norms = (norm_low, norm_high)
    rest_even = rest_odd = rest
    for outer_no in range(OUTER):
        last = outer_no == OUTER - 1
        if outer_no:
            row_even, row_odd = call(
                edge_kernel, [sent_rows] * 2,
                [(strip, cols), (strip, cols), (2 * layers, cols)], 800,
                (*inputs, threshold, factor, kept, kept_before, edge_low, edge_high, *norms,
                 col_even, col_odd, below, above),
            )
        if not last:
            row_even, row_odd = row_even[:strip], row_odd[:strip]
        row_even, row_odd = exchange("gx", "gy", row_even, row_odd)
        if last:
            rest_even, rest_odd = row_even[strip:], row_odd[strip:]
            row_even, row_odd = row_even[:strip], row_odd[:strip]
        outs = [wide, packed_two, packed_two, whole]
        if outer_no:
            across, low_cols, high_cols, plastic = call(
                main_kernel, outs, [packed] * 5, 4500,
                (*inputs, factor, kept, edge_low, edge_high, *norms, col_even, col_odd, norm_last,
                 fixed, rows_band, *columns),
            )
        else:
            across, low_cols, high_cols, plastic, factor = call(
                first_main_kernel, outs + [whole], [packed] * 4, 4500, (*inputs, rows_band, *columns),
            )
        col_even, col_odd, own_cols = call(
            corner_kernel, [sent_cols, sent_cols, packed], [], 400,
            (row_even, row_odd, rest_even, rest_odd, low_cols, high_cols, norm_last, plastic, *columns),
        )
        if not outer_no:
            (fixed,) = call(prepare_kernel, [packed], [], 800, (stress, strain, threshold, col_odd))
        used = last_cols if last else rows
        col_even, col_odd = col_even[:used], col_odd[:used]
        col_even, col_odd = exchange("gy", "gx", col_even, col_odd)
        if last:
            last_even, last_odd = col_even[rows:], col_odd[rows:]
            col_even, col_odd = col_even[:rows], col_odd[:rows]
        kept, kept_before, edge_low, edge_high, plastic_out = call(
            functools.partial(column_kernel, depth), [whole, top, packed, packed, whole],
            [wide, pltpu.SemaphoreType.DMA(())], 1800,
            (across, row_even, row_odd, rest_even, rest_odd, threshold, norm, cols_band, own_cols,
             plastic),
            outs_space=[pltpu.VMEM] * 4 + [pltpu.HBM],
        )
    damage, force = call(
        final_kernel, [whole, (2, *whole)],
        [packed] * 3 + [whole, (2, *whole), wide, wide, wide,
         pltpu.SemaphoreType.DMA((3, layers))],
        3000,
        (stress, strain, plastic, kept, kept_before, edge_low, edge_high, *norms, col_even, col_odd,
         last_even, last_odd, rest_even, rest_odd, norm_before, own_cols),
        outs_space=[pltpu.HBM] * 2,
    )
    return plastic_out, damage, force


def solution(mesh):
    split_in = P(None, "gx", "gy")
    return jax.shard_map(
        local,
        mesh=mesh,
        in_specs=(split_in,) * 5,
        out_specs=(split_in, split_in, P(None, None, "gx", "gy")),
        check_vma=False,
    )
```
